32 devices in a mesh: gx: 4 (over y, core), gy: 8 (over z, x).
Axes of the slice: x: 2, y: 2, z: 4, core: 2. Of those that a mesh axis runs over, the one named last changes fastest.
Arguments:
- field: float32 [8, 2048, 2048], P(None, 'gy', 'gx'), may hold values from -6 to 6
- row_scale: float32 [2048], replicated, may hold values from 0.5 to 2
- col_scale: float32 [2048], P('gx'), may hold values from 0.5 to 2
- row_rate: float32 [2048], replicated, may hold values from 0.2 to 1
- col_shift: float32 [2048], P('gx'), may hold values from -1 to 1
- col_mix: float32 [2048], P('gx'), may hold values from -1 to 1
Outputs:
- latent: float32 [2, 8, 2048, 2048], P(None, 'gy', None, 'gx')
- loglik: float32 [], replicated
The draws below stay inside these ranges and needn't reach their ends.
All inputs are finite; a program needn't handle non-finite values.
Results may differ from the reference program's by a relative error of at most 0.000075.
Values sent between devices are 32-bit elements; how exact they have to be, the bound alone decides.
No kernel may reach another device: no remote copies, remote signals or barrier semaphores. Data moves between devices by JAX's collectives and lax.ppermute only.
A program may use at most 128 MiB of HBM per device.

```python
import math
import jax
import jax.numpy as jnp
import numpy as np

NX = 2048
NY = 2048
ZW = 8
N_GX = 4


def block_scale(own_key, dims, split, low, top_value):
    factor_of, own = 1.0, jax.random.fold_in(own_key, 6)
    for dim, parts in split:
        heights = jnp.exp(jax.random.uniform(jax.random.fold_in(own, dim), (parts,), jnp.float32, low / len(split), top_value / len(split)))
        factor_of = factor_of * jnp.repeat(heights, dims[dim] // parts).reshape([-1 if axis == dim else 1 for axis in range(len(dims))])
    return factor_of


def centred(rng, shape, scale, most, cuts=(), kind=jnp.bfloat16):
    drawn = scale * jax.random.normal(rng, shape, jnp.float32)
    if cuts:
        drawn = drawn * block_scale(rng, shape, cuts, -0.22, 0.18)
    return jnp.clip(drawn, -most, most).astype(kind)


def setup_inputs(seed: int = 0) -> dict:
    key_list = jax.random.split(jax.random.key(seed), 7)
    return {
        "field": centred(key_list[0], (ZW, NY, NX), 1.0, 6.0, ((1, 8), (2, 4)), jnp.float32),
        "row_scale": jnp.clip(jnp.exp(jax.random.uniform(key_list[1], (NY,), jnp.float32, math.log(0.5), math.log(2.0))), 0.5, 2.0),
        "col_scale": jnp.clip(jnp.exp(math.log(2.0) - 1.3862944 * jax.random.uniform(key_list[2], (NX,), jnp.float32) ** block_scale(key_list[2], (NX,), ((0, 4),), -0.2, 0.2)), 0.5, 2.0),
        "row_rate": jnp.clip(jax.random.uniform(key_list[3], (NY,), jnp.float32, 0.2, 1.0), 0.2, 1.0),
        "col_shift": jnp.clip(jax.random.uniform(key_list[4], (NX,), jnp.float32, -1.0, 1.0) * block_scale(key_list[4], (NX,), ((0, 4),), -0.4, 0.0), -1.0, 1.0),
        "col_mix": jnp.clip(jax.random.uniform(key_list[5], (NX,), jnp.float32, -1.0, 1.0) * block_scale(key_list[5], (NX,), ((0, 4),), -0.4, 0.0), -1.0, 1.0),
    }


def column_order(total_cols, groups):
    levels = groups.bit_length() - 1
    width = total_cols // groups
    column = np.arange(total_cols)
    block = column // width
    flipped = block * 0
    for place in range(levels):
        flipped = flipped + (block >> place & 1) * (1 << levels - 1 - place)
    return flipped + groups * (column % width)

def reference(field, row_scale, col_scale, row_rate, col_shift, col_mix):
    spectrum = jnp.fft.fft(jnp.fft.fft(field, axis=2), axis=1)
    spectrum = spectrum[:, :, column_order(NX, N_GX)]
    norm_factor = 1.0 / math.sqrt(NX * NY)
    scale = row_scale[None, :, None] * col_scale[None, None, :]
    latent_u = jnp.real(spectrum) * norm_factor * scale
    latent_v = jnp.imag(spectrum) * norm_factor * scale
    log_scale = row_rate[None, :, None] * jnp.tanh(latent_u + col_shift[None, None, :])
    latent_w = latent_v * jnp.exp(log_scale) + col_mix[None, None, :] * latent_u
    terms = -0.5 * (latent_u * latent_u + latent_w * latent_w) - math.log(2.0 * math.pi) + log_scale + 2.0 * jnp.log(scale)
    loglik = jnp.sum(terms) / (ZW * NY * NX)
    return (jnp.stack([latent_u, latent_w]), loglik)
```

```python
import math

import jax
import jax.numpy as jnp
from jax import lax
from jax.sharding import PartitionSpec as P

precision_top = lax.Precision.HIGHEST
precision_mid = lax.Precision.HIGH


def from_partner(value, axis, stride):
    mask = 2**stride
    pairs = [(source, source ^ mask) for source in range(lax.axis_size(axis))]
    return lax.ppermute(value, axis, pairs)


def reverse_bits(value, count):
    result = value * 0
    for place in range(count):
        result = result + (value >> place & 1) * (1 << count - 1 - place)
    return result


def root_table(row_index, freqs, length):
    phase = row_index[:, None] * freqs[None, :] % length
    angle = phase.astype(jnp.float32) * (-2.0 * math.pi / length)
    return (jnp.cos(angle), jnp.sin(angle))


def complex_einsum(form, real_part, imag_part, cos_part, sin_part, precision=precision_top):
    first = jnp.einsum(form, real_part, cos_part, precision=precision)
    second = jnp.einsum(form, real_part, sin_part, precision=precision)
    first = first - jnp.einsum(form, imag_part, sin_part, precision=precision)
    second = second + jnp.einsum(form, imag_part, cos_part, precision=precision)
    return (first, second)


def x_tables(width, devices, position):
    levels = devices.bit_length() - 1
    local_index = jnp.arange(width, dtype=jnp.int32)
    freqs = reverse_bits(position, levels) + devices * local_index
    return root_table(local_index, freqs, devices * width)


def x_butterfly(field):
    devices = lax.axis_size("gx")
    levels = devices.bit_length() - 1
    position = lax.axis_index("gx")
    real_part, imag_part = field, jnp.zeros_like(field)
    for level in range(levels - 1, -1, -1):
        half = 1 << level
        lower = position // half % 2 == 0
        offset = position % half
        angle = offset.astype(jnp.float32) * (-math.pi / half)
        cos_twist = jnp.where(lower, 1.0, jnp.cos(angle))
        sin_twist = jnp.where(lower, 0.0, jnp.sin(angle))
        other = from_partner(jnp.stack([real_part, imag_part]), "gx", level)
        diff_real = jnp.where(lower, real_part + other[0], other[0] - real_part)
        diff_imag = jnp.where(lower, imag_part + other[1], other[1] - imag_part)
        real_part = diff_real * cos_twist - diff_imag * sin_twist
        imag_part = diff_real * sin_twist + diff_imag * cos_twist
    cos_part, sin_part = x_tables(field.shape[2], devices, position)
    real_part, imag_part = complex_einsum("zyn,nk->zyk", real_part, imag_part, cos_part, sin_part)
    return (to_planes(real_part), to_planes(imag_part))


def to_planes(values):
    return lax.all_to_all(values, "gy", split_axis=0, concat_axis=1, tiled=True)


def x_four(field):
    position = lax.axis_index("gx")
    half = field.shape[2] // 2
    sign = jnp.where(position < 2, 1.0, -1.0)
    first, second = field[:, :, :half], field[:, :, half:]
    first = from_partner(first, "gx", 1) + sign * first
    second = to_planes(second)
    first = to_planes(first)
    second = from_partner(second, "gx", 1) + sign * second
    parts = []
    for own in (first, second):
        other = from_partner(own, "gx", 0)
        own_real = jnp.array([1.0, -1.0, 1.0, 0.0])[position]
        other_real = jnp.array([1.0, 1.0, 0.0, 1.0])[position]
        own_imag = jnp.array([0.0, 0.0, 0.0, 1.0])[position]
        other_imag = jnp.array([0.0, 0.0, -1.0, 0.0])[position]
        parts.append((own * own_real + other * other_real, own * own_imag + other * other_imag))
    real_part = jnp.concatenate([parts[0][0], parts[1][0]], axis=2)
    imag_part = jnp.concatenate([parts[0][1], parts[1][1]], axis=2)
    cos_part, sin_part = x_tables(field.shape[2], 4, position)
    return complex_einsum("zyn,nk->zyk", real_part, imag_part, cos_part, sin_part, precision_mid)


def y_transform(real_part, imag_part):
    planes, length, width = real_part.shape
    outer = 1 << (length.bit_length() - 1) // 2
    inner = length // outer
    outer_index = jnp.arange(outer, dtype=jnp.int32)
    inner_index = jnp.arange(inner, dtype=jnp.int32)
    cos_one, sin_one = root_table(outer_index, outer_index, outer)
    cos_two, sin_two = root_table(inner_index, inner_index, inner)
    cos_mid, sin_mid = root_table(outer_index, inner_index, length)
    shaped_real = real_part.reshape(planes, outer, inner, width)
    shaped_imag = imag_part.reshape(planes, outer, inner, width)
    step_real, step_imag = complex_einsum(
        "zabc,ak->zkbc", shaped_real, shaped_imag, cos_one, sin_one, precision_mid
    )
    twist_cos = cos_mid[None, :, :, None]
    twist_sin = sin_mid[None, :, :, None]
    turned_real = step_real * twist_cos - step_imag * twist_sin
    turned_imag = step_real * twist_sin + step_imag * twist_cos
    final_real, final_imag = complex_einsum(
        "zkbc,bj->zjkc", turned_real, turned_imag, cos_two, sin_two, precision_mid
    )
    return (final_real.reshape(planes, length, width), final_imag.reshape(planes, length, width))


def per_device(field, row_scale, col_scale, row_rate, col_shift, col_mix):
    x_transform = x_four if lax.axis_size("gx") == 4 else x_butterfly
    real_part, imag_part = x_transform(field)
    spec_real, spec_imag = y_transform(real_part, imag_part)
    length = spec_real.shape[1]
    total_cols = spec_real.shape[2] * lax.axis_size("gx")
    norm_factor = 1.0 / math.sqrt(length * total_cols)
    scale = row_scale[None, :, None] * col_scale[None, None, :]
    latent_u = spec_real * norm_factor * scale
    latent_v = spec_imag * norm_factor * scale
    log_scale = row_rate[None, :, None] * jnp.tanh(latent_u + col_shift[None, None, :])
    latent_w = latent_v * jnp.exp(log_scale) + col_mix[None, None, :] * latent_u
    terms = (
        -0.5 * (latent_u * latent_u + latent_w * latent_w)
        - math.log(2.0 * math.pi)
        + log_scale
        + 2.0 * jnp.log(scale)
    )
    total_sum = lax.psum(jnp.sum(terms), ("gx", "gy"))
    mode_count = spec_real.size * lax.axis_size("gx") * lax.axis_size("gy")
    loglik = total_sum / mode_count
    return (jnp.stack([latent_u, latent_w]), loglik)


def solution(mesh):
    return jax.shard_map(
        per_device,
        mesh=mesh,
        in_specs=(P(None, "gy", "gx"), P(), P("gx"), P(), P("gx"), P("gx")),
        out_specs=(P(None, "gy", None, "gx"), P()),
        check_vma=False,
    )
```

```python
import functools
import math

import jax
import jax.numpy as jnp
from jax import lax
from jax.experimental import pallas as pl
from jax.experimental.pallas import tpu as pltpu
from jax.sharding import PartitionSpec as P

precision_top = lax.Precision.HIGHEST
RADIX = 8
VMEM_BYTES = 40 * 1024 * 1024


def from_partner(value, axis, stride):
    mask = 2**stride
    pairs = [(source, source ^ mask) for source in range(lax.axis_size(axis))]
    return lax.ppermute(value, axis, pairs)


def to_planes(values):
    return lax.all_to_all(values, "gy", split_axis=0, concat_axis=1, tiled=True)


def reverse_bits(value, count):
    result = value * 0
    for place in range(count):
        result = result + (value >> place & 1) * (1 << count - 1 - place)
    return result


def root_table(row_index, freqs, length):
    phase = row_index[:, None] * freqs[None, :] % length
    angle = phase.astype(jnp.float32) * (-2.0 * math.pi / length)
    return (jnp.cos(angle), jnp.sin(angle))


def x_tables(width, devices, position):
    levels = devices.bit_length() - 1
    local_index = jnp.arange(width, dtype=jnp.int32)
    freqs = reverse_bits(position, levels) + devices * local_index
    return root_table(local_index, freqs, devices * width)


def split_table(table):
    high = lax.reduce_precision(table, 8, 7)
    return jnp.stack([high.astype(jnp.bfloat16), (table - high).astype(jnp.bfloat16)])


def split_value(value):
    high = value.astype(jnp.bfloat16)
    return high, (value - high.astype(jnp.float32)).astype(jnp.bfloat16)


def small_fft(values):
    count = len(values)
    if count == 1:
        return values
    even, odd = small_fft(values[0::2]), small_fft(values[1::2])
    first, second = [], []
    root_half = math.sqrt(0.5)
    for place in range(count // 2):
        (er, ei), (re, im) = even[place], odd[place]
        turn = place * 8 // count
        if turn == 1:
            re, im = (re + im) * root_half, (im - re) * root_half
        elif turn == 2:
            re, im = im, -re
        elif turn == 3:
            re, im = (im - re) * root_half, (re + im) * -root_half
        first.append((er + re, ei + im))
        second.append((er - re, ei - im))
    return first + second


def dot(left, right):
    return jnp.dot(left, right, preferred_element_type=jnp.float32)


def dot_split(left_high, left_low, right_high, right_low):
    return dot(left_high, right_high) + (dot(left_high, right_low) + dot(left_low, right_high))


def y_kernel(count, coef_ref, *refs):
    inputs, (table_ref, twist_ref, out_ref, high_ref, low_ref, step_ref) = refs[:count], refs[count:]
    length, width = inputs[0].shape
    inner = length // RADIX
    for s in range(RADIX):
        parts = [ref[pl.ds(s, inner, stride=RADIX), :] for ref in inputs]
        for which in range(2):
            mixed = parts[0] * coef_ref[which, 0]
            for place in range(1, count):
                mixed = mixed + parts[place] * coef_ref[which, place]
            high, low = split_value(mixed)
            rows, cols = pl.ds(which * inner, inner), pl.ds(s * width, width)
            high_ref[rows, cols] = high
            low_ref[rows, cols] = low
    piece = 2 * width

    @pl.loop(0, RADIX * width // piece)
    def _(block):
        cols = pl.ds(pl.multiple_of(block * piece, piece), piece)
        step_ref[:, cols] = dot_split(table_ref[0], table_ref[1], high_ref[:, cols], low_ref[:, cols])

    rows_each = 16

    @pl.loop(0, inner // rows_each)
    def _(block):
        start = pl.multiple_of(block * rows_each, rows_each)
        values = []
        for s in range(RADIX):
            cols = pl.ds(s * width, width)
            re = step_ref[pl.ds(start, rows_each), cols]
            im = step_ref[pl.ds(pl.multiple_of(start + inner, rows_each), rows_each), cols]
            if s:
                cos, sin = twist_ref[0, s, pl.ds(start, rows_each), :], twist_ref[1, s, pl.ds(start, rows_each), :]
                re, im = re * cos - im * sin, re * sin + im * cos
            values.append((re, im))
        for kb, pair in enumerate(small_fft(values)):
            rows = pl.ds(pl.multiple_of(kb * inner + start, rows_each), rows_each)
            for which in range(2):
                high, low = split_value(pair[which])
                out_ref[2 * which, rows, :] = high
                out_ref[2 * which + 1, rows, :] = low


def y_dft(inputs, coefs, table, twist):
    count = len(inputs)
    length, width = inputs[0].shape
    inner = length // RADIX
    whole = pl.BlockSpec(memory_space=pltpu.VMEM)
    return pl.pallas_call(
        functools.partial(y_kernel, count),
        out_shape=jax.ShapeDtypeStruct((4, length, width), jnp.bfloat16),
        in_specs=[pl.BlockSpec(memory_space=pltpu.SMEM)] + [whole] * (count + 2),
        out_specs=whole,
        scratch_shapes=[
            pltpu.VMEM((2 * inner, RADIX * width), jnp.bfloat16),
            pltpu.VMEM((2 * inner, RADIX * width), jnp.bfloat16),
            pltpu.VMEM((2 * inner, RADIX * width), jnp.float32),
        ],
        compiler_params=pltpu.CompilerParams(vmem_limit_bytes=VMEM_BYTES),
        cost_estimate=pl.CostEstimate(
            flops=24 * inner * length * width, bytes_accessed=4 * length * width * (count + 3), transcendentals=0
        ),
        name="y_dft",
    )(coefs, *inputs, table, twist)


def x_product(parts, table_ref):
    high = jnp.concatenate([ref[which] for ref in parts for which in (0, 2)], axis=1)
    low = jnp.concatenate([ref[which] for ref in parts for which in (1, 3)], axis=1)
    return dot_split(high, low, table_ref[0], table_ref[1])


def x_first_kernel(count, *refs):
    parts, (table_ref, out_ref) = refs[:count], refs[count:]
    out_ref[...] = x_product(parts, table_ref)


def x_first(parts, table):
    count = len(parts)
    _, length, width = parts[0].shape
    columns = table.shape[2]
    rows = 256
    return pl.pallas_call(
        functools.partial(x_first_kernel, count),
        out_shape=jax.ShapeDtypeStruct((length, columns), jnp.float32),
        grid=(length // rows,),
        in_specs=[pl.BlockSpec((4, rows, width), lambda i: (0, i, 0))] * count
        + [pl.BlockSpec(table.shape, lambda i: (0, 0, 0))],
        out_specs=pl.BlockSpec((rows, columns), lambda i: (i, 0)),
        compiler_params=pltpu.CompilerParams(vmem_limit_bytes=VMEM_BYTES),
        cost_estimate=pl.CostEstimate(
            flops=12 * count * length * width * columns, bytes_accessed=8 * length * columns, transcendentals=0
        ),
        name="x_first",
    )(*parts, table)


def x_last_kernel(count, *refs):
    parts, (table_ref, sum_ref, row_ref, col_ref, out_ref, total_ref) = refs[:count], refs[count:]
    spec = sum_ref[...] + x_product(parts, table_ref)
    columns = spec.shape[1] // 2
    lanes = row_ref.shape[2]
    total = None
    for tile in range(columns // lanes):
        cols = pl.ds(tile * lanes, lanes)
        col_scale, col_shift, col_mix = col_ref[0:1, cols], col_ref[1:2, cols], col_ref[2:3, cols]
        scale = row_ref[0] * col_scale
        latent_u = spec[:, tile * lanes : (tile + 1) * lanes] * scale
        latent_v = spec[:, columns + tile * lanes : columns + (tile + 1) * lanes] * scale
        log_scale = row_ref[1] * jnp.tanh(latent_u + col_shift)
        latent_w = latent_v * jnp.exp(log_scale) + col_mix * latent_u
        out_ref[0, 0, :, cols] = latent_u
        out_ref[1, 0, :, cols] = latent_w
        terms = log_scale - 0.5 * (latent_u * latent_u + latent_w * latent_w)
        terms = jnp.sum(terms.reshape(-1, 8, lanes), axis=0)
        total = terms if total is None else total + terms

    @pl.when(pl.program_id(0) == 0)
    def _():
        total_ref[...] = jnp.zeros_like(total_ref)

    total_ref[...] += total


def x_last(parts, table, sums, row_pair, col_trio):
    count = len(parts)
    _, length, width = parts[0].shape
    columns = table.shape[2]
    rows = 256
    return pl.pallas_call(
        functools.partial(x_last_kernel, count),
        out_shape=(
            jax.ShapeDtypeStruct((2, 1, length, columns // 2), jnp.float32),
            jax.ShapeDtypeStruct((8, row_pair.shape[2]), jnp.float32),
        ),
        grid=(length // rows,),
        in_specs=[pl.BlockSpec((4, rows, width), lambda i: (0, i, 0))] * count
        + [
            pl.BlockSpec(table.shape, lambda i: (0, 0, 0)),
            pl.BlockSpec((rows, columns), lambda i: (i, 0)),
            pl.BlockSpec((2, rows, row_pair.shape[2]), lambda i: (0, i, 0)),
            pl.BlockSpec(col_trio.shape, lambda i: (0, 0)),
        ],
        out_specs=(
            pl.BlockSpec((2, 1, rows, columns // 2), lambda i: (0, 0, i, 0)),
            pl.BlockSpec((8, row_pair.shape[2]), lambda i: (0, 0)),
        ),
        compiler_params=pltpu.CompilerParams(vmem_limit_bytes=VMEM_BYTES),
        cost_estimate=pl.CostEstimate(
            flops=12 * count * length * width * columns,
            bytes_accessed=12 * length * columns,
            transcendentals=length * columns,
        ),
        name="x_last",
    )(*parts, table, sums, row_pair, col_trio)


def sum_everywhere(tile):
    axes = ("gx", "gy")
    devices = lax.axis_size("gx") * lax.axis_size("gy")
    copies = jnp.broadcast_to(tile[None], (devices,) + tile.shape)
    return jnp.sum(lax.all_to_all(copies, axes, split_axis=0, concat_axis=0, tiled=True))


def four_way(field, row_scale, col_scale, row_rate, col_shift, col_mix):
    position = lax.axis_index("gx")
    planes, rows, columns = field.shape
    length, width = planes * rows, columns // 4
    cuts = lax.optimization_barrier(tuple(field[:, :, c * width : (c + 1) * width] for c in range(4)))
    sign = jnp.where(position < 2, 1.0, -1.0)

    own_real = jnp.where(position == 1, -1.0, jnp.where(position == 3, 0.0, 1.0))
    other_real = jnp.where(position == 2, 0.0, 1.0)
    own_imag = jnp.where(position == 3, 1.0, 0.0)
    other_imag = jnp.where(position == 2, -1.0, 0.0)
    coefs_a = jnp.stack([own_real, other_real, own_imag, other_imag]).reshape(2, 2)
    coefs_b = jnp.concatenate([coefs_a, coefs_a * sign], axis=1)

    inner = length // RADIX
    index = jnp.arange(inner, dtype=jnp.int32)
    cos, sin = root_table(index, index, inner)
    y_table = split_table(jnp.concatenate([jnp.concatenate([cos, -sin], 1), jnp.concatenate([sin, cos], 1)], 0))
    cos, sin = root_table(jnp.arange(RADIX, dtype=jnp.int32), index, length)
    twist = jnp.broadcast_to(jnp.stack([cos, sin])[:, :, :, None], (2, RADIX, inner, width))
    cos, sin = x_tables(columns, 4, position)
    real_rows, imag_rows = jnp.concatenate([cos, sin], 1), jnp.concatenate([-sin, cos], 1)

    def x_table(chunks):
        spans = [slice(c * width, (c + 1) * width) for c in chunks]
        return split_table(jnp.concatenate([rows[s] for s in spans for rows in (real_rows, imag_rows)], 0))

    norm = 1.0 / math.sqrt(length * columns * 4)
    row_pair = jnp.broadcast_to(jnp.stack([row_scale * norm, row_rate])[:, :, None], (2, length, 128))
    col_trio = jnp.stack([col_scale, col_shift, col_mix])
    fixed = 2.0 * (columns * jnp.sum(jnp.log(row_scale)) + length * jnp.sum(jnp.log(col_scale)))
    fixed = fixed - length * columns * math.log(2.0 * math.pi)

    first_a = [from_partner(cuts[c], "gx", 1) + sign * cuts[c] for c in (0, 1)]
    first_b = [to_planes(cuts[c])[0] for c in (2, 3)]
    second_a = [to_planes(value)[0] for value in first_a]
    second_b = [from_partner(value, "gx", 1) for value in first_b]
    parts = []
    for step in range(2):
        own, other = second_a[step], from_partner(second_a[step], "gx", 0)
        parts.append(y_dft([own, other], coefs_a, y_table, twist))
        late, early = second_b[step], first_b[step]
        group = [late, from_partner(late, "gx", 0), early, from_partner(early, "gx", 0)]
        parts.append(y_dft(group, coefs_b, y_table, twist))
    sums = x_first(parts[:2], x_table((0, 2)))
    latent, tile = x_last(parts[2:], x_table((1, 3)), sums, row_pair, col_trio)
    tile = tile + fixed / tile.size
    modes = length * columns * lax.axis_size("gx") * lax.axis_size("gy")
    return (latent, sum_everywhere(tile) / modes)


def complex_einsum(form, real_part, imag_part, cos_part, sin_part):
    first = jnp.einsum(form, real_part, cos_part, precision=precision_top)
    second = jnp.einsum(form, real_part, sin_part, precision=precision_top)
    first = first - jnp.einsum(form, imag_part, sin_part, precision=precision_top)
    second = second + jnp.einsum(form, imag_part, cos_part, precision=precision_top)
    return (first, second)


def x_butterfly(field):
    devices = lax.axis_size("gx")
    levels = devices.bit_length() - 1
    position = lax.axis_index("gx")
    real_part, imag_part = field, jnp.zeros_like(field)
    for level in range(levels - 1, -1, -1):
        half = 1 << level
        lower = position // half % 2 == 0
        offset = position % half
        angle = offset.astype(jnp.float32) * (-math.pi / half)
        cos_twist = jnp.where(lower, 1.0, jnp.cos(angle))
        sin_twist = jnp.where(lower, 0.0, jnp.sin(angle))
        other = from_partner(jnp.stack([real_part, imag_part]), "gx", level)
        diff_real = jnp.where(lower, real_part + other[0], other[0] - real_part)
        diff_imag = jnp.where(lower, imag_part + other[1], other[1] - imag_part)
        real_part = diff_real * cos_twist - diff_imag * sin_twist
        imag_part = diff_real * sin_twist + diff_imag * cos_twist
    cos_part, sin_part = x_tables(field.shape[2], devices, position)
    real_part, imag_part = complex_einsum("zyn,nk->zyk", real_part, imag_part, cos_part, sin_part)
    return (to_planes(real_part), to_planes(imag_part))


def y_transform(real_part, imag_part):
    planes, length, width = real_part.shape
    outer = 1 << (length.bit_length() - 1) // 2
    inner = length // outer
    outer_index = jnp.arange(outer, dtype=jnp.int32)
    inner_index = jnp.arange(inner, dtype=jnp.int32)
    cos_one, sin_one = root_table(outer_index, outer_index, outer)
    cos_two, sin_two = root_table(inner_index, inner_index, inner)
    cos_mid, sin_mid = root_table(outer_index, inner_index, length)
    shaped_real = real_part.reshape(planes, outer, inner, width)
    shaped_imag = imag_part.reshape(planes, outer, inner, width)
    step_real, step_imag = complex_einsum("zabc,ak->zkbc", shaped_real, shaped_imag, cos_one, sin_one)
    twist_cos = cos_mid[None, :, :, None]
    twist_sin = sin_mid[None, :, :, None]
    turned_real = step_real * twist_cos - step_imag * twist_sin
    turned_imag = step_real * twist_sin + step_imag * twist_cos
    final_real, final_imag = complex_einsum("zkbc,bj->zjkc", turned_real, turned_imag, cos_two, sin_two)
    return (final_real.reshape(planes, length, width), final_imag.reshape(planes, length, width))


def any_way(field, row_scale, col_scale, row_rate, col_shift, col_mix):
    spec_real, spec_imag = y_transform(*x_butterfly(field))
    length = spec_real.shape[1]
    total_cols = spec_real.shape[2] * lax.axis_size("gx")
    norm_factor = 1.0 / math.sqrt(length * total_cols)
    scale = row_scale[None, :, None] * col_scale[None, None, :]
    latent_u = spec_real * norm_factor * scale
    latent_v = spec_imag * norm_factor * scale
    log_scale = row_rate[None, :, None] * jnp.tanh(latent_u + col_shift[None, None, :])
    latent_w = latent_v * jnp.exp(log_scale) + col_mix[None, None, :] * latent_u
    terms = (
        -0.5 * (latent_u * latent_u + latent_w * latent_w)
        - math.log(2.0 * math.pi)
        + log_scale
        + 2.0 * jnp.log(scale)
    )
    mode_count = spec_real.size * lax.axis_size("gx") * lax.axis_size("gy")
    loglik = lax.psum(jnp.sum(terms), ("gx", "gy")) / mode_count
    return (jnp.stack([latent_u, latent_w]), loglik)


def per_device(field, *scales):
    return (four_way if lax.axis_size("gx") == 4 else any_way)(field, *scales)


def solution(mesh):
    return jax.shard_map(
        per_device,
        mesh=mesh,
        in_specs=(P(None, "gy", "gx"), P(), P("gx"), P(), P("gx"), P("gx")),
        out_specs=(P(None, "gy", None, "gx"), P()),
        check_vma=False,
    )
```

```python
import functools
import math

import jax
import jax.numpy as jnp
from jax import lax
from jax.experimental import pallas as pl
from jax.experimental.pallas import tpu as pltpu
from jax.sharding import PartitionSpec as P

precision_top = lax.Precision.HIGHEST
RADIX = 8
VMEM_BYTES = 40 * 1024 * 1024


def from_partner(value, axis, stride):
    mask = 2**stride
    pairs = [(source, source ^ mask) for source in range(lax.axis_size(axis))]
    return lax.ppermute(value, axis, pairs)


def to_planes(values):
    return lax.all_to_all(values, "gy", split_axis=0, concat_axis=1, tiled=True)


def split_kernel(count, me_ref, *refs):
    inputs, outputs = refs[: len(refs) - count], refs[len(refs) - count :]
    for place, out_ref in enumerate(outputs):
        plane = me_ref[0] ^ place
        if len(inputs) == 1:
            out_ref[...] = inputs[0][plane]
        else:
            sign = (1 - 2 * me_ref[1]).astype(jnp.float32)
            out_ref[...] = inputs[0][plane] + sign * inputs[1][plane]


def split_pieces(numbers, inputs):
    planes, rows, width = inputs[0].shape
    whole = pl.BlockSpec(memory_space=pltpu.VMEM)
    return pl.pallas_call(
        functools.partial(split_kernel, planes),
        out_shape=[jax.ShapeDtypeStruct((rows, width), jnp.float32)] * planes,
        in_specs=[pl.BlockSpec(memory_space=pltpu.SMEM)] + [whole] * len(inputs),
        out_specs=[whole] * planes,
        compiler_params=pltpu.CompilerParams(vmem_limit_bytes=VMEM_BYTES),
        cost_estimate=pl.CostEstimate(
            flops=planes * rows * width, bytes_accessed=8 * planes * rows * width, transcendentals=0
        ),
        name="split_pieces",
    )(numbers, *inputs)


def exchange(pieces, held):
    devices = lax.axis_size("gy")
    near = range(1, devices // 2)
    if held is not None:
        waited = lax.optimization_barrier((held, [pieces[m] for m in near]))[1]
        pieces = [pieces[0], *waited, *pieces[devices // 2 :]]
    received = {0: pieces[0]}
    for m in (*range(devices // 2, devices), *near):
        received[m] = lax.ppermute(pieces[m], "gy", [(source, source ^ m) for source in range(devices)])
    return [received[m] for m in range(devices)]


def reverse_bits(value, count):
    result = value * 0
    for place in range(count):
        result = result + (value >> place & 1) * (1 << count - 1 - place)
    return result


def root_table(row_index, freqs, length):
    phase = row_index[:, None] * freqs[None, :] % length
    angle = phase.astype(jnp.float32) * (-2.0 * math.pi / length)
    return (jnp.cos(angle), jnp.sin(angle))


def x_tables(width, devices, position):
    levels = devices.bit_length() - 1
    local_index = jnp.arange(width, dtype=jnp.int32)
    freqs = reverse_bits(position, levels) + devices * local_index
    return root_table(local_index, freqs, devices * width)


def split_table(table):
    high = lax.reduce_precision(table, 8, 7)
    return jnp.stack([high.astype(jnp.bfloat16), (table - high).astype(jnp.bfloat16)])


def split_value(value):
    high = value.astype(jnp.bfloat16)
    return high, (value - high.astype(jnp.float32)).astype(jnp.bfloat16)


def small_fft(values):
    count = len(values)
    if count == 1:
        return values
    even, odd = small_fft(values[0::2]), small_fft(values[1::2])
    first, second = [], []
    root_half = math.sqrt(0.5)
    for place in range(count // 2):
        (er, ei), (re, im) = even[place], odd[place]
        turn = place * 8 // count
        if turn == 1:
            re, im = (re + im) * root_half, (im - re) * root_half
        elif turn == 2:
            re, im = im, -re
        elif turn == 3:
            re, im = (im - re) * root_half, (re + im) * -root_half
        first.append((er + re, ei + im))
        second.append((er - re, ei - im))
    return first + second


def dot(left, right):
    return jnp.dot(left, right, preferred_element_type=jnp.float32)


def dot_split(left_high, left_low, right_high, right_low):
    return dot(left_high, right_high) + (dot(left_high, right_low) + dot(left_low, right_high))


def y_kernel(count, coef_ref, *refs):
    inputs, (table_ref, twist_ref, out_ref, high_ref, low_ref, step_ref) = refs[:count], refs[count:]
    length, width = inputs[0].shape
    inner = length // RADIX
    for s in range(RADIX):
        parts = [ref[pl.ds(s, inner, stride=RADIX), :] for ref in inputs]
        for which in range(2):
            mixed = parts[0] * coef_ref[which, 0]
            for place in range(1, count):
                mixed = mixed + parts[place] * coef_ref[which, place]
            high, low = split_value(mixed)
            rows, cols = pl.ds(which * inner, inner), pl.ds(s * width, width)
            high_ref[rows, cols] = high
            low_ref[rows, cols] = low
    piece = 2 * width

    @pl.loop(0, RADIX * width // piece)
    def _(block):
        cols = pl.ds(pl.multiple_of(block * piece, piece), piece)
        step_ref[:, cols] = dot_split(table_ref[0], table_ref[1], high_ref[:, cols], low_ref[:, cols])

    rows_each = 16

    @pl.loop(0, inner // rows_each)
    def _(block):
        start = pl.multiple_of(block * rows_each, rows_each)
        values = []
        for s in range(RADIX):
            cols = pl.ds(s * width, width)
            re = step_ref[pl.ds(start, rows_each), cols]
            im = step_ref[pl.ds(pl.multiple_of(start + inner, rows_each), rows_each), cols]
            if s:
                cos, sin = twist_ref[0, s, pl.ds(start, rows_each), :], twist_ref[1, s, pl.ds(start, rows_each), :]
                re, im = re * cos - im * sin, re * sin + im * cos
            values.append((re, im))
        for kb, pair in enumerate(small_fft(values)):
            rows = pl.ds(pl.multiple_of(kb * inner + start, rows_each), rows_each)
            for which in range(2):
                high, low = split_value(pair[which])
                out_ref[2 * which, rows, :] = high
                out_ref[2 * which + 1, rows, :] = low


def y_dft(inputs, coefs, table, twist):
    count = len(inputs)
    length, width = inputs[0].shape
    inner = length // RADIX
    whole = pl.BlockSpec(memory_space=pltpu.VMEM)
    return pl.pallas_call(
        functools.partial(y_kernel, count),
        out_shape=jax.ShapeDtypeStruct((4, length, width), jnp.bfloat16),
        in_specs=[pl.BlockSpec(memory_space=pltpu.SMEM)] + [whole] * (count + 2),
        out_specs=whole,
        scratch_shapes=[
            pltpu.VMEM((2 * inner, RADIX * width), jnp.bfloat16),
            pltpu.VMEM((2 * inner, RADIX * width), jnp.bfloat16),
            pltpu.VMEM((2 * inner, RADIX * width), jnp.float32),
        ],
        compiler_params=pltpu.CompilerParams(vmem_limit_bytes=VMEM_BYTES),
        cost_estimate=pl.CostEstimate(
            flops=24 * inner * length * width, bytes_accessed=4 * length * width * (count + 3), transcendentals=0
        ),
        name="y_dft",
    )(coefs, *inputs, table, twist)


def x_product(parts, table_ref):
    high = jnp.concatenate([ref[which] for ref in parts for which in (0, 2)], axis=1)
    low = jnp.concatenate([ref[which] for ref in parts for which in (1, 3)], axis=1)
    return dot_split(high, low, table_ref[0], table_ref[1])


def x_first_kernel(count, *refs):
    parts, (table_ref, out_ref) = refs[:count], refs[count:]
    out_ref[...] = x_product(parts, table_ref)


def x_first(parts, table):
    count = len(parts)
    _, length, width = parts[0].shape
    columns = table.shape[2]
    rows = 256
    return pl.pallas_call(
        functools.partial(x_first_kernel, count),
        out_shape=jax.ShapeDtypeStruct((length, columns), jnp.float32),
        grid=(length // rows,),
        in_specs=[pl.BlockSpec((4, rows, width), lambda i: (0, i, 0))] * count
        + [pl.BlockSpec(table.shape, lambda i: (0, 0, 0))],
        out_specs=pl.BlockSpec((rows, columns), lambda i: (i, 0)),
        compiler_params=pltpu.CompilerParams(vmem_limit_bytes=VMEM_BYTES),
        cost_estimate=pl.CostEstimate(
            flops=12 * count * length * width * columns, bytes_accessed=8 * length * columns, transcendentals=0
        ),
        name="x_first",
    )(*parts, table)


def x_last_kernel(count, *refs):
    parts, (table_ref, sum_ref, row_ref, col_ref, out_ref, total_ref) = refs[:count], refs[count:]
    spec = sum_ref[...] + x_product(parts, table_ref)
    columns = spec.shape[1] // 2
    lanes = row_ref.shape[2]
    total = None
    for tile in range(columns // lanes):
        cols = pl.ds(tile * lanes, lanes)
        col_scale, col_shift, col_mix = col_ref[0:1, cols], col_ref[1:2, cols], col_ref[2:3, cols]
        scale = row_ref[0] * col_scale
        latent_u = spec[:, tile * lanes : (tile + 1) * lanes] * scale
        latent_v = spec[:, columns + tile * lanes : columns + (tile + 1) * lanes] * scale
        log_scale = row_ref[1] * jnp.tanh(latent_u + col_shift)
        latent_w = latent_v * jnp.exp(log_scale) + col_mix * latent_u
        out_ref[0, 0, :, cols] = latent_u
        out_ref[1, 0, :, cols] = latent_w
        terms = log_scale - 0.5 * (latent_u * latent_u + latent_w * latent_w)
        terms = jnp.sum(terms.reshape(-1, 8, lanes), axis=0)
        total = terms if total is None else total + terms

    @pl.when(pl.program_id(0) == 0)
    def _():
        total_ref[...] = jnp.zeros_like(total_ref)

    total_ref[...] += total


def x_last(parts, table, sums, row_pair, col_trio):
    count = len(parts)
    _, length, width = parts[0].shape
    columns = table.shape[2]
    rows = 256
    return pl.pallas_call(
        functools.partial(x_last_kernel, count),
        out_shape=(
            jax.ShapeDtypeStruct((2, 1, length, columns // 2), jnp.float32),
            jax.ShapeDtypeStruct((8, row_pair.shape[2]), jnp.float32),
        ),
        grid=(length // rows,),
        in_specs=[pl.BlockSpec((4, rows, width), lambda i: (0, i, 0))] * count
        + [
            pl.BlockSpec(table.shape, lambda i: (0, 0, 0)),
            pl.BlockSpec((rows, columns), lambda i: (i, 0)),
            pl.BlockSpec((2, rows, row_pair.shape[2]), lambda i: (0, i, 0)),
            pl.BlockSpec(col_trio.shape, lambda i: (0, 0)),
        ],
        out_specs=(
            pl.BlockSpec((2, 1, rows, columns // 2), lambda i: (0, 0, i, 0)),
            pl.BlockSpec((8, row_pair.shape[2]), lambda i: (0, 0)),
        ),
        compiler_params=pltpu.CompilerParams(vmem_limit_bytes=VMEM_BYTES),
        cost_estimate=pl.CostEstimate(
            flops=12 * count * length * width * columns,
            bytes_accessed=12 * length * columns,
            transcendentals=length * columns,
        ),
        name="x_last",
    )(*parts, table, sums, row_pair, col_trio)


def sum_everywhere(tile):
    for axis in ("gx", "gy"):
        devices = lax.axis_size(axis)
        others = [lax.ppermute(tile, axis, [(s, s ^ m) for s in range(devices)]) for m in range(1, devices)]
        tile = functools.reduce(jnp.add, others, tile)
    return jnp.sum(tile)


def four_way(field, row_scale, col_scale, row_rate, col_shift, col_mix):
    position = lax.axis_index("gx")
    planes, rows, columns = field.shape
    length, width = planes * rows, columns // 4
    cuts = lax.optimization_barrier(tuple(field[:, :, c * width : (c + 1) * width] for c in range(4)))
    sign = jnp.where(position < 2, 1.0, -1.0)

    own_real = jnp.where(position == 1, -1.0, jnp.where(position == 3, 0.0, 1.0))
    other_real = jnp.where(position == 2, 0.0, 1.0)
    own_imag = jnp.where(position == 3, 1.0, 0.0)
    other_imag = jnp.where(position == 2, -1.0, 0.0)
    coefs_a = jnp.stack([own_real, other_real, own_imag, other_imag]).reshape(2, 2)
    coefs_b = jnp.concatenate([coefs_a, coefs_a * sign], axis=1)

    inner = length // RADIX
    index = jnp.arange(inner, dtype=jnp.int32)
    block = inner // planes
    arrived = ((index // block) ^ lax.axis_index("gy")) * block + index % block
    cos, sin = root_table(index, arrived, inner)
    y_table = split_table(jnp.concatenate([jnp.concatenate([cos, -sin], 1), jnp.concatenate([sin, cos], 1)], 0))
    cos, sin = root_table(jnp.arange(RADIX, dtype=jnp.int32), index, length)
    twist = jnp.broadcast_to(jnp.stack([cos, sin])[:, :, :, None], (2, RADIX, inner, width))
    cos, sin = x_tables(columns, 4, position)
    real_rows, imag_rows = jnp.concatenate([cos, sin], 1), jnp.concatenate([-sin, cos], 1)

    def x_table(chunks):
        spans = [slice(c * width, (c + 1) * width) for c in chunks]
        return split_table(jnp.concatenate([rows[s] for s in spans for rows in (real_rows, imag_rows)], 0))

    norm = 1.0 / math.sqrt(length * columns * 4)
    row_pair = jnp.broadcast_to(jnp.stack([row_scale * norm, row_rate])[:, :, None], (2, length, 128))
    col_trio = jnp.stack([col_scale, col_shift, col_mix])
    fixed = 2.0 * (columns * jnp.sum(jnp.log(row_scale)) + length * jnp.sum(jnp.log(col_scale)))
    fixed = fixed - length * columns * math.log(2.0 * math.pi)

    numbers = jnp.stack([lax.axis_index("gy"), position // 2]).astype(jnp.int32)

    def gather(inputs, held):
        return jnp.concatenate(exchange(split_pieces(numbers, inputs), held), axis=0)

    first_a = [from_partner(cuts[c], "gx", 1) for c in (0, 1)]
    first_b = [gather([cuts[2]], None), gather([cuts[3]], first_a[0])]
    second_b = [from_partner(value, "gx", 1) for value in first_b]
    second_a = [gather([first_a[0], cuts[0]], first_a[1]), gather([first_a[1], cuts[1]], second_b[0])]
    parts = []
    for step in range(2):
        own, other = second_a[step], from_partner(second_a[step], "gx", 0)
        parts.append(y_dft([own, other], coefs_a, y_table, twist))
        late, early = second_b[step], first_b[step]
        group = [late, from_partner(late, "gx", 0), early, from_partner(early, "gx", 0)]
        parts.append(y_dft(group, coefs_b, y_table, twist))
    sums = x_first(parts[:2], x_table((0, 2)))
    latent, tile = x_last(parts[2:], x_table((1, 3)), sums, row_pair, col_trio)
    tile = tile + fixed / tile.size
    modes = length * columns * lax.axis_size("gx") * lax.axis_size("gy")
    return (latent, sum_everywhere(tile) / modes)


def complex_einsum(form, real_part, imag_part, cos_part, sin_part):
    first = jnp.einsum(form, real_part, cos_part, precision=precision_top)
    second = jnp.einsum(form, real_part, sin_part, precision=precision_top)
    first = first - jnp.einsum(form, imag_part, sin_part, precision=precision_top)
    second = second + jnp.einsum(form, imag_part, cos_part, precision=precision_top)
    return (first, second)


def x_butterfly(field):
    devices = lax.axis_size("gx")
    levels = devices.bit_length() - 1
    position = lax.axis_index("gx")
    real_part, imag_part = field, jnp.zeros_like(field)
    for level in range(levels - 1, -1, -1):
        half = 1 << level
        lower = position // half % 2 == 0
        offset = position % half
        angle = offset.astype(jnp.float32) * (-math.pi / half)
        cos_twist = jnp.where(lower, 1.0, jnp.cos(angle))
        sin_twist = jnp.where(lower, 0.0, jnp.sin(angle))
        other = from_partner(jnp.stack([real_part, imag_part]), "gx", level)
        diff_real = jnp.where(lower, real_part + other[0], other[0] - real_part)
        diff_imag = jnp.where(lower, imag_part + other[1], other[1] - imag_part)
        real_part = diff_real * cos_twist - diff_imag * sin_twist
        imag_part = diff_real * sin_twist + diff_imag * cos_twist
    cos_part, sin_part = x_tables(field.shape[2], devices, position)
    real_part, imag_part = complex_einsum("zyn,nk->zyk", real_part, imag_part, cos_part, sin_part)
    return (to_planes(real_part), to_planes(imag_part))


def y_transform(real_part, imag_part):
    planes, length, width = real_part.shape
    outer = 1 << (length.bit_length() - 1) // 2
    inner = length // outer
    outer_index = jnp.arange(outer, dtype=jnp.int32)
    inner_index = jnp.arange(inner, dtype=jnp.int32)
    cos_one, sin_one = root_table(outer_index, outer_index, outer)
    cos_two, sin_two = root_table(inner_index, inner_index, inner)
    cos_mid, sin_mid = root_table(outer_index, inner_index, length)
    shaped_real = real_part.reshape(planes, outer, inner, width)
    shaped_imag = imag_part.reshape(planes, outer, inner, width)
    step_real, step_imag = complex_einsum("zabc,ak->zkbc", shaped_real, shaped_imag, cos_one, sin_one)
    twist_cos = cos_mid[None, :, :, None]
    twist_sin = sin_mid[None, :, :, None]
    turned_real = step_real * twist_cos - step_imag * twist_sin
    turned_imag = step_real * twist_sin + step_imag * twist_cos
    final_real, final_imag = complex_einsum("zkbc,bj->zjkc", turned_real, turned_imag, cos_two, sin_two)
    return (final_real.reshape(planes, length, width), final_imag.reshape(planes, length, width))


def any_way(field, row_scale, col_scale, row_rate, col_shift, col_mix):
    spec_real, spec_imag = y_transform(*x_butterfly(field))
    length = spec_real.shape[1]
    total_cols = spec_real.shape[2] * lax.axis_size("gx")
    norm_factor = 1.0 / math.sqrt(length * total_cols)
    scale = row_scale[None, :, None] * col_scale[None, None, :]
    latent_u = spec_real * norm_factor * scale
    latent_v = spec_imag * norm_factor * scale
    log_scale = row_rate[None, :, None] * jnp.tanh(latent_u + col_shift[None, None, :])
    latent_w = latent_v * jnp.exp(log_scale) + col_mix[None, None, :] * latent_u
    terms = (
        -0.5 * (latent_u * latent_u + latent_w * latent_w)
        - math.log(2.0 * math.pi)
        + log_scale
        + 2.0 * jnp.log(scale)
    )
    mode_count = spec_real.size * lax.axis_size("gx") * lax.axis_size("gy")
    loglik = lax.psum(jnp.sum(terms), ("gx", "gy")) / mode_count
    return (jnp.stack([latent_u, latent_w]), loglik)


def per_device(field, *scales):
    return (four_way if lax.axis_size("gx") == 4 else any_way)(field, *scales)


def solution(mesh):
    return jax.shard_map(
        per_device,
        mesh=mesh,
        in_specs=(P(None, "gy", "gx"), P(), P("gx"), P(), P("gx"), P("gx")),
        out_specs=(P(None, "gy", None, "gx"), P()),
        check_vma=False,
    )
```

```python
import functools
import math

import jax
import jax.numpy as jnp
from jax import lax
from jax.experimental import pallas as pl
from jax.experimental.pallas import tpu as pltpu
from jax.sharding import PartitionSpec as P

precision_top = lax.Precision.HIGHEST
RADIX = 8
VMEM_BYTES = 40 * 1024 * 1024


def from_partner(value, axis, stride):
    mask = 2**stride
    pairs = [(source, source ^ mask) for source in range(lax.axis_size(axis))]
    return lax.ppermute(value, axis, pairs)


def to_planes(values):
    return lax.all_to_all(values, "gy", split_axis=0, concat_axis=1, tiled=True)


def reverse_bits(value, count):
    result = value * 0
    for place in range(count):
        result = result + (value >> place & 1) * (1 << count - 1 - place)
    return result


def root_table(row_index, freqs, length):
    phase = row_index[:, None] * freqs[None, :] % length
    angle = phase.astype(jnp.float32) * (-2.0 * math.pi / length)
    return (jnp.cos(angle), jnp.sin(angle))


def x_tables(width, devices, position):
    levels = devices.bit_length() - 1
    local_index = jnp.arange(width, dtype=jnp.int32)
    freqs = reverse_bits(position, levels) + devices * local_index
    return root_table(local_index, freqs, devices * width)


def split_table(table):
    high = lax.reduce_precision(table, 8, 7)
    return jnp.stack([high.astype(jnp.bfloat16), (table - high).astype(jnp.bfloat16)])


def split_value(value):
    high = value.astype(jnp.bfloat16)
    return high, (value - high.astype(jnp.float32)).astype(jnp.bfloat16)


def small_fft(values):
    count = len(values)
    if count == 1:
        return values
    even, odd = small_fft(values[0::2]), small_fft(values[1::2])
    first, second = [], []
    root_half = math.sqrt(0.5)
    for place in range(count // 2):
        (er, ei), (re, im) = even[place], odd[place]
        turn = place * 8 // count
        if turn == 1:
            re, im = (re + im) * root_half, (im - re) * root_half
        elif turn == 2:
            re, im = im, -re
        elif turn == 3:
            re, im = (im - re) * root_half, (re + im) * -root_half
        first.append((er + re, ei + im))
        second.append((er - re, ei - im))
    return first + second


def dot(left, right):
    return jnp.dot(left, right, preferred_element_type=jnp.float32)


def dot_split(left_high, left_low, right_high, right_low):
    return dot(left_high, right_high) + (dot(left_high, right_low) + dot(left_low, right_high))


def y_kernel(count, coef_ref, *refs):
    inputs, (table_ref, twist_ref, out_ref, high_ref, low_ref, step_ref) = refs[:count], refs[count:]
    length, width = inputs[0].shape
    inner = length // RADIX
    for s in range(RADIX):
        parts = [ref[pl.ds(s, inner, stride=RADIX), :] for ref in inputs]
        for which in range(2):
            mixed = parts[0] * coef_ref[which, 0]
            for place in range(1, count):
                mixed = mixed + parts[place] * coef_ref[which, place]
            high, low = split_value(mixed)
            rows, cols = pl.ds(which * inner, inner), pl.ds(s * width, width)
            high_ref[rows, cols] = high
            low_ref[rows, cols] = low
    piece = 2 * width

    @pl.loop(0, RADIX * width // piece)
    def _(block):
        cols = pl.ds(pl.multiple_of(block * piece, piece), piece)
        step_ref[:, cols] = dot_split(table_ref[0], table_ref[1], high_ref[:, cols], low_ref[:, cols])

    rows_each = 16

    @pl.loop(0, inner // rows_each)
    def _(block):
        start = pl.multiple_of(block * rows_each, rows_each)
        values = []
        for s in range(RADIX):
            cols = pl.ds(s * width, width)
            re = step_ref[pl.ds(start, rows_each), cols]
            im = step_ref[pl.ds(pl.multiple_of(start + inner, rows_each), rows_each), cols]
            if s:
                cos, sin = twist_ref[0, s, pl.ds(start, rows_each), :], twist_ref[1, s, pl.ds(start, rows_each), :]
                re, im = re * cos - im * sin, re * sin + im * cos
            values.append((re, im))
        for kb, pair in enumerate(small_fft(values)):
            rows = pl.ds(pl.multiple_of(kb * inner + start, rows_each), rows_each)
            for which in range(2):
                high, low = split_value(pair[which])
                out_ref[2 * which, rows, :] = high
                out_ref[2 * which + 1, rows, :] = low


def y_dft(inputs, coefs, table, twist):
    count = len(inputs)
    length, width = inputs[0].shape
    inner = length // RADIX
    whole = pl.BlockSpec(memory_space=pltpu.VMEM)
    return pl.pallas_call(
        functools.partial(y_kernel, count),
        out_shape=jax.ShapeDtypeStruct((4, length, width), jnp.bfloat16),
        in_specs=[pl.BlockSpec(memory_space=pltpu.SMEM)] + [whole] * (count + 2),
        out_specs=whole,
        scratch_shapes=[
            pltpu.VMEM((2 * inner, RADIX * width), jnp.bfloat16),
            pltpu.VMEM((2 * inner, RADIX * width), jnp.bfloat16),
            pltpu.VMEM((2 * inner, RADIX * width), jnp.float32),
        ],
        compiler_params=pltpu.CompilerParams(vmem_limit_bytes=VMEM_BYTES),
        cost_estimate=pl.CostEstimate(
            flops=24 * inner * length * width, bytes_accessed=4 * length * width * (count + 3), transcendentals=0
        ),
        name="y_dft",
    )(coefs, *inputs, table, twist)


def x_product(parts, table_ref):
    high = jnp.concatenate([ref[which] for ref in parts for which in (0, 2)], axis=1)
    low = jnp.concatenate([ref[which] for ref in parts for which in (1, 3)], axis=1)
    return dot_split(high, low, table_ref[0], table_ref[1])


def x_first_kernel(count, *refs):
    parts, (table_ref, out_ref) = refs[:count], refs[count:]
    out_ref[...] = x_product(parts, table_ref)


def x_first(parts, table):
    count = len(parts)
    _, length, width = parts[0].shape
    columns = table.shape[2]
    rows = 256
    return pl.pallas_call(
        functools.partial(x_first_kernel, count),
        out_shape=jax.ShapeDtypeStruct((length, columns), jnp.float32),
        grid=(length // rows,),
        in_specs=[pl.BlockSpec((4, rows, width), lambda i: (0, i, 0))] * count
        + [pl.BlockSpec(table.shape, lambda i: (0, 0, 0))],
        out_specs=pl.BlockSpec((rows, columns), lambda i: (i, 0)),
        compiler_params=pltpu.CompilerParams(vmem_limit_bytes=VMEM_BYTES),
        cost_estimate=pl.CostEstimate(
            flops=12 * count * length * width * columns, bytes_accessed=8 * length * columns, transcendentals=0
        ),
        name="x_first",
    )(*parts, table)


def x_last_kernel(count, *refs):
    parts, (table_ref, sum_ref, row_ref, col_ref, out_ref, total_ref) = refs[:count], refs[count:]
    spec = sum_ref[...] + x_product(parts, table_ref)
    columns = spec.shape[1] // 2
    lanes = row_ref.shape[2]
    total = None
    for tile in range(columns // lanes):
        cols = pl.ds(tile * lanes, lanes)
        col_scale, col_shift, col_mix = col_ref[0:1, cols], col_ref[1:2, cols], col_ref[2:3, cols]
        scale = row_ref[0] * col_scale
        latent_u = spec[:, tile * lanes : (tile + 1) * lanes] * scale
        latent_v = spec[:, columns + tile * lanes : columns + (tile + 1) * lanes] * scale
        log_scale = row_ref[1] * jnp.tanh(latent_u + col_shift)
        latent_w = latent_v * jnp.exp(log_scale) + col_mix * latent_u
        out_ref[0, 0, :, cols] = latent_u
        out_ref[1, 0, :, cols] = latent_w
        terms = log_scale - 0.5 * (latent_u * latent_u + latent_w * latent_w)
        terms = jnp.sum(terms.reshape(-1, 8, lanes), axis=0)
        total = terms if total is None else total + terms

    @pl.when(pl.program_id(0) == 0)
    def _():
        total_ref[...] = jnp.zeros_like(total_ref)

    total_ref[...] += total


def x_last(parts, table, sums, row_pair, col_trio):
    count = len(parts)
    _, length, width = parts[0].shape
    columns = table.shape[2]
    rows = 256
    return pl.pallas_call(
        functools.partial(x_last_kernel, count),
        out_shape=(
            jax.ShapeDtypeStruct((2, 1, length, columns // 2), jnp.float32),
            jax.ShapeDtypeStruct((8, row_pair.shape[2]), jnp.float32),
        ),
        grid=(length // rows,),
        in_specs=[pl.BlockSpec((4, rows, width), lambda i: (0, i, 0))] * count
        + [
            pl.BlockSpec(table.shape, lambda i: (0, 0, 0)),
            pl.BlockSpec((rows, columns), lambda i: (i, 0)),
            pl.BlockSpec((2, rows, row_pair.shape[2]), lambda i: (0, i, 0)),
            pl.BlockSpec(col_trio.shape, lambda i: (0, 0)),
        ],
        out_specs=(
            pl.BlockSpec((2, 1, rows, columns // 2), lambda i: (0, 0, i, 0)),
            pl.BlockSpec((8, row_pair.shape[2]), lambda i: (0, 0)),
        ),
        compiler_params=pltpu.CompilerParams(vmem_limit_bytes=VMEM_BYTES),
        cost_estimate=pl.CostEstimate(
            flops=12 * count * length * width * columns,
            bytes_accessed=12 * length * columns,
            transcendentals=length * columns,
        ),
        name="x_last",
    )(*parts, table, sums, row_pair, col_trio)


def sum_everywhere(tile):
    return jnp.sum(lax.all_gather(jnp.sum(tile, axis=0, keepdims=True), ("gx", "gy")))


def four_way(field, row_scale, col_scale, row_rate, col_shift, col_mix):
    position = lax.axis_index("gx")
    planes, rows, columns = field.shape
    length, width = planes * rows, columns // 4
    field_a, field_b = lax.optimization_barrier((field[:, :, : 2 * width], field[:, :, 2 * width :]))
    sign = jnp.where(position < 2, 1.0, -1.0)

    own_real = jnp.where(position == 1, -1.0, jnp.where(position == 3, 0.0, 1.0))
    other_real = jnp.where(position == 2, 0.0, 1.0)
    own_imag = jnp.where(position == 3, 1.0, 0.0)
    other_imag = jnp.where(position == 2, -1.0, 0.0)
    coefs_a = jnp.stack([own_real, other_real, own_imag, other_imag]).reshape(2, 2)
    coefs_b = jnp.concatenate([coefs_a, coefs_a * sign], axis=1)

    inner = length // RADIX
    index = jnp.arange(inner, dtype=jnp.int32)
    cos, sin = root_table(index, index, inner)
    y_table = split_table(jnp.concatenate([jnp.concatenate([cos, -sin], 1), jnp.concatenate([sin, cos], 1)], 0))
    cos, sin = root_table(jnp.arange(RADIX, dtype=jnp.int32), index, length)
    twist = jnp.broadcast_to(jnp.stack([cos, sin])[:, :, :, None], (2, RADIX, inner, width))
    cos, sin = x_tables(columns, 4, position)
    real_rows, imag_rows = jnp.concatenate([cos, sin], 1), jnp.concatenate([-sin, cos], 1)

    def x_table(chunks):
        spans = [slice(c * width, (c + 1) * width) for c in chunks]
        return split_table(jnp.concatenate([rows[s] for s in spans for rows in (real_rows, imag_rows)], 0))

    norm = 1.0 / math.sqrt(length * columns * 4)
    row_pair = jnp.broadcast_to(jnp.stack([row_scale * norm, row_rate])[:, :, None], (2, length, 128))
    col_trio = jnp.stack([col_scale, col_shift, col_mix])
    fixed = 2.0 * (columns * jnp.sum(jnp.log(row_scale)) + length * jnp.sum(jnp.log(col_scale)))
    fixed = fixed - length * columns * math.log(2.0 * math.pi)

    first_a, first_b = lax.optimization_barrier((from_partner(field_a, "gx", 1), to_planes(field_b)[0]))
    first_a = [first_a[:, :, span] + sign * field_a[:, :, span] for span in (slice(0, width), slice(width, None))]
    first_b = [first_b[:, :width], first_b[:, width:]]
    first_a, first_b = lax.optimization_barrier((first_a, first_b))
    second_b, second_a = [from_partner(first_b[0], "gx", 1)], [to_planes(first_a[0])[0]]
    first_a[1], second_b[0] = lax.optimization_barrier((first_a[1], second_b[0]))
    second_b.append(from_partner(first_b[1], "gx", 1))
    second_a.append(to_planes(first_a[1])[0])
    parts = []
    for step in range(2):
        own, other = second_a[step], from_partner(second_a[step], "gx", 0)
        parts.append(y_dft([own, other], coefs_a, y_table, twist))
        late, early = second_b[step], first_b[step]
        group = [late, from_partner(late, "gx", 0), early, from_partner(early, "gx", 0)]
        parts.append(y_dft(group, coefs_b, y_table, twist))
    sums = x_first(parts[:2], x_table((0, 2)))
    latent, tile = x_last(parts[2:], x_table((1, 3)), sums, row_pair, col_trio)
    tile = tile + fixed / tile.size
    modes = length * columns * lax.axis_size("gx") * lax.axis_size("gy")
    return (latent, sum_everywhere(tile) / modes)


def complex_einsum(form, real_part, imag_part, cos_part, sin_part):
    first = jnp.einsum(form, real_part, cos_part, precision=precision_top)
    second = jnp.einsum(form, real_part, sin_part, precision=precision_top)
    first = first - jnp.einsum(form, imag_part, sin_part, precision=precision_top)
    second = second + jnp.einsum(form, imag_part, cos_part, precision=precision_top)
    return (first, second)


def x_butterfly(field):
    devices = lax.axis_size("gx")
    levels = devices.bit_length() - 1
    position = lax.axis_index("gx")
    real_part, imag_part = field, jnp.zeros_like(field)
    for level in range(levels - 1, -1, -1):
        half = 1 << level
        lower = position // half % 2 == 0
        offset = position % half
        angle = offset.astype(jnp.float32) * (-math.pi / half)
        cos_twist = jnp.where(lower, 1.0, jnp.cos(angle))
        sin_twist = jnp.where(lower, 0.0, jnp.sin(angle))
        other = from_partner(jnp.stack([real_part, imag_part]), "gx", level)
        diff_real = jnp.where(lower, real_part + other[0], other[0] - real_part)
        diff_imag = jnp.where(lower, imag_part + other[1], other[1] - imag_part)
        real_part = diff_real * cos_twist - diff_imag * sin_twist
        imag_part = diff_real * sin_twist + diff_imag * cos_twist
    cos_part, sin_part = x_tables(field.shape[2], devices, position)
    real_part, imag_part = complex_einsum("zyn,nk->zyk", real_part, imag_part, cos_part, sin_part)
    return (to_planes(real_part), to_planes(imag_part))


def y_transform(real_part, imag_part):
    planes, length, width = real_part.shape
    outer = 1 << (length.bit_length() - 1) // 2
    inner = length // outer
    outer_index = jnp.arange(outer, dtype=jnp.int32)
    inner_index = jnp.arange(inner, dtype=jnp.int32)
    cos_one, sin_one = root_table(outer_index, outer_index, outer)
    cos_two, sin_two = root_table(inner_index, inner_index, inner)
    cos_mid, sin_mid = root_table(outer_index, inner_index, length)
    shaped_real = real_part.reshape(planes, outer, inner, width)
    shaped_imag = imag_part.reshape(planes, outer, inner, width)
    step_real, step_imag = complex_einsum("zabc,ak->zkbc", shaped_real, shaped_imag, cos_one, sin_one)
    twist_cos = cos_mid[None, :, :, None]
    twist_sin = sin_mid[None, :, :, None]
    turned_real = step_real * twist_cos - step_imag * twist_sin
    turned_imag = step_real * twist_sin + step_imag * twist_cos
    final_real, final_imag = complex_einsum("zkbc,bj->zjkc", turned_real, turned_imag, cos_two, sin_two)
    return (final_real.reshape(planes, length, width), final_imag.reshape(planes, length, width))


def any_way(field, row_scale, col_scale, row_rate, col_shift, col_mix):
    spec_real, spec_imag = y_transform(*x_butterfly(field))
    length = spec_real.shape[1]
    total_cols = spec_real.shape[2] * lax.axis_size("gx")
    norm_factor = 1.0 / math.sqrt(length * total_cols)
    scale = row_scale[None, :, None] * col_scale[None, None, :]
    latent_u = spec_real * norm_factor * scale
    latent_v = spec_imag * norm_factor * scale
    log_scale = row_rate[None, :, None] * jnp.tanh(latent_u + col_shift[None, None, :])
    latent_w = latent_v * jnp.exp(log_scale) + col_mix[None, None, :] * latent_u
    terms = (
        -0.5 * (latent_u * latent_u + latent_w * latent_w)
        - math.log(2.0 * math.pi)
        + log_scale
        + 2.0 * jnp.log(scale)
    )
    mode_count = spec_real.size * lax.axis_size("gx") * lax.axis_size("gy")
    loglik = lax.psum(jnp.sum(terms), ("gx", "gy")) / mode_count
    return (jnp.stack([latent_u, latent_w]), loglik)


def per_device(field, *scales):
    return (four_way if lax.axis_size("gx") == 4 else any_way)(field, *scales)


def solution(mesh):
    return jax.shard_map(
        per_device,
        mesh=mesh,
        in_specs=(P(None, "gy", "gx"), P(), P("gx"), P(), P("gx"), P("gx")),
        out_specs=(P(None, "gy", None, "gx"), P()),
        check_vma=False,
    )
```

```python
import functools
import math

import jax
import jax.numpy as jnp
from jax import lax
from jax.experimental import pallas as pl
from jax.experimental.pallas import tpu as pltpu
from jax.sharding import PartitionSpec as P

precision_top = lax.Precision.HIGHEST
RADIX = 8
Y_BYTES, X_BYTES = 20 * 1024 * 1024, 30 * 1024 * 1024


def from_partner(value, axis, stride):
    mask = 2**stride
    pairs = [(source, source ^ mask) for source in range(lax.axis_size(axis))]
    return lax.ppermute(value, axis, pairs)


def to_planes(values):
    return lax.all_to_all(values, "gy", split_axis=0, concat_axis=1, tiled=True)


def reverse_bits(value, count):
    result = value * 0
    for place in range(count):
        result = result + (value >> place & 1) * (1 << count - 1 - place)
    return result


def root_table(row_index, freqs, length):
    phase = row_index[:, None] * freqs[None, :] % length
    angle = phase.astype(jnp.float32) * (-2.0 * math.pi / length)
    return (jnp.cos(angle), jnp.sin(angle))


def x_tables(width, devices, position):
    levels = devices.bit_length() - 1
    local_index = jnp.arange(width, dtype=jnp.int32)
    freqs = reverse_bits(position, levels) + devices * local_index
    return root_table(local_index, freqs, devices * width)


def split_table(table, axis, order):
    high = lax.reduce_precision(table, 8, 7)
    parts = [high.astype(jnp.bfloat16), (table - high).astype(jnp.bfloat16)]
    return jnp.concatenate([parts[which] for which in order], axis)


def split_value(value):
    high = value.astype(jnp.bfloat16)
    return high, (value - high.astype(jnp.float32)).astype(jnp.bfloat16)


def small_fft(values):
    count = len(values)
    if count == 1:
        return values
    even, odd = small_fft(values[0::2]), small_fft(values[1::2])
    first, second = [], []
    root_half = math.sqrt(0.5)
    for place in range(count // 2):
        (er, ei), (re, im) = even[place], odd[place]
        turn = place * 8 // count
        if turn == 1:
            re, im = (re + im) * root_half, (im - re) * root_half
        elif turn == 2:
            re, im = im, -re
        elif turn == 3:
            re, im = (im - re) * root_half, (re + im) * -root_half
        first.append((er + re, ei + im))
        second.append((er - re, ei - im))
    return first + second


def dot(left, right):
    return jnp.dot(left, right, preferred_element_type=jnp.float32)


def y_kernel(count, coef_ref, *refs):
    inputs, (table_ref, twist_ref, out_ref, split_ref, step_ref) = refs[:count], refs[count:]
    length, width = inputs[0].shape
    inner = length // RADIX
    for s in range(RADIX):
        parts = [ref[pl.ds(s, inner, stride=RADIX), :] for ref in inputs]
        for which in range(2):
            mixed = parts[0] * coef_ref[which, 0]
            for place in range(1, count):
                mixed = mixed + parts[place] * coef_ref[which, place]
            high, low = split_value(mixed)
            cols = pl.ds(s * width, width)
            for place, value in enumerate((high, high, low)):
                split_ref[pl.ds((2 * place + which) * inner, inner), cols] = value
    step_ref[...] = dot(table_ref[...], split_ref[...])
    rows_each = 16

    @pl.loop(0, inner // rows_each)
    def _(block):
        start = pl.multiple_of(block * rows_each, rows_each)
        values = []
        for s in range(RADIX):
            cols = pl.ds(s * width, width)
            re = step_ref[pl.ds(start, rows_each), cols]
            im = step_ref[pl.ds(pl.multiple_of(start + inner, rows_each), rows_each), cols]
            if s:
                cos, sin = twist_ref[0, s, pl.ds(start, rows_each), :], twist_ref[1, s, pl.ds(start, rows_each), :]
                re, im = re * cos - im * sin, re * sin + im * cos
            values.append((re, im))
        for kb, pair in enumerate(small_fft(values)):
            rows = pl.ds(pl.multiple_of(kb * inner + start, rows_each), rows_each)
            for which in range(2):
                high, low = split_value(pair[which])
                out_ref[2 * which, rows, :] = high
                out_ref[2 * which + 1, rows, :] = low


def y_dft(inputs, coefs, table, twist):
    count = len(inputs)
    length, width = inputs[0].shape
    inner = length // RADIX
    whole = pl.BlockSpec(memory_space=pltpu.VMEM)
    return pl.pallas_call(
        functools.partial(y_kernel, count),
        out_shape=jax.ShapeDtypeStruct((4, length, width), jnp.bfloat16),
        in_specs=[pl.BlockSpec(memory_space=pltpu.SMEM)] + [whole] * (count + 2),
        out_specs=whole,
        scratch_shapes=[
            pltpu.VMEM((6 * inner, RADIX * width), jnp.bfloat16),
            pltpu.VMEM((2 * inner, RADIX * width), jnp.float32),
        ],
        compiler_params=pltpu.CompilerParams(vmem_limit_bytes=Y_BYTES),
        cost_estimate=pl.CostEstimate(
            flops=24 * inner * length * width, bytes_accessed=4 * length * width * (count + 3), transcendentals=0
        ),
        name="y_dft",
    )(coefs, *inputs, table, twist)


def x_product(parts, table_ref):
    high = [ref[which] for ref in parts for which in (0, 2)]
    low = [ref[which] for ref in parts for which in (1, 3)]
    return dot(jnp.concatenate(high + low + high, axis=1), table_ref[...])


def x_first_kernel(count, *refs):
    parts, (table_ref, out_ref) = refs[:count], refs[count:]
    out_ref[...] = x_product(parts, table_ref)


def x_first(parts, table):
    count = len(parts)
    _, length, width = parts[0].shape
    columns = table.shape[1]
    rows = length // 4
    return pl.pallas_call(
        functools.partial(x_first_kernel, count),
        out_shape=jax.ShapeDtypeStruct((length, columns), jnp.float32),
        grid=(length // rows,),
        in_specs=[pl.BlockSpec((4, rows, width), lambda i: (0, i, 0))] * count
        + [pl.BlockSpec(table.shape, lambda i: (0, 0))],
        out_specs=pl.BlockSpec((rows, columns), lambda i: (i, 0)),
        compiler_params=pltpu.CompilerParams(vmem_limit_bytes=X_BYTES),
        cost_estimate=pl.CostEstimate(
            flops=12 * count * length * width * columns, bytes_accessed=8 * length * columns, transcendentals=0
        ),
        name="x_first",
    )(*parts, table)


def x_last_kernel(count, *refs):
    parts, (table_ref, sum_ref, row_ref, col_ref, out_ref, total_ref) = refs[:count], refs[count:]
    spec = sum_ref[...] + x_product(parts, table_ref)
    columns = spec.shape[1] // 2
    lanes = row_ref.shape[2]
    total = None
    for tile in range(columns // lanes):
        cols = pl.ds(tile * lanes, lanes)
        col_scale, col_shift, col_mix = col_ref[0:1, cols], col_ref[1:2, cols], col_ref[2:3, cols]
        scale = row_ref[0] * col_scale
        latent_u = spec[:, tile * lanes : (tile + 1) * lanes] * scale
        latent_v = spec[:, columns + tile * lanes : columns + (tile + 1) * lanes] * scale
        log_scale = row_ref[1] * jnp.tanh(latent_u + col_shift)
        latent_w = latent_v * jnp.exp(log_scale) + col_mix * latent_u
        out_ref[0, 0, :, cols] = latent_u
        out_ref[1, 0, :, cols] = latent_w
        terms = log_scale - 0.5 * (latent_u * latent_u + latent_w * latent_w)
        terms = jnp.sum(terms.reshape(-1, 8, lanes), axis=0)
        total = terms if total is None else total + terms

    @pl.when(pl.program_id(0) == 0)
    def _():
        total_ref[...] = jnp.zeros_like(total_ref)

    total_ref[...] += total


def x_last(parts, table, sums, row_pair, col_trio):
    count = len(parts)
    _, length, width = parts[0].shape
    columns = table.shape[1]
    rows = length // 4
    return pl.pallas_call(
        functools.partial(x_last_kernel, count),
        out_shape=(
            jax.ShapeDtypeStruct((2, 1, length, columns // 2), jnp.float32),
            jax.ShapeDtypeStruct((8, row_pair.shape[2]), jnp.float32),
        ),
        grid=(length // rows,),
        in_specs=[pl.BlockSpec((4, rows, width), lambda i: (0, i, 0))] * count
        + [
            pl.BlockSpec(table.shape, lambda i: (0, 0)),
            pl.BlockSpec((rows, columns), lambda i: (i, 0)),
            pl.BlockSpec((2, rows, row_pair.shape[2]), lambda i: (0, i, 0)),
            pl.BlockSpec(col_trio.shape, lambda i: (0, 0)),
        ],
        out_specs=(
            pl.BlockSpec((2, 1, rows, columns // 2), lambda i: (0, 0, i, 0)),
            pl.BlockSpec((8, row_pair.shape[2]), lambda i: (0, 0)),
        ),
        compiler_params=pltpu.CompilerParams(vmem_limit_bytes=X_BYTES),
        cost_estimate=pl.CostEstimate(
            flops=12 * count * length * width * columns,
            bytes_accessed=12 * length * columns,
            transcendentals=length * columns,
        ),
        name="x_last",
    )(*parts, table, sums, row_pair, col_trio)


def sum_everywhere(tile):
    devices = lax.axis_size("gx")
    others = [lax.ppermute(tile, "gx", [(s, s ^ m) for s in range(devices)]) for m in range(1, devices)]
    tile = functools.reduce(jnp.add, others, tile)
    copies = jnp.broadcast_to(tile[None], (lax.axis_size("gy"),) + tile.shape)
    return jnp.sum(lax.all_to_all(copies, "gy", split_axis=0, concat_axis=0, tiled=True))


def four_way(field, row_scale, col_scale, row_rate, col_shift, col_mix):
    position = lax.axis_index("gx")
    planes, rows, columns = field.shape
    length, width = planes * rows, columns // 4
    field_a, field_b = (field[:, :, : 2 * width], lax.optimization_barrier(field)[:, :, 2 * width :])
    sign = jnp.where(position < 2, 1.0, -1.0)

    own_real = jnp.where(position == 1, -1.0, jnp.where(position == 3, 0.0, 1.0))
    other_real = jnp.where(position == 2, 0.0, 1.0)
    own_imag = jnp.where(position == 3, 1.0, 0.0)
    other_imag = jnp.where(position == 2, -1.0, 0.0)
    coefs_a = jnp.stack([own_real, other_real, own_imag, other_imag]).reshape(2, 2)
    coefs_b = jnp.concatenate([coefs_a, coefs_a * sign], axis=1)

    inner = length // RADIX
    index = jnp.arange(inner, dtype=jnp.int32)
    cos, sin = root_table(index, index, inner)
    y_table = jnp.concatenate([jnp.concatenate([cos, -sin], 1), jnp.concatenate([sin, cos], 1)], 0)
    y_table = split_table(y_table, 1, (0, 1, 0))
    cos, sin = root_table(jnp.arange(RADIX, dtype=jnp.int32), index, length)
    twist = jnp.broadcast_to(jnp.stack([cos, sin])[:, :, :, None], (2, RADIX, inner, width))
    cos, sin = x_tables(columns, 4, position)
    real_rows, imag_rows = jnp.concatenate([cos, sin], 1), jnp.concatenate([-sin, cos], 1)

    def x_table(chunks):
        spans = [slice(c * width, (c + 1) * width) for c in chunks]
        return split_table(jnp.concatenate([rows[s] for s in spans for rows in (real_rows, imag_rows)], 0), 0, (0, 0, 1))

    norm = 1.0 / math.sqrt(length * columns * 4)
    row_pair = jnp.broadcast_to(jnp.stack([row_scale * norm, row_rate])[:, :, None], (2, length, 128))
    col_trio = jnp.stack([col_scale, col_shift, col_mix])
    fixed = 2.0 * (columns * jnp.sum(jnp.log(row_scale)) + length * jnp.sum(jnp.log(col_scale)))
    fixed = fixed - length * columns * math.log(2.0 * math.pi)

    tables = (y_table, twist, x_table((0, 2)), x_table((1, 3)), row_pair, col_trio, coefs_a, coefs_b, fixed)
    received, first_b, tables = lax.optimization_barrier((from_partner(field_a, "gx", 1), to_planes(field_b)[0], tables))
    y_table, twist, table_one, table_two, row_pair, col_trio, coefs_a, coefs_b, fixed = tables
    received_too, field_too = lax.optimization_barrier((received, field_a))
    first_a = [
        received[:, :, :width] + sign * field_a[:, :, :width],
        received_too[:, :, width:] + sign * field_too[:, :, width:],
    ]
    first_b = [first_b[:, :width], lax.optimization_barrier(first_b)[:, width:]]

    def y_part_a(own):
        return y_dft([own, from_partner(own, "gx", 0)], coefs_a, y_table, twist)

    def y_part_b(late, early):
        group = [late, from_partner(late, "gx", 0), early, from_partner(early, "gx", 0)]
        return y_dft(group, coefs_b, y_table, twist)

    second_a, second_b = to_planes(first_a[0])[0], from_partner(first_b[0], "gx", 1)
    first_a[1], second_b = lax.optimization_barrier((first_a[1], second_b))
    sums = x_first([y_part_a(second_a), y_part_b(second_b, first_b[0])], table_one)
    second_a, second_b = to_planes(first_a[1])[0], from_partner(first_b[1], "gx", 1)
    sums, second_a, second_b = lax.optimization_barrier((sums, second_a, second_b))
    parts = [y_part_a(second_a), y_part_b(second_b, first_b[1])]
    latent, tile = x_last(parts, table_two, sums, row_pair, col_trio)
    tile = tile + fixed / tile.size
    modes = length * columns * lax.axis_size("gx") * lax.axis_size("gy")
    return (latent, sum_everywhere(tile) / modes)


def complex_einsum(form, real_part, imag_part, cos_part, sin_part):
    first = jnp.einsum(form, real_part, cos_part, precision=precision_top)
    second = jnp.einsum(form, real_part, sin_part, precision=precision_top)
    first = first - jnp.einsum(form, imag_part, sin_part, precision=precision_top)
    second = second + jnp.einsum(form, imag_part, cos_part, precision=precision_top)
    return (first, second)


def x_butterfly(field):
    devices = lax.axis_size("gx")
    levels = devices.bit_length() - 1
    position = lax.axis_index("gx")
    real_part, imag_part = field, jnp.zeros_like(field)
    for level in range(levels - 1, -1, -1):
        half = 1 << level
        lower = position // half % 2 == 0
        offset = position % half
        angle = offset.astype(jnp.float32) * (-math.pi / half)
        cos_twist = jnp.where(lower, 1.0, jnp.cos(angle))
        sin_twist = jnp.where(lower, 0.0, jnp.sin(angle))
        other = from_partner(jnp.stack([real_part, imag_part]), "gx", level)
        diff_real = jnp.where(lower, real_part + other[0], other[0] - real_part)
        diff_imag = jnp.where(lower, imag_part + other[1], other[1] - imag_part)
        real_part = diff_real * cos_twist - diff_imag * sin_twist
        imag_part = diff_real * sin_twist + diff_imag * cos_twist
    cos_part, sin_part = x_tables(field.shape[2], devices, position)
    real_part, imag_part = complex_einsum("zyn,nk->zyk", real_part, imag_part, cos_part, sin_part)
    return (to_planes(real_part), to_planes(imag_part))


def y_transform(real_part, imag_part):
    planes, length, width = real_part.shape
    outer = 1 << (length.bit_length() - 1) // 2
    inner = length // outer
    outer_index = jnp.arange(outer, dtype=jnp.int32)
    inner_index = jnp.arange(inner, dtype=jnp.int32)
    cos_one, sin_one = root_table(outer_index, outer_index, outer)
    cos_two, sin_two = root_table(inner_index, inner_index, inner)
    cos_mid, sin_mid = root_table(outer_index, inner_index, length)
    shaped_real = real_part.reshape(planes, outer, inner, width)
    shaped_imag = imag_part.reshape(planes, outer, inner, width)
    step_real, step_imag = complex_einsum("zabc,ak->zkbc", shaped_real, shaped_imag, cos_one, sin_one)
    twist_cos = cos_mid[None, :, :, None]
    twist_sin = sin_mid[None, :, :, None]
    turned_real = step_real * twist_cos - step_imag * twist_sin
    turned_imag = step_real * twist_sin + step_imag * twist_cos
    final_real, final_imag = complex_einsum("zkbc,bj->zjkc", turned_real, turned_imag, cos_two, sin_two)
    return (final_real.reshape(planes, length, width), final_imag.reshape(planes, length, width))


def any_way(field, row_scale, col_scale, row_rate, col_shift, col_mix):
    spec_real, spec_imag = y_transform(*x_butterfly(field))
    length = spec_real.shape[1]
    total_cols = spec_real.shape[2] * lax.axis_size("gx")
    norm_factor = 1.0 / math.sqrt(length * total_cols)
    scale = row_scale[None, :, None] * col_scale[None, None, :]
    latent_u = spec_real * norm_factor * scale
    latent_v = spec_imag * norm_factor * scale
    log_scale = row_rate[None, :, None] * jnp.tanh(latent_u + col_shift[None, None, :])
    latent_w = latent_v * jnp.exp(log_scale) + col_mix[None, None, :] * latent_u
    terms = (
        -0.5 * (latent_u * latent_u + latent_w * latent_w)
        - math.log(2.0 * math.pi)
        + log_scale
        + 2.0 * jnp.log(scale)
    )
    mode_count = spec_real.size * lax.axis_size("gx") * lax.axis_size("gy")
    loglik = lax.psum(jnp.sum(terms), ("gx", "gy")) / mode_count
    return (jnp.stack([latent_u, latent_w]), loglik)


def per_device(field, *scales):
    return (four_way if lax.axis_size("gx") == 4 else any_way)(field, *scales)


def solution(mesh):
    return jax.shard_map(
        per_device,
        mesh=mesh,
        in_specs=(P(None, "gy", "gx"), P(), P("gx"), P(), P("gx"), P("gx")),
        out_specs=(P(None, "gy", None, "gx"), P()),
        check_vma=False,
    )
```

```python
import functools
import math

import jax
import jax.numpy as jnp
from jax import lax
from jax.experimental import pallas as pl
from jax.experimental.pallas import tpu as pltpu
from jax.sharding import PartitionSpec as P

precision_top = lax.Precision.HIGHEST
RADIX = 8
LANES = 128
Y_BYTES, X_BYTES = 28 * 1024 * 1024, 30 * 1024 * 1024


def from_partner(value, axis, stride):
    mask = 2**stride
    pairs = [(source, source ^ mask) for source in range(lax.axis_size(axis))]
    return lax.ppermute(value, axis, pairs)


def to_planes(values):
    return lax.all_to_all(values, "gy", split_axis=0, concat_axis=1, tiled=True)


def reverse_bits(value, count):
    result = value * 0
    for place in range(count):
        result = result + (value >> place & 1) * (1 << count - 1 - place)
    return result


def root_table(row_index, freqs, length):
    phase = row_index[:, None] * freqs[None, :] % length
    angle = phase.astype(jnp.float32) * (-2.0 * math.pi / length)
    return (jnp.cos(angle), jnp.sin(angle))


def x_tables(width, devices, position):
    levels = devices.bit_length() - 1
    local_index = jnp.arange(width, dtype=jnp.int32)
    freqs = reverse_bits(position, levels) + devices * local_index
    return root_table(local_index, freqs, devices * width)


def split_table(table, axis, order):
    high = lax.reduce_precision(table, 8, 7)
    parts = [high.astype(jnp.bfloat16), (table - high).astype(jnp.bfloat16)]
    return jnp.concatenate([parts[which] for which in order], axis)


def split_value(value):
    high = value.astype(jnp.bfloat16)
    return high, (value - high.astype(jnp.float32)).astype(jnp.bfloat16)


def small_fft(values):
    count = len(values)
    if count == 1:
        return values
    even, odd = small_fft(values[0::2]), small_fft(values[1::2])
    first, second = [], []
    root_half = math.sqrt(0.5)
    for place in range(count // 2):
        (er, ei), (re, im) = even[place], odd[place]
        turn = place * 8 // count
        if turn == 1:
            re, im = (re + im) * root_half, (im - re) * root_half
        elif turn == 2:
            re, im = im, -re
        elif turn == 3:
            re, im = (im - re) * root_half, (re + im) * -root_half
        first.append((er + re, ei + im))
        second.append((er - re, ei - im))
    return first + second


def dot(left, right):
    return jnp.dot(left, right, preferred_element_type=jnp.float32)


def y_kernel(count, coef_ref, *refs):
    inputs, (table_ref, twist_ref, out_ref, mix_ref, split_ref, step_ref) = refs[:count], refs[count:]
    length, width = inputs[0].shape
    inner = length // RADIX
    for lane in range(0, width, LANES):
        parts = [ref[:, pl.ds(lane, LANES)] for ref in inputs]
        for which in range(2):
            mixed = parts[0] * coef_ref[which, 0]
            for place in range(1, count):
                mixed = mixed + parts[place] * coef_ref[which, place]
            mix_ref[...] = mixed
            for s in range(RADIX):
                high, low = split_value(mix_ref[pl.ds(s, inner, stride=RADIX), :])
                cols = pl.ds(s * width + lane, LANES)
                for place, value in enumerate((high, high, low)):
                    split_ref[pl.ds((2 * place + which) * inner, inner), cols] = value
    step_ref[...] = dot(table_ref[...], split_ref[...])
    rows_each = 16

    def finish(start, lane):
        values = []
        for s in range(RADIX):
            cols = pl.ds(s * width + lane, LANES)
            re = step_ref[pl.ds(start, rows_each), cols]
            im = step_ref[pl.ds(pl.multiple_of(start + inner, rows_each), rows_each), cols]
            if s:
                cos, sin = twist_ref[0, s, pl.ds(start, rows_each), :], twist_ref[1, s, pl.ds(start, rows_each), :]
                re, im = re * cos - im * sin, re * sin + im * cos
            values.append((re, im))
        for kb, pair in enumerate(small_fft(values)):
            rows = pl.ds(pl.multiple_of(kb * inner + start, rows_each), rows_each)
            for which in range(2):
                high, low = split_value(pair[which])
                out_ref[2 * which, rows, pl.ds(lane, LANES)] = high
                out_ref[2 * which + 1, rows, pl.ds(lane, LANES)] = low

    @pl.loop(0, inner // rows_each)
    def _(block):
        start = pl.multiple_of(block * rows_each, rows_each)
        for lane in range(0, width, LANES):
            finish(start, lane)


def y_dft(inputs, coefs, table, twist):
    count = len(inputs)
    length, width = inputs[0].shape
    inner = length // RADIX
    whole = pl.BlockSpec(memory_space=pltpu.VMEM)
    return pl.pallas_call(
        functools.partial(y_kernel, count),
        out_shape=jax.ShapeDtypeStruct((4, length, width), jnp.bfloat16),
        in_specs=[pl.BlockSpec(memory_space=pltpu.SMEM)] + [whole] * (count + 2),
        out_specs=whole,
        scratch_shapes=[
            pltpu.VMEM((length, LANES), jnp.float32),
            pltpu.VMEM((6 * inner, RADIX * width), jnp.bfloat16),
            pltpu.VMEM((2 * inner, RADIX * width), jnp.float32),
        ],
        compiler_params=pltpu.CompilerParams(vmem_limit_bytes=Y_BYTES),
        cost_estimate=pl.CostEstimate(
            flops=24 * inner * length * width, bytes_accessed=4 * length * width * (count + 3), transcendentals=0
        ),
        name="y_dft",
    )(coefs, *inputs, table, twist)


def x_product(parts, table_ref):
    high = [ref[which] for ref in parts for which in (0, 2)]
    low = [ref[which] for ref in parts for which in (1, 3)]
    return dot(jnp.concatenate(high + low + high, axis=1), table_ref[...])


def x_first_kernel(count, *refs):
    parts, (table_ref, out_ref) = refs[:count], refs[count:]
    out_ref[...] = x_product(parts, table_ref)


def x_first(parts, table):
    count, length = len(parts), parts[0].shape[1]
    columns = table.shape[1]
    rows = length // 4
    return pl.pallas_call(
        functools.partial(x_first_kernel, count),
        out_shape=jax.ShapeDtypeStruct((length, columns), jnp.float32),
        grid=(length // rows,),
        in_specs=[pl.BlockSpec((4, rows, part.shape[2]), lambda i: (0, i, 0)) for part in parts]
        + [pl.BlockSpec(table.shape, lambda i: (0, 0))],
        out_specs=pl.BlockSpec((rows, columns), lambda i: (i, 0)),
        compiler_params=pltpu.CompilerParams(vmem_limit_bytes=X_BYTES),
        cost_estimate=pl.CostEstimate(
            flops=2 * length * table.size, bytes_accessed=8 * length * columns, transcendentals=0
        ),
        name="x_first",
    )(*parts, table)


def x_last_kernel(count, *refs):
    parts, (table_ref, sum_ref, row_ref, col_ref, out_ref, total_ref) = refs[:count], refs[count:]
    spec = sum_ref[...] + x_product(parts, table_ref)
    columns = spec.shape[1] // 2
    lanes = LANES
    row_scale, row_rate = [
        jnp.concatenate(
            [jnp.broadcast_to(row_ref[which, 0, c : c + 1, :], (lanes, lanes)).T for c in range(row_ref.shape[2])], 0
        )
        for which in range(2)
    ]
    total = None
    for tile in range(columns // lanes):
        cols = pl.ds(tile * lanes, lanes)
        col_scale, col_shift, col_mix = col_ref[0:1, cols], col_ref[1:2, cols], col_ref[2:3, cols]
        scale = row_scale * col_scale
        latent_u = spec[:, tile * lanes : (tile + 1) * lanes] * scale
        latent_v = spec[:, columns + tile * lanes : columns + (tile + 1) * lanes] * scale
        log_scale = row_rate * jnp.tanh(latent_u + col_shift)
        latent_w = latent_v * jnp.exp(log_scale) + col_mix * latent_u
        out_ref[0, 0, :, cols] = latent_u
        out_ref[1, 0, :, cols] = latent_w
        terms = log_scale - 0.5 * (latent_u * latent_u + latent_w * latent_w)
        terms = jnp.sum(terms.reshape(-1, 8, lanes), axis=0)
        total = terms if total is None else total + terms

    @pl.when(pl.program_id(0) == 0)
    def _():
        total_ref[...] = jnp.zeros_like(total_ref)

    total_ref[...] += total


def x_last(parts, table, sums, row_pair, col_trio):
    count, length = len(parts), parts[0].shape[1]
    columns = table.shape[1]
    rows = length // 4
    return pl.pallas_call(
        functools.partial(x_last_kernel, count),
        out_shape=(
            jax.ShapeDtypeStruct((2, 1, length, columns // 2), jnp.float32),
            jax.ShapeDtypeStruct((8, LANES), jnp.float32),
        ),
        grid=(length // rows,),
        in_specs=[pl.BlockSpec((4, rows, part.shape[2]), lambda i: (0, i, 0)) for part in parts]
        + [
            pl.BlockSpec(table.shape, lambda i: (0, 0)),
            pl.BlockSpec((rows, columns), lambda i: (i, 0)),
            pl.BlockSpec((2, 1, rows // LANES, LANES), lambda i: (0, i, 0, 0)),
            pl.BlockSpec(col_trio.shape, lambda i: (0, 0)),
        ],
        out_specs=(
            pl.BlockSpec((2, 1, rows, columns // 2), lambda i: (0, 0, i, 0)),
            pl.BlockSpec((8, LANES), lambda i: (0, 0)),
        ),
        compiler_params=pltpu.CompilerParams(vmem_limit_bytes=X_BYTES),
        cost_estimate=pl.CostEstimate(
            flops=2 * length * table.size,
            bytes_accessed=12 * length * columns,
            transcendentals=length * columns,
        ),
        name="x_last",
    )(*parts, table, sums, row_pair, col_trio)


def sum_everywhere(tile):
    axes = ("gx", "gy")
    devices = lax.axis_size("gx") * lax.axis_size("gy")
    copies = jnp.broadcast_to(tile[None], (devices,) + tile.shape)
    return jnp.sum(lax.all_to_all(copies, axes, split_axis=0, concat_axis=0, tiled=True))


def four_way(field, row_scale, col_scale, row_rate, col_shift, col_mix):
    position = lax.axis_index("gx")
    planes, rows, columns = field.shape
    length, width = planes * rows, columns // 4
    quarters = [slice(0, width), slice(width, 2 * width)]
    field_b, field_rest = lax.optimization_barrier((field[:, :, 2 * width :], field))
    field_a = field_rest[:, :, : 2 * width]
    sign = jnp.where(position < 2, 1.0, -1.0)

    own_real = jnp.where(position == 1, -1.0, jnp.where(position == 3, 0.0, 1.0))
    other_real = jnp.where(position == 2, 0.0, 1.0)
    own_imag = jnp.where(position == 3, 1.0, 0.0)
    other_imag = jnp.where(position == 2, -1.0, 0.0)
    coefs_a = jnp.stack([own_real, other_real, own_imag, other_imag]).reshape(2, 2)
    coefs_b = jnp.concatenate([coefs_a, coefs_a * sign], axis=1)

    inner = length // RADIX
    index = jnp.arange(inner, dtype=jnp.int32)
    cos, sin = root_table(index, index, inner)
    y_table = jnp.concatenate([jnp.concatenate([cos, -sin], 1), jnp.concatenate([sin, cos], 1)], 0)
    y_table = split_table(y_table, 1, (0, 1, 0))
    grid = [lax.broadcasted_iota(jnp.int32, (RADIX, inner, LANES), axis) for axis in range(2)]
    angle = (grid[0] * grid[1]).astype(jnp.float32) * (-2.0 * math.pi / length)
    twist = jnp.stack([jnp.cos(angle), jnp.sin(angle)])
    cos, sin = x_tables(columns, 4, position)
    real_rows, imag_rows = jnp.concatenate([cos, sin], 1), jnp.concatenate([-sin, cos], 1)

    def x_table(*spans):
        return split_table(jnp.concatenate([rows[s] for s in spans for rows in (real_rows, imag_rows)], 0), 0, (0, 0, 1))

    norm = 1.0 / math.sqrt(length * columns * 4)
    row_pair = jnp.stack([row_scale * norm, row_rate]).reshape(2, 4, length // 4 // LANES, LANES)
    col_trio = jnp.stack([col_scale, col_shift, col_mix])
    fixed = 2.0 * (columns * jnp.sum(jnp.log(row_scale)) + length * jnp.sum(jnp.log(col_scale)))
    fixed = fixed - length * columns * math.log(2.0 * math.pi)

    received = from_partner(field_a, "gx", 1)
    first_a = [received[:, :, span] + sign * field_a[:, :, span] for span in quarters]
    tables = (y_table, twist, x_table(quarters[0]), x_table(slice(2 * width, None), quarters[1]), row_pair, col_trio)
    state = lax.optimization_barrier((first_a, to_planes(field_b)[0], tables, coefs_a, coefs_b, fixed))
    first_a, first_b, (y_table, twist, table_one, table_two, row_pair, col_trio), coefs_a, coefs_b, fixed = state

    def y_part_a(own):
        return y_dft([own, from_partner(own, "gx", 0)], coefs_a, y_table, twist)

    second_b = from_partner(first_b, "gx", 1)
    second_a = to_planes(first_a[0])[0]
    second_a, first_a[1] = lax.optimization_barrier((second_a, first_a[1]))
    last_a = to_planes(first_a[1])[0]
    sums = x_first([y_part_a(second_a)], table_one)
    group = [second_b, from_partner(second_b, "gx", 0), first_b, from_partner(first_b, "gx", 0)]
    part_b = y_dft(group, coefs_b, y_table, twist)
    sums, part_b, last_a = lax.optimization_barrier((sums, part_b, last_a))
    latent, tile = x_last([part_b, y_part_a(last_a)], table_two, sums, row_pair, col_trio)
    tile = tile + fixed / tile.size
    modes = length * columns * lax.axis_size("gx") * lax.axis_size("gy")
    return (latent, sum_everywhere(tile) / modes)


def complex_einsum(form, real_part, imag_part, cos_part, sin_part):
    first = jnp.einsum(form, real_part, cos_part, precision=precision_top)
    second = jnp.einsum(form, real_part, sin_part, precision=precision_top)
    first = first - jnp.einsum(form, imag_part, sin_part, precision=precision_top)
    second = second + jnp.einsum(form, imag_part, cos_part, precision=precision_top)
    return (first, second)


def x_butterfly(field):
    devices = lax.axis_size("gx")
    levels = devices.bit_length() - 1
    position = lax.axis_index("gx")
    real_part, imag_part = field, jnp.zeros_like(field)
    for level in range(levels - 1, -1, -1):
        half = 1 << level
        lower = position // half % 2 == 0
        offset = position % half
        angle = offset.astype(jnp.float32) * (-math.pi / half)
        cos_twist = jnp.where(lower, 1.0, jnp.cos(angle))
        sin_twist = jnp.where(lower, 0.0, jnp.sin(angle))
        other = from_partner(jnp.stack([real_part, imag_part]), "gx", level)
        diff_real = jnp.where(lower, real_part + other[0], other[0] - real_part)
        diff_imag = jnp.where(lower, imag_part + other[1], other[1] - imag_part)
        real_part = diff_real * cos_twist - diff_imag * sin_twist
        imag_part = diff_real * sin_twist + diff_imag * cos_twist
    cos_part, sin_part = x_tables(field.shape[2], devices, position)
    real_part, imag_part = complex_einsum("zyn,nk->zyk", real_part, imag_part, cos_part, sin_part)
    return (to_planes(real_part), to_planes(imag_part))


def y_transform(real_part, imag_part):
    planes, length, width = real_part.shape
    outer = 1 << (length.bit_length() - 1) // 2
    inner = length // outer
    outer_index = jnp.arange(outer, dtype=jnp.int32)
    inner_index = jnp.arange(inner, dtype=jnp.int32)
    cos_one, sin_one = root_table(outer_index, outer_index, outer)
    cos_two, sin_two = root_table(inner_index, inner_index, inner)
    cos_mid, sin_mid = root_table(outer_index, inner_index, length)
    shaped_real = real_part.reshape(planes, outer, inner, width)
    shaped_imag = imag_part.reshape(planes, outer, inner, width)
    step_real, step_imag = complex_einsum("zabc,ak->zkbc", shaped_real, shaped_imag, cos_one, sin_one)
    twist_cos = cos_mid[None, :, :, None]
    twist_sin = sin_mid[None, :, :, None]
    turned_real = step_real * twist_cos - step_imag * twist_sin
    turned_imag = step_real * twist_sin + step_imag * twist_cos
    final_real, final_imag = complex_einsum("zkbc,bj->zjkc", turned_real, turned_imag, cos_two, sin_two)
    return (final_real.reshape(planes, length, width), final_imag.reshape(planes, length, width))


def any_way(field, row_scale, col_scale, row_rate, col_shift, col_mix):
    spec_real, spec_imag = y_transform(*x_butterfly(field))
    length = spec_real.shape[1]
    total_cols = spec_real.shape[2] * lax.axis_size("gx")
    norm_factor = 1.0 / math.sqrt(length * total_cols)
    scale = row_scale[None, :, None] * col_scale[None, None, :]
    latent_u = spec_real * norm_factor * scale
    latent_v = spec_imag * norm_factor * scale
    log_scale = row_rate[None, :, None] * jnp.tanh(latent_u + col_shift[None, None, :])
    latent_w = latent_v * jnp.exp(log_scale) + col_mix[None, None, :] * latent_u
    terms = (
        -0.5 * (latent_u * latent_u + latent_w * latent_w)
        - math.log(2.0 * math.pi)
        + log_scale
        + 2.0 * jnp.log(scale)
    )
    mode_count = spec_real.size * lax.axis_size("gx") * lax.axis_size("gy")
    loglik = lax.psum(jnp.sum(terms), ("gx", "gy")) / mode_count
    return (jnp.stack([latent_u, latent_w]), loglik)


def per_device(field, *scales):
    return (four_way if lax.axis_size("gx") == 4 else any_way)(field, *scales)


def solution(mesh):
    return jax.shard_map(
        per_device,
        mesh=mesh,
        in_specs=(P(None, "gy", "gx"), P(), P("gx"), P(), P("gx"), P("gx")),
        out_specs=(P(None, "gy", None, "gx"), P()),
        check_vma=False,
    )
```

```python
import functools
import math

import jax
import jax.numpy as jnp
from jax import lax
from jax.experimental import pallas as pl
from jax.experimental.pallas import tpu as pltpu
from jax.sharding import PartitionSpec as P

precision_top = lax.Precision.HIGHEST
RADIX = 8
LANES = 128
X_BYTES = 30 * 1024 * 1024


def from_partner(value, axis, stride):
    mask = 2**stride
    pairs = [(source, source ^ mask) for source in range(lax.axis_size(axis))]
    return lax.ppermute(value, axis, pairs)


def to_planes(values):
    return lax.all_to_all(values, "gy", split_axis=0, concat_axis=1, tiled=True)


def cut_kernel(field_ref, left_ref, right_ref, sems):
    half = left_ref.shape[2]
    copies = [
        pltpu.make_async_copy(field_ref.at[:, :, pl.ds(place * half, half)], out_ref, sems.at[place])
        for place, out_ref in enumerate((left_ref, right_ref))
    ]
    for copy in copies:
        copy.start()
    for copy in copies:
        copy.wait()


def cut_in_half(field):
    planes, rows, columns = field.shape
    return pl.pallas_call(
        cut_kernel,
        out_shape=[jax.ShapeDtypeStruct((planes, rows, columns // 2), jnp.float32)] * 2,
        in_specs=[pl.BlockSpec(memory_space=pl.ANY)],
        out_specs=[pl.BlockSpec(memory_space=pltpu.VMEM)] * 2,
        scratch_shapes=[pltpu.SemaphoreType.DMA((2,))],
        compiler_params=pltpu.CompilerParams(vmem_limit_bytes=56 * 1024 * 1024),
        cost_estimate=pl.CostEstimate(flops=0, bytes_accessed=8 * field.size, transcendentals=0),
        name="cut_in_half",
    )(field)


def reverse_bits(value, count):
    result = value * 0
    for place in range(count):
        result = result + (value >> place & 1) * (1 << count - 1 - place)
    return result


def root_table(row_index, freqs, length):
    phase = row_index[:, None] * freqs[None, :] % length
    angle = phase.astype(jnp.float32) * (-2.0 * math.pi / length)
    return (jnp.cos(angle), jnp.sin(angle))


def x_tables(width, devices, position):
    levels = devices.bit_length() - 1
    local_index = jnp.arange(width, dtype=jnp.int32)
    freqs = reverse_bits(position, levels) + devices * local_index
    return root_table(local_index, freqs, devices * width)


def split_table(table, axis, order):
    high = lax.reduce_precision(table, 8, 7)
    parts = [high.astype(jnp.bfloat16), (table - high).astype(jnp.bfloat16)]
    return jnp.concatenate([parts[which] for which in order], axis)


def split_value(value):
    high = value.astype(jnp.bfloat16)
    return high, (value - high.astype(jnp.float32)).astype(jnp.bfloat16)


def small_fft(values):
    count = len(values)
    if count == 1:
        return values
    even, odd = small_fft(values[0::2]), small_fft(values[1::2])
    first, second = [], []
    root_half = math.sqrt(0.5)
    for place in range(count // 2):
        (er, ei), (re, im) = even[place], odd[place]
        turn = place * 8 // count
        if turn == 1:
            re, im = (re + im) * root_half, (im - re) * root_half
        elif turn == 2:
            re, im = im, -re
        elif turn == 3:
            re, im = (im - re) * root_half, (re + im) * -root_half
        first.append((er + re, ei + im))
        second.append((er - re, ei - im))
    return first + second


def dot(left, right):
    return jnp.dot(left, right, preferred_element_type=jnp.float32)


def y_kernel(count, coef_ref, *refs):
    inputs, (table_ref, twist_ref, out_ref, mix_ref, split_ref, step_ref) = refs[:count], refs[count:]
    length, width = inputs[0].shape
    inner = length // RADIX
    for lane in range(0, width, LANES):
        parts = [ref[:, pl.ds(lane, LANES)] for ref in inputs]
        for which in range(2):
            mixed = parts[0] * coef_ref[which, 0]
            for place in range(1, count):
                mixed = mixed + parts[place] * coef_ref[which, place]
            mix_ref[...] = mixed
            for s in range(RADIX):
                high, low = split_value(mix_ref[pl.ds(s, inner, stride=RADIX), :])
                cols = pl.ds(s * width + lane, LANES)
                for place, value in enumerate((high, high, low)):
                    split_ref[pl.ds((2 * place + which) * inner, inner), cols] = value
    step_ref[...] = dot(table_ref[...], split_ref[...])
    rows_each = 16

    def finish(start, lane):
        values = []
        for s in range(RADIX):
            cols = pl.ds(s * width + lane, LANES)
            re = step_ref[pl.ds(start, rows_each), cols]
            im = step_ref[pl.ds(pl.multiple_of(start + inner, rows_each), rows_each), cols]
            if s:
                cos, sin = twist_ref[0, s, pl.ds(start, rows_each), :], twist_ref[1, s, pl.ds(start, rows_each), :]
                re, im = re * cos - im * sin, re * sin + im * cos
            values.append((re, im))
        for kb, pair in enumerate(small_fft(values)):
            rows = pl.ds(pl.multiple_of(kb * inner + start, rows_each), rows_each)
            for which in range(2):
                high, low = split_value(pair[which])
                out_ref[2 * which, rows, pl.ds(lane, LANES)] = high
                out_ref[2 * which + 1, rows, pl.ds(lane, LANES)] = low

    @pl.loop(0, inner // rows_each)
    def _(block):
        start = pl.multiple_of(block * rows_each, rows_each)
        for lane in range(0, width, LANES):
            finish(start, lane)


def y_dft(inputs, coefs, table, twist):
    count = len(inputs)
    length, width = inputs[0].shape
    inner = length // RADIX
    whole = pl.BlockSpec(memory_space=pltpu.VMEM)
    return pl.pallas_call(
        functools.partial(y_kernel, count),
        out_shape=jax.ShapeDtypeStruct((4, length, width), jnp.bfloat16),
        in_specs=[pl.BlockSpec(memory_space=pltpu.SMEM)] + [whole] * (count + 2),
        out_specs=whole,
        scratch_shapes=[
            pltpu.VMEM((length, LANES), jnp.float32),
            pltpu.VMEM((6 * inner, RADIX * width), jnp.bfloat16),
            pltpu.VMEM((2 * inner, RADIX * width), jnp.float32),
        ],
        compiler_params=pltpu.CompilerParams(vmem_limit_bytes=(8 + 20 * width // 256) * 1024 * 1024),
        cost_estimate=pl.CostEstimate(
            flops=24 * inner * length * width, bytes_accessed=4 * length * width * (count + 3), transcendentals=0
        ),
        name="y_dft",
    )(coefs, *inputs, table, twist)


def x_product(parts, table_ref):
    high = [ref[which] for ref in parts for which in (0, 2)]
    low = [ref[which] for ref in parts for which in (1, 3)]
    return dot(jnp.concatenate(high + low + high, axis=1), table_ref[...])


def x_first_kernel(count, *refs):
    parts, (table_ref, out_ref) = refs[:count], refs[count:]
    out_ref[...] = x_product(parts, table_ref)


def x_first(parts, table):
    count, length = len(parts), parts[0].shape[1]
    columns = table.shape[1]
    rows = length // 4
    return pl.pallas_call(
        functools.partial(x_first_kernel, count),
        out_shape=jax.ShapeDtypeStruct((length, columns), jnp.float32),
        grid=(length // rows,),
        in_specs=[pl.BlockSpec((4, rows, part.shape[2]), lambda i: (0, i, 0)) for part in parts]
        + [pl.BlockSpec(table.shape, lambda i: (0, 0), pipeline_mode=pl.Buffered(1))],
        out_specs=pl.BlockSpec((rows, columns), lambda i: (i, 0)),
        compiler_params=pltpu.CompilerParams(vmem_limit_bytes=X_BYTES),
        cost_estimate=pl.CostEstimate(
            flops=2 * length * table.size, bytes_accessed=8 * length * columns, transcendentals=0
        ),
        name="x_first",
    )(*parts, table)


def x_last_kernel(count, *refs):
    parts, (table_ref, sum_ref, row_ref, col_ref, out_ref, total_ref) = refs[:count], refs[count:]
    spec = sum_ref[...] + x_product(parts, table_ref)
    columns = spec.shape[1] // 2
    lanes = LANES
    row_scale, row_rate = [
        jnp.concatenate(
            [jnp.broadcast_to(row_ref[which, 0, c : c + 1, :], (lanes, lanes)).T for c in range(row_ref.shape[2])], 0
        )
        for which in range(2)
    ]
    total = None
    for tile in range(columns // lanes):
        cols = pl.ds(tile * lanes, lanes)
        col_scale, col_shift, col_mix = col_ref[0:1, cols], col_ref[1:2, cols], col_ref[2:3, cols]
        scale = row_scale * col_scale
        latent_u = spec[:, tile * lanes : (tile + 1) * lanes] * scale
        latent_v = spec[:, columns + tile * lanes : columns + (tile + 1) * lanes] * scale
        log_scale = row_rate * jnp.tanh(latent_u + col_shift)
        latent_w = latent_v * jnp.exp(log_scale) + col_mix * latent_u
        out_ref[0, 0, :, cols] = latent_u
        out_ref[1, 0, :, cols] = latent_w
        terms = log_scale - 0.5 * (latent_u * latent_u + latent_w * latent_w)
        terms = jnp.sum(terms.reshape(-1, 8, lanes), axis=0)
        total = terms if total is None else total + terms

    @pl.when(pl.program_id(0) == 0)
    def _():
        total_ref[...] = jnp.zeros_like(total_ref)

    total_ref[...] += total


def x_last(parts, table, sums, row_pair, col_trio):
    count, length = len(parts), parts[0].shape[1]
    columns = table.shape[1]
    rows = length // 4
    return pl.pallas_call(
        functools.partial(x_last_kernel, count),
        out_shape=(
            jax.ShapeDtypeStruct((2, 1, length, columns // 2), jnp.float32),
            jax.ShapeDtypeStruct((8, LANES), jnp.float32),
        ),
        grid=(length // rows,),
        in_specs=[pl.BlockSpec((4, rows, part.shape[2]), lambda i: (0, i, 0)) for part in parts]
        + [
            pl.BlockSpec(table.shape, lambda i: (0, 0), pipeline_mode=pl.Buffered(1)),
            pl.BlockSpec((rows, columns), lambda i: (i, 0)),
            pl.BlockSpec((2, 1, rows // LANES, LANES), lambda i: (0, i, 0, 0)),
            pl.BlockSpec(col_trio.shape, lambda i: (0, 0)),
        ],
        out_specs=(
            pl.BlockSpec((2, 1, rows, columns // 2), lambda i: (0, 0, i, 0)),
            pl.BlockSpec((8, LANES), lambda i: (0, 0)),
        ),
        compiler_params=pltpu.CompilerParams(vmem_limit_bytes=X_BYTES),
        cost_estimate=pl.CostEstimate(
            flops=2 * length * table.size,
            bytes_accessed=12 * length * columns,
            transcendentals=length * columns,
        ),
        name="x_last",
    )(*parts, table, sums, row_pair, col_trio)


def sum_everywhere(tile):
    axes = ("gx", "gy")
    devices = lax.axis_size("gx") * lax.axis_size("gy")
    copies = jnp.broadcast_to(tile[None], (devices,) + tile.shape)
    return jnp.sum(lax.all_to_all(copies, axes, split_axis=0, concat_axis=0, tiled=True))


def four_way(field, row_scale, col_scale, row_rate, col_shift, col_mix):
    position = lax.axis_index("gx")
    planes, rows, columns = field.shape
    length, width = planes * rows, columns // 4
    field_a, field_b = cut_in_half(field)
    sign = jnp.where(position < 2, 1.0, -1.0)

    own_real = jnp.where(position == 1, -1.0, jnp.where(position == 3, 0.0, 1.0))
    other_real = jnp.where(position == 2, 0.0, 1.0)
    own_imag = jnp.where(position == 3, 1.0, 0.0)
    other_imag = jnp.where(position == 2, -1.0, 0.0)
    coefs_a = jnp.stack([own_real, other_real, own_imag, other_imag]).reshape(2, 2)
    coefs_b = jnp.concatenate([coefs_a, coefs_a * sign], axis=1)

    inner = length // RADIX
    index = jnp.arange(inner, dtype=jnp.int32)
    cos, sin = root_table(index, index, inner)
    y_table = jnp.concatenate([jnp.concatenate([cos, -sin], 1), jnp.concatenate([sin, cos], 1)], 0)
    y_table = split_table(y_table, 1, (0, 1, 0))
    grid = [lax.broadcasted_iota(jnp.int32, (RADIX, inner, LANES), axis) for axis in range(2)]
    angle = (grid[0] * grid[1]).astype(jnp.float32) * (-2.0 * math.pi / length)
    twist = jnp.stack([jnp.cos(angle), jnp.sin(angle)])
    cos, sin = x_tables(columns, 4, position)
    real_rows, imag_rows = jnp.concatenate([cos, sin], 1), jnp.concatenate([-sin, cos], 1)

    def x_table(*spans):
        return split_table(jnp.concatenate([rows[s] for s in spans for rows in (real_rows, imag_rows)], 0), 0, (0, 0, 1))

    norm = 1.0 / math.sqrt(length * columns * 4)
    row_pair = jnp.stack([row_scale * norm, row_rate]).reshape(2, 4, length // 4 // LANES, LANES)
    col_trio = jnp.stack([col_scale, col_shift, col_mix])
    fixed = 2.0 * (columns * jnp.sum(jnp.log(row_scale)) + length * jnp.sum(jnp.log(col_scale)))
    fixed = fixed - length * columns * math.log(2.0 * math.pi)

    first_a = from_partner(field_a, "gx", 1) + sign * field_a
    spans = [slice(2 * width, 3 * width), slice(3 * width, None), slice(0, 2 * width)]
    tables = (y_table, twist, x_table(spans[0]), x_table(*spans[1:]), row_pair, col_trio)
    state = lax.optimization_barrier((first_a, to_planes(field_b)[0], tables, coefs_a, coefs_b, fixed))
    first_a, first_b, (y_table, twist, table_one, table_two, row_pair, col_trio), coefs_a, coefs_b, fixed = state
    second_a = to_planes(first_a)[0]

    def y_part_b(early):
        late = from_partner(early, "gx", 1)
        group = [late, from_partner(late, "gx", 0), early, from_partner(early, "gx", 0)]
        return y_dft(group, coefs_b, y_table, twist)

    parts = [y_part_b(first_b[:, :width]), y_part_b(first_b[:, width:])]
    sums = x_first(parts[:1], table_one)
    sums, parts[1], second_a = lax.optimization_barrier((sums, parts[1], second_a))
    parts.append(y_dft([second_a, from_partner(second_a, "gx", 0)], coefs_a, y_table, twist))
    latent, tile = x_last(parts[1:], table_two, sums, row_pair, col_trio)
    tile = tile + fixed / tile.size
    modes = length * columns * lax.axis_size("gx") * lax.axis_size("gy")
    return (latent, sum_everywhere(tile) / modes)


def complex_einsum(form, real_part, imag_part, cos_part, sin_part):
    first = jnp.einsum(form, real_part, cos_part, precision=precision_top)
    second = jnp.einsum(form, real_part, sin_part, precision=precision_top)
    first = first - jnp.einsum(form, imag_part, sin_part, precision=precision_top)
    second = second + jnp.einsum(form, imag_part, cos_part, precision=precision_top)
    return (first, second)


def x_butterfly(field):
    devices = lax.axis_size("gx")
    levels = devices.bit_length() - 1
    position = lax.axis_index("gx")
    real_part, imag_part = field, jnp.zeros_like(field)
    for level in range(levels - 1, -1, -1):
        half = 1 << level
        lower = position // half % 2 == 0
        offset = position % half
        angle = offset.astype(jnp.float32) * (-math.pi / half)
        cos_twist = jnp.where(lower, 1.0, jnp.cos(angle))
        sin_twist = jnp.where(lower, 0.0, jnp.sin(angle))
        other = from_partner(jnp.stack([real_part, imag_part]), "gx", level)
        diff_real = jnp.where(lower, real_part + other[0], other[0] - real_part)
        diff_imag = jnp.where(lower, imag_part + other[1], other[1] - imag_part)
        real_part = diff_real * cos_twist - diff_imag * sin_twist
        imag_part = diff_real * sin_twist + diff_imag * cos_twist
    cos_part, sin_part = x_tables(field.shape[2], devices, position)
    real_part, imag_part = complex_einsum("zyn,nk->zyk", real_part, imag_part, cos_part, sin_part)
    return (to_planes(real_part), to_planes(imag_part))


def y_transform(real_part, imag_part):
    planes, length, width = real_part.shape
    outer = 1 << (length.bit_length() - 1) // 2
    inner = length // outer
    outer_index = jnp.arange(outer, dtype=jnp.int32)
    inner_index = jnp.arange(inner, dtype=jnp.int32)
    cos_one, sin_one = root_table(outer_index, outer_index, outer)
    cos_two, sin_two = root_table(inner_index, inner_index, inner)
    cos_mid, sin_mid = root_table(outer_index, inner_index, length)
    shaped_real = real_part.reshape(planes, outer, inner, width)
    shaped_imag = imag_part.reshape(planes, outer, inner, width)
    step_real, step_imag = complex_einsum("zabc,ak->zkbc", shaped_real, shaped_imag, cos_one, sin_one)
    twist_cos = cos_mid[None, :, :, None]
    twist_sin = sin_mid[None, :, :, None]
    turned_real = step_real * twist_cos - step_imag * twist_sin
    turned_imag = step_real * twist_sin + step_imag * twist_cos
    final_real, final_imag = complex_einsum("zkbc,bj->zjkc", turned_real, turned_imag, cos_two, sin_two)
    return (final_real.reshape(planes, length, width), final_imag.reshape(planes, length, width))


def any_way(field, row_scale, col_scale, row_rate, col_shift, col_mix):
    spec_real, spec_imag = y_transform(*x_butterfly(field))
    length = spec_real.shape[1]
    total_cols = spec_real.shape[2] * lax.axis_size("gx")
    norm_factor = 1.0 / math.sqrt(length * total_cols)
    scale = row_scale[None, :, None] * col_scale[None, None, :]
    latent_u = spec_real * norm_factor * scale
    latent_v = spec_imag * norm_factor * scale
    log_scale = row_rate[None, :, None] * jnp.tanh(latent_u + col_shift[None, None, :])
    latent_w = latent_v * jnp.exp(log_scale) + col_mix[None, None, :] * latent_u
    terms = (
        -0.5 * (latent_u * latent_u + latent_w * latent_w)
        - math.log(2.0 * math.pi)
        + log_scale
        + 2.0 * jnp.log(scale)
    )
    mode_count = spec_real.size * lax.axis_size("gx") * lax.axis_size("gy")
    loglik = lax.psum(jnp.sum(terms), ("gx", "gy")) / mode_count
    return (jnp.stack([latent_u, latent_w]), loglik)


def per_device(field, *scales):
    return (four_way if lax.axis_size("gx") == 4 else any_way)(field, *scales)


def solution(mesh):
    return jax.shard_map(
        per_device,
        mesh=mesh,
        in_specs=(P(None, "gy", "gx"), P(), P("gx"), P(), P("gx"), P("gx")),
        out_specs=(P(None, "gy", None, "gx"), P()),
        check_vma=False,
    )
```

```python
import functools
import math

import jax
import jax.numpy as jnp
from jax import lax
from jax.experimental import pallas as pl
from jax.experimental.pallas import tpu as pltpu
from jax.sharding import PartitionSpec as P

precision_top = lax.Precision.HIGHEST
RADIX = 8
LANES = 128
CUT_BYTES, SMALL_BYTES, Y_BYTES, X_BYTES = [size * 1024 * 1024 for size in (56, 8, 20, 24)]


def from_partner(value, axis, stride):
    mask = 2**stride
    pairs = [(source, source ^ mask) for source in range(lax.axis_size(axis))]
    return lax.ppermute(value, axis, pairs)


def to_planes(values):
    return lax.all_to_all(values, "gy", split_axis=0, concat_axis=1, tiled=True)


def cut_kernel(place, field_ref, *refs):
    out_ref, sem = refs[-2:]
    half = out_ref.shape[2]
    copy = pltpu.make_async_copy(field_ref.at[:, :, pl.ds(place * half, half)], out_ref, sem)
    copy.start()
    copy.wait()


def cut_half(field, place, *earlier):
    planes, rows, columns = field.shape
    anywhere = pl.BlockSpec(memory_space=pl.ANY)
    return pl.pallas_call(
        functools.partial(cut_kernel, place),
        out_shape=jax.ShapeDtypeStruct((planes, rows, columns // 2), jnp.float32),
        in_specs=[anywhere] * (1 + len(earlier)),
        out_specs=anywhere,
        scratch_shapes=[pltpu.SemaphoreType.DMA],
        compiler_params=pltpu.CompilerParams(vmem_limit_bytes=CUT_BYTES),
        cost_estimate=pl.CostEstimate(flops=0, bytes_accessed=4 * field.size, transcendentals=0),
        name="cut_half",
    )(field, *earlier)


def pick_columns(left, right, odd):
    lane = lax.broadcasted_iota(jnp.int32, left.shape, 1)
    index = (2 * lane + odd) % LANES
    chosen = [jnp.take_along_axis(tile, index, axis=1, mode="promise_in_bounds") for tile in (left, right)]
    return jnp.where(lane < LANES // 2, *chosen)


def combine_kernel(sign_ref, late_ref, early_ref, out_ref):
    sign = sign_ref[0]
    left, right = [
        late_ref[0, :, pl.ds(lane, LANES)] + sign * early_ref[0, :, pl.ds(lane, LANES)] for lane in (0, LANES)
    ]
    for odd in range(2):
        out_ref[0, :, pl.ds(odd * LANES, LANES)] = pick_columns(left, right, odd)


def combine(sign, late, early):
    planes, rows, columns = late.shape
    block = pl.BlockSpec((1, rows, columns), lambda i: (i, 0, 0))
    return pl.pallas_call(
        combine_kernel,
        out_shape=jax.ShapeDtypeStruct(late.shape, jnp.float32),
        grid=(planes,),
        in_specs=[pl.BlockSpec(memory_space=pltpu.SMEM), block, block],
        out_specs=block,
        cost_estimate=pl.CostEstimate(flops=2 * late.size, bytes_accessed=12 * late.size, transcendentals=0),
        compiler_params=pltpu.CompilerParams(vmem_limit_bytes=SMALL_BYTES),
        name="combine",
    )(sign, late, early)


def part_kernel(value_ref, *out_refs):
    left, right = [value_ref[:, pl.ds(lane, LANES)] for lane in (0, LANES)]
    for odd, out_ref in enumerate(out_refs):
        out_ref[...] = pick_columns(left, right, odd)


def part_columns(value):
    length, columns = value.shape
    rows = length // 8
    return pl.pallas_call(
        part_kernel,
        out_shape=[jax.ShapeDtypeStruct((length, columns // 2), jnp.float32)] * 2,
        grid=(length // rows,),
        in_specs=[pl.BlockSpec((rows, columns), lambda i: (i, 0))],
        out_specs=[pl.BlockSpec((rows, columns // 2), lambda i: (i, 0))] * 2,
        cost_estimate=pl.CostEstimate(flops=value.size, bytes_accessed=8 * value.size, transcendentals=0),
        compiler_params=pltpu.CompilerParams(vmem_limit_bytes=SMALL_BYTES),
        name="part_columns",
    )(value)


def reverse_bits(value, count):
    result = value * 0
    for place in range(count):
        result = result + (value >> place & 1) * (1 << count - 1 - place)
    return result


def root_table(row_index, freqs, length):
    phase = row_index[:, None] * freqs[None, :] % length
    angle = phase.astype(jnp.float32) * (-2.0 * math.pi / length)
    return (jnp.cos(angle), jnp.sin(angle))


def x_tables(rows, width, devices, position):
    levels = devices.bit_length() - 1
    local_index = jnp.arange(width, dtype=jnp.int32)
    freqs = reverse_bits(position, levels) + devices * local_index
    return root_table(rows, freqs, devices * width)


def split_table(table, axis, order):
    high = lax.reduce_precision(table, 8, 7)
    parts = [high.astype(jnp.bfloat16), (table - high).astype(jnp.bfloat16)]
    return jnp.concatenate([parts[which] for which in order], axis)


def split_value(value):
    high = value.astype(jnp.bfloat16)
    return high, (value - high.astype(jnp.float32)).astype(jnp.bfloat16)


def small_fft(values):
    count = len(values)
    if count == 1:
        return values
    even, odd = small_fft(values[0::2]), small_fft(values[1::2])
    first, second = [], []
    root_half = math.sqrt(0.5)
    for place in range(count // 2):
        (er, ei), (re, im) = even[place], odd[place]
        turn = place * 8 // count
        if turn == 1:
            re, im = (re + im) * root_half, (im - re) * root_half
        elif turn == 2:
            re, im = im, -re
        elif turn == 3:
            re, im = (im - re) * root_half, (re + im) * -root_half
        first.append((er + re, ei + im))
        second.append((er - re, ei - im))
    return first + second


def dot(left, right):
    return jnp.dot(left, right, preferred_element_type=jnp.float32)


def y_kernel(lanes, coef_ref, *refs):
    count = len(lanes)
    inputs, (table_ref, twist_ref, out_ref, mix_ref, split_ref, step_ref) = refs[:count], refs[count:]
    inner = mix_ref.shape[0] // RADIX
    parts = [ref[:, pl.ds(lane, LANES)] for ref, lane in zip(inputs, lanes)]
    for which in range(2):
        mixed = parts[0] * coef_ref[which, 0]
        for place in range(1, count):
            mixed = mixed + parts[place] * coef_ref[which, place]
        mix_ref[...] = mixed
        for s in range(RADIX):
            high, low = split_value(mix_ref[pl.ds(s, inner, stride=RADIX), :])
            for place, value in enumerate((high, high, low)):
                split_ref[pl.ds((2 * place + which) * inner, inner), pl.ds(s * LANES, LANES)] = value
    step_ref[...] = dot(table_ref[...], split_ref[...])
    rows_each = 16

    @pl.loop(0, inner // rows_each, unroll=2)
    def _(block):
        start = pl.multiple_of(block * rows_each, rows_each)
        values = []
        for s in range(RADIX):
            cols = pl.ds(s * LANES, LANES)
            re = step_ref[pl.ds(start, rows_each), cols]
            im = step_ref[pl.ds(pl.multiple_of(start + inner, rows_each), rows_each), cols]
            if s:
                cos, sin = twist_ref[0, s, pl.ds(start, rows_each), :], twist_ref[1, s, pl.ds(start, rows_each), :]
                re, im = re * cos - im * sin, re * sin + im * cos
            values.append((re, im))
        for kb, pair in enumerate(small_fft(values)):
            rows = pl.ds(pl.multiple_of(kb * inner + start, rows_each), rows_each)
            for which in range(2):
                high, low = split_value(pair[which])
                out_ref[2 * which, rows, :] = high
                out_ref[2 * which + 1, rows, :] = low


def y_dft(inputs, coefs, table, twist):
    arrays, lanes = zip(*inputs)
    length = arrays[0].shape[0]
    inner = length // RADIX
    whole = pl.BlockSpec(memory_space=pltpu.VMEM)
    return pl.pallas_call(
        functools.partial(y_kernel, lanes),
        out_shape=jax.ShapeDtypeStruct((4, length, LANES), jnp.bfloat16),
        in_specs=[pl.BlockSpec(memory_space=pltpu.SMEM)] + [whole] * (len(arrays) + 2),
        out_specs=whole,
        scratch_shapes=[
            pltpu.VMEM((length, LANES), jnp.float32),
            pltpu.VMEM((6 * inner, RADIX * LANES), jnp.bfloat16),
            pltpu.VMEM((2 * inner, RADIX * LANES), jnp.float32),
        ],
        compiler_params=pltpu.CompilerParams(vmem_limit_bytes=Y_BYTES),
        cost_estimate=pl.CostEstimate(
            flops=24 * inner * length * LANES, bytes_accessed=4 * length * LANES * (len(arrays) + 3), transcendentals=0
        ),
        name="y_dft",
    )(coefs, *arrays, table, twist)


def x_product(parts, table_ref):
    high = [ref[which] for ref in parts for which in (0, 2)]
    low = [ref[which] for ref in parts for which in (1, 3)]
    return dot(jnp.concatenate(high + low + high, axis=1), table_ref[...])


def x_kernel(count, *refs):
    parts, (even_ref, odd_ref, row_ref, col_ref, out_ref, total_ref) = refs[: 2 * count], refs[2 * count :]
    even, odd = x_product(parts[:count], even_ref), x_product(parts[count:], odd_ref)
    half = even.shape[1] // 2
    lanes = LANES
    row_scale, row_rate = [
        jnp.concatenate(
            [jnp.broadcast_to(row_ref[which, 0, c : c + 1, :], (lanes, lanes)).T for c in range(row_ref.shape[2])], 0
        )
        for which in range(2)
    ]
    total = None
    for tile in range(half // lanes):
        real, imag = [slice(start, start + lanes) for start in (tile * lanes, half + tile * lanes)]
        for upper in range(2):
            cols = pl.ds(upper * half + tile * lanes, lanes)
            spec_real = even[:, real] - odd[:, real] if upper else even[:, real] + odd[:, real]
            spec_imag = even[:, imag] - odd[:, imag] if upper else even[:, imag] + odd[:, imag]
            col_scale, col_shift, col_mix = col_ref[0:1, cols], col_ref[1:2, cols], col_ref[2:3, cols]
            scale = row_scale * col_scale
            latent_u = spec_real * scale
            latent_v = spec_imag * scale
            log_scale = row_rate * jnp.tanh(latent_u + col_shift)
            latent_w = latent_v * jnp.exp(log_scale) + col_mix * latent_u
            out_ref[0, 0, :, cols] = latent_u
            out_ref[1, 0, :, cols] = latent_w
            terms = log_scale - 0.5 * (latent_u * latent_u + latent_w * latent_w)
            terms = jnp.sum(terms.reshape(-1, 8, lanes), axis=0)
            total = terms if total is None else total + terms

    @pl.when(pl.program_id(0) == 0)
    def _():
        total_ref[...] = jnp.zeros_like(total_ref)

    total_ref[...] += total


def x_dft(even_parts, odd_parts, even_table, odd_table, row_pair, col_trio):
    parts, count, length = even_parts + odd_parts, len(even_parts), even_parts[0].shape[1]
    columns = even_table.shape[1]
    rows = length // row_pair.shape[1]
    fixed = [pl.BlockSpec(table.shape, lambda i: (0, 0), pipeline_mode=pl.Buffered(1)) for table in (even_table, odd_table)]
    return pl.pallas_call(
        functools.partial(x_kernel, count),
        out_shape=(
            jax.ShapeDtypeStruct((2, 1, length, columns), jnp.float32),
            jax.ShapeDtypeStruct((8, LANES), jnp.float32),
        ),
        grid=(length // rows,),
        in_specs=[pl.BlockSpec((4, rows, part.shape[2]), lambda i: (0, i, 0)) for part in parts]
        + fixed
        + [
            pl.BlockSpec((2, 1, rows // LANES, LANES), lambda i: (0, i, 0, 0)),
            pl.BlockSpec(col_trio.shape, lambda i: (0, 0)),
        ],
        out_specs=(
            pl.BlockSpec((2, 1, rows, columns), lambda i: (0, 0, i, 0)),
            pl.BlockSpec((8, LANES), lambda i: (0, 0)),
        ),
        compiler_params=pltpu.CompilerParams(vmem_limit_bytes=X_BYTES),
        cost_estimate=pl.CostEstimate(
            flops=4 * length * even_table.size,
            bytes_accessed=16 * length * columns,
            transcendentals=2 * length * columns,
        ),
        name="x_dft",
    )(*parts, even_table, odd_table, row_pair, col_trio)


def sum_everywhere(tile):
    axes = ("gx", "gy")
    devices = lax.axis_size("gx") * lax.axis_size("gy")
    copies = jnp.broadcast_to(tile[None], (devices,) + tile.shape)
    return jnp.sum(lax.all_to_all(copies, axes, split_axis=0, concat_axis=0, tiled=True))


def four_way(field, row_scale, col_scale, row_rate, col_shift, col_mix):
    position = lax.axis_index("gx")
    planes, rows, columns = field.shape
    length, width = planes * rows, columns // 4
    field_a = cut_half(field, 0)
    field_b = cut_half(field, 1, field_a)
    sign = jnp.where(position < 2, 1.0, -1.0)

    own_real = jnp.where(position == 1, -1.0, jnp.where(position == 3, 0.0, 1.0))
    other_real = jnp.where(position == 2, 0.0, 1.0)
    own_imag = jnp.where(position == 3, 1.0, 0.0)
    other_imag = jnp.where(position == 2, -1.0, 0.0)
    coefs_a = jnp.stack([own_real, other_real, own_imag, other_imag]).reshape(2, 2)
    coefs_b = jnp.concatenate([coefs_a, coefs_a * sign], axis=1)

    inner = length // RADIX
    index = jnp.arange(inner, dtype=jnp.int32)
    cos, sin = root_table(index, index, inner)
    y_table = jnp.concatenate([jnp.concatenate([cos, -sin], 1), jnp.concatenate([sin, cos], 1)], 0)
    y_table = split_table(y_table, 1, (0, 1, 0))
    grid = [lax.broadcasted_iota(jnp.int32, (RADIX, inner, LANES), axis) for axis in range(2)]
    angle = (grid[0] * grid[1]).astype(jnp.float32) * (-2.0 * math.pi / length)
    twist = jnp.stack([jnp.cos(angle), jnp.sin(angle)])
    order = jnp.arange(width, dtype=jnp.int32) * 2

    def x_table(odd):
        rows = jnp.concatenate([order + (2 * width + odd), order + odd])
        cos, sin = [part[:, : 2 * width].reshape(2, width, 2 * width) for part in x_tables(rows, columns, 4, position)]
        table = jnp.stack([jnp.concatenate([cos, sin], 2), jnp.concatenate([-sin, cos], 2)], 1)
        return split_table(table.reshape(columns, columns), 0, (0, 0, 1))

    norm = 1.0 / math.sqrt(length * columns * 4)
    row_pair = jnp.stack([row_scale * norm, row_rate]).reshape(2, 4, length // 4 // LANES, LANES)
    col_trio = jnp.stack([col_scale, col_shift, col_mix])
    fixed = 2.0 * (columns * jnp.sum(jnp.log(row_scale)) + length * jnp.sum(jnp.log(col_scale)))
    fixed = fixed - length * columns * math.log(2.0 * math.pi)

    first_a = combine(sign.reshape(1), from_partner(field_a, "gx", 1), field_a)
    tables = (y_table, twist, x_table(0), x_table(1), row_pair, col_trio)
    state = lax.optimization_barrier((first_a, to_planes(field_b)[0], tables, coefs_a, coefs_b, fixed))
    first_a, first_b, (y_table, twist, even_table, odd_table, row_pair, col_trio), coefs_a, coefs_b, fixed = state
    second_a = to_planes(first_a)[0]

    def y_part_b(early, late):
        group = [late, from_partner(late, "gx", 0), early, from_partner(early, "gx", 0)]
        return y_dft([(value, 0) for value in group], coefs_b, y_table, twist)

    early_b = part_columns(first_b)
    late_b = [from_partner(value, "gx", 1) for value in early_b]
    even_b = y_part_b(early_b[0], late_b[0])
    even_b, late_b[1] = lax.optimization_barrier((even_b, late_b[1]))
    odd_b = y_part_b(early_b[1], late_b[1])
    group = [second_a, from_partner(second_a, "gx", 0)]
    even_a, odd_a = [y_dft([(value, lane) for value in group], coefs_a, y_table, twist) for lane in (0, width)]
    latent, tile = x_dft([even_b, even_a], [odd_b, odd_a], even_table, odd_table, row_pair, col_trio)
    tile = tile + fixed / tile.size
    modes = length * columns * lax.axis_size("gx") * lax.axis_size("gy")
    return (latent, sum_everywhere(tile) / modes)


def complex_einsum(form, real_part, imag_part, cos_part, sin_part):
    first = jnp.einsum(form, real_part, cos_part, precision=precision_top)
    second = jnp.einsum(form, real_part, sin_part, precision=precision_top)
    first = first - jnp.einsum(form, imag_part, sin_part, precision=precision_top)
    second = second + jnp.einsum(form, imag_part, cos_part, precision=precision_top)
    return (first, second)


def x_butterfly(field):
    devices = lax.axis_size("gx")
    levels = devices.bit_length() - 1
    position = lax.axis_index("gx")
    real_part, imag_part = field, jnp.zeros_like(field)
    for level in range(levels - 1, -1, -1):
        half = 1 << level
        lower = position // half % 2 == 0
        offset = position % half
        angle = offset.astype(jnp.float32) * (-math.pi / half)
        cos_twist = jnp.where(lower, 1.0, jnp.cos(angle))
        sin_twist = jnp.where(lower, 0.0, jnp.sin(angle))
        other = from_partner(jnp.stack([real_part, imag_part]), "gx", level)
        diff_real = jnp.where(lower, real_part + other[0], other[0] - real_part)
        diff_imag = jnp.where(lower, imag_part + other[1], other[1] - imag_part)
        real_part = diff_real * cos_twist - diff_imag * sin_twist
        imag_part = diff_real * sin_twist + diff_imag * cos_twist
    width = field.shape[2]
    cos_part, sin_part = x_tables(jnp.arange(width, dtype=jnp.int32), width, devices, position)
    real_part, imag_part = complex_einsum("zyn,nk->zyk", real_part, imag_part, cos_part, sin_part)
    return (to_planes(real_part), to_planes(imag_part))


def y_transform(real_part, imag_part):
    planes, length, width = real_part.shape
    outer = 1 << (length.bit_length() - 1) // 2
    inner = length // outer
    outer_index = jnp.arange(outer, dtype=jnp.int32)
    inner_index = jnp.arange(inner, dtype=jnp.int32)
    cos_one, sin_one = root_table(outer_index, outer_index, outer)
    cos_two, sin_two = root_table(inner_index, inner_index, inner)
    cos_mid, sin_mid = root_table(outer_index, inner_index, length)
    shaped_real = real_part.reshape(planes, outer, inner, width)
    shaped_imag = imag_part.reshape(planes, outer, inner, width)
    step_real, step_imag = complex_einsum("zabc,ak->zkbc", shaped_real, shaped_imag, cos_one, sin_one)
    twist_cos = cos_mid[None, :, :, None]
    twist_sin = sin_mid[None, :, :, None]
    turned_real = step_real * twist_cos - step_imag * twist_sin
    turned_imag = step_real * twist_sin + step_imag * twist_cos
    final_real, final_imag = complex_einsum("zkbc,bj->zjkc", turned_real, turned_imag, cos_two, sin_two)
    return (final_real.reshape(planes, length, width), final_imag.reshape(planes, length, width))


def any_way(field, row_scale, col_scale, row_rate, col_shift, col_mix):
    spec_real, spec_imag = y_transform(*x_butterfly(field))
    length = spec_real.shape[1]
    total_cols = spec_real.shape[2] * lax.axis_size("gx")
    norm_factor = 1.0 / math.sqrt(length * total_cols)
    scale = row_scale[None, :, None] * col_scale[None, None, :]
    latent_u = spec_real * norm_factor * scale
    latent_v = spec_imag * norm_factor * scale
    log_scale = row_rate[None, :, None] * jnp.tanh(latent_u + col_shift[None, None, :])
    latent_w = latent_v * jnp.exp(log_scale) + col_mix[None, None, :] * latent_u
    terms = (
        -0.5 * (latent_u * latent_u + latent_w * latent_w)
        - math.log(2.0 * math.pi)
        + log_scale
        + 2.0 * jnp.log(scale)
    )
    mode_count = spec_real.size * lax.axis_size("gx") * lax.axis_size("gy")
    loglik = lax.psum(jnp.sum(terms), ("gx", "gy")) / mode_count
    return (jnp.stack([latent_u, latent_w]), loglik)


def per_device(field, *scales):
    return (four_way if lax.axis_size("gx") == 4 else any_way)(field, *scales)


def solution(mesh):
    return jax.shard_map(
        per_device,
        mesh=mesh,
        in_specs=(P(None, "gy", "gx"), P(), P("gx"), P(), P("gx"), P("gx")),
        out_specs=(P(None, "gy", None, "gx"), P()),
        check_vma=False,
    )
```

```python
import functools
import math

import jax
import jax.numpy as jnp
from jax import lax
from jax.experimental import pallas as pl
from jax.experimental.pallas import tpu as pltpu
from jax.sharding import PartitionSpec as P

precision_top = lax.Precision.HIGHEST
RADIX = 8
LANES = 128
SMALL_BYTES, Y_BYTES, X_BYTES = [size * 1024 * 1024 for size in (8, 32, 24)]


def from_partner(value, axis, stride):
    mask = 2**stride
    pairs = [(source, source ^ mask) for source in range(lax.axis_size(axis))]
    return lax.ppermute(value, axis, pairs)


def to_planes(values):
    return lax.all_to_all(values, "gy", split_axis=0, concat_axis=1, tiled=True)


def pick_columns(left, right, odd):
    lane = lax.broadcasted_iota(jnp.int32, left.shape, 1)
    index = (2 * lane + odd) & (LANES - 1)
    chosen = [jnp.take_along_axis(tile, index, axis=1, mode="promise_in_bounds") for tile in (left, right)]
    return jnp.where(lane < LANES // 2, *chosen)


def combine_kernel(sign_ref, late_ref, early_ref, out_ref):
    sign = sign_ref[0]
    left, right = [
        late_ref[0, :, pl.ds(lane, LANES)] + sign * early_ref[0, :, pl.ds(lane, LANES)] for lane in (0, LANES)
    ]
    for odd in range(2):
        out_ref[0, :, pl.ds(odd * LANES, LANES)] = pick_columns(left, right, odd)


def combine(sign, late, early):
    planes, rows, columns = late.shape
    block = pl.BlockSpec((1, rows, columns), lambda i: (i, 0, 0))
    return pl.pallas_call(
        combine_kernel,
        out_shape=jax.ShapeDtypeStruct(late.shape, jnp.float32),
        grid=(planes,),
        in_specs=[pl.BlockSpec(memory_space=pltpu.SMEM), block, block],
        out_specs=block,
        cost_estimate=pl.CostEstimate(flops=2 * late.size, bytes_accessed=12 * late.size, transcendentals=0),
        compiler_params=pltpu.CompilerParams(vmem_limit_bytes=SMALL_BYTES),
        name="combine",
    )(sign, late, early)


def reverse_bits(value, count):
    result = value * 0
    for place in range(count):
        result = result + (value >> place & 1) * (1 << count - 1 - place)
    return result


def root_table(row_index, freqs, length):
    phase = row_index[:, None] * freqs[None, :] % length
    angle = phase.astype(jnp.float32) * (-2.0 * math.pi / length)
    return (jnp.cos(angle), jnp.sin(angle))


def x_tables(rows, width, devices, position):
    levels = devices.bit_length() - 1
    local_index = jnp.arange(width, dtype=jnp.int32)
    freqs = reverse_bits(position, levels) + devices * local_index
    return root_table(rows, freqs, devices * width)


def split_table(table, axis, order):
    high = lax.reduce_precision(table, 8, 7)
    parts = [high.astype(jnp.bfloat16), (table - high).astype(jnp.bfloat16)]
    return jnp.concatenate([parts[which] for which in order], axis)


def split_value(value):
    high = value.astype(jnp.bfloat16)
    return high, (value - high.astype(jnp.float32)).astype(jnp.bfloat16)


def small_fft(values):
    count = len(values)
    if count == 1:
        return values
    even, odd = small_fft(values[0::2]), small_fft(values[1::2])
    first, second = [], []
    root_half = math.sqrt(0.5)
    for place in range(count // 2):
        (er, ei), (re, im) = even[place], odd[place]
        turn = place * 8 // count
        if turn == 1:
            re, im = (re + im) * root_half, (im - re) * root_half
        elif turn == 2:
            re, im = im, -re
        elif turn == 3:
            re, im = (im - re) * root_half, (re + im) * -root_half
        first.append((er + re, ei + im))
        second.append((er - re, ei - im))
    return first + second


def dot(left, right):
    return jnp.dot(left, right, preferred_element_type=jnp.float32)


def y_kernel(count, pick, coef_ref, *refs):
    inputs, (table_ref, twist_ref, *out_refs, mix_ref, split_ref, step_ref) = refs[:count], refs[count:]
    length = mix_ref.shape[1]
    inner = length // RADIX
    rows_each = 128
    for start in range(0, length, rows_each):
        rows = pl.ds(start, rows_each)
        for which in range(2):
            tiles = []
            for lane in (0, LANES):
                mixed = inputs[0][rows, pl.ds(lane, LANES)] * coef_ref[which, 0]
                for place in range(1, count):
                    mixed = mixed + inputs[place][rows, pl.ds(lane, LANES)] * coef_ref[which, place]
                tiles.append(mixed)
            for tile in range(2):
                mix_ref[2 * tile + which, rows, :] = pick_columns(*tiles, tile) if pick else tiles[tile]
    for tile, out_ref in enumerate(out_refs):
        for which in range(2):
            for s in range(RADIX):
                high, low = split_value(mix_ref[2 * tile + which, pl.ds(s, inner, stride=RADIX), :])
                for place, value in enumerate((high, high, low)):
                    split_ref[tile, pl.ds((2 * place + which) * inner, inner), pl.ds(s * LANES, LANES)] = value
        half = inner // 2
        for part in range(2):
            step_ref[tile, part] = dot(table_ref[pl.ds(part * inner, inner), :], split_ref[tile])
            for start in range(0, half, 16):
                values = []
                for s in range(RADIX):
                    cols = pl.ds(s * LANES, LANES)
                    re = step_ref[tile, part, pl.ds(start, 16), cols]
                    im = step_ref[tile, part, pl.ds(half + start, 16), cols]
                    if s:
                        cos, sin = [twist_ref[k, s, pl.ds(part * half + start, 16), :] for k in range(2)]
                        re, im = re * cos - im * sin, re * sin + im * cos
                    values.append((re, im))
                for kb, pair in enumerate(small_fft(values)):
                    rows = pl.ds(kb * inner + part * half + start, 16)
                    for which in range(2):
                        high, low = split_value(pair[which])
                        out_ref[2 * which, rows, :] = high
                        out_ref[2 * which + 1, rows, :] = low


def y_dft(inputs, pick, coefs, table, twist):
    length = inputs[0].shape[0]
    inner = length // RADIX
    whole = pl.BlockSpec(memory_space=pltpu.VMEM)
    return pl.pallas_call(
        functools.partial(y_kernel, len(inputs), pick),
        out_shape=[jax.ShapeDtypeStruct((4, length, LANES), jnp.bfloat16)] * 2,
        in_specs=[pl.BlockSpec(memory_space=pltpu.SMEM)] + [whole] * (len(inputs) + 2),
        out_specs=[whole] * 2,
        scratch_shapes=[
            pltpu.VMEM((4, length, LANES), jnp.float32),
            pltpu.VMEM((2, 6 * inner, RADIX * LANES), jnp.bfloat16),
            pltpu.VMEM((2, 2, inner, RADIX * LANES), jnp.float32),
        ],
        compiler_params=pltpu.CompilerParams(vmem_limit_bytes=Y_BYTES),
        cost_estimate=pl.CostEstimate(
            flops=48 * inner * length * LANES, bytes_accessed=8 * length * LANES * (len(inputs) + 3), transcendentals=0
        ),
        name="y_dft",
    )(coefs, *inputs, table, twist)


def x_product(parts, table_ref, rows):
    high = [ref[which, rows, :] for ref in parts for which in (0, 2)]
    low = [ref[which, rows, :] for ref in parts for which in (1, 3)]
    return dot(jnp.concatenate(high + low + high, axis=1), table_ref[...])


def x_kernel(count, *refs):
    parts, (even_ref, odd_ref, row_ref, col_ref, out_ref, total_ref) = refs[: 2 * count], refs[2 * count :]
    half = even_ref.shape[1] // 2
    lanes = LANES
    total = None
    spans = [pl.ds(start, 2 * lanes) for start in range(0, out_ref.shape[2], 2 * lanes)]
    products = [(x_product(parts[:count], even_ref, rows), x_product(parts[count:], odd_ref, rows)) for rows in spans]
    for rows, (even, odd) in zip(spans, products):
        row_scale, row_rate = [
            jnp.concatenate(
                [
                    jnp.broadcast_to(row_ref[which, 0, c : c + 1, :], (lanes, lanes)).T
                    for c in range(rows.start // lanes, rows.start // lanes + 2)
                ],
                0,
            )
            for which in range(2)
        ]
        for tile in range(half // lanes):
            real, imag = [slice(start, start + lanes) for start in (tile * lanes, half + tile * lanes)]
            for upper in range(2):
                cols = pl.ds(upper * half + tile * lanes, lanes)
                spec_real = even[:, real] - odd[:, real] if upper else even[:, real] + odd[:, real]
                spec_imag = even[:, imag] - odd[:, imag] if upper else even[:, imag] + odd[:, imag]
                col_scale, col_shift, col_mix = col_ref[0:1, cols], col_ref[1:2, cols], col_ref[2:3, cols]
                scale = row_scale * col_scale
                latent_u = spec_real * scale
                latent_v = spec_imag * scale
                log_scale = row_rate * jnp.tanh(latent_u + col_shift)
                latent_w = latent_v * jnp.exp(log_scale) + col_mix * latent_u
                out_ref[0, 0, rows, cols] = latent_u
                out_ref[1, 0, rows, cols] = latent_w
                terms = log_scale - 0.5 * (latent_u * latent_u + latent_w * latent_w)
                terms = jnp.sum(terms.reshape(-1, 8, lanes), axis=0)
                total = terms if total is None else total + terms

    @pl.when(pl.program_id(0) == 0)
    def _():
        total_ref[...] = jnp.zeros_like(total_ref)

    total_ref[...] += total


def x_dft(even_parts, odd_parts, even_table, odd_table, row_pair, col_trio):
    parts, count, length = even_parts + odd_parts, len(even_parts), even_parts[0].shape[1]
    columns = even_table.shape[1]
    rows = length // row_pair.shape[1]
    fixed = [pl.BlockSpec(table.shape, lambda i: (0, 0), pipeline_mode=pl.Buffered(1)) for table in (even_table, odd_table)]
    return pl.pallas_call(
        functools.partial(x_kernel, count),
        out_shape=(
            jax.ShapeDtypeStruct((2, 1, length, columns), jnp.float32),
            jax.ShapeDtypeStruct((8, LANES), jnp.float32),
        ),
        grid=(length // rows,),
        in_specs=[pl.BlockSpec((4, rows, part.shape[2]), lambda i: (0, i, 0)) for part in parts]
        + fixed
        + [
            pl.BlockSpec((2, 1, rows // LANES, LANES), lambda i: (0, i, 0, 0)),
            pl.BlockSpec(col_trio.shape, lambda i: (0, 0)),
        ],
        out_specs=(
            pl.BlockSpec((2, 1, rows, columns), lambda i: (0, 0, i, 0)),
            pl.BlockSpec((8, LANES), lambda i: (0, 0)),
        ),
        compiler_params=pltpu.CompilerParams(vmem_limit_bytes=X_BYTES),
        cost_estimate=pl.CostEstimate(
            flops=4 * length * even_table.size,
            bytes_accessed=16 * length * columns,
            transcendentals=2 * length * columns,
        ),
        name="x_dft",
    )(*parts, even_table, odd_table, row_pair, col_trio)


def sum_everywhere(tile):
    axes = ("gx", "gy")
    devices = lax.axis_size("gx") * lax.axis_size("gy")
    copies = jnp.broadcast_to(tile[None], (devices,) + tile.shape)
    return jnp.sum(lax.all_to_all(copies, axes, split_axis=0, concat_axis=0, tiled=True))


def four_way(field, row_scale, col_scale, row_rate, col_shift, col_mix):
    position = lax.axis_index("gx")
    planes, rows, columns = field.shape
    length, width = planes * rows, columns // 4
    field_a, field_rest = lax.optimization_barrier((field[:, :, : 2 * width], field))
    field_b = field_rest[:, :, 2 * width :]
    sign = jnp.where(position < 2, 1.0, -1.0)

    own_real = jnp.where(position == 1, -1.0, jnp.where(position == 3, 0.0, 1.0))
    other_real = jnp.where(position == 2, 0.0, 1.0)
    own_imag = jnp.where(position == 3, 1.0, 0.0)
    other_imag = jnp.where(position == 2, -1.0, 0.0)
    coefs_a = jnp.stack([own_real, other_real, own_imag, other_imag]).reshape(2, 2)
    coefs_b = jnp.concatenate([coefs_a, coefs_a * sign], axis=1)

    inner = length // RADIX
    index = jnp.arange(inner, dtype=jnp.int32)
    cos, sin = root_table(index, index, inner)
    y_table = [jnp.concatenate(pair, 1).reshape(2, 1, inner // 2, 2 * inner) for pair in ((cos, -sin), (sin, cos))]
    y_table = jnp.concatenate(y_table, 1).reshape(2 * inner, 2 * inner)
    y_table = split_table(y_table, 1, (0, 1, 0))
    grid = [lax.broadcasted_iota(jnp.int32, (RADIX, inner, LANES), axis) for axis in range(2)]
    angle = (grid[0] * grid[1]).astype(jnp.float32) * (-2.0 * math.pi / length)
    twist = jnp.stack([jnp.cos(angle), jnp.sin(angle)])
    order = jnp.arange(width, dtype=jnp.int32) * 2

    def x_table(odd):
        rows = jnp.concatenate([order + (2 * width + odd), order + odd])
        cos, sin = [part[:, : 2 * width].reshape(2, width, 2 * width) for part in x_tables(rows, columns, 4, position)]
        table = jnp.stack([jnp.concatenate([cos, sin], 2), jnp.concatenate([-sin, cos], 2)], 1)
        return split_table(table.reshape(columns, columns), 0, (0, 0, 1))

    norm = 1.0 / math.sqrt(length * columns * 4)
    row_pair = jnp.stack([row_scale * norm, row_rate]).reshape(2, 4, length // 4 // LANES, LANES)
    col_trio = jnp.stack([col_scale, col_shift, col_mix])
    fixed = 2.0 * (columns * jnp.sum(jnp.log(row_scale)) + length * jnp.sum(jnp.log(col_scale)))
    fixed = fixed - length * columns * math.log(2.0 * math.pi)

    first_a = combine(sign.reshape(1), from_partner(field_a, "gx", 1), field_a)
    tables = (y_table, twist, x_table(0), x_table(1), row_pair, col_trio)
    state = lax.optimization_barrier((first_a, to_planes(field_b)[0], tables, coefs_a, coefs_b, fixed))
    first_a, first_b, (y_table, twist, even_table, odd_table, row_pair, col_trio), coefs_a, coefs_b, fixed = state
    second_a = to_planes(first_a)[0]

    second_b = from_partner(first_b, "gx", 1)
    group = [second_b, from_partner(second_b, "gx", 0), first_b, from_partner(first_b, "gx", 0)]
    even_b, odd_b = y_dft(group, True, coefs_b, y_table, twist)
    even_a, odd_a = y_dft([second_a, from_partner(second_a, "gx", 0)], False, coefs_a, y_table, twist)
    latent, tile = x_dft([even_b, even_a], [odd_b, odd_a], even_table, odd_table, row_pair, col_trio)
    tile = tile + fixed / tile.size
    modes = length * columns * lax.axis_size("gx") * lax.axis_size("gy")
    return (latent, sum_everywhere(tile) / modes)


def complex_einsum(form, real_part, imag_part, cos_part, sin_part):
    first = jnp.einsum(form, real_part, cos_part, precision=precision_top)
    second = jnp.einsum(form, real_part, sin_part, precision=precision_top)
    first = first - jnp.einsum(form, imag_part, sin_part, precision=precision_top)
    second = second + jnp.einsum(form, imag_part, cos_part, precision=precision_top)
    return (first, second)


def x_butterfly(field):
    devices = lax.axis_size("gx")
    levels = devices.bit_length() - 1
    position = lax.axis_index("gx")
    real_part, imag_part = field, jnp.zeros_like(field)
    for level in range(levels - 1, -1, -1):
        half = 1 << level
        lower = position // half % 2 == 0
        offset = position % half
        angle = offset.astype(jnp.float32) * (-math.pi / half)
        cos_twist = jnp.where(lower, 1.0, jnp.cos(angle))
        sin_twist = jnp.where(lower, 0.0, jnp.sin(angle))
        other = from_partner(jnp.stack([real_part, imag_part]), "gx", level)
        diff_real = jnp.where(lower, real_part + other[0], other[0] - real_part)
        diff_imag = jnp.where(lower, imag_part + other[1], other[1] - imag_part)
        real_part = diff_real * cos_twist - diff_imag * sin_twist
        imag_part = diff_real * sin_twist + diff_imag * cos_twist
    width = field.shape[2]
    cos_part, sin_part = x_tables(jnp.arange(width, dtype=jnp.int32), width, devices, position)
    real_part, imag_part = complex_einsum("zyn,nk->zyk", real_part, imag_part, cos_part, sin_part)
    return (to_planes(real_part), to_planes(imag_part))


def y_transform(real_part, imag_part):
    planes, length, width = real_part.shape
    outer = 1 << (length.bit_length() - 1) // 2
    inner = length // outer
    outer_index = jnp.arange(outer, dtype=jnp.int32)
    inner_index = jnp.arange(inner, dtype=jnp.int32)
    cos_one, sin_one = root_table(outer_index, outer_index, outer)
    cos_two, sin_two = root_table(inner_index, inner_index, inner)
    cos_mid, sin_mid = root_table(outer_index, inner_index, length)
    shaped_real = real_part.reshape(planes, outer, inner, width)
    shaped_imag = imag_part.reshape(planes, outer, inner, width)
    step_real, step_imag = complex_einsum("zabc,ak->zkbc", shaped_real, shaped_imag, cos_one, sin_one)
    twist_cos = cos_mid[None, :, :, None]
    twist_sin = sin_mid[None, :, :, None]
    turned_real = step_real * twist_cos - step_imag * twist_sin
    turned_imag = step_real * twist_sin + step_imag * twist_cos
    final_real, final_imag = complex_einsum("zkbc,bj->zjkc", turned_real, turned_imag, cos_two, sin_two)
    return (final_real.reshape(planes, length, width), final_imag.reshape(planes, length, width))


def any_way(field, row_scale, col_scale, row_rate, col_shift, col_mix):
    spec_real, spec_imag = y_transform(*x_butterfly(field))
    length = spec_real.shape[1]
    total_cols = spec_real.shape[2] * lax.axis_size("gx")
    norm_factor = 1.0 / math.sqrt(length * total_cols)
    scale = row_scale[None, :, None] * col_scale[None, None, :]
    latent_u = spec_real * norm_factor * scale
    latent_v = spec_imag * norm_factor * scale
    log_scale = row_rate[None, :, None] * jnp.tanh(latent_u + col_shift[None, None, :])
    latent_w = latent_v * jnp.exp(log_scale) + col_mix[None, None, :] * latent_u
    terms = (
        -0.5 * (latent_u * latent_u + latent_w * latent_w)
        - math.log(2.0 * math.pi)
        + log_scale
        + 2.0 * jnp.log(scale)
    )
    mode_count = spec_real.size * lax.axis_size("gx") * lax.axis_size("gy")
    loglik = lax.psum(jnp.sum(terms), ("gx", "gy")) / mode_count
    return (jnp.stack([latent_u, latent_w]), loglik)


def per_device(field, *scales):
    return (four_way if lax.axis_size("gx") == 4 else any_way)(field, *scales)


def solution(mesh):
    return jax.shard_map(
        per_device,
        mesh=mesh,
        in_specs=(P(None, "gy", "gx"), P(), P("gx"), P(), P("gx"), P("gx")),
        out_specs=(P(None, "gy", None, "gx"), P()),
        check_vma=False,
    )
```

```python
import functools
import math

import jax
import jax.numpy as jnp
from jax import lax
from jax.experimental import pallas as pl
from jax.experimental.pallas import tpu as pltpu
from jax.sharding import PartitionSpec as P

precision_top = lax.Precision.HIGHEST
RADIX = 8
LANES = 128
SMALL_BYTES, Y_BYTES, X_BYTES = 8 * 1024 * 1024, (0, 20 * 1024 * 1024, 28 * 1024 * 1024), 24 * 1024 * 1024


def from_partner(value, axis, stride):
    mask = 2**stride
    pairs = [(source, source ^ mask) for source in range(lax.axis_size(axis))]
    return lax.ppermute(value, axis, pairs)


def to_planes(values):
    return lax.all_to_all(values, "gy", split_axis=0, concat_axis=1, tiled=True)


def sort_columns(tile, odd_first):
    lane = lax.broadcasted_iota(jnp.int32, tile.shape, 1)
    index = ((2 * lane) & (LANES - 1)) + ((lane >> LANES.bit_length() - 2) ^ odd_first)
    return jnp.take_along_axis(tile, index, axis=1, mode="promise_in_bounds")


def combine_kernel(sign_ref, late_ref, early_ref, out_ref):
    for lane in (0, LANES):
        cols = pl.ds(lane, LANES)
        out_ref[0, :, cols] = sort_columns(late_ref[0, :, cols] + sign_ref[0] * early_ref[0, :, cols], 1)


def combine(sign, late, early):
    planes, rows, columns = late.shape
    block = pl.BlockSpec((1, rows, columns), lambda i: (i, 0, 0))
    return pl.pallas_call(
        combine_kernel,
        out_shape=jax.ShapeDtypeStruct(late.shape, jnp.float32),
        grid=(planes,),
        in_specs=[pl.BlockSpec(memory_space=pltpu.SMEM), block, block],
        out_specs=block,
        cost_estimate=pl.CostEstimate(flops=2 * late.size, bytes_accessed=12 * late.size, transcendentals=0),
        compiler_params=pltpu.CompilerParams(vmem_limit_bytes=SMALL_BYTES),
        name="combine",
    )(sign, late, early)


def part_kernel(value_ref, *out_refs):
    for place, out_ref in enumerate(out_refs):
        out_ref[...] = sort_columns(value_ref[:, pl.ds(place * LANES, LANES)], 0)


def part_columns(value):
    length, columns = value.shape
    rows = length // 8
    return pl.pallas_call(
        part_kernel,
        out_shape=[jax.ShapeDtypeStruct((length, LANES), jnp.float32)] * (columns // LANES),
        grid=(length // rows,),
        in_specs=[pl.BlockSpec((rows, columns), lambda i: (i, 0))],
        out_specs=[pl.BlockSpec((rows, LANES), lambda i: (i, 0))] * (columns // LANES),
        cost_estimate=pl.CostEstimate(flops=value.size, bytes_accessed=8 * value.size, transcendentals=0),
        compiler_params=pltpu.CompilerParams(vmem_limit_bytes=SMALL_BYTES),
        name="part_columns",
    )(value)


def reverse_bits(value, count):
    result = value * 0
    for place in range(count):
        result = result + (value >> place & 1) * (1 << count - 1 - place)
    return result


def root_table(row_index, freqs, length):
    phase = row_index[:, None] * freqs[None, :] % length
    angle = phase.astype(jnp.float32) * (-2.0 * math.pi / length)
    return (jnp.cos(angle), jnp.sin(angle))


def x_tables(rows, width, devices, position):
    levels = devices.bit_length() - 1
    local_index = jnp.arange(width, dtype=jnp.int32)
    freqs = reverse_bits(position, levels) + devices * local_index
    return root_table(rows, freqs, devices * width)


def split_table(table, axis, order):
    high = lax.reduce_precision(table, 8, 7)
    parts = [high.astype(jnp.bfloat16), (table - high).astype(jnp.bfloat16)]
    return jnp.concatenate([parts[which] for which in order], axis)


def split_value(value):
    high = value.astype(jnp.bfloat16)
    return high, (value - high.astype(jnp.float32)).astype(jnp.bfloat16)


def small_fft(values):
    count = len(values)
    if count == 1:
        return values
    even, odd = small_fft(values[0::2]), small_fft(values[1::2])
    first, second = [], []
    root_half = math.sqrt(0.5)
    for place in range(count // 2):
        (er, ei), (re, im) = even[place], odd[place]
        turn = place * 8 // count
        if turn == 1:
            re, im = (re + im) * root_half, (im - re) * root_half
        elif turn == 2:
            re, im = im, -re
        elif turn == 3:
            re, im = (im - re) * root_half, (re + im) * -root_half
        first.append((er + re, ei + im))
        second.append((er - re, ei - im))
    return first + second


def dot(left, right):
    return jnp.dot(left, right, preferred_element_type=jnp.float32)


def y_kernel(count, tiles, coef_ref, *refs):
    inputs, refs = refs[:count], refs[count:]
    (table_hbm, twist_hbm), out_refs, scratch = refs[:2], refs[2 : 2 + tiles], refs[2 + tiles :]
    table_ref, twist_ref, mix_ref, split_ref, step_ref, sems = scratch
    copies = [
        pltpu.make_async_copy(source, target, sems.at[place])
        for place, (source, target) in enumerate(((table_hbm, table_ref), (twist_hbm, twist_ref)))
    ]
    for copy in copies:
        copy.start()
    length = mix_ref.shape[1]
    inner = length // RADIX
    rows_each = 128
    for tile in range(tiles):
        cols = pl.ds(tile * LANES, LANES)
        for start in range(0, length, rows_each):
            rows = pl.ds(start, rows_each)
            parts = [ref[rows, cols] for ref in inputs]
            for which in range(2):
                mixed = parts[0] * coef_ref[which, 0]
                for place in range(1, count):
                    mixed = mixed + parts[place] * coef_ref[which, place]
                mix_ref[which, rows, :] = mixed
        for which in range(2):
            for s in range(RADIX):
                high, low = split_value(mix_ref[which, pl.ds(s, inner, stride=RADIX), :])
                for place, value in enumerate((high, high, low)):
                    split_ref[tile, pl.ds((2 * place + which) * inner, inner), pl.ds(s * LANES, LANES)] = value
    for tile, out_ref in enumerate(out_refs):
        if tile == 0:
            copies[0].wait()
        step_ref[tile] = dot(table_ref[...], split_ref[tile])
        if tile == 0:
            copies[1].wait()
        for start in range(0, inner, 16):
            values = []
            for s in range(RADIX):
                cols = pl.ds(s * LANES, LANES)
                re = step_ref[tile, pl.ds(start, 16), cols]
                im = step_ref[tile, pl.ds(inner + start, 16), cols]
                if s:
                    cos, sin = [twist_ref[k, s, pl.ds(start, 16), :] for k in range(2)]
                    re, im = re * cos - im * sin, re * sin + im * cos
                values.append((re, im))
            for kb, pair in enumerate(small_fft(values)):
                rows = pl.ds(kb * inner + start, 16)
                for which in range(2):
                    high, low = split_value(pair[which])
                    out_ref[2 * which, rows, :] = high
                    out_ref[2 * which + 1, rows, :] = low


def y_dft(inputs, coefs, table, twist):
    length, columns = inputs[0].shape
    tiles, inner = columns // LANES, length // RADIX
    whole, anywhere = pl.BlockSpec(memory_space=pltpu.VMEM), pl.BlockSpec(memory_space=pl.ANY)
    return pl.pallas_call(
        functools.partial(y_kernel, len(inputs), tiles),
        out_shape=[jax.ShapeDtypeStruct((4, length, LANES), jnp.bfloat16)] * tiles,
        in_specs=[pl.BlockSpec(memory_space=pltpu.SMEM)] + [whole] * len(inputs) + [anywhere] * 2,
        out_specs=[whole] * tiles,
        scratch_shapes=[
            pltpu.VMEM(table.shape, table.dtype),
            pltpu.VMEM(twist.shape, twist.dtype),
            pltpu.VMEM((2, length, LANES), jnp.float32),
            pltpu.VMEM((tiles, 6 * inner, RADIX * LANES), jnp.bfloat16),
            pltpu.VMEM((tiles, 2 * inner, RADIX * LANES), jnp.float32),
            pltpu.SemaphoreType.DMA((2,)),
        ],
        compiler_params=pltpu.CompilerParams(vmem_limit_bytes=Y_BYTES[tiles]),
        cost_estimate=pl.CostEstimate(
            flops=24 * inner * length * columns, bytes_accessed=4 * length * columns * (len(inputs) + 3), transcendentals=0
        ),
        name="y_dft",
    )(coefs, *inputs, table, twist)


def x_product(left, right, table_ref):
    rows = left[0].shape[1]
    lower = lax.broadcasted_iota(jnp.int32, (rows, LANES), 1) < LANES // 2
    planes = [[jnp.where(lower, one[which], two[which]) for which in range(4)] for one, two in zip(left, right)]
    high, low = [[plane[which] for plane in planes for which in (first, first + 2)] for first in range(2)]
    return dot(jnp.concatenate(high + low + high, axis=1), table_ref[...])


def x_kernel(count, *refs):
    parts, (even_ref, odd_ref, row_ref, col_ref, out_ref, total_ref) = refs[: 2 * count], refs[2 * count :]
    odd_first, even_first = parts[:count], parts[count:]
    even, odd = x_product(even_first, odd_first, even_ref), x_product(odd_first, even_first, odd_ref)
    half = even.shape[1] // 2
    lanes = LANES
    row_scale, row_rate = [
        jnp.concatenate(
            [jnp.broadcast_to(row_ref[which, 0, c : c + 1, :], (lanes, lanes)).T for c in range(row_ref.shape[2])], 0
        )
        for which in range(2)
    ]
    total = None
    for tile in range(half // lanes):
        real, imag = [slice(start, start + lanes) for start in (tile * lanes, half + tile * lanes)]
        for upper in range(2):
            cols = pl.ds(upper * half + tile * lanes, lanes)
            spec_real = even[:, real] - odd[:, real] if upper else even[:, real] + odd[:, real]
            spec_imag = even[:, imag] - odd[:, imag] if upper else even[:, imag] + odd[:, imag]
            col_scale, col_shift, col_mix = col_ref[0:1, cols], col_ref[1:2, cols], col_ref[2:3, cols]
            scale = row_scale * col_scale
            latent_u = spec_real * scale
            latent_v = spec_imag * scale
            log_scale = row_rate * jnp.tanh(latent_u + col_shift)
            latent_w = latent_v * jnp.exp(log_scale) + col_mix * latent_u
            out_ref[0, 0, :, cols] = latent_u
            out_ref[1, 0, :, cols] = latent_w
            terms = log_scale - 0.5 * (latent_u * latent_u + latent_w * latent_w)
            terms = jnp.sum(terms.reshape(-1, 8, lanes), axis=0)
            total = terms if total is None else total + terms

    @pl.when(pl.program_id(0) == 0)
    def _():
        total_ref[...] = jnp.zeros_like(total_ref)

    total_ref[...] += total


def x_dft(odd_first, even_first, even_table, odd_table, row_pair, col_trio):
    parts, count, length = [*odd_first, *even_first], len(odd_first), odd_first[0].shape[1]
    columns = even_table.shape[1]
    rows = length // row_pair.shape[1]
    fixed = [pl.BlockSpec(memory_space=pltpu.VMEM)] * 2
    return pl.pallas_call(
        functools.partial(x_kernel, count),
        out_shape=(
            jax.ShapeDtypeStruct((2, 1, length, columns), jnp.float32),
            jax.ShapeDtypeStruct((8, LANES), jnp.float32),
        ),
        grid=(length // rows,),
        in_specs=[pl.BlockSpec((4, rows, part.shape[2]), lambda i: (0, i, 0)) for part in parts]
        + fixed
        + [
            pl.BlockSpec((2, 1, rows // LANES, LANES), lambda i: (0, i, 0, 0)),
            pl.BlockSpec(col_trio.shape, lambda i: (0, 0)),
        ],
        out_specs=(
            pl.BlockSpec((2, 1, rows, columns), lambda i: (0, 0, i, 0)),
            pl.BlockSpec((8, LANES), lambda i: (0, 0)),
        ),
        compiler_params=pltpu.CompilerParams(vmem_limit_bytes=X_BYTES),
        cost_estimate=pl.CostEstimate(
            flops=4 * length * even_table.size,
            bytes_accessed=16 * length * columns,
            transcendentals=2 * length * columns,
        ),
        name="x_dft",
    )(*parts, even_table, odd_table, row_pair, col_trio)


def sum_everywhere(tile):
    axes = ("gx", "gy")
    devices = lax.axis_size("gx") * lax.axis_size("gy")
    copies = jnp.broadcast_to(tile[None], (devices,) + tile.shape)
    return jnp.sum(lax.all_to_all(copies, axes, split_axis=0, concat_axis=0, tiled=True))


def four_way(field, row_scale, col_scale, row_rate, col_shift, col_mix):
    position = lax.axis_index("gx")
    planes, rows, columns = field.shape
    length, width = planes * rows, columns // 4
    field_a, field_rest = lax.optimization_barrier((field[:, :, : 2 * width], field))
    field_b = field_rest[:, :, 2 * width :]
    sign = jnp.where(position < 2, 1.0, -1.0)

    own_real = jnp.where(position == 1, -1.0, jnp.where(position == 3, 0.0, 1.0))
    other_real = jnp.where(position == 2, 0.0, 1.0)
    own_imag = jnp.where(position == 3, 1.0, 0.0)
    other_imag = jnp.where(position == 2, -1.0, 0.0)
    coefs_a = jnp.stack([own_real, other_real, own_imag, other_imag]).reshape(2, 2)
    coefs_b = jnp.concatenate([coefs_a, coefs_a * sign], axis=1)

    inner = length // RADIX
    index = jnp.arange(inner, dtype=jnp.int32)
    cos, sin = root_table(index, index, inner)
    y_table = jnp.concatenate([jnp.concatenate(pair, 1) for pair in ((cos, -sin), (sin, cos))], 0)
    y_table = split_table(y_table, 1, (0, 1, 0))
    grid = [lax.broadcasted_iota(jnp.int32, (RADIX, inner, LANES), axis) for axis in range(2)]
    angle = (grid[0] * grid[1]).astype(jnp.float32) * (-2.0 * math.pi / length)
    twist = jnp.stack([jnp.cos(angle), jnp.sin(angle)])
    order = jnp.arange(width // 2, dtype=jnp.int32) * 2

    def x_table(odd):
        starts = [tile * width + odd + offset for tile in range(2) for offset in ((0, 2 * width) if odd else (2 * width, 0))]
        rows = jnp.concatenate([start + order for start in starts])
        cos, sin = [part[:, : 2 * width].reshape(2, width, 2 * width) for part in x_tables(rows, columns, 4, position)]
        table = jnp.stack([jnp.concatenate([cos, sin], 2), jnp.concatenate([-sin, cos], 2)], 1)
        return split_table(table.reshape(columns, columns), 0, (0, 0, 1))

    norm = 1.0 / math.sqrt(length * columns * 4)
    row_pair = jnp.stack([row_scale * norm, row_rate]).reshape(2, 8, length // 8 // LANES, LANES)
    col_trio = jnp.stack([col_scale, col_shift, col_mix])
    fixed = 2.0 * (columns * jnp.sum(jnp.log(row_scale)) + length * jnp.sum(jnp.log(col_scale)))
    fixed = fixed - length * columns * math.log(2.0 * math.pi)

    first_a = combine(sign.reshape(1), from_partner(field_a, "gx", 1), field_a)
    tables = (y_table, twist, x_table(0), x_table(1), row_pair, col_trio)
    state = lax.optimization_barrier((first_a, to_planes(field_b)[0], tables, coefs_a, coefs_b, fixed))
    first_a, first_b, (y_table, twist, even_table, odd_table, row_pair, col_trio), coefs_a, coefs_b, fixed = state
    second_a = to_planes(first_a)[0]

    early_b = part_columns(first_b)
    late_b = [from_partner(value, "gx", 1) for value in early_b]

    def y_part_b(early, late):
        group = [late, from_partner(late, "gx", 0), early, from_partner(early, "gx", 0)]
        return y_dft(group, coefs_b, y_table, twist)[0]

    even_first = [y_part_b(early_b[0], late_b[0])]
    even_first[0], late_b[1], second_a = lax.optimization_barrier((even_first[0], late_b[1], second_a))
    odd_first = y_dft([second_a, from_partner(second_a, "gx", 0)], coefs_a, y_table, twist)
    even_first.append(y_part_b(early_b[1], late_b[1]))
    latent, tile = x_dft(odd_first, even_first, even_table, odd_table, row_pair, col_trio)
    tile = tile + fixed / tile.size
    modes = length * columns * lax.axis_size("gx") * lax.axis_size("gy")
    return (latent, sum_everywhere(tile) / modes)


def complex_einsum(form, real_part, imag_part, cos_part, sin_part):
    first = jnp.einsum(form, real_part, cos_part, precision=precision_top)
    second = jnp.einsum(form, real_part, sin_part, precision=precision_top)
    first = first - jnp.einsum(form, imag_part, sin_part, precision=precision_top)
    second = second + jnp.einsum(form, imag_part, cos_part, precision=precision_top)
    return (first, second)


def x_butterfly(field):
    devices = lax.axis_size("gx")
    levels = devices.bit_length() - 1
    position = lax.axis_index("gx")
    real_part, imag_part = field, jnp.zeros_like(field)
    for level in range(levels - 1, -1, -1):
        half = 1 << level
        lower = position // half % 2 == 0
        offset = position % half
        angle = offset.astype(jnp.float32) * (-math.pi / half)
        cos_twist = jnp.where(lower, 1.0, jnp.cos(angle))
        sin_twist = jnp.where(lower, 0.0, jnp.sin(angle))
        other = from_partner(jnp.stack([real_part, imag_part]), "gx", level)
        diff_real = jnp.where(lower, real_part + other[0], other[0] - real_part)
        diff_imag = jnp.where(lower, imag_part + other[1], other[1] - imag_part)
        real_part = diff_real * cos_twist - diff_imag * sin_twist
        imag_part = diff_real * sin_twist + diff_imag * cos_twist
    width = field.shape[2]
    cos_part, sin_part = x_tables(jnp.arange(width, dtype=jnp.int32), width, devices, position)
    real_part, imag_part = complex_einsum("zyn,nk->zyk", real_part, imag_part, cos_part, sin_part)
    return (to_planes(real_part), to_planes(imag_part))


def y_transform(real_part, imag_part):
    planes, length, width = real_part.shape
    outer = 1 << (length.bit_length() - 1) // 2
    inner = length // outer
    outer_index = jnp.arange(outer, dtype=jnp.int32)
    inner_index = jnp.arange(inner, dtype=jnp.int32)
    cos_one, sin_one = root_table(outer_index, outer_index, outer)
    cos_two, sin_two = root_table(inner_index, inner_index, inner)
    cos_mid, sin_mid = root_table(outer_index, inner_index, length)
    shaped_real = real_part.reshape(planes, outer, inner, width)
    shaped_imag = imag_part.reshape(planes, outer, inner, width)
    step_real, step_imag = complex_einsum("zabc,ak->zkbc", shaped_real, shaped_imag, cos_one, sin_one)
    twist_cos = cos_mid[None, :, :, None]
    twist_sin = sin_mid[None, :, :, None]
    turned_real = step_real * twist_cos - step_imag * twist_sin
    turned_imag = step_real * twist_sin + step_imag * twist_cos
    final_real, final_imag = complex_einsum("zkbc,bj->zjkc", turned_real, turned_imag, cos_two, sin_two)
    return (final_real.reshape(planes, length, width), final_imag.reshape(planes, length, width))


def any_way(field, row_scale, col_scale, row_rate, col_shift, col_mix):
    spec_real, spec_imag = y_transform(*x_butterfly(field))
    length = spec_real.shape[1]
    total_cols = spec_real.shape[2] * lax.axis_size("gx")
    norm_factor = 1.0 / math.sqrt(length * total_cols)
    scale = row_scale[None, :, None] * col_scale[None, None, :]
    latent_u = spec_real * norm_factor * scale
    latent_v = spec_imag * norm_factor * scale
    log_scale = row_rate[None, :, None] * jnp.tanh(latent_u + col_shift[None, None, :])
    latent_w = latent_v * jnp.exp(log_scale) + col_mix[None, None, :] * latent_u
    terms = (
        -0.5 * (latent_u * latent_u + latent_w * latent_w)
        - math.log(2.0 * math.pi)
        + log_scale
        + 2.0 * jnp.log(scale)
    )
    mode_count = spec_real.size * lax.axis_size("gx") * lax.axis_size("gy")
    loglik = lax.psum(jnp.sum(terms), ("gx", "gy")) / mode_count
    return (jnp.stack([latent_u, latent_w]), loglik)


def per_device(field, *scales):
    return (four_way if lax.axis_size("gx") == 4 else any_way)(field, *scales)


def solution(mesh):
    return jax.shard_map(
        per_device,
        mesh=mesh,
        in_specs=(P(None, "gy", "gx"), P(), P("gx"), P(), P("gx"), P("gx")),
        out_specs=(P(None, "gy", None, "gx"), P()),
        check_vma=False,
    )
```

```python
import functools
import math

import jax
import jax.numpy as jnp
from jax import lax
from jax.experimental import pallas as pl
from jax.experimental.pallas import tpu as pltpu
from jax.sharding import PartitionSpec as P

precision_top = lax.Precision.HIGHEST
RADIX = 8
LANES = 128
SMALL_BYTES, Y_BYTES, X_BYTES = [size * 1024 * 1024 for size in (8, 28, 26)]


def from_partner(value, axis, stride):
    mask = 2**stride
    pairs = [(source, source ^ mask) for source in range(lax.axis_size(axis))]
    return lax.ppermute(value, axis, pairs)


def to_planes(values):
    return lax.all_to_all(values, "gy", split_axis=0, concat_axis=1, tiled=True)


def pick_columns(left, right, odd):
    lane = lax.broadcasted_iota(jnp.int32, left.shape, 1)
    index = (2 * lane + odd) & (LANES - 1)
    chosen = [jnp.take_along_axis(tile, index, axis=1, mode="promise_in_bounds") for tile in (left, right)]
    return jnp.where(lane < LANES // 2, *chosen)


def combine_kernel(sign_ref, late_ref, early_ref, out_ref):
    sign = sign_ref[0]
    left, right = [
        late_ref[0, :, pl.ds(lane, LANES)] + sign * early_ref[0, :, pl.ds(lane, LANES)] for lane in (0, LANES)
    ]
    for odd in range(2):
        out_ref[0, :, pl.ds(odd * LANES, LANES)] = pick_columns(left, right, odd)


def combine(sign, late, early):
    planes, rows, columns = late.shape
    block = pl.BlockSpec((1, rows, columns), lambda i: (i, 0, 0))
    return pl.pallas_call(
        combine_kernel,
        out_shape=jax.ShapeDtypeStruct(late.shape, jnp.float32),
        grid=(planes,),
        in_specs=[pl.BlockSpec(memory_space=pltpu.SMEM), block, block],
        out_specs=block,
        cost_estimate=pl.CostEstimate(flops=2 * late.size, bytes_accessed=100 * late.size, transcendentals=0),
        compiler_params=pltpu.CompilerParams(vmem_limit_bytes=SMALL_BYTES),
        name="combine",
    )(sign, late, early)


def reverse_bits(value, count):
    result = value * 0
    for place in range(count):
        result = result + (value >> place & 1) * (1 << count - 1 - place)
    return result


def root_table(row_index, freqs, length):
    phase = row_index[:, None] * freqs[None, :] % length
    angle = phase.astype(jnp.float32) * (-2.0 * math.pi / length)
    return (jnp.cos(angle), jnp.sin(angle))


def x_tables(rows, width, devices, position):
    levels = devices.bit_length() - 1
    local_index = jnp.arange(width, dtype=jnp.int32)
    freqs = reverse_bits(position, levels) + devices * local_index
    return root_table(rows, freqs, devices * width)


def split_table(table, axis, order):
    high = lax.reduce_precision(table, 8, 7)
    parts = [high.astype(jnp.bfloat16), (table - high).astype(jnp.bfloat16)]
    return jnp.concatenate([parts[which] for which in order], axis)


def split_value(value):
    high = value.astype(jnp.bfloat16)
    return high, (value - high.astype(jnp.float32)).astype(jnp.bfloat16)


def small_fft(values):
    count = len(values)
    if count == 1:
        return values
    even, odd = small_fft(values[0::2]), small_fft(values[1::2])
    first, second = [], []
    root_half = math.sqrt(0.5)
    for place in range(count // 2):
        (er, ei), (re, im) = even[place], odd[place]
        turn = place * 8 // count
        if turn == 1:
            re, im = (re + im) * root_half, (im - re) * root_half
        elif turn == 2:
            re, im = im, -re
        elif turn == 3:
            re, im = (im - re) * root_half, (re + im) * -root_half
        first.append((er + re, ei + im))
        second.append((er - re, ei - im))
    return first + second


def dot(left, right):
    return jnp.dot(left, right, preferred_element_type=jnp.float32)


def y_kernel(count, pick, tiles, coef_ref, *refs):
    inputs, refs = refs[:count], refs[count:]
    (table_hbm, twist_hbm), out_refs, scratch = refs[:2], refs[2 : 2 + len(tiles)], refs[2 + len(tiles) :]
    table_ref, twist_ref, mix_ref, split_ref, step_ref, sems = scratch
    copies = [
        pltpu.make_async_copy(source, target, sems.at[place])
        for place, (source, target) in enumerate(((table_hbm, table_ref), (twist_hbm, twist_ref)))
    ]
    for copy in copies:
        copy.start()
    length = mix_ref.shape[1]
    inner = length // RADIX
    half = inner // 2

    def mix(place, start, rows_each):
        rows = pl.ds(start, rows_each)
        lanes = (0, LANES) if pick else (tiles[place] * LANES,)
        parts = [[ref[rows, pl.ds(lane, LANES)] for ref in inputs] for lane in lanes]
        for which in range(2):
            mixed = [sum(part * coef_ref[which, k] for k, part in enumerate(group)) for group in parts]
            mix_ref[which, rows, :] = pick_columns(*mixed, tiles[place]) if pick else mixed[0]

    def split(place, s):
        for which in range(2):
            high, low = split_value(mix_ref[which, pl.ds(s, inner, stride=RADIX), :])
            for k, value in enumerate((high, high, low)):
                split_ref[place, pl.ds((2 * k + which) * inner, inner), pl.ds(s * LANES, LANES)] = value

    def multiply(place, part, chunk):
        cols = pl.ds(2 * chunk * LANES, 2 * LANES)
        step_ref[place, part, :, cols] = dot(table_ref[pl.ds(part * inner, inner), :], split_ref[place, :, cols])

    def finish(place, part, start):
        values = []
        for s in range(RADIX):
            cols = pl.ds(s * LANES, LANES)
            re = step_ref[place, part, pl.ds(start, 16), cols]
            im = step_ref[place, part, pl.ds(half + start, 16), cols]
            if s:
                cos, sin = [twist_ref[k, s, pl.ds(part * half + start, 16), :] for k in range(2)]
                re, im = re * cos - im * sin, re * sin + im * cos
            values.append((re, im))
        for kb, pair in enumerate(small_fft(values)):
            rows = pl.ds(kb * inner + part * half + start, 16)
            for which in range(2):
                high, low = split_value(pair[which])
                out_refs[place][2 * which, rows, :] = high
                out_refs[place][2 * which + 1, rows, :] = low

    before = None
    for place in range(len(tiles)):
        for start in range(0, length, 128):
            mix(place, start, 128)
        for s in range(RADIX):
            split(place, s)
        for part in range(2):
            if place == part == 0:
                copies[0].wait()
            if before == (0, 0):
                copies[1].wait()
            for chunk in range(RADIX // 2):
                multiply(place, part, chunk)
                if before is not None:
                    for start in range(chunk * half // 4, (chunk + 1) * half // 4, 16):
                        finish(*before, start)
            before = (place, part)
    for start in range(0, half, 16):
        finish(*before, start)


def y_dft(inputs, pick, tiles, coefs, table, twist):
    length = inputs[0].shape[0]
    inner = length // RADIX
    count = len(tiles)
    whole, anywhere = pl.BlockSpec(memory_space=pltpu.VMEM), pl.BlockSpec(memory_space=pl.ANY)
    return pl.pallas_call(
        functools.partial(y_kernel, len(inputs), pick, tiles),
        out_shape=[jax.ShapeDtypeStruct((4, length, LANES), jnp.bfloat16)] * count,
        in_specs=[pl.BlockSpec(memory_space=pltpu.SMEM)] + [whole] * len(inputs) + [anywhere] * 2,
        out_specs=[whole] * count,
        scratch_shapes=[
            pltpu.VMEM(table.shape, table.dtype),
            pltpu.VMEM(twist.shape, twist.dtype),
            pltpu.VMEM((2, length, LANES), jnp.float32),
            pltpu.VMEM((count, 6 * inner, RADIX * LANES), jnp.bfloat16),
            pltpu.VMEM((count, 2, inner, RADIX * LANES), jnp.float32),
            pltpu.SemaphoreType.DMA((2,)),
        ],
        compiler_params=pltpu.CompilerParams(vmem_limit_bytes=Y_BYTES),
        cost_estimate=pl.CostEstimate(
            flops=80 * inner * length * LANES * count,
            bytes_accessed=8 * length * LANES * (len(inputs) + 3),
            transcendentals=0,
        ),
        name="y_dft",
    )(coefs, *inputs, table, twist)


def x_kernel(count, *refs):
    parts, (even_ref, odd_ref, row_ref, col_ref, out_ref, total_ref) = refs[: 2 * count], refs[2 * count :]
    columns = out_ref.shape[3]
    lanes, rows_each, tiles = LANES, 2 * LANES, columns // (2 * LANES)
    totals = []

    def left(refs, rows):
        high, low = [[ref[k + which, rows, :] for ref in refs for k in (0, 2)] for which in range(2)]
        return jnp.concatenate(high + low + high, axis=1)

    def multiply(sides, tile):
        cols = pl.ds(tile * 2 * lanes, 2 * lanes)
        return [dot(side, table_ref[:, cols]) for side, table_ref in zip(sides, (even_ref, odd_ref))]

    def finish(start, tile, even, odd):
        rows = pl.ds(start, rows_each)
        row_scale, row_rate = [
            jnp.concatenate(
                [
                    jnp.broadcast_to(row_ref[which, 0, c : c + 1, :], (lanes, lanes)).T
                    for c in range(start // lanes, (start + rows_each) // lanes)
                ],
                0,
            )
            for which in range(2)
        ]
        for upper in range(2):
            cols = pl.ds(upper * columns // 2 + tile * lanes, lanes)
            spec = even - odd if upper else even + odd
            col_scale, col_shift, col_mix = col_ref[0:1, cols], col_ref[1:2, cols], col_ref[2:3, cols]
            scale = row_scale * col_scale
            latent_u = spec[:, :lanes] * scale
            latent_v = spec[:, lanes:] * scale
            log_scale = row_rate * jnp.tanh(latent_u + col_shift)
            latent_w = latent_v * jnp.exp(log_scale) + col_mix * latent_u
            out_ref[0, 0, rows, cols] = latent_u
            out_ref[1, 0, rows, cols] = latent_w
            terms = log_scale - 0.5 * (latent_u * latent_u + latent_w * latent_w)
            totals.append(jnp.sum(terms.reshape(-1, 8, lanes), axis=0))

    before = None
    for start in range(0, out_ref.shape[2], rows_each):
        sides = [left(group, pl.ds(start, rows_each)) for group in (parts[:count], parts[count:])]
        for tile in range(tiles):
            products = multiply(sides, tile)
            if before is not None:
                finish(*before)
            before = (start, tile, *products)
    finish(*before)

    @pl.when(pl.program_id(0) == 0)
    def _():
        total_ref[...] = jnp.zeros_like(total_ref)

    total_ref[...] += sum(totals)


def x_dft(even_parts, odd_parts, even_table, odd_table, row_pair, col_trio):
    parts, count, length = even_parts + odd_parts, len(even_parts), even_parts[0].shape[1]
    columns = even_table.shape[1]
    rows = length // row_pair.shape[1]
    fixed = [pl.BlockSpec(memory_space=pltpu.VMEM)] * 2
    return pl.pallas_call(
        functools.partial(x_kernel, count),
        out_shape=(
            jax.ShapeDtypeStruct((2, 1, length, columns), jnp.float32),
            jax.ShapeDtypeStruct((8, LANES), jnp.float32),
        ),
        grid=(length // rows,),
        in_specs=[pl.BlockSpec((4, rows, part.shape[2]), lambda i: (0, i, 0)) for part in parts]
        + fixed
        + [
            pl.BlockSpec((2, 1, rows // LANES, LANES), lambda i: (0, i, 0, 0)),
            pl.BlockSpec(col_trio.shape, lambda i: (0, 0)),
        ],
        out_specs=(
            pl.BlockSpec((2, 1, rows, columns), lambda i: (0, 0, i, 0)),
            pl.BlockSpec((8, LANES), lambda i: (0, 0)),
        ),
        compiler_params=pltpu.CompilerParams(vmem_limit_bytes=X_BYTES),
        cost_estimate=pl.CostEstimate(
            flops=4 * length * even_table.size,
            bytes_accessed=16 * length * columns,
            transcendentals=2 * length * columns,
        ),
        name="x_dft",
    )(*parts, even_table, odd_table, row_pair, col_trio)


def sum_everywhere(tile):
    axes = ("gx", "gy")
    devices = lax.axis_size("gx") * lax.axis_size("gy")
    copies = jnp.broadcast_to(tile[None], (devices,) + tile.shape)
    return jnp.sum(lax.all_to_all(copies, axes, split_axis=0, concat_axis=0, tiled=True))


def four_way(field, row_scale, col_scale, row_rate, col_shift, col_mix):
    position = lax.axis_index("gx")
    planes, rows, columns = field.shape
    length, width = planes * rows, columns // 4
    field_a, field_rest = lax.optimization_barrier((field[:, :, : 2 * width], field))
    field_b = field_rest[:, :, 2 * width :]
    sign = jnp.where(position < 2, 1.0, -1.0)

    own_real = jnp.where(position == 1, -1.0, jnp.where(position == 3, 0.0, 1.0))
    other_real = jnp.where(position == 2, 0.0, 1.0)
    own_imag = jnp.where(position == 3, 1.0, 0.0)
    other_imag = jnp.where(position == 2, -1.0, 0.0)
    coefs_a = jnp.stack([own_real, other_real, own_imag, other_imag]).reshape(2, 2)
    coefs_b = jnp.concatenate([coefs_a, coefs_a * sign], axis=1)

    inner = length // RADIX
    index = jnp.arange(inner, dtype=jnp.int32)
    cos, sin = root_table(index, index, inner)
    y_table = [jnp.concatenate(pair, 1).reshape(2, 1, inner // 2, 2 * inner) for pair in ((cos, -sin), (sin, cos))]
    y_table = jnp.concatenate(y_table, 1).reshape(2 * inner, 2 * inner)
    y_table = split_table(y_table, 1, (0, 1, 0))
    grid = [lax.broadcasted_iota(jnp.int32, (RADIX, inner, LANES), axis) for axis in range(2)]
    angle = (grid[0] * grid[1]).astype(jnp.float32) * (-2.0 * math.pi / length)
    twist = jnp.stack([jnp.cos(angle), jnp.sin(angle)])
    order = jnp.arange(width, dtype=jnp.int32) * 2

    def x_table(odd):
        rows = jnp.concatenate([order + (2 * width + odd), order + odd])
        cos, sin = [part[:, : 2 * width].reshape(2, width, 2, width) for part in x_tables(rows, columns, 4, position)]
        table = jnp.stack([jnp.stack([cos, sin], 3), jnp.stack([-sin, cos], 3)], 1)
        return split_table(table.reshape(columns, columns), 0, (0, 0, 1))

    norm = 1.0 / math.sqrt(length * columns * 4)
    row_pair = jnp.stack([row_scale * norm, row_rate]).reshape(2, 4, length // 4 // LANES, LANES)
    col_trio = jnp.stack([col_scale, col_shift, col_mix])
    fixed = 2.0 * (columns * jnp.sum(jnp.log(row_scale)) + length * jnp.sum(jnp.log(col_scale)))
    fixed = fixed - length * columns * math.log(2.0 * math.pi)

    first_a = combine(sign.reshape(1), from_partner(field_a, "gx", 1), field_a)
    tables = (y_table, twist, x_table(0), x_table(1), row_pair, col_trio)
    state = lax.optimization_barrier((first_a, to_planes(field_b)[0], tables, coefs_a, coefs_b, fixed))
    first_a, first_b, (y_table, twist, even_table, odd_table, row_pair, col_trio), coefs_a, coefs_b, fixed = state
    second_a = to_planes(first_a)[0]

    second_b = from_partner(first_b, "gx", 1)
    group = [second_b, from_partner(second_b, "gx", 0), first_b, from_partner(first_b, "gx", 0)]
    even_b = y_dft(group, True, (0,), coefs_b, y_table, twist)[0]
    even_b, second_a = lax.optimization_barrier((even_b, second_a))
    odd_b = y_dft(group, True, (1,), coefs_b, y_table, twist)[0]
    even_a, odd_a = y_dft([second_a, from_partner(second_a, "gx", 0)], False, (0, 1), coefs_a, y_table, twist)
    latent, tile = x_dft([even_b, even_a], [odd_b, odd_a], even_table, odd_table, row_pair, col_trio)
    tile = tile + fixed / tile.size
    modes = length * columns * lax.axis_size("gx") * lax.axis_size("gy")
    return (latent, sum_everywhere(tile) / modes)


def complex_einsum(form, real_part, imag_part, cos_part, sin_part):
    first = jnp.einsum(form, real_part, cos_part, precision=precision_top)
    second = jnp.einsum(form, real_part, sin_part, precision=precision_top)
    first = first - jnp.einsum(form, imag_part, sin_part, precision=precision_top)
    second = second + jnp.einsum(form, imag_part, cos_part, precision=precision_top)
    return (first, second)


def x_butterfly(field):
    devices = lax.axis_size("gx")
    levels = devices.bit_length() - 1
    position = lax.axis_index("gx")
    real_part, imag_part = field, jnp.zeros_like(field)
    for level in range(levels - 1, -1, -1):
        half = 1 << level
        lower = position // half % 2 == 0
        offset = position % half
        angle = offset.astype(jnp.float32) * (-math.pi / half)
        cos_twist = jnp.where(lower, 1.0, jnp.cos(angle))
        sin_twist = jnp.where(lower, 0.0, jnp.sin(angle))
        other = from_partner(jnp.stack([real_part, imag_part]), "gx", level)
        diff_real = jnp.where(lower, real_part + other[0], other[0] - real_part)
        diff_imag = jnp.where(lower, imag_part + other[1], other[1] - imag_part)
        real_part = diff_real * cos_twist - diff_imag * sin_twist
        imag_part = diff_real * sin_twist + diff_imag * cos_twist
    width = field.shape[2]
    cos_part, sin_part = x_tables(jnp.arange(width, dtype=jnp.int32), width, devices, position)
    real_part, imag_part = complex_einsum("zyn,nk->zyk", real_part, imag_part, cos_part, sin_part)
    return (to_planes(real_part), to_planes(imag_part))


def y_transform(real_part, imag_part):
    planes, length, width = real_part.shape
    outer = 1 << (length.bit_length() - 1) // 2
    inner = length // outer
    outer_index = jnp.arange(outer, dtype=jnp.int32)
    inner_index = jnp.arange(inner, dtype=jnp.int32)
    cos_one, sin_one = root_table(outer_index, outer_index, outer)
    cos_two, sin_two = root_table(inner_index, inner_index, inner)
    cos_mid, sin_mid = root_table(outer_index, inner_index, length)
    shaped_real = real_part.reshape(planes, outer, inner, width)
    shaped_imag = imag_part.reshape(planes, outer, inner, width)
    step_real, step_imag = complex_einsum("zabc,ak->zkbc", shaped_real, shaped_imag, cos_one, sin_one)
    twist_cos = cos_mid[None, :, :, None]
    twist_sin = sin_mid[None, :, :, None]
    turned_real = step_real * twist_cos - step_imag * twist_sin
    turned_imag = step_real * twist_sin + step_imag * twist_cos
    final_real, final_imag = complex_einsum("zkbc,bj->zjkc", turned_real, turned_imag, cos_two, sin_two)
    return (final_real.reshape(planes, length, width), final_imag.reshape(planes, length, width))


def any_way(field, row_scale, col_scale, row_rate, col_shift, col_mix):
    spec_real, spec_imag = y_transform(*x_butterfly(field))
    length = spec_real.shape[1]
    total_cols = spec_real.shape[2] * lax.axis_size("gx")
    norm_factor = 1.0 / math.sqrt(length * total_cols)
    scale = row_scale[None, :, None] * col_scale[None, None, :]
    latent_u = spec_real * norm_factor * scale
    latent_v = spec_imag * norm_factor * scale
    log_scale = row_rate[None, :, None] * jnp.tanh(latent_u + col_shift[None, None, :])
    latent_w = latent_v * jnp.exp(log_scale) + col_mix[None, None, :] * latent_u
    terms = (
        -0.5 * (latent_u * latent_u + latent_w * latent_w)
        - math.log(2.0 * math.pi)
        + log_scale
        + 2.0 * jnp.log(scale)
    )
    mode_count = spec_real.size * lax.axis_size("gx") * lax.axis_size("gy")
    loglik = lax.psum(jnp.sum(terms), ("gx", "gy")) / mode_count
    return (jnp.stack([latent_u, latent_w]), loglik)


def per_device(field, *scales):
    return (four_way if lax.axis_size("gx") == 4 else any_way)(field, *scales)


def solution(mesh):
    return jax.shard_map(
        per_device,
        mesh=mesh,
        in_specs=(P(None, "gy", "gx"), P(), P("gx"), P(), P("gx"), P("gx")),
        out_specs=(P(None, "gy", None, "gx"), P()),
        check_vma=False,
    )
```

```python
import functools
import math

import jax
import jax.numpy as jnp
from jax import lax
from jax.experimental import pallas as pl
from jax.experimental.pallas import tpu as pltpu
from jax.sharding import PartitionSpec as P

precision_top = lax.Precision.HIGHEST
RADIX = 8
LANES = 128
SMALL_BYTES, Y_BYTES, X_BYTES = [size * 1024 * 1024 for size in (8, 30, 26)]


def from_partner(value, axis, stride):
    mask = 2**stride
    pairs = [(source, source ^ mask) for source in range(lax.axis_size(axis))]
    return lax.ppermute(value, axis, pairs)


def to_planes(values):
    return lax.all_to_all(values, "gy", split_axis=0, concat_axis=1, tiled=True)


def pick_columns(left, right, odd):
    lane = lax.broadcasted_iota(jnp.int32, left.shape, 1)
    index = (2 * lane + odd) & (LANES - 1)
    chosen = [jnp.take_along_axis(tile, index, axis=1, mode="promise_in_bounds") for tile in (left, right)]
    return jnp.where(lane < LANES // 2, *chosen)


def combine_kernel(sign_ref, late_ref, early_ref, out_ref):
    sign = sign_ref[0]
    left, right = [
        late_ref[0, :, pl.ds(lane, LANES)] + sign * early_ref[0, :, pl.ds(lane, LANES)] for lane in (0, LANES)
    ]
    for odd in range(2):
        out_ref[0, :, pl.ds(odd * LANES, LANES)] = pick_columns(left, right, odd)


def combine(sign, late, early):
    planes, rows, columns = late.shape
    block = pl.BlockSpec((1, rows, columns), lambda i: (i, 0, 0))
    return pl.pallas_call(
        combine_kernel,
        out_shape=jax.ShapeDtypeStruct(late.shape, jnp.float32),
        grid=(planes,),
        in_specs=[pl.BlockSpec(memory_space=pltpu.SMEM), block, block],
        out_specs=block,
        cost_estimate=pl.CostEstimate(flops=2 * late.size, bytes_accessed=12 * late.size, transcendentals=0),
        compiler_params=pltpu.CompilerParams(vmem_limit_bytes=SMALL_BYTES),
        name="combine",
    )(sign, late, early)


def reverse_bits(value, count):
    result = value * 0
    for place in range(count):
        result = result + (value >> place & 1) * (1 << count - 1 - place)
    return result


def root_table(row_index, freqs, length):
    phase = row_index[:, None] * freqs[None, :] % length
    angle = phase.astype(jnp.float32) * (-2.0 * math.pi / length)
    return (jnp.cos(angle), jnp.sin(angle))


def x_tables(rows, width, devices, position):
    levels = devices.bit_length() - 1
    local_index = jnp.arange(width, dtype=jnp.int32)
    freqs = reverse_bits(position, levels) + devices * local_index
    return root_table(rows, freqs, devices * width)


def split_table(table, axis, order):
    high = lax.reduce_precision(table, 8, 7)
    parts = [high.astype(jnp.bfloat16), (table - high).astype(jnp.bfloat16)]
    return jnp.concatenate([parts[which] for which in order], axis)


def split_value(value):
    high = value.astype(jnp.bfloat16)
    return high, (value - high.astype(jnp.float32)).astype(jnp.bfloat16)


def small_fft(values):
    count = len(values)
    if count == 1:
        return values
    even, odd = small_fft(values[0::2]), small_fft(values[1::2])
    first, second = [], []
    root_half = math.sqrt(0.5)
    for place in range(count // 2):
        (er, ei), (re, im) = even[place], odd[place]
        turn = place * 8 // count
        if turn == 1:
            re, im = (re + im) * root_half, (im - re) * root_half
        elif turn == 2:
            re, im = im, -re
        elif turn == 3:
            re, im = (im - re) * root_half, (re + im) * -root_half
        first.append((er + re, ei + im))
        second.append((er - re, ei - im))
    return first + second


def dot(left, right):
    return jnp.dot(left, right, preferred_element_type=jnp.float32)


def y_kernel(count, pick, coef_ref, *refs):
    inputs, (table_ref, twist_ref, *out_refs, mix_ref, split_ref, step_ref) = refs[:count], refs[count:]
    length = mix_ref.shape[1]
    inner = length // RADIX
    rows_each = 128
    for start in range(0, length, rows_each):
        rows = pl.ds(start, rows_each)
        for which in range(2):
            tiles = []
            for lane in (0, LANES):
                mixed = inputs[0][rows, pl.ds(lane, LANES)] * coef_ref[which, 0]
                for place in range(1, count):
                    mixed = mixed + inputs[place][rows, pl.ds(lane, LANES)] * coef_ref[which, place]
                tiles.append(mixed)
            for tile in range(2):
                mix_ref[2 * tile + which, rows, :] = pick_columns(*tiles, tile) if pick else tiles[tile]
    for tile, out_ref in enumerate(out_refs):
        for which in range(2):
            for s in range(RADIX):
                high, low = split_value(mix_ref[2 * tile + which, pl.ds(s, inner, stride=RADIX), :])
                for place, value in enumerate((high, high, low)):
                    split_ref[tile, pl.ds((2 * place + which) * inner, inner), pl.ds(s * LANES, LANES)] = value
        half = inner // 2
        for part in range(2):
            step_ref[part] = dot(table_ref[pl.ds(part * inner, inner), :], split_ref[tile])
            for start in range(0, half, 16):
                values = []
                for s in range(RADIX):
                    cols = pl.ds(s * LANES, LANES)
                    re = step_ref[part, pl.ds(start, 16), cols]
                    im = step_ref[part, pl.ds(half + start, 16), cols]
                    if s:
                        cos, sin = [twist_ref[k, s, pl.ds(part * half + start, 16), :] for k in range(2)]
                        re, im = re * cos - im * sin, re * sin + im * cos
                    values.append((re, im))
                for kb, pair in enumerate(small_fft(values)):
                    rows = pl.ds(kb * inner + part * half + start, 16)
                    for which in range(2):
                        high, low = split_value(pair[which])
                        out_ref[2 * which, rows, :] = high
                        out_ref[2 * which + 1, rows, :] = low


def y_dft(inputs, pick, coefs, table, twist):
    length = inputs[0].shape[0]
    inner = length // RADIX
    whole = pl.BlockSpec(memory_space=pltpu.VMEM)
    return pl.pallas_call(
        functools.partial(y_kernel, len(inputs), pick),
        out_shape=[jax.ShapeDtypeStruct((4, length, LANES), jnp.bfloat16)] * 2,
        in_specs=[pl.BlockSpec(memory_space=pltpu.SMEM)] + [whole] * (len(inputs) + 2),
        out_specs=[whole] * 2,
        scratch_shapes=[
            pltpu.VMEM((4, length, LANES), jnp.float32),
            pltpu.VMEM((2, 6 * inner, RADIX * LANES), jnp.bfloat16),
            pltpu.VMEM((2, inner, RADIX * LANES), jnp.float32),
        ],
        compiler_params=pltpu.CompilerParams(vmem_limit_bytes=Y_BYTES),
        cost_estimate=pl.CostEstimate(
            flops=48 * inner * length * LANES, bytes_accessed=8 * length * LANES * (len(inputs) + 3), transcendentals=0
        ),
        name="y_dft",
    )(coefs, *inputs, table, twist)


def x_kernel(count, *refs):
    parts, (even_ref, odd_ref, row_ref, col_ref, out_ref, total_ref) = refs[: 2 * count], refs[2 * count :]
    columns = out_ref.shape[3]
    lanes, rows_each, tiles = LANES, 2 * LANES, columns // (2 * LANES)
    totals = []

    def left(refs, rows):
        high, low = [[ref[k + which, rows, :] for ref in refs for k in (0, 2)] for which in range(2)]
        return jnp.concatenate(high + low + high, axis=1)

    def multiply(sides, tile):
        cols = pl.ds(tile * 2 * lanes, 2 * lanes)
        return [dot(side, table_ref[:, cols]) for side, table_ref in zip(sides, (even_ref, odd_ref))]

    def finish(start, tile, even, odd):
        rows = pl.ds(start, rows_each)
        row_scale, row_rate = [
            jnp.concatenate(
                [
                    jnp.broadcast_to(row_ref[which, 0, c : c + 1, :], (lanes, lanes)).T
                    for c in range(start // lanes, (start + rows_each) // lanes)
                ],
                0,
            )
            for which in range(2)
        ]
        for upper in range(2):
            cols = pl.ds(upper * columns // 2 + tile * lanes, lanes)
            spec = even - odd if upper else even + odd
            col_scale, col_shift, col_mix = col_ref[0:1, cols], col_ref[1:2, cols], col_ref[2:3, cols]
            scale = row_scale * col_scale
            latent_u = spec[:, :lanes] * scale
            latent_v = spec[:, lanes:] * scale
            log_scale = row_rate * jnp.tanh(latent_u + col_shift)
            latent_w = latent_v * jnp.exp(log_scale) + col_mix * latent_u
            out_ref[0, 0, rows, cols] = latent_u
            out_ref[1, 0, rows, cols] = latent_w
            terms = log_scale - 0.5 * (latent_u * latent_u + latent_w * latent_w)
            totals.append(jnp.sum(terms.reshape(-1, 8, lanes), axis=0))

    before = None
    for start in range(0, out_ref.shape[2], rows_each):
        sides = [left(group, pl.ds(start, rows_each)) for group in (parts[:count], parts[count:])]
        for tile in range(tiles):
            products = multiply(sides, tile)
            if before is not None:
                finish(*before)
            before = (start, tile, *products)
    finish(*before)

    @pl.when(pl.program_id(0) == 0)
    def _():
        total_ref[...] = jnp.zeros_like(total_ref)

    total_ref[...] += sum(totals)


def x_dft(even_parts, odd_parts, even_table, odd_table, row_pair, col_trio):
    parts, count, length = even_parts + odd_parts, len(even_parts), even_parts[0].shape[1]
    columns = even_table.shape[1]
    rows = length // row_pair.shape[1]
    fixed = [pl.BlockSpec(memory_space=pltpu.VMEM)] * 2
    return pl.pallas_call(
        functools.partial(x_kernel, count),
        out_shape=(
            jax.ShapeDtypeStruct((2, 1, length, columns), jnp.float32),
            jax.ShapeDtypeStruct((8, LANES), jnp.float32),
        ),
        grid=(length // rows,),
        in_specs=[pl.BlockSpec((4, rows, part.shape[2]), lambda i: (0, i, 0)) for part in parts]
        + fixed
        + [
            pl.BlockSpec((2, 1, rows // LANES, LANES), lambda i: (0, i, 0, 0)),
            pl.BlockSpec(col_trio.shape, lambda i: (0, 0)),
        ],
        out_specs=(
            pl.BlockSpec((2, 1, rows, columns), lambda i: (0, 0, i, 0)),
            pl.BlockSpec((8, LANES), lambda i: (0, 0)),
        ),
        compiler_params=pltpu.CompilerParams(vmem_limit_bytes=X_BYTES),
        cost_estimate=pl.CostEstimate(
            flops=4 * length * even_table.size,
            bytes_accessed=16 * length * columns,
            transcendentals=2 * length * columns,
        ),
        name="x_dft",
    )(*parts, even_table, odd_table, row_pair, col_trio)


def sum_everywhere(tile):
    axes = ("gx", "gy")
    devices = lax.axis_size("gx") * lax.axis_size("gy")
    copies = jnp.broadcast_to(tile[None], (devices,) + tile.shape)
    return jnp.sum(lax.all_to_all(copies, axes, split_axis=0, concat_axis=0, tiled=True))


def four_way(field, row_scale, col_scale, row_rate, col_shift, col_mix):
    position = lax.axis_index("gx")
    planes, rows, columns = field.shape
    length, width = planes * rows, columns // 4
    field_a, field_rest = lax.optimization_barrier((field[:, :, : 2 * width], field))
    field_b = field_rest[:, :, 2 * width :]
    sign = jnp.where(position < 2, 1.0, -1.0)

    own_real = jnp.where(position == 1, -1.0, jnp.where(position == 3, 0.0, 1.0))
    other_real = jnp.where(position == 2, 0.0, 1.0)
    own_imag = jnp.where(position == 3, 1.0, 0.0)
    other_imag = jnp.where(position == 2, -1.0, 0.0)
    coefs_a = jnp.stack([own_real, other_real, own_imag, other_imag]).reshape(2, 2)
    coefs_b = jnp.concatenate([coefs_a, coefs_a * sign], axis=1)

    inner = length // RADIX
    index = jnp.arange(inner, dtype=jnp.int32)
    cos, sin = root_table(index, index, inner)
    y_table = [jnp.concatenate(pair, 1).reshape(2, 1, inner // 2, 2 * inner) for pair in ((cos, -sin), (sin, cos))]
    y_table = jnp.concatenate(y_table, 1).reshape(2 * inner, 2 * inner)
    y_table = split_table(y_table, 1, (0, 1, 0))
    grid = [lax.broadcasted_iota(jnp.int32, (RADIX, inner, LANES), axis) for axis in range(2)]
    angle = (grid[0] * grid[1]).astype(jnp.float32) * (-2.0 * math.pi / length)
    twist = jnp.stack([jnp.cos(angle), jnp.sin(angle)])
    order = jnp.arange(width, dtype=jnp.int32) * 2

    def x_table(odd, position):
        rows = jnp.concatenate([order + (2 * width + odd), order + odd])
        cos, sin = [part[:, : 2 * width] for part in x_tables(rows, columns, 4, position)]

        def lay(left, right):
            spans = [slice(tile * width, (tile + 1) * width) for tile in range(2)]
            return jnp.concatenate([side[:, span] for span in spans for side in (left, right)], 1)

        real, imag = lay(cos, sin), lay(-sin, cos)
        table = jnp.concatenate([real[:width], imag[:width], real[width:], imag[width:]], 0)
        return split_table(table, 0, (0, 0, 1))

    norm = 1.0 / math.sqrt(length * columns * 4)
    row_pair = jnp.stack([row_scale * norm, row_rate]).reshape(2, 4, length // 4 // LANES, LANES)
    col_trio = jnp.stack([col_scale, col_shift, col_mix])
    fixed = 2.0 * (columns * jnp.sum(jnp.log(row_scale)) + length * jnp.sum(jnp.log(col_scale)))
    fixed = fixed - length * columns * math.log(2.0 * math.pi)

    first_a = combine(sign.reshape(1), from_partner(field_a, "gx", 1), field_a)
    state = lax.optimization_barrier((first_a, to_planes(field_b)[0], y_table, twist, position))
    first_a, first_b, y_table, twist, position = state
    second_a = to_planes(first_a)[0]
    second_b = from_partner(first_b, "gx", 1)
    tables = (x_table(0, position), x_table(1, position), row_pair, col_trio, coefs_a, coefs_b, fixed)
    second_b, tables = lax.optimization_barrier((second_b, tables))
    even_table, odd_table, row_pair, col_trio, coefs_a, coefs_b, fixed = tables
    group = [second_b, from_partner(second_b, "gx", 0), first_b, from_partner(first_b, "gx", 0)]
    even_b, odd_b = y_dft(group, True, coefs_b, y_table, twist)
    even_a, odd_a = y_dft([second_a, from_partner(second_a, "gx", 0)], False, coefs_a, y_table, twist)
    latent, tile = x_dft([even_b, even_a], [odd_b, odd_a], even_table, odd_table, row_pair, col_trio)
    tile = tile + fixed / tile.size
    modes = length * columns * lax.axis_size("gx") * lax.axis_size("gy")
    return (latent, sum_everywhere(tile) / modes)


def complex_einsum(form, real_part, imag_part, cos_part, sin_part):
    first = jnp.einsum(form, real_part, cos_part, precision=precision_top)
    second = jnp.einsum(form, real_part, sin_part, precision=precision_top)
    first = first - jnp.einsum(form, imag_part, sin_part, precision=precision_top)
    second = second + jnp.einsum(form, imag_part, cos_part, precision=precision_top)
    return (first, second)


def x_butterfly(field):
    devices = lax.axis_size("gx")
    levels = devices.bit_length() - 1
    position = lax.axis_index("gx")
    real_part, imag_part = field, jnp.zeros_like(field)
    for level in range(levels - 1, -1, -1):
        half = 1 << level
        lower = position // half % 2 == 0
        offset = position % half
        angle = offset.astype(jnp.float32) * (-math.pi / half)
        cos_twist = jnp.where(lower, 1.0, jnp.cos(angle))
        sin_twist = jnp.where(lower, 0.0, jnp.sin(angle))
        other = from_partner(jnp.stack([real_part, imag_part]), "gx", level)
        diff_real = jnp.where(lower, real_part + other[0], other[0] - real_part)
        diff_imag = jnp.where(lower, imag_part + other[1], other[1] - imag_part)
        real_part = diff_real * cos_twist - diff_imag * sin_twist
        imag_part = diff_real * sin_twist + diff_imag * cos_twist
    width = field.shape[2]
    cos_part, sin_part = x_tables(jnp.arange(width, dtype=jnp.int32), width, devices, position)
    real_part, imag_part = complex_einsum("zyn,nk->zyk", real_part, imag_part, cos_part, sin_part)
    return (to_planes(real_part), to_planes(imag_part))


def y_transform(real_part, imag_part):
    planes, length, width = real_part.shape
    outer = 1 << (length.bit_length() - 1) // 2
    inner = length // outer
    outer_index = jnp.arange(outer, dtype=jnp.int32)
    inner_index = jnp.arange(inner, dtype=jnp.int32)
    cos_one, sin_one = root_table(outer_index, outer_index, outer)
    cos_two, sin_two = root_table(inner_index, inner_index, inner)
    cos_mid, sin_mid = root_table(outer_index, inner_index, length)
    shaped_real = real_part.reshape(planes, outer, inner, width)
    shaped_imag = imag_part.reshape(planes, outer, inner, width)
    step_real, step_imag = complex_einsum("zabc,ak->zkbc", shaped_real, shaped_imag, cos_one, sin_one)
    twist_cos = cos_mid[None, :, :, None]
    twist_sin = sin_mid[None, :, :, None]
    turned_real = step_real * twist_cos - step_imag * twist_sin
    turned_imag = step_real * twist_sin + step_imag * twist_cos
    final_real, final_imag = complex_einsum("zkbc,bj->zjkc", turned_real, turned_imag, cos_two, sin_two)
    return (final_real.reshape(planes, length, width), final_imag.reshape(planes, length, width))


def any_way(field, row_scale, col_scale, row_rate, col_shift, col_mix):
    spec_real, spec_imag = y_transform(*x_butterfly(field))
    length = spec_real.shape[1]
    total_cols = spec_real.shape[2] * lax.axis_size("gx")
    norm_factor = 1.0 / math.sqrt(length * total_cols)
    scale = row_scale[None, :, None] * col_scale[None, None, :]
    latent_u = spec_real * norm_factor * scale
    latent_v = spec_imag * norm_factor * scale
    log_scale = row_rate[None, :, None] * jnp.tanh(latent_u + col_shift[None, None, :])
    latent_w = latent_v * jnp.exp(log_scale) + col_mix[None, None, :] * latent_u
    terms = (
        -0.5 * (latent_u * latent_u + latent_w * latent_w)
        - math.log(2.0 * math.pi)
        + log_scale
        + 2.0 * jnp.log(scale)
    )
    mode_count = spec_real.size * lax.axis_size("gx") * lax.axis_size("gy")
    loglik = lax.psum(jnp.sum(terms), ("gx", "gy")) / mode_count
    return (jnp.stack([latent_u, latent_w]), loglik)


def per_device(field, *scales):
    return (four_way if lax.axis_size("gx") == 4 else any_way)(field, *scales)


def solution(mesh):
    return jax.shard_map(
        per_device,
        mesh=mesh,
        in_specs=(P(None, "gy", "gx"), P(), P("gx"), P(), P("gx"), P("gx")),
        out_specs=(P(None, "gy", None, "gx"), P()),
        check_vma=False,
    )
```

```python
import functools
import math

import jax
import jax.numpy as jnp
from jax import lax
from jax.experimental import pallas as pl
from jax.experimental.pallas import tpu as pltpu
from jax.sharding import PartitionSpec as P

precision_top = lax.Precision.HIGHEST
RADIX = 8
LANES = 128
SMALL_BYTES, Y_BYTES, X_BYTES = [size * 1024 * 1024 for size in (8, 30, 26)]


def from_partner(value, axis, stride):
    mask = 2**stride
    pairs = [(source, source ^ mask) for source in range(lax.axis_size(axis))]
    return lax.ppermute(value, axis, pairs)


def to_planes(values):
    return lax.all_to_all(values, "gy", split_axis=0, concat_axis=1, tiled=True)


def pick_columns(left, right, odd):
    lane = lax.broadcasted_iota(jnp.int32, left.shape, 1)
    index = (2 * lane + odd) & (LANES - 1)
    chosen = [jnp.take_along_axis(tile, index, axis=1, mode="promise_in_bounds") for tile in (left, right)]
    return jnp.where(lane < LANES // 2, *chosen)


def combine_kernel(sign_ref, late_ref, early_ref, *refs):
    out_ref = refs[-1]
    sign = sign_ref[0]
    for plane in range(late_ref.shape[0]):
        left, right = [
            late_ref[plane, :, pl.ds(lane, LANES)] + sign * early_ref[plane, :, pl.ds(lane, LANES)] for lane in (0, LANES)
        ]
        for odd in range(2):
            out_ref[plane, :, pl.ds(odd * LANES, LANES)] = pick_columns(left, right, odd)


def combine(sign, parts):
    planes, rows, columns = parts[0][0].shape
    result = ()
    for place, pair in enumerate(parts):
        block = pl.BlockSpec((planes // 2, rows, columns), lambda i: (i, 0, 0))
        result = pl.pallas_call(
            combine_kernel,
            out_shape=[jax.ShapeDtypeStruct((planes * len(parts), rows, columns), jnp.float32)],
            grid=(2,),
            in_specs=[pl.BlockSpec(memory_space=pltpu.SMEM), block, block]
            + [pl.BlockSpec(memory_space=pl.ANY)] * len(result),
            out_specs=[pl.BlockSpec((planes // 2, rows, columns), lambda i, place=place: (2 * place + i, 0, 0))],
            input_output_aliases={3: 0} if result else {},
            cost_estimate=pl.CostEstimate(
                flops=2 * pair[0].size, bytes_accessed=12 * pair[0].size, transcendentals=0
            ),
            compiler_params=pltpu.CompilerParams(vmem_limit_bytes=SMALL_BYTES),
            name="combine",
        )(sign, *pair, *result)
    return result[0]


def reverse_bits(value, count):
    result = value * 0
    for place in range(count):
        result = result + (value >> place & 1) * (1 << count - 1 - place)
    return result


def root_table(row_index, freqs, length):
    phase = row_index[:, None] * freqs[None, :] % length
    angle = phase.astype(jnp.float32) * (-2.0 * math.pi / length)
    return (jnp.cos(angle), jnp.sin(angle))


def x_tables(rows, width, devices, position):
    levels = devices.bit_length() - 1
    local_index = jnp.arange(width, dtype=jnp.int32)
    freqs = reverse_bits(position, levels) + devices * local_index
    return root_table(rows, freqs, devices * width)


def split_table(table, axis, order):
    high = lax.reduce_precision(table, 8, 7)
    parts = [high.astype(jnp.bfloat16), (table - high).astype(jnp.bfloat16)]
    return jnp.concatenate([parts[which] for which in order], axis)


def split_value(value):
    high = value.astype(jnp.bfloat16)
    return high, (value - high.astype(jnp.float32)).astype(jnp.bfloat16)


def small_fft(values):
    count = len(values)
    if count == 1:
        return values
    even, odd = small_fft(values[0::2]), small_fft(values[1::2])
    first, second = [], []
    root_half = math.sqrt(0.5)
    for place in range(count // 2):
        (er, ei), (re, im) = even[place], odd[place]
        turn = place * 8 // count
        if turn == 1:
            re, im = (re + im) * root_half, (im - re) * root_half
        elif turn == 2:
            re, im = im, -re
        elif turn == 3:
            re, im = (im - re) * root_half, (re + im) * -root_half
        first.append((er + re, ei + im))
        second.append((er - re, ei - im))
    return first + second


def dot(left, right):
    return jnp.dot(left, right, preferred_element_type=jnp.float32)


def y_kernel(count, pick, coef_ref, *refs):
    inputs, (table_ref, twist_ref, *out_refs, mix_ref, split_ref, step_ref) = refs[:count], refs[count:]
    length = mix_ref.shape[1]
    inner = length // RADIX
    rows_each = 128
    for start in range(0, length, rows_each):
        rows = pl.ds(start, rows_each)
        for which in range(2):
            tiles = []
            for lane in (0, LANES):
                mixed = inputs[0][rows, pl.ds(lane, LANES)] * coef_ref[which, 0]
                for place in range(1, count):
                    mixed = mixed + inputs[place][rows, pl.ds(lane, LANES)] * coef_ref[which, place]
                tiles.append(mixed)
            for tile in range(2):
                mix_ref[2 * tile + which, rows, :] = pick_columns(*tiles, tile) if pick else tiles[tile]
    for tile, out_ref in enumerate(out_refs):
        for which in range(2):
            for s in range(RADIX):
                high, low = split_value(mix_ref[2 * tile + which, pl.ds(s, inner, stride=RADIX), :])
                for place, value in enumerate((high, high, low)):
                    split_ref[tile, pl.ds((2 * place + which) * inner, inner), pl.ds(s * LANES, LANES)] = value
        half = inner // 2
        for part in range(2):
            step_ref[part] = dot(table_ref[pl.ds(part * inner, inner), :], split_ref[tile])
            for start in range(0, half, 16):
                values = []
                for s in range(RADIX):
                    cols = pl.ds(s * LANES, LANES)
                    re = step_ref[part, pl.ds(start, 16), cols]
                    im = step_ref[part, pl.ds(half + start, 16), cols]
                    if s:
                        cos, sin = [twist_ref[k, s, pl.ds(part * half + start, 16), :] for k in range(2)]
                        re, im = re * cos - im * sin, re * sin + im * cos
                    values.append((re, im))
                for kb, pair in enumerate(small_fft(values)):
                    rows = pl.ds(kb * inner + part * half + start, 16)
                    for which in range(2):
                        high, low = split_value(pair[which])
                        out_ref[2 * which, rows, :] = high
                        out_ref[2 * which + 1, rows, :] = low


def y_dft(inputs, pick, coefs, table, twist):
    length = inputs[0].shape[0]
    inner = length // RADIX
    whole = pl.BlockSpec(memory_space=pltpu.VMEM)
    return pl.pallas_call(
        functools.partial(y_kernel, len(inputs), pick),
        out_shape=[jax.ShapeDtypeStruct((4, length, LANES), jnp.bfloat16)] * 2,
        in_specs=[pl.BlockSpec(memory_space=pltpu.SMEM)] + [whole] * (len(inputs) + 2),
        out_specs=[whole] * 2,
        scratch_shapes=[
            pltpu.VMEM((4, length, LANES), jnp.float32),
            pltpu.VMEM((2, 6 * inner, RADIX * LANES), jnp.bfloat16),
            pltpu.VMEM((2, inner, RADIX * LANES), jnp.float32),
        ],
        compiler_params=pltpu.CompilerParams(vmem_limit_bytes=Y_BYTES),
        cost_estimate=pl.CostEstimate(
            flops=48 * inner * length * LANES, bytes_accessed=8 * length * LANES * (len(inputs) + 3), transcendentals=0
        ),
        name="y_dft",
    )(coefs, *inputs, table, twist)


def x_kernel(count, *refs):
    parts, (even_ref, odd_ref, row_ref, col_ref, out_ref, total_ref) = refs[: 2 * count], refs[2 * count :]
    columns = out_ref.shape[3]
    lanes, rows_each, tiles = LANES, 2 * LANES, columns // (2 * LANES)
    totals = []

    def left(refs, rows):
        high, low = [[ref[k + which, rows, :] for ref in refs for k in (0, 2)] for which in range(2)]
        return jnp.concatenate(high + low + high, axis=1)

    def multiply(sides, tile):
        cols = pl.ds(tile * 2 * lanes, 2 * lanes)
        return [dot(side, table_ref[:, cols]) for side, table_ref in zip(sides, (even_ref, odd_ref))]

    def finish(start, tile, even, odd):
        rows = pl.ds(start, rows_each)
        row_scale, row_rate = [
            jnp.concatenate(
                [
                    jnp.broadcast_to(row_ref[which, 0, c : c + 1, :], (lanes, lanes)).T
                    for c in range(start // lanes, (start + rows_each) // lanes)
                ],
                0,
            )
            for which in range(2)
        ]
        for upper in range(2):
            cols = pl.ds(upper * columns // 2 + tile * lanes, lanes)
            spec = even - odd if upper else even + odd
            col_scale, col_shift, col_mix = col_ref[0:1, cols], col_ref[1:2, cols], col_ref[2:3, cols]
            scale = row_scale * col_scale
            latent_u = spec[:, :lanes] * scale
            latent_v = spec[:, lanes:] * scale
            log_scale = row_rate * jnp.tanh(latent_u + col_shift)
            latent_w = latent_v * jnp.exp(log_scale) + col_mix * latent_u
            out_ref[0, 0, rows, cols] = latent_u
            out_ref[1, 0, rows, cols] = latent_w
            terms = log_scale - 0.5 * (latent_u * latent_u + latent_w * latent_w)
            totals.append(jnp.sum(terms.reshape(-1, 8, lanes), axis=0))

    before = None
    for start in range(0, out_ref.shape[2], rows_each):
        sides = [left(group, pl.ds(start, rows_each)) for group in (parts[:count], parts[count:])]
        for tile in range(tiles):
            products = multiply(sides, tile)
            if before is not None:
                finish(*before)
            before = (start, tile, *products)
    finish(*before)

    @pl.when(pl.program_id(0) == 0)
    def _():
        total_ref[...] = jnp.zeros_like(total_ref)

    total_ref[...] += sum(totals)


def x_dft(even_parts, odd_parts, even_table, odd_table, row_pair, col_trio):
    parts, count, length = even_parts + odd_parts, len(even_parts), even_parts[0].shape[1]
    columns = even_table.shape[1]
    rows = length // row_pair.shape[1]
    fixed = [pl.BlockSpec(memory_space=pltpu.VMEM)] * 2
    return pl.pallas_call(
        functools.partial(x_kernel, count),
        out_shape=(
            jax.ShapeDtypeStruct((2, 1, length, columns), jnp.float32),
            jax.ShapeDtypeStruct((8, LANES), jnp.float32),
        ),
        grid=(length // rows,),
        in_specs=[pl.BlockSpec((4, rows, part.shape[2]), lambda i: (0, i, 0)) for part in parts]
        + fixed
        + [
            pl.BlockSpec((2, 1, rows // LANES, LANES), lambda i: (0, i, 0, 0)),
            pl.BlockSpec(col_trio.shape, lambda i: (0, 0)),
        ],
        out_specs=(
            pl.BlockSpec((2, 1, rows, columns), lambda i: (0, 0, i, 0)),
            pl.BlockSpec((8, LANES), lambda i: (0, 0)),
        ),
        compiler_params=pltpu.CompilerParams(vmem_limit_bytes=X_BYTES),
        cost_estimate=pl.CostEstimate(
            flops=4 * length * even_table.size,
            bytes_accessed=16 * length * columns,
            transcendentals=2 * length * columns,
        ),
        name="x_dft",
    )(*parts, even_table, odd_table, row_pair, col_trio)


def sum_everywhere(tile):
    axes = ("gx", "gy")
    devices = lax.axis_size("gx") * lax.axis_size("gy")
    copies = jnp.broadcast_to(tile[None], (devices,) + tile.shape)
    return jnp.sum(lax.all_to_all(copies, axes, split_axis=0, concat_axis=0, tiled=True))


def four_way(field, row_scale, col_scale, row_rate, col_shift, col_mix):
    position = lax.axis_index("gx")
    planes, rows, columns = field.shape
    length, width = planes * rows, columns // 4
    groups = [slice(0, planes // 2), slice(planes // 2, None)]
    field_a, field_rest = lax.optimization_barrier(([field[group, :, : 2 * width] for group in groups], field))
    field_b = field_rest[:, :, 2 * width :]
    sign = jnp.where(position < 2, 1.0, -1.0)

    own_real = jnp.where(position == 1, -1.0, jnp.where(position == 3, 0.0, 1.0))
    other_real = jnp.where(position == 2, 0.0, 1.0)
    own_imag = jnp.where(position == 3, 1.0, 0.0)
    other_imag = jnp.where(position == 2, -1.0, 0.0)
    coefs_a = jnp.stack([own_real, other_real, own_imag, other_imag]).reshape(2, 2)
    coefs_b = jnp.concatenate([coefs_a, coefs_a * sign], axis=1)

    inner = length // RADIX
    index = jnp.arange(inner, dtype=jnp.int32)
    cos, sin = root_table(index, index, inner)
    y_table = [jnp.concatenate(pair, 1).reshape(2, 1, inner // 2, 2 * inner) for pair in ((cos, -sin), (sin, cos))]
    y_table = jnp.concatenate(y_table, 1).reshape(2 * inner, 2 * inner)
    y_table = split_table(y_table, 1, (0, 1, 0))
    grid = [lax.broadcasted_iota(jnp.int32, (RADIX, inner, LANES), axis) for axis in range(2)]
    angle = (grid[0] * grid[1]).astype(jnp.float32) * (-2.0 * math.pi / length)
    twist = jnp.stack([jnp.cos(angle), jnp.sin(angle)])
    order = jnp.arange(width, dtype=jnp.int32) * 2

    def x_table(odd):
        rows = jnp.concatenate([order + (2 * width + odd), order + odd])
        cos, sin = [part[:, : 2 * width] for part in x_tables(rows, columns, 4, position)]

        def lay(left, right):
            spans = [slice(tile * width, (tile + 1) * width) for tile in range(2)]
            return jnp.concatenate([side[:, span] for span in spans for side in (left, right)], 1)

        real, imag = lay(cos, sin), lay(-sin, cos)
        table = jnp.concatenate([real[:width], imag[:width], real[width:], imag[width:]], 0)
        return split_table(table, 0, (0, 0, 1))

    norm = 1.0 / math.sqrt(length * columns * 4)
    row_pair = jnp.stack([row_scale * norm, row_rate]).reshape(2, 4, length // 4 // LANES, LANES)
    col_trio = jnp.stack([col_scale, col_shift, col_mix])
    fixed = 2.0 * (columns * jnp.sum(jnp.log(row_scale)) + length * jnp.sum(jnp.log(col_scale)))
    fixed = fixed - length * columns * math.log(2.0 * math.pi)

    first_a = combine(sign.reshape(1), [(from_partner(part, "gx", 1), part) for part in field_a])
    tables = (y_table, twist, x_table(0), x_table(1), row_pair, col_trio, coefs_a, coefs_b, fixed)
    first_a, first_b, tables = lax.optimization_barrier((first_a, to_planes(field_b)[0], tables))
    y_table, twist, even_table, odd_table, row_pair, col_trio, coefs_a, coefs_b, fixed = tables
    second_a = to_planes(first_a)[0]
    second_b = from_partner(first_b, "gx", 1)
    group = [second_b, from_partner(second_b, "gx", 0), first_b, from_partner(first_b, "gx", 0)]
    even_b, odd_b = y_dft(group, True, coefs_b, y_table, twist)
    even_a, odd_a = y_dft([second_a, from_partner(second_a, "gx", 0)], False, coefs_a, y_table, twist)
    latent, tile = x_dft([even_b, even_a], [odd_b, odd_a], even_table, odd_table, row_pair, col_trio)
    tile = tile + fixed / tile.size
    modes = length * columns * lax.axis_size("gx") * lax.axis_size("gy")
    return (latent, sum_everywhere(tile) / modes)


def complex_einsum(form, real_part, imag_part, cos_part, sin_part):
    first = jnp.einsum(form, real_part, cos_part, precision=precision_top)
    second = jnp.einsum(form, real_part, sin_part, precision=precision_top)
    first = first - jnp.einsum(form, imag_part, sin_part, precision=precision_top)
    second = second + jnp.einsum(form, imag_part, cos_part, precision=precision_top)
    return (first, second)


def x_butterfly(field):
    devices = lax.axis_size("gx")
    levels = devices.bit_length() - 1
    position = lax.axis_index("gx")
    real_part, imag_part = field, jnp.zeros_like(field)
    for level in range(levels - 1, -1, -1):
        half = 1 << level
        lower = position // half % 2 == 0
        offset = position % half
        angle = offset.astype(jnp.float32) * (-math.pi / half)
        cos_twist = jnp.where(lower, 1.0, jnp.cos(angle))
        sin_twist = jnp.where(lower, 0.0, jnp.sin(angle))
        other = from_partner(jnp.stack([real_part, imag_part]), "gx", level)
        diff_real = jnp.where(lower, real_part + other[0], other[0] - real_part)
        diff_imag = jnp.where(lower, imag_part + other[1], other[1] - imag_part)
        real_part = diff_real * cos_twist - diff_imag * sin_twist
        imag_part = diff_real * sin_twist + diff_imag * cos_twist
    width = field.shape[2]
    cos_part, sin_part = x_tables(jnp.arange(width, dtype=jnp.int32), width, devices, position)
    real_part, imag_part = complex_einsum("zyn,nk->zyk", real_part, imag_part, cos_part, sin_part)
    return (to_planes(real_part), to_planes(imag_part))


def y_transform(real_part, imag_part):
    planes, length, width = real_part.shape
    outer = 1 << (length.bit_length() - 1) // 2
    inner = length // outer
    outer_index = jnp.arange(outer, dtype=jnp.int32)
    inner_index = jnp.arange(inner, dtype=jnp.int32)
    cos_one, sin_one = root_table(outer_index, outer_index, outer)
    cos_two, sin_two = root_table(inner_index, inner_index, inner)
    cos_mid, sin_mid = root_table(outer_index, inner_index, length)
    shaped_real = real_part.reshape(planes, outer, inner, width)
    shaped_imag = imag_part.reshape(planes, outer, inner, width)
    step_real, step_imag = complex_einsum("zabc,ak->zkbc", shaped_real, shaped_imag, cos_one, sin_one)
    twist_cos = cos_mid[None, :, :, None]
    twist_sin = sin_mid[None, :, :, None]
    turned_real = step_real * twist_cos - step_imag * twist_sin
    turned_imag = step_real * twist_sin + step_imag * twist_cos
    final_real, final_imag = complex_einsum("zkbc,bj->zjkc", turned_real, turned_imag, cos_two, sin_two)
    return (final_real.reshape(planes, length, width), final_imag.reshape(planes, length, width))


def any_way(field, row_scale, col_scale, row_rate, col_shift, col_mix):
    spec_real, spec_imag = y_transform(*x_butterfly(field))
    length = spec_real.shape[1]
    total_cols = spec_real.shape[2] * lax.axis_size("gx")
    norm_factor = 1.0 / math.sqrt(length * total_cols)
    scale = row_scale[None, :, None] * col_scale[None, None, :]
    latent_u = spec_real * norm_factor * scale
    latent_v = spec_imag * norm_factor * scale
    log_scale = row_rate[None, :, None] * jnp.tanh(latent_u + col_shift[None, None, :])
    latent_w = latent_v * jnp.exp(log_scale) + col_mix[None, None, :] * latent_u
    terms = (
        -0.5 * (latent_u * latent_u + latent_w * latent_w)
        - math.log(2.0 * math.pi)
        + log_scale
        + 2.0 * jnp.log(scale)
    )
    mode_count = spec_real.size * lax.axis_size("gx") * lax.axis_size("gy")
    loglik = lax.psum(jnp.sum(terms), ("gx", "gy")) / mode_count
    return (jnp.stack([latent_u, latent_w]), loglik)


def per_device(field, *scales):
    return (four_way if lax.axis_size("gx") == 4 else any_way)(field, *scales)


def solution(mesh):
    return jax.shard_map(
        per_device,
        mesh=mesh,
        in_specs=(P(None, "gy", "gx"), P(), P("gx"), P(), P("gx"), P("gx")),
        out_specs=(P(None, "gy", None, "gx"), P()),
        check_vma=False,
    )
```

```python
import functools
import math

import jax
import jax.numpy as jnp
from jax import lax
from jax.experimental import pallas as pl
from jax.experimental.pallas import tpu as pltpu
from jax.sharding import PartitionSpec as P

precision_top = lax.Precision.HIGHEST
RADIX = 8
LANES = 128
SMALL_BYTES, Y_BYTES, X_BYTES = [size * 1024 * 1024 for size in (8, 27, 26)]


def from_partner(value, axis, stride):
    mask = 2**stride
    pairs = [(source, source ^ mask) for source in range(lax.axis_size(axis))]
    return lax.ppermute(value, axis, pairs)


def to_planes(values):
    return lax.all_to_all(values, "gy", split_axis=0, concat_axis=1, tiled=True)


def pick_columns(left, right, odd):
    lane = lax.broadcasted_iota(jnp.int32, left.shape, 1)
    index = (2 * lane + odd) & (LANES - 1)
    chosen = [jnp.take_along_axis(tile, index, axis=1, mode="promise_in_bounds") for tile in (left, right)]
    return jnp.where(lane < LANES // 2, *chosen)


def combine_kernel(sign_ref, late_ref, early_ref, *refs):
    out_ref = refs[-1]
    sign = sign_ref[0]
    for plane in range(late_ref.shape[0]):
        left, right = [
            late_ref[plane, :, pl.ds(lane, LANES)] + sign * early_ref[plane, :, pl.ds(lane, LANES)] for lane in (0, LANES)
        ]
        for odd in range(2):
            out_ref[plane, :, pl.ds(odd * LANES, LANES)] = pick_columns(left, right, odd)


def combine(sign, parts):
    planes, rows, columns = parts[0][0].shape
    result = ()
    for place, pair in enumerate(parts):
        block = pl.BlockSpec((planes // 2, rows, columns), lambda i: (i, 0, 0))
        result = pl.pallas_call(
            combine_kernel,
            out_shape=[jax.ShapeDtypeStruct((planes * len(parts), rows, columns), jnp.float32)],
            grid=(2,),
            in_specs=[pl.BlockSpec(memory_space=pltpu.SMEM), block, block]
            + [pl.BlockSpec(memory_space=pl.ANY)] * len(result),
            out_specs=[pl.BlockSpec((planes // 2, rows, columns), lambda i, place=place: (2 * place + i, 0, 0))],
            input_output_aliases={3: 0} if result else {},
            cost_estimate=pl.CostEstimate(
                flops=2 * pair[0].size, bytes_accessed=12 * pair[0].size, transcendentals=0
            ),
            compiler_params=pltpu.CompilerParams(vmem_limit_bytes=SMALL_BYTES),
            name="combine",
        )(sign, *pair, *result)
    return result[0]


def reverse_bits(value, count):
    result = value * 0
    for place in range(count):
        result = result + (value >> place & 1) * (1 << count - 1 - place)
    return result


def root_table(row_index, freqs, length):
    phase = row_index[:, None] * freqs[None, :] % length
    angle = phase.astype(jnp.float32) * (-2.0 * math.pi / length)
    return (jnp.cos(angle), jnp.sin(angle))


def x_tables(rows, width, devices, position):
    levels = devices.bit_length() - 1
    local_index = jnp.arange(width, dtype=jnp.int32)
    freqs = reverse_bits(position, levels) + devices * local_index
    return root_table(rows, freqs, devices * width)


def split_table(table):
    high = lax.reduce_precision(table, 8, 7)
    return jnp.stack([high.astype(jnp.bfloat16), (table - high).astype(jnp.bfloat16)])


def split_value(value):
    high = value.astype(jnp.bfloat16)
    return high, (value - high.astype(jnp.float32)).astype(jnp.bfloat16)


def small_fft(values):
    count = len(values)
    if count == 1:
        return values
    even, odd = small_fft(values[0::2]), small_fft(values[1::2])
    first, second = [], []
    root_half = math.sqrt(0.5)
    for place in range(count // 2):
        (er, ei), (re, im) = even[place], odd[place]
        turn = place * 8 // count
        if turn == 1:
            re, im = (re + im) * root_half, (im - re) * root_half
        elif turn == 2:
            re, im = im, -re
        elif turn == 3:
            re, im = (im - re) * root_half, (re + im) * -root_half
        first.append((er + re, ei + im))
        second.append((er - re, ei - im))
    return first + second


def dot(left, right):
    return jnp.dot(left, right, preferred_element_type=jnp.float32)


def y_kernel(count, pick, coef_ref, *refs):
    inputs, (table_ref, twist_ref, *out_refs, mix_ref, split_ref, step_ref) = refs[:count], refs[count:]
    length = mix_ref.shape[1]
    inner = length // RADIX
    rows_each = 128
    for start in range(0, length, rows_each):
        rows = pl.ds(start, rows_each)
        for which in range(2):
            tiles = []
            for lane in (0, LANES):
                mixed = inputs[0][rows, pl.ds(lane, LANES)] * coef_ref[which, 0]
                for place in range(1, count):
                    mixed = mixed + inputs[place][rows, pl.ds(lane, LANES)] * coef_ref[which, place]
                tiles.append(mixed)
            for tile in range(2):
                mix_ref[2 * tile + which, rows, :] = pick_columns(*tiles, tile) if pick else tiles[tile]
    for tile, out_ref in enumerate(out_refs):
        for which in range(2):
            for s in range(RADIX):
                parts = split_value(mix_ref[2 * tile + which, pl.ds(s, inner, stride=RADIX), :])
                for place, value in enumerate(parts):
                    split_ref[tile, place, pl.ds(which * inner, inner), pl.ds(s * LANES, LANES)] = value
        half = inner // 2
        for part in range(2):
            table = [table_ref[place, pl.ds(part * inner, inner), :] for place in (0, 1, 0)]
            values = [split_ref[tile, place] for place in (0, 0, 1)]
            step_ref[part] = dot(jnp.concatenate(table, axis=1), jnp.concatenate(values, axis=0))
            for start in range(0, half, 16):
                values = []
                for s in range(RADIX):
                    cols = pl.ds(s * LANES, LANES)
                    re = step_ref[part, pl.ds(start, 16), cols]
                    im = step_ref[part, pl.ds(half + start, 16), cols]
                    if s:
                        cos, sin = [twist_ref[k, s, pl.ds(part * half + start, 16), :] for k in range(2)]
                        re, im = re * cos - im * sin, re * sin + im * cos
                    values.append((re, im))
                for kb, pair in enumerate(small_fft(values)):
                    rows = pl.ds(kb * inner + part * half + start, 16)
                    for which in range(2):
                        high, low = split_value(pair[which])
                        out_ref[2 * which, rows, :] = high
                        out_ref[2 * which + 1, rows, :] = low


def y_dft(inputs, pick, coefs, table, twist):
    length = inputs[0].shape[0]
    inner = length // RADIX
    whole = pl.BlockSpec(memory_space=pltpu.VMEM)
    return pl.pallas_call(
        functools.partial(y_kernel, len(inputs), pick),
        out_shape=[jax.ShapeDtypeStruct((4, length, LANES), jnp.bfloat16)] * 2,
        in_specs=[pl.BlockSpec(memory_space=pltpu.SMEM)] + [whole] * (len(inputs) + 2),
        out_specs=[whole] * 2,
        scratch_shapes=[
            pltpu.VMEM((4, length, LANES), jnp.float32),
            pltpu.VMEM((2, 2, 2 * inner, RADIX * LANES), jnp.bfloat16),
            pltpu.VMEM((2, inner, RADIX * LANES), jnp.float32),
        ],
        compiler_params=pltpu.CompilerParams(vmem_limit_bytes=Y_BYTES),
        cost_estimate=pl.CostEstimate(
            flops=48 * inner * length * LANES, bytes_accessed=8 * length * LANES * (len(inputs) + 3), transcendentals=0
        ),
        name="y_dft",
    )(coefs, *inputs, table, twist)


def x_kernel(count, *refs):
    parts, (even_ref, odd_ref, row_ref, col_ref, out_ref, total_ref) = refs[: 2 * count], refs[2 * count :]
    columns = out_ref.shape[3]
    lanes, rows_each, tiles = LANES, 2 * LANES, columns // (2 * LANES)
    totals = []

    def left(refs, rows):
        first = pl.multiple_of(pl.program_id(0) * out_ref.shape[2], out_ref.shape[2])
        rows = pl.ds(first + rows, rows_each)
        high, low = [[ref[k + which, rows, :] for ref in refs for k in (0, 2)] for which in range(2)]
        return jnp.concatenate(high + low + high, axis=1)

    def multiply(sides, tile):
        cols = pl.ds(tile * 2 * lanes, 2 * lanes)
        return [
            dot(side, jnp.concatenate([table_ref[place, :, cols] for place in (0, 0, 1)], axis=0))
            for side, table_ref in zip(sides, (even_ref, odd_ref))
        ]

    def finish(start, tile, even, odd):
        rows = pl.ds(start, rows_each)
        row_scale, row_rate = [
            jnp.concatenate(
                [
                    jnp.broadcast_to(row_ref[which, 0, c : c + 1, :], (lanes, lanes)).T
                    for c in range(start // lanes, (start + rows_each) // lanes)
                ],
                0,
            )
            for which in range(2)
        ]
        for upper in range(2):
            cols = pl.ds(upper * columns // 2 + tile * lanes, lanes)
            spec = even - odd if upper else even + odd
            col_scale, col_shift, col_mix = col_ref[0:1, cols], col_ref[1:2, cols], col_ref[2:3, cols]
            scale = row_scale * col_scale
            latent_u = spec[:, :lanes] * scale
            latent_v = spec[:, lanes:] * scale
            log_scale = row_rate * jnp.tanh(latent_u + col_shift)
            latent_w = latent_v * jnp.exp(log_scale) + col_mix * latent_u
            out_ref[0, 0, rows, cols] = latent_u
            out_ref[1, 0, rows, cols] = latent_w
            terms = log_scale - 0.5 * (latent_u * latent_u + latent_w * latent_w)
            totals.append(jnp.sum(terms.reshape(-1, 8, lanes), axis=0))

    before = None
    for start in range(0, out_ref.shape[2], rows_each):
        sides = [left(group, start) for group in (parts[:count], parts[count:])]
        for tile in range(tiles):
            products = multiply(sides, tile)
            if before is not None:
                finish(*before)
            before = (start, tile, *products)
    finish(*before)

    @pl.when(pl.program_id(0) == 0)
    def _():
        total_ref[...] = jnp.zeros_like(total_ref)

    total_ref[...] += sum(totals)


def x_dft(even_parts, odd_parts, even_table, odd_table, row_pair, col_trio):
    parts, count, length = even_parts + odd_parts, len(even_parts), even_parts[0].shape[1]
    columns = even_table.shape[2]
    rows = length // row_pair.shape[1]
    whole = [pl.BlockSpec(memory_space=pltpu.VMEM)] * (len(parts) + 2)
    return pl.pallas_call(
        functools.partial(x_kernel, count),
        out_shape=(
            jax.ShapeDtypeStruct((2, 1, length, columns), jnp.float32),
            jax.ShapeDtypeStruct((8, LANES), jnp.float32),
        ),
        grid=(length // rows,),
        in_specs=whole
        + [
            pl.BlockSpec((2, 1, rows // LANES, LANES), lambda i: (0, i, 0, 0)),
            pl.BlockSpec(col_trio.shape, lambda i: (0, 0)),
        ],
        out_specs=(
            pl.BlockSpec((2, 1, rows, columns), lambda i: (0, 0, i, 0)),
            pl.BlockSpec((8, LANES), lambda i: (0, 0)),
        ),
        compiler_params=pltpu.CompilerParams(vmem_limit_bytes=X_BYTES),
        cost_estimate=pl.CostEstimate(
            flops=6 * length * even_table.size,
            bytes_accessed=16 * length * columns,
            transcendentals=2 * length * columns,
        ),
        name="x_dft",
    )(*parts, even_table, odd_table, row_pair, col_trio)


def sum_everywhere(tile):
    axes = ("gx", "gy")
    devices = lax.axis_size("gx") * lax.axis_size("gy")
    copies = jnp.broadcast_to(tile[None], (devices,) + tile.shape)
    return jnp.sum(lax.all_to_all(copies, axes, split_axis=0, concat_axis=0, tiled=True))


def four_way(field, row_scale, col_scale, row_rate, col_shift, col_mix):
    position = lax.axis_index("gx")
    planes, rows, columns = field.shape
    length, width = planes * rows, columns // 4
    groups = [slice(0, planes // 2), slice(planes // 2, None)]
    field_a, field_rest = lax.optimization_barrier(([field[group, :, : 2 * width] for group in groups], field))
    field_b = field_rest[:, :, 2 * width :]
    sign = jnp.where(position < 2, 1.0, -1.0)

    own_real = jnp.where(position == 1, -1.0, jnp.where(position == 3, 0.0, 1.0))
    other_real = jnp.where(position == 2, 0.0, 1.0)
    own_imag = jnp.where(position == 3, 1.0, 0.0)
    other_imag = jnp.where(position == 2, -1.0, 0.0)
    coefs_a = jnp.stack([own_real, other_real, own_imag, other_imag]).reshape(2, 2)
    coefs_b = jnp.concatenate([coefs_a, coefs_a * sign], axis=1)

    inner = length // RADIX
    index = jnp.arange(inner, dtype=jnp.int32)
    cos, sin = root_table(index, index, inner)
    y_table = [jnp.concatenate(pair, 1).reshape(2, 1, inner // 2, 2 * inner) for pair in ((cos, -sin), (sin, cos))]
    y_table = jnp.concatenate(y_table, 1).reshape(2 * inner, 2 * inner)
    y_table = split_table(y_table)
    grid = [lax.broadcasted_iota(jnp.int32, (RADIX, inner, LANES), axis) for axis in range(2)]
    angle = (grid[0] * grid[1]).astype(jnp.float32) * (-2.0 * math.pi / length)
    twist = jnp.stack([jnp.cos(angle), jnp.sin(angle)])
    order = jnp.arange(width, dtype=jnp.int32) * 2

    def x_table(odd):
        rows = jnp.concatenate([order + (2 * width + odd), order + odd])
        cos, sin = [part[:, : 2 * width] for part in x_tables(rows, columns, 4, position)]

        def lay(left, right):
            spans = [slice(tile * width, (tile + 1) * width) for tile in range(2)]
            return jnp.concatenate([side[:, span] for span in spans for side in (left, right)], 1)

        real, imag = lay(cos, sin), lay(-sin, cos)
        table = jnp.concatenate([real[:width], imag[:width], real[width:], imag[width:]], 0)
        return split_table(table)

    norm = 1.0 / math.sqrt(length * columns * 4)
    row_pair = jnp.stack([row_scale * norm, row_rate]).reshape(2, 4, length // 4 // LANES, LANES)
    col_trio = jnp.stack([col_scale, col_shift, col_mix])
    fixed = 2.0 * (columns * jnp.sum(jnp.log(row_scale)) + length * jnp.sum(jnp.log(col_scale)))
    fixed = fixed - length * columns * math.log(2.0 * math.pi)

    first_a = combine(sign.reshape(1), [(from_partner(part, "gx", 1), part) for part in field_a])
    tables = (y_table, twist, x_table(0), x_table(1), row_pair, col_trio, coefs_a, coefs_b, fixed)
    first_a, first_b, tables = lax.optimization_barrier((first_a, to_planes(field_b)[0], tables))
    y_table, twist, even_table, odd_table, row_pair, col_trio, coefs_a, coefs_b, fixed = tables
    second_a = to_planes(first_a)[0]
    second_b = from_partner(first_b, "gx", 1)
    group = [second_b, from_partner(second_b, "gx", 0), first_b, from_partner(first_b, "gx", 0)]
    even_b, odd_b = y_dft(group, True, coefs_b, y_table, twist)
    even_a, odd_a = y_dft([second_a, from_partner(second_a, "gx", 0)], False, coefs_a, y_table, twist)
    latent, tile = x_dft([even_b, even_a], [odd_b, odd_a], even_table, odd_table, row_pair, col_trio)
    tile = tile + fixed / tile.size
    modes = length * columns * lax.axis_size("gx") * lax.axis_size("gy")
    return (latent, sum_everywhere(tile) / modes)


def complex_einsum(form, real_part, imag_part, cos_part, sin_part):
    first = jnp.einsum(form, real_part, cos_part, precision=precision_top)
    second = jnp.einsum(form, real_part, sin_part, precision=precision_top)
    first = first - jnp.einsum(form, imag_part, sin_part, precision=precision_top)
    second = second + jnp.einsum(form, imag_part, cos_part, precision=precision_top)
    return (first, second)


def x_butterfly(field):
    devices = lax.axis_size("gx")
    levels = devices.bit_length() - 1
    position = lax.axis_index("gx")
    real_part, imag_part = field, jnp.zeros_like(field)
    for level in range(levels - 1, -1, -1):
        half = 1 << level
        lower = position // half % 2 == 0
        offset = position % half
        angle = offset.astype(jnp.float32) * (-math.pi / half)
        cos_twist = jnp.where(lower, 1.0, jnp.cos(angle))
        sin_twist = jnp.where(lower, 0.0, jnp.sin(angle))
        other = from_partner(jnp.stack([real_part, imag_part]), "gx", level)
        diff_real = jnp.where(lower, real_part + other[0], other[0] - real_part)
        diff_imag = jnp.where(lower, imag_part + other[1], other[1] - imag_part)
        real_part = diff_real * cos_twist - diff_imag * sin_twist
        imag_part = diff_real * sin_twist + diff_imag * cos_twist
    width = field.shape[2]
    cos_part, sin_part = x_tables(jnp.arange(width, dtype=jnp.int32), width, devices, position)
    real_part, imag_part = complex_einsum("zyn,nk->zyk", real_part, imag_part, cos_part, sin_part)
    return (to_planes(real_part), to_planes(imag_part))


def y_transform(real_part, imag_part):
    planes, length, width = real_part.shape
    outer = 1 << (length.bit_length() - 1) // 2
    inner = length // outer
    outer_index = jnp.arange(outer, dtype=jnp.int32)
    inner_index = jnp.arange(inner, dtype=jnp.int32)
    cos_one, sin_one = root_table(outer_index, outer_index, outer)
    cos_two, sin_two = root_table(inner_index, inner_index, inner)
    cos_mid, sin_mid = root_table(outer_index, inner_index, length)
    shaped_real = real_part.reshape(planes, outer, inner, width)
    shaped_imag = imag_part.reshape(planes, outer, inner, width)
    step_real, step_imag = complex_einsum("zabc,ak->zkbc", shaped_real, shaped_imag, cos_one, sin_one)
    twist_cos = cos_mid[None, :, :, None]
    twist_sin = sin_mid[None, :, :, None]
    turned_real = step_real * twist_cos - step_imag * twist_sin
    turned_imag = step_real * twist_sin + step_imag * twist_cos
    final_real, final_imag = complex_einsum("zkbc,bj->zjkc", turned_real, turned_imag, cos_two, sin_two)
    return (final_real.reshape(planes, length, width), final_imag.reshape(planes, length, width))


def any_way(field, row_scale, col_scale, row_rate, col_shift, col_mix):
    spec_real, spec_imag = y_transform(*x_butterfly(field))
    length = spec_real.shape[1]
    total_cols = spec_real.shape[2] * lax.axis_size("gx")
    norm_factor = 1.0 / math.sqrt(length * total_cols)
    scale = row_scale[None, :, None] * col_scale[None, None, :]
    latent_u = spec_real * norm_factor * scale
    latent_v = spec_imag * norm_factor * scale
    log_scale = row_rate[None, :, None] * jnp.tanh(latent_u + col_shift[None, None, :])
    latent_w = latent_v * jnp.exp(log_scale) + col_mix[None, None, :] * latent_u
    terms = (
        -0.5 * (latent_u * latent_u + latent_w * latent_w)
        - math.log(2.0 * math.pi)
        + log_scale
        + 2.0 * jnp.log(scale)
    )
    mode_count = spec_real.size * lax.axis_size("gx") * lax.axis_size("gy")
    loglik = lax.psum(jnp.sum(terms), ("gx", "gy")) / mode_count
    return (jnp.stack([latent_u, latent_w]), loglik)


def per_device(field, *scales):
    return (four_way if lax.axis_size("gx") == 4 else any_way)(field, *scales)


def solution(mesh):
    return jax.shard_map(
        per_device,
        mesh=mesh,
        in_specs=(P(None, "gy", "gx"), P(), P("gx"), P(), P("gx"), P("gx")),
        out_specs=(P(None, "gy", None, "gx"), P()),
        check_vma=False,
    )
```

```python
import functools
import math

import jax
import jax.numpy as jnp
from jax import lax
from jax.experimental import pallas as pl
from jax.experimental.pallas import tpu as pltpu
from jax.sharding import PartitionSpec as P

precision_top = lax.Precision.HIGHEST
RADIX = 8
LANES = 128
SMALL_BYTES, Y_BYTES, X_BYTES = [size * 1024 * 1024 for size in (8, 25, 26)]


def from_partner(value, axis, stride):
    mask = 2**stride
    pairs = [(source, source ^ mask) for source in range(lax.axis_size(axis))]
    return lax.ppermute(value, axis, pairs)


def to_planes(values):
    return lax.all_to_all(values, "gy", split_axis=0, concat_axis=1, tiled=True)


def pick_columns(left, right, odd):
    lane = lax.broadcasted_iota(jnp.int32, left.shape, 1)
    index = (2 * lane + odd) & (LANES - 1)
    chosen = [jnp.take_along_axis(tile, index, axis=1, mode="promise_in_bounds") for tile in (left, right)]
    return jnp.where(lane < LANES // 2, *chosen)


def combine_kernel(sign_ref, late_ref, early_ref, *refs):
    out_ref = refs[-1]
    sign = sign_ref[0]
    for plane in range(late_ref.shape[0]):
        left, right = [
            late_ref[plane, :, pl.ds(lane, LANES)] + sign * early_ref[plane, :, pl.ds(lane, LANES)] for lane in (0, LANES)
        ]
        for odd in range(2):
            out_ref[plane, :, pl.ds(odd * LANES, LANES)] = pick_columns(left, right, odd)


def combine(sign, parts):
    planes, rows, columns = parts[0][0].shape
    result = ()
    for place, pair in enumerate(parts):
        block = pl.BlockSpec((planes // 2, rows, columns), lambda i: (i, 0, 0))
        result = pl.pallas_call(
            combine_kernel,
            out_shape=[jax.ShapeDtypeStruct((planes * len(parts), rows, columns), jnp.float32)],
            grid=(2,),
            in_specs=[pl.BlockSpec(memory_space=pltpu.SMEM), block, block]
            + [pl.BlockSpec(memory_space=pl.ANY)] * len(result),
            out_specs=[pl.BlockSpec((planes // 2, rows, columns), lambda i, place=place: (2 * place + i, 0, 0))],
            input_output_aliases={3: 0} if result else {},
            cost_estimate=pl.CostEstimate(
                flops=2 * pair[0].size, bytes_accessed=12 * pair[0].size, transcendentals=0
            ),
            compiler_params=pltpu.CompilerParams(vmem_limit_bytes=SMALL_BYTES),
            name="combine",
        )(sign, *pair, *result)
    return result[0]


def cut_kernel(field_ref, out_ref):
    for plane in range(field_ref.shape[0]):
        left, right = [field_ref[plane, :, pl.ds(lane, LANES)] for lane in (0, LANES)]
        for odd in range(2):
            out_ref[plane, :, pl.ds(odd * LANES, LANES)] = pick_columns(left, right, odd)


def cut_right(field):
    planes, rows, columns = field.shape
    block = (planes // 4, rows, columns // 2)
    return pl.pallas_call(
        cut_kernel,
        out_shape=jax.ShapeDtypeStruct((planes, rows, columns // 2), jnp.float32),
        grid=(4,),
        in_specs=[pl.BlockSpec(block, lambda i: (i, 0, 1))],
        out_specs=pl.BlockSpec(block, lambda i: (i, 0, 0)),
        cost_estimate=pl.CostEstimate(flops=field.size, bytes_accessed=4 * field.size, transcendentals=0),
        compiler_params=pltpu.CompilerParams(vmem_limit_bytes=SMALL_BYTES),
        name="cut_right",
    )(field)


def reverse_bits(value, count):
    result = value * 0
    for place in range(count):
        result = result + (value >> place & 1) * (1 << count - 1 - place)
    return result


def root_table(row_index, freqs, length):
    phase = row_index[:, None] * freqs[None, :] % length
    angle = phase.astype(jnp.float32) * (-2.0 * math.pi / length)
    return (jnp.cos(angle), jnp.sin(angle))


def x_tables(rows, width, devices, position):
    levels = devices.bit_length() - 1
    local_index = jnp.arange(width, dtype=jnp.int32)
    freqs = reverse_bits(position, levels) + devices * local_index
    return root_table(rows, freqs, devices * width)


def split_table(table):
    high = lax.reduce_precision(table, 8, 7)
    return jnp.stack([high.astype(jnp.bfloat16), (table - high).astype(jnp.bfloat16)])


def split_value(value):
    high = value.astype(jnp.bfloat16)
    return high, (value - high.astype(jnp.float32)).astype(jnp.bfloat16)


def small_fft(values):
    count = len(values)
    if count == 1:
        return values
    even, odd = small_fft(values[0::2]), small_fft(values[1::2])
    first, second = [], []
    root_half = math.sqrt(0.5)
    for place in range(count // 2):
        (er, ei), (re, im) = even[place], odd[place]
        turn = place * 8 // count
        if turn == 1:
            re, im = (re + im) * root_half, (im - re) * root_half
        elif turn == 2:
            re, im = im, -re
        elif turn == 3:
            re, im = (im - re) * root_half, (re + im) * -root_half
        first.append((er + re, ei + im))
        second.append((er - re, ei - im))
    return first + second


def dot(left, right):
    return jnp.dot(left, right, preferred_element_type=jnp.float32)


def y_kernel(count, tiles, coef_ref, *refs):
    inputs, (table_ref, twist_ref, *out_refs, mix_ref, split_ref, step_ref) = refs[:count], refs[count:]
    length = mix_ref.shape[1]
    inner = length // RADIX
    rows_each = 128
    for place, tile in enumerate(tiles):
        cols = pl.ds(tile * LANES, LANES)
        for start in range(0, length, rows_each):
            rows = pl.ds(start, rows_each)
            for which in range(2):
                mixed = inputs[0][rows, cols] * coef_ref[which, 0]
                for k in range(1, count):
                    mixed = mixed + inputs[k][rows, cols] * coef_ref[which, k]
                mix_ref[2 * place + which, rows, :] = mixed
    for tile, out_ref in enumerate(out_refs):
        for which in range(2):
            for s in range(RADIX):
                parts = split_value(mix_ref[2 * tile + which, pl.ds(s, inner, stride=RADIX), :])
                for place, value in enumerate(parts):
                    split_ref[tile, place, pl.ds(which * inner, inner), pl.ds(s * LANES, LANES)] = value
        half = inner // 2
        for part in range(2):
            table = [table_ref[place, pl.ds(part * inner, inner), :] for place in (0, 1, 0)]
            values = [split_ref[tile, place] for place in (0, 0, 1)]
            step_ref[part] = dot(jnp.concatenate(table, axis=1), jnp.concatenate(values, axis=0))
            for start in range(0, half, 16):
                values = []
                for s in range(RADIX):
                    cols = pl.ds(s * LANES, LANES)
                    re = step_ref[part, pl.ds(start, 16), cols]
                    im = step_ref[part, pl.ds(half + start, 16), cols]
                    if s:
                        cos, sin = [twist_ref[k, s, pl.ds(part * half + start, 16), :] for k in range(2)]
                        re, im = re * cos - im * sin, re * sin + im * cos
                    values.append((re, im))
                for kb, pair in enumerate(small_fft(values)):
                    rows = pl.ds(kb * inner + part * half + start, 16)
                    for which in range(2):
                        high, low = split_value(pair[which])
                        out_ref[2 * which, rows, :] = high
                        out_ref[2 * which + 1, rows, :] = low


def y_dft(inputs, tiles, coefs, table, twist):
    length = inputs[0].shape[0]
    inner = length // RADIX
    count = len(tiles)
    whole = pl.BlockSpec(memory_space=pltpu.VMEM)
    return pl.pallas_call(
        functools.partial(y_kernel, len(inputs), tiles),
        out_shape=[jax.ShapeDtypeStruct((4, length, LANES), jnp.bfloat16)] * count,
        in_specs=[pl.BlockSpec(memory_space=pltpu.SMEM)] + [whole] * (len(inputs) + 2),
        out_specs=[whole] * count,
        scratch_shapes=[
            pltpu.VMEM((2 * count, length, LANES), jnp.float32),
            pltpu.VMEM((count, 2, 2 * inner, RADIX * LANES), jnp.bfloat16),
            pltpu.VMEM((2, inner, RADIX * LANES), jnp.float32),
        ],
        compiler_params=pltpu.CompilerParams(vmem_limit_bytes=Y_BYTES),
        cost_estimate=pl.CostEstimate(
            flops=80 * inner * length * LANES * count,
            bytes_accessed=8 * length * LANES * (len(inputs) + 3),
            transcendentals=0,
        ),
        name="y_dft",
    )(coefs, *inputs, table, twist)


def x_kernel(count, *refs):
    parts, (even_ref, odd_ref, row_ref, col_ref, out_ref, total_ref) = refs[: 2 * count], refs[2 * count :]
    columns = out_ref.shape[3]
    lanes, rows_each, tiles = LANES, 2 * LANES, columns // (2 * LANES)
    totals = []

    def left(refs, rows):
        first = pl.multiple_of(pl.program_id(0) * out_ref.shape[2], out_ref.shape[2])
        rows = pl.ds(first + rows, rows_each)
        high, low = [[ref[k + which, rows, :] for ref in refs for k in (0, 2)] for which in range(2)]
        return jnp.concatenate(high + low + high, axis=1)

    def multiply(sides, tile):
        cols = pl.ds(tile * 2 * lanes, 2 * lanes)
        return [
            dot(side, jnp.concatenate([table_ref[place, :, cols] for place in (0, 0, 1)], axis=0))
            for side, table_ref in zip(sides, (even_ref, odd_ref))
        ]

    def finish(start, tile, even, odd):
        rows = pl.ds(start, rows_each)
        row_scale, row_rate = [
            jnp.concatenate(
                [
                    jnp.broadcast_to(row_ref[which, 0, c : c + 1, :], (lanes, lanes)).T
                    for c in range(start // lanes, (start + rows_each) // lanes)
                ],
                0,
            )
            for which in range(2)
        ]
        for upper in range(2):
            cols = pl.ds(upper * columns // 2 + tile * lanes, lanes)
            spec = even - odd if upper else even + odd
            col_scale, col_shift, col_mix = col_ref[0:1, cols], col_ref[1:2, cols], col_ref[2:3, cols]
            scale = row_scale * col_scale
            latent_u = spec[:, :lanes] * scale
            latent_v = spec[:, lanes:] * scale
            log_scale = row_rate * jnp.tanh(latent_u + col_shift)
            latent_w = latent_v * jnp.exp(log_scale) + col_mix * latent_u
            out_ref[0, 0, rows, cols] = latent_u
            out_ref[1, 0, rows, cols] = latent_w
            terms = log_scale - 0.5 * (latent_u * latent_u + latent_w * latent_w)
            totals.append(jnp.sum(terms.reshape(-1, 8, lanes), axis=0))

    before = None
    for start in range(0, out_ref.shape[2], rows_each):
        sides = [left(group, start) for group in (parts[:count], parts[count:])]
        for tile in range(tiles):
            products = multiply(sides, tile)
            if before is not None:
                finish(*before)
            before = (start, tile, *products)
    finish(*before)

    @pl.when(pl.program_id(0) == 0)
    def _():
        total_ref[...] = jnp.zeros_like(total_ref)

    total_ref[...] += sum(totals)


def x_dft(even_parts, odd_parts, even_table, odd_table, row_pair, col_trio):
    parts, count, length = even_parts + odd_parts, len(even_parts), even_parts[0].shape[1]
    columns = even_table.shape[2]
    rows = length // row_pair.shape[1]
    whole = [pl.BlockSpec(memory_space=pltpu.VMEM)] * (len(parts) + 2)
    return pl.pallas_call(
        functools.partial(x_kernel, count),
        out_shape=(
            jax.ShapeDtypeStruct((2, 1, length, columns), jnp.float32),
            jax.ShapeDtypeStruct((8, LANES), jnp.float32),
        ),
        grid=(length // rows,),
        in_specs=whole
        + [
            pl.BlockSpec((2, 1, rows // LANES, LANES), lambda i: (0, i, 0, 0)),
            pl.BlockSpec(col_trio.shape, lambda i: (0, 0)),
        ],
        out_specs=(
            pl.BlockSpec((2, 1, rows, columns), lambda i: (0, 0, i, 0)),
            pl.BlockSpec((8, LANES), lambda i: (0, 0)),
        ),
        compiler_params=pltpu.CompilerParams(vmem_limit_bytes=X_BYTES),
        cost_estimate=pl.CostEstimate(
            flops=6 * length * even_table.size,
            bytes_accessed=16 * length * columns,
            transcendentals=2 * length * columns,
        ),
        name="x_dft",
    )(*parts, even_table, odd_table, row_pair, col_trio)


def sum_everywhere(tile):
    axes = ("gx", "gy")
    devices = lax.axis_size("gx") * lax.axis_size("gy")
    copies = jnp.broadcast_to(tile[None], (devices,) + tile.shape)
    return jnp.sum(lax.all_to_all(copies, axes, split_axis=0, concat_axis=0, tiled=True))


def four_way(field, row_scale, col_scale, row_rate, col_shift, col_mix):
    position = lax.axis_index("gx")
    planes, rows, columns = field.shape
    length, width = planes * rows, columns // 4
    groups = [slice(0, planes // 2), slice(planes // 2, None)]
    field_a, field_rest = lax.optimization_barrier(([field[group, :, : 2 * width] for group in groups], field))
    field_b = cut_right(field_rest)
    sign = jnp.where(position < 2, 1.0, -1.0)

    own_real = jnp.where(position == 1, -1.0, jnp.where(position == 3, 0.0, 1.0))
    other_real = jnp.where(position == 2, 0.0, 1.0)
    own_imag = jnp.where(position == 3, 1.0, 0.0)
    other_imag = jnp.where(position == 2, -1.0, 0.0)
    coefs_a = jnp.stack([own_real, other_real, own_imag, other_imag]).reshape(2, 2)
    coefs_b = jnp.concatenate([coefs_a, coefs_a * sign], axis=1)

    inner = length // RADIX
    index = jnp.arange(inner, dtype=jnp.int32)
    cos, sin = root_table(index, index, inner)
    y_table = [jnp.concatenate(pair, 1).reshape(2, 1, inner // 2, 2 * inner) for pair in ((cos, -sin), (sin, cos))]
    y_table = jnp.concatenate(y_table, 1).reshape(2 * inner, 2 * inner)
    y_table = split_table(y_table)
    grid = [lax.broadcasted_iota(jnp.int32, (RADIX, inner, LANES), axis) for axis in range(2)]
    angle = (grid[0] * grid[1]).astype(jnp.float32) * (-2.0 * math.pi / length)
    twist = jnp.stack([jnp.cos(angle), jnp.sin(angle)])
    order = jnp.arange(width, dtype=jnp.int32) * 2

    def x_table(odd):
        rows = jnp.concatenate([order + (2 * width + odd), order + odd])
        cos, sin = [part[:, : 2 * width] for part in x_tables(rows, columns, 4, position)]

        def lay(left, right):
            spans = [slice(tile * width, (tile + 1) * width) for tile in range(2)]
            return jnp.concatenate([side[:, span] for span in spans for side in (left, right)], 1)

        real, imag = lay(cos, sin), lay(-sin, cos)
        table = jnp.concatenate([real[:width], imag[:width], real[width:], imag[width:]], 0)
        return split_table(table)

    norm = 1.0 / math.sqrt(length * columns * 4)
    row_pair = jnp.stack([row_scale * norm, row_rate]).reshape(2, 4, length // 4 // LANES, LANES)
    col_trio = jnp.stack([col_scale, col_shift, col_mix])
    fixed = 2.0 * (columns * jnp.sum(jnp.log(row_scale)) + length * jnp.sum(jnp.log(col_scale)))
    fixed = fixed - length * columns * math.log(2.0 * math.pi)

    first_a = combine(sign.reshape(1), [(from_partner(part, "gx", 1), part) for part in field_a])
    tables = (y_table, twist, x_table(0), x_table(1), row_pair, col_trio, coefs_a, coefs_b, fixed)
    first_a, first_b, tables = lax.optimization_barrier((first_a, to_planes(field_b)[0], tables))
    y_table, twist, even_table, odd_table, row_pair, col_trio, coefs_a, coefs_b, fixed = tables
    second_a = to_planes(first_a)[0]
    second_b = from_partner(first_b, "gx", 1)
    group = [second_b, from_partner(second_b, "gx", 0), first_b, from_partner(first_b, "gx", 0)]
    even_b = y_dft(group, (0,), coefs_b, y_table, twist)[0]
    even_b, second_a = lax.optimization_barrier((even_b, second_a))
    odd_b = y_dft(group, (1,), coefs_b, y_table, twist)[0]
    even_a, odd_a = y_dft([second_a, from_partner(second_a, "gx", 0)], (0, 1), coefs_a, y_table, twist)
    latent, tile = x_dft([even_b, even_a], [odd_b, odd_a], even_table, odd_table, row_pair, col_trio)
    tile = tile + fixed / tile.size
    modes = length * columns * lax.axis_size("gx") * lax.axis_size("gy")
    return (latent, sum_everywhere(tile) / modes)


def complex_einsum(form, real_part, imag_part, cos_part, sin_part):
    first = jnp.einsum(form, real_part, cos_part, precision=precision_top)
    second = jnp.einsum(form, real_part, sin_part, precision=precision_top)
    first = first - jnp.einsum(form, imag_part, sin_part, precision=precision_top)
    second = second + jnp.einsum(form, imag_part, cos_part, precision=precision_top)
    return (first, second)


def x_butterfly(field):
    devices = lax.axis_size("gx")
    levels = devices.bit_length() - 1
    position = lax.axis_index("gx")
    real_part, imag_part = field, jnp.zeros_like(field)
    for level in range(levels - 1, -1, -1):
        half = 1 << level
        lower = position // half % 2 == 0
        offset = position % half
        angle = offset.astype(jnp.float32) * (-math.pi / half)
        cos_twist = jnp.where(lower, 1.0, jnp.cos(angle))
        sin_twist = jnp.where(lower, 0.0, jnp.sin(angle))
        other = from_partner(jnp.stack([real_part, imag_part]), "gx", level)
        diff_real = jnp.where(lower, real_part + other[0], other[0] - real_part)
        diff_imag = jnp.where(lower, imag_part + other[1], other[1] - imag_part)
        real_part = diff_real * cos_twist - diff_imag * sin_twist
        imag_part = diff_real * sin_twist + diff_imag * cos_twist
    width = field.shape[2]
    cos_part, sin_part = x_tables(jnp.arange(width, dtype=jnp.int32), width, devices, position)
    real_part, imag_part = complex_einsum("zyn,nk->zyk", real_part, imag_part, cos_part, sin_part)
    return (to_planes(real_part), to_planes(imag_part))


def y_transform(real_part, imag_part):
    planes, length, width = real_part.shape
    outer = 1 << (length.bit_length() - 1) // 2
    inner = length // outer
    outer_index = jnp.arange(outer, dtype=jnp.int32)
    inner_index = jnp.arange(inner, dtype=jnp.int32)
    cos_one, sin_one = root_table(outer_index, outer_index, outer)
    cos_two, sin_two = root_table(inner_index, inner_index, inner)
    cos_mid, sin_mid = root_table(outer_index, inner_index, length)
    shaped_real = real_part.reshape(planes, outer, inner, width)
    shaped_imag = imag_part.reshape(planes, outer, inner, width)
    step_real, step_imag = complex_einsum("zabc,ak->zkbc", shaped_real, shaped_imag, cos_one, sin_one)
    twist_cos = cos_mid[None, :, :, None]
    twist_sin = sin_mid[None, :, :, None]
    turned_real = step_real * twist_cos - step_imag * twist_sin
    turned_imag = step_real * twist_sin + step_imag * twist_cos
    final_real, final_imag = complex_einsum("zkbc,bj->zjkc", turned_real, turned_imag, cos_two, sin_two)
    return (final_real.reshape(planes, length, width), final_imag.reshape(planes, length, width))


def any_way(field, row_scale, col_scale, row_rate, col_shift, col_mix):
    spec_real, spec_imag = y_transform(*x_butterfly(field))
    length = spec_real.shape[1]
    total_cols = spec_real.shape[2] * lax.axis_size("gx")
    norm_factor = 1.0 / math.sqrt(length * total_cols)
    scale = row_scale[None, :, None] * col_scale[None, None, :]
    latent_u = spec_real * norm_factor * scale
    latent_v = spec_imag * norm_factor * scale
    log_scale = row_rate[None, :, None] * jnp.tanh(latent_u + col_shift[None, None, :])
    latent_w = latent_v * jnp.exp(log_scale) + col_mix[None, None, :] * latent_u
    terms = (
        -0.5 * (latent_u * latent_u + latent_w * latent_w)
        - math.log(2.0 * math.pi)
        + log_scale
        + 2.0 * jnp.log(scale)
    )
    mode_count = spec_real.size * lax.axis_size("gx") * lax.axis_size("gy")
    loglik = lax.psum(jnp.sum(terms), ("gx", "gy")) / mode_count
    return (jnp.stack([latent_u, latent_w]), loglik)


def per_device(field, *scales):
    return (four_way if lax.axis_size("gx") == 4 else any_way)(field, *scales)


def solution(mesh):
    return jax.shard_map(
        per_device,
        mesh=mesh,
        in_specs=(P(None, "gy", "gx"), P(), P("gx"), P(), P("gx"), P("gx")),
        out_specs=(P(None, "gy", None, "gx"), P()),
        check_vma=False,
    )
```

```python
import functools
import math

import jax
import jax.numpy as jnp
from jax import lax
from jax.experimental import pallas as pl
from jax.experimental.pallas import tpu as pltpu
from jax.sharding import PartitionSpec as P

precision_top = lax.Precision.HIGHEST
RADIX = 8
LANES = 128
SMALL_BYTES, Y_BYTES, X_BYTES = [size * 1024 * 1024 for size in (8, 28, 26)]


def from_partner(value, axis, stride):
    mask = 2**stride
    pairs = [(source, source ^ mask) for source in range(lax.axis_size(axis))]
    return lax.ppermute(value, axis, pairs)


def to_planes(values):
    return lax.all_to_all(values, "gy", split_axis=0, concat_axis=1, tiled=True)


def pick_columns(left, right, odd):
    lane = lax.broadcasted_iota(jnp.int32, left.shape, 1)
    index = (2 * lane + odd) & (LANES - 1)
    chosen = [jnp.take_along_axis(tile, index, axis=1, mode="promise_in_bounds") for tile in (left, right)]
    return jnp.where(lane < LANES // 2, *chosen)


def combine_kernel(sign_ref, late_ref, early_ref, *refs):
    out_ref = refs[-1]
    sign = sign_ref[0]
    for plane in range(late_ref.shape[0]):
        left, right = [
            late_ref[plane, :, pl.ds(lane, LANES)] + sign * early_ref[plane, :, pl.ds(lane, LANES)] for lane in (0, LANES)
        ]
        for odd in range(2):
            out_ref[plane, :, pl.ds(odd * LANES, LANES)] = pick_columns(left, right, odd)


def combine(sign, parts):
    planes, rows, columns = parts[0][0].shape
    result = ()
    for place, pair in enumerate(parts):
        block = pl.BlockSpec((planes // 2, rows, columns), lambda i: (i, 0, 0))
        result = pl.pallas_call(
            combine_kernel,
            out_shape=[jax.ShapeDtypeStruct((planes * len(parts), rows, columns), jnp.float32)],
            grid=(2,),
            in_specs=[pl.BlockSpec(memory_space=pltpu.SMEM), block, block]
            + [pl.BlockSpec(memory_space=pl.ANY)] * len(result),
            out_specs=[pl.BlockSpec((planes // 2, rows, columns), lambda i, place=place: (2 * place + i, 0, 0))],
            input_output_aliases={3: 0} if result else {},
            cost_estimate=pl.CostEstimate(
                flops=2 * pair[0].size, bytes_accessed=12 * pair[0].size, transcendentals=0
            ),
            compiler_params=pltpu.CompilerParams(vmem_limit_bytes=SMALL_BYTES),
            name="combine",
        )(sign, *pair, *result)
    return result[0]


def cut_kernel(field_ref, out_ref):
    for plane in range(field_ref.shape[0]):
        left, right = [field_ref[plane, :, pl.ds(lane, LANES)] for lane in (0, LANES)]
        for odd in range(2):
            out_ref[plane, :, pl.ds(odd * LANES, LANES)] = pick_columns(left, right, odd)


def cut_right(field):
    planes, rows, columns = field.shape
    block = (planes // 4, rows, columns // 2)
    return pl.pallas_call(
        cut_kernel,
        out_shape=jax.ShapeDtypeStruct((planes, rows, columns // 2), jnp.float32),
        grid=(4,),
        in_specs=[pl.BlockSpec(block, lambda i: (i, 0, 1))],
        out_specs=pl.BlockSpec(block, lambda i: (i, 0, 0)),
        cost_estimate=pl.CostEstimate(flops=field.size, bytes_accessed=4 * field.size, transcendentals=0),
        compiler_params=pltpu.CompilerParams(vmem_limit_bytes=SMALL_BYTES),
        name="cut_right",
    )(field)


def reverse_bits(value, count):
    result = value * 0
    for place in range(count):
        result = result + (value >> place & 1) * (1 << count - 1 - place)
    return result


def root_table(row_index, freqs, length):
    phase = row_index[:, None] * freqs[None, :] % length
    angle = phase.astype(jnp.float32) * (-2.0 * math.pi / length)
    return (jnp.cos(angle), jnp.sin(angle))


def x_tables(rows, width, devices, position):
    levels = devices.bit_length() - 1
    local_index = jnp.arange(width, dtype=jnp.int32)
    freqs = reverse_bits(position, levels) + devices * local_index
    return root_table(rows, freqs, devices * width)


def split_table(table):
    high = lax.reduce_precision(table, 8, 7)
    return jnp.stack([high.astype(jnp.bfloat16), (table - high).astype(jnp.bfloat16)])


def split_value(value):
    high = value.astype(jnp.bfloat16)
    return high, (value - high.astype(jnp.float32)).astype(jnp.bfloat16)


def small_fft(values):
    count = len(values)
    if count == 1:
        return values
    even, odd = small_fft(values[0::2]), small_fft(values[1::2])
    first, second = [], []
    root_half = math.sqrt(0.5)
    for place in range(count // 2):
        (er, ei), (re, im) = even[place], odd[place]
        turn = place * 8 // count
        if turn == 1:
            re, im = (re + im) * root_half, (im - re) * root_half
        elif turn == 2:
            re, im = im, -re
        elif turn == 3:
            re, im = (im - re) * root_half, (re + im) * -root_half
        first.append((er + re, ei + im))
        second.append((er - re, ei - im))
    return first + second


def dot(left, right):
    return jnp.dot(left, right, preferred_element_type=jnp.float32)


def y_kernel(count, coef_ref, *refs):
    inputs, (table_hbm, twist_hbm, *refs) = refs[:count], refs[count:]
    *out_refs, table_ref, twist_ref, in_ref, mix_ref, split_ref, step_ref, table_sems, sems = refs
    length = mix_ref.shape[1]
    inner = length // RADIX
    rows_each, rows_half = 128, length // 2

    def fetch(tile, half):
        rows, cols = pl.ds(half * rows_half, rows_half), pl.ds(tile * LANES, LANES)
        return [
            pltpu.make_async_copy(ref.at[rows, cols], in_ref.at[tile, k, rows, :], sems.at[tile, half, k])
            for k, ref in enumerate(inputs)
        ]

    table_copies = [
        pltpu.make_async_copy(source, target, table_sems.at[place])
        for place, (source, target) in enumerate(((table_hbm, table_ref), (twist_hbm, twist_ref)))
    ]
    copies = {(tile, half): fetch(tile, half) for tile in range(len(out_refs)) for half in range(2)}
    for copy in (*copies[0, 0], *copies[0, 1], *table_copies):
        copy.start()
    for tile in range(1, len(out_refs)):
        for copy in (*copies[tile, 0], *copies[tile, 1]):
            copy.start()
    for tile, out_ref in enumerate(out_refs):
        for start in range(0, length, rows_each):
            if start % rows_half == 0:
                for copy in copies[tile, start // rows_half]:
                    copy.wait()
            rows = pl.ds(start, rows_each)
            for which in range(2):
                mixed = in_ref[tile, 0, rows, :] * coef_ref[which, 0]
                for k in range(1, count):
                    mixed = mixed + in_ref[tile, k, rows, :] * coef_ref[which, k]
                mix_ref[which, rows, :] = mixed
        for which in range(2):
            for s in range(RADIX):
                parts = split_value(mix_ref[which, pl.ds(s, inner, stride=RADIX), :])
                for place, value in enumerate(parts):
                    split_ref[tile, place, pl.ds(which * inner, inner), pl.ds(s * LANES, LANES)] = value
        half = inner // 2
        for part in range(2):
            if tile == part == 0:
                table_copies[0].wait()
            table = [table_ref[place, pl.ds(part * inner, inner), :] for place in (0, 1, 0)]
            values = [split_ref[tile, place] for place in (0, 0, 1)]
            step_ref[part] = dot(jnp.concatenate(table, axis=1), jnp.concatenate(values, axis=0))
            if tile == part == 0:
                table_copies[1].wait()
            for start in range(0, half, 16):
                values = []
                for s in range(RADIX):
                    cols = pl.ds(s * LANES, LANES)
                    re = step_ref[part, pl.ds(start, 16), cols]
                    im = step_ref[part, pl.ds(half + start, 16), cols]
                    if s:
                        cos, sin = [twist_ref[k, s, pl.ds(part * half + start, 16), :] for k in range(2)]
                        re, im = re * cos - im * sin, re * sin + im * cos
                    values.append((re, im))
                for kb, pair in enumerate(small_fft(values)):
                    rows = pl.ds(kb * inner + part * half + start, 16)
                    for which in range(2):
                        high, low = split_value(pair[which])
                        out_ref[2 * which, rows, :] = high
                        out_ref[2 * which + 1, rows, :] = low


def y_dft(inputs, coefs, table, twist):
    length, columns = inputs[0].shape
    inner = length // RADIX
    tiles, count = columns // LANES, len(inputs)
    whole, anywhere = pl.BlockSpec(memory_space=pltpu.VMEM), pl.BlockSpec(memory_space=pl.ANY)
    return pl.pallas_call(
        functools.partial(y_kernel, count),
        out_shape=[jax.ShapeDtypeStruct((4, length, LANES), jnp.bfloat16)] * tiles,
        in_specs=[pl.BlockSpec(memory_space=pltpu.SMEM)] + [anywhere] * (count + 2),
        out_specs=[whole] * tiles,
        scratch_shapes=[
            pltpu.VMEM(table.shape, table.dtype),
            pltpu.VMEM(twist.shape, twist.dtype),
            pltpu.VMEM((tiles, count, length, LANES), jnp.float32),
            pltpu.VMEM((2, length, LANES), jnp.float32),
            pltpu.VMEM((tiles, 2, 2 * inner, RADIX * LANES), jnp.bfloat16),
            pltpu.VMEM((2, inner, RADIX * LANES), jnp.float32),
            pltpu.SemaphoreType.DMA((2,)),
            pltpu.SemaphoreType.DMA((tiles, 2, count)),
        ],
        compiler_params=pltpu.CompilerParams(vmem_limit_bytes=Y_BYTES),
        cost_estimate=pl.CostEstimate(
            flops=24 * inner * length * columns,
            bytes_accessed=4 * length * columns * (count + 3),
            transcendentals=0,
        ),
        name="y_dft",
    )(coefs, *inputs, table, twist)


def x_kernel(count, *refs):
    parts, (even_ref, odd_ref, row_ref, col_ref, out_ref, total_ref) = refs[: 2 * count], refs[2 * count :]
    columns = out_ref.shape[3]
    lanes, rows_each, tiles = LANES, 2 * LANES, columns // (2 * LANES)
    totals = []

    def left(refs, rows):
        first = pl.multiple_of(pl.program_id(0) * out_ref.shape[2], out_ref.shape[2])
        rows = pl.ds(first + rows, rows_each)
        high, low = [[ref[k + which, rows, :] for ref in refs for k in (0, 2)] for which in range(2)]
        return jnp.concatenate(high + low + high, axis=1)

    def multiply(sides, tile):
        cols = pl.ds(tile * 2 * lanes, 2 * lanes)
        return [
            dot(side, jnp.concatenate([table_ref[place, :, cols] for place in (0, 0, 1)], axis=0))
            for side, table_ref in zip(sides, (even_ref, odd_ref))
        ]

    def finish(start, tile, even, odd):
        rows = pl.ds(start, rows_each)
        row_scale, row_rate = [
            jnp.concatenate(
                [
                    jnp.broadcast_to(row_ref[which, 0, c : c + 1, :], (lanes, lanes)).T
                    for c in range(start // lanes, (start + rows_each) // lanes)
                ],
                0,
            )
            for which in range(2)
        ]
        for upper in range(2):
            cols = pl.ds(upper * columns // 2 + tile * lanes, lanes)
            spec = even - odd if upper else even + odd
            col_scale, col_shift, col_mix = col_ref[0:1, cols], col_ref[1:2, cols], col_ref[2:3, cols]
            scale = row_scale * col_scale
            latent_u = spec[:, :lanes] * scale
            latent_v = spec[:, lanes:] * scale
            log_scale = row_rate * jnp.tanh(latent_u + col_shift)
            latent_w = latent_v * jnp.exp(log_scale) + col_mix * latent_u
            out_ref[0, 0, rows, cols] = latent_u
            out_ref[1, 0, rows, cols] = latent_w
            terms = log_scale - 0.5 * (latent_u * latent_u + latent_w * latent_w)
            totals.append(jnp.sum(terms.reshape(-1, 8, lanes), axis=0))

    before = None
    for start in range(0, out_ref.shape[2], rows_each):
        sides = [left(group, start) for group in (parts[:count], parts[count:])]
        for tile in range(tiles):
            products = multiply(sides, tile)
            if before is not None:
                finish(*before)
            before = (start, tile, *products)
    finish(*before)

    @pl.when(pl.program_id(0) == 0)
    def _():
        total_ref[...] = jnp.zeros_like(total_ref)

    total_ref[...] += sum(totals)


def x_dft(even_parts, odd_parts, even_table, odd_table, row_pair, col_trio):
    parts, count, length = even_parts + odd_parts, len(even_parts), even_parts[0].shape[1]
    columns = even_table.shape[2]
    rows = length // row_pair.shape[1]
    whole = [pl.BlockSpec(memory_space=pltpu.VMEM)] * (len(parts) + 2)
    return pl.pallas_call(
        functools.partial(x_kernel, count),
        out_shape=(
            jax.ShapeDtypeStruct((2, 1, length, columns), jnp.float32),
            jax.ShapeDtypeStruct((8, LANES), jnp.float32),
        ),
        grid=(length // rows,),
        in_specs=whole
        + [
            pl.BlockSpec((2, 1, rows // LANES, LANES), lambda i: (0, i, 0, 0)),
            pl.BlockSpec(col_trio.shape, lambda i: (0, 0)),
        ],
        out_specs=(
            pl.BlockSpec((2, 1, rows, columns), lambda i: (0, 0, i, 0)),
            pl.BlockSpec((8, LANES), lambda i: (0, 0)),
        ),
        compiler_params=pltpu.CompilerParams(vmem_limit_bytes=X_BYTES),
        cost_estimate=pl.CostEstimate(
            flops=6 * length * even_table.size,
            bytes_accessed=16 * length * columns,
            transcendentals=2 * length * columns,
        ),
        name="x_dft",
    )(*parts, even_table, odd_table, row_pair, col_trio)


def sum_everywhere(tile):
    axes = ("gx", "gy")
    devices = lax.axis_size("gx") * lax.axis_size("gy")
    copies = jnp.broadcast_to(tile[None], (devices,) + tile.shape)
    return jnp.sum(lax.all_to_all(copies, axes, split_axis=0, concat_axis=0, tiled=True))


def four_way(field, row_scale, col_scale, row_rate, col_shift, col_mix):
    position = lax.axis_index("gx")
    planes, rows, columns = field.shape
    length, width = planes * rows, columns // 4
    groups = [slice(0, planes // 2), slice(planes // 2, None)]
    field_a, field_rest = lax.optimization_barrier(([field[group, :, : 2 * width] for group in groups], field))
    field_b = cut_right(field_rest)
    sign = jnp.where(position < 2, 1.0, -1.0)

    own_real = jnp.where(position == 1, -1.0, jnp.where(position == 3, 0.0, 1.0))
    other_real = jnp.where(position == 2, 0.0, 1.0)
    own_imag = jnp.where(position == 3, 1.0, 0.0)
    other_imag = jnp.where(position == 2, -1.0, 0.0)
    coefs_a = jnp.stack([own_real, other_real, own_imag, other_imag]).reshape(2, 2)
    coefs_b = jnp.concatenate([coefs_a, coefs_a * sign], axis=1)

    inner = length // RADIX
    index = jnp.arange(inner, dtype=jnp.int32)
    cos, sin = root_table(index, index, inner)
    y_table = [jnp.concatenate(pair, 1).reshape(2, 1, inner // 2, 2 * inner) for pair in ((cos, -sin), (sin, cos))]
    y_table = jnp.concatenate(y_table, 1).reshape(2 * inner, 2 * inner)
    y_table = split_table(y_table)
    grid = [lax.broadcasted_iota(jnp.int32, (RADIX, inner, LANES), axis) for axis in range(2)]
    angle = (grid[0] * grid[1]).astype(jnp.float32) * (-2.0 * math.pi / length)
    twist = jnp.stack([jnp.cos(angle), jnp.sin(angle)])
    order = jnp.arange(width, dtype=jnp.int32) * 2

    def x_table(odd):
        rows = jnp.concatenate([order + (2 * width + odd), order + odd])
        cos, sin = [part[:, : 2 * width] for part in x_tables(rows, columns, 4, position)]

        def lay(left, right):
            spans = [slice(tile * width, (tile + 1) * width) for tile in range(2)]
            return jnp.concatenate([side[:, span] for span in spans for side in (left, right)], 1)

        real, imag = lay(cos, sin), lay(-sin, cos)
        table = jnp.concatenate([real[:width], imag[:width], real[width:], imag[width:]], 0)
        return split_table(table)

    norm = 1.0 / math.sqrt(length * columns * 4)
    row_pair = jnp.stack([row_scale * norm, row_rate]).reshape(2, 4, length // 4 // LANES, LANES)
    col_trio = jnp.stack([col_scale, col_shift, col_mix])
    fixed = 2.0 * (columns * jnp.sum(jnp.log(row_scale)) + length * jnp.sum(jnp.log(col_scale)))
    fixed = fixed - length * columns * math.log(2.0 * math.pi)

    first_a = combine(sign.reshape(1), [(from_partner(part, "gx", 1), part) for part in field_a])
    tables = (y_table, twist, x_table(0), x_table(1), row_pair, col_trio, coefs_a, coefs_b, fixed)
    first_a, first_b, tables = lax.optimization_barrier((first_a, to_planes(field_b)[0], tables))
    y_table, twist, even_table, odd_table, row_pair, col_trio, coefs_a, coefs_b, fixed = tables
    second_a = to_planes(first_a)[0]
    second_b = from_partner(first_b, "gx", 1)
    group = [second_b, from_partner(second_b, "gx", 0), first_b, from_partner(first_b, "gx", 0)]
    even_b, odd_b = y_dft(group, coefs_b, y_table, twist)
    even_a, odd_a = y_dft([second_a, from_partner(second_a, "gx", 0)], coefs_a, y_table, twist)
    latent, tile = x_dft([even_b, even_a], [odd_b, odd_a], even_table, odd_table, row_pair, col_trio)
    tile = tile + fixed / tile.size
    modes = length * columns * lax.axis_size("gx") * lax.axis_size("gy")
    return (latent, sum_everywhere(tile) / modes)


def complex_einsum(form, real_part, imag_part, cos_part, sin_part):
    first = jnp.einsum(form, real_part, cos_part, precision=precision_top)
    second = jnp.einsum(form, real_part, sin_part, precision=precision_top)
    first = first - jnp.einsum(form, imag_part, sin_part, precision=precision_top)
    second = second + jnp.einsum(form, imag_part, cos_part, precision=precision_top)
    return (first, second)


def x_butterfly(field):
    devices = lax.axis_size("gx")
    levels = devices.bit_length() - 1
    position = lax.axis_index("gx")
    real_part, imag_part = field, jnp.zeros_like(field)
    for level in range(levels - 1, -1, -1):
        half = 1 << level
        lower = position // half % 2 == 0
        offset = position % half
        angle = offset.astype(jnp.float32) * (-math.pi / half)
        cos_twist = jnp.where(lower, 1.0, jnp.cos(angle))
        sin_twist = jnp.where(lower, 0.0, jnp.sin(angle))
        other = from_partner(jnp.stack([real_part, imag_part]), "gx", level)
        diff_real = jnp.where(lower, real_part + other[0], other[0] - real_part)
        diff_imag = jnp.where(lower, imag_part + other[1], other[1] - imag_part)
        real_part = diff_real * cos_twist - diff_imag * sin_twist
        imag_part = diff_real * sin_twist + diff_imag * cos_twist
    width = field.shape[2]
    cos_part, sin_part = x_tables(jnp.arange(width, dtype=jnp.int32), width, devices, position)
    real_part, imag_part = complex_einsum("zyn,nk->zyk", real_part, imag_part, cos_part, sin_part)
    return (to_planes(real_part), to_planes(imag_part))


def y_transform(real_part, imag_part):
    planes, length, width = real_part.shape
    outer = 1 << (length.bit_length() - 1) // 2
    inner = length // outer
    outer_index = jnp.arange(outer, dtype=jnp.int32)
    inner_index = jnp.arange(inner, dtype=jnp.int32)
    cos_one, sin_one = root_table(outer_index, outer_index, outer)
    cos_two, sin_two = root_table(inner_index, inner_index, inner)
    cos_mid, sin_mid = root_table(outer_index, inner_index, length)
    shaped_real = real_part.reshape(planes, outer, inner, width)
    shaped_imag = imag_part.reshape(planes, outer, inner, width)
    step_real, step_imag = complex_einsum("zabc,ak->zkbc", shaped_real, shaped_imag, cos_one, sin_one)
    twist_cos = cos_mid[None, :, :, None]
    twist_sin = sin_mid[None, :, :, None]
    turned_real = step_real * twist_cos - step_imag * twist_sin
    turned_imag = step_real * twist_sin + step_imag * twist_cos
    final_real, final_imag = complex_einsum("zkbc,bj->zjkc", turned_real, turned_imag, cos_two, sin_two)
    return (final_real.reshape(planes, length, width), final_imag.reshape(planes, length, width))


def any_way(field, row_scale, col_scale, row_rate, col_shift, col_mix):
    spec_real, spec_imag = y_transform(*x_butterfly(field))
    length = spec_real.shape[1]
    total_cols = spec_real.shape[2] * lax.axis_size("gx")
    norm_factor = 1.0 / math.sqrt(length * total_cols)
    scale = row_scale[None, :, None] * col_scale[None, None, :]
    latent_u = spec_real * norm_factor * scale
    latent_v = spec_imag * norm_factor * scale
    log_scale = row_rate[None, :, None] * jnp.tanh(latent_u + col_shift[None, None, :])
    latent_w = latent_v * jnp.exp(log_scale) + col_mix[None, None, :] * latent_u
    terms = (
        -0.5 * (latent_u * latent_u + latent_w * latent_w)
        - math.log(2.0 * math.pi)
        + log_scale
        + 2.0 * jnp.log(scale)
    )
    mode_count = spec_real.size * lax.axis_size("gx") * lax.axis_size("gy")
    loglik = lax.psum(jnp.sum(terms), ("gx", "gy")) / mode_count
    return (jnp.stack([latent_u, latent_w]), loglik)


def per_device(field, *scales):
    return (four_way if lax.axis_size("gx") == 4 else any_way)(field, *scales)


def solution(mesh):
    return jax.shard_map(
        per_device,
        mesh=mesh,
        in_specs=(P(None, "gy", "gx"), P(), P("gx"), P(), P("gx"), P("gx")),
        out_specs=(P(None, "gy", None, "gx"), P()),
        check_vma=False,
    )
```

```python
import functools
import math

import jax
import jax.numpy as jnp
from jax import lax
from jax.experimental import pallas as pl
from jax.experimental.pallas import tpu as pltpu
from jax.sharding import PartitionSpec as P

precision_top = lax.Precision.HIGHEST
RADIX = 8
LANES = 128
SMALL_BYTES, Y_BYTES, X_BYTES = [size * 1024 * 1024 for size in (8, 27, 26)]


def from_partner(value, axis, stride):
    mask = 2**stride
    pairs = [(source, source ^ mask) for source in range(lax.axis_size(axis))]
    return lax.ppermute(value, axis, pairs)


def to_planes(values):
    return lax.all_to_all(values, "gy", split_axis=0, concat_axis=1, tiled=True)


def pick_columns(left, right, odd):
    lane = lax.broadcasted_iota(jnp.int32, left.shape, 1)
    index = (2 * lane + odd) & (LANES - 1)
    chosen = [jnp.take_along_axis(tile, index, axis=1, mode="promise_in_bounds") for tile in (left, right)]
    return jnp.where(lane < LANES // 2, *chosen)


def combine_kernel(sign_ref, late_ref, early_ref, *refs):
    out_ref = refs[-1]
    sign = sign_ref[0]
    for plane in range(late_ref.shape[0]):
        left, right = [
            late_ref[plane, :, pl.ds(lane, LANES)] + sign * early_ref[plane, :, pl.ds(lane, LANES)] for lane in (0, LANES)
        ]
        for odd in range(2):
            out_ref[plane, :, pl.ds(odd * LANES, LANES)] = pick_columns(left, right, odd)


def combine(sign, parts):
    planes, rows, columns = parts[0][0].shape
    result = ()
    for place, pair in enumerate(parts):
        block = pl.BlockSpec((planes // 2, rows, columns), lambda i: (i, 0, 0))
        result = pl.pallas_call(
            combine_kernel,
            out_shape=[jax.ShapeDtypeStruct((planes * len(parts), rows, columns), jnp.float32)],
            grid=(2,),
            in_specs=[pl.BlockSpec(memory_space=pltpu.SMEM), block, block]
            + [pl.BlockSpec(memory_space=pl.ANY)] * len(result),
            out_specs=[pl.BlockSpec((planes // 2, rows, columns), lambda i, place=place: (2 * place + i, 0, 0))],
            input_output_aliases={3: 0} if result else {},
            cost_estimate=pl.CostEstimate(
                flops=2 * pair[0].size, bytes_accessed=12 * pair[0].size, transcendentals=0
            ),
            compiler_params=pltpu.CompilerParams(vmem_limit_bytes=SMALL_BYTES),
            name="combine",
        )(sign, *pair, *result)
    return result[0]


def reverse_bits(value, count):
    result = value * 0
    for place in range(count):
        result = result + (value >> place & 1) * (1 << count - 1 - place)
    return result


def root_table(row_index, freqs, length):
    phase = row_index[:, None] * freqs[None, :] % length
    angle = phase.astype(jnp.float32) * (-2.0 * math.pi / length)
    return (jnp.cos(angle), jnp.sin(angle))


def x_tables(rows, width, devices, position):
    levels = devices.bit_length() - 1
    local_index = jnp.arange(width, dtype=jnp.int32)
    freqs = reverse_bits(position, levels) + devices * local_index
    return root_table(rows, freqs, devices * width)


def split_table(table):
    high = lax.reduce_precision(table, 8, 7)
    return jnp.stack([high.astype(jnp.bfloat16), (table - high).astype(jnp.bfloat16)])


def split_value(value):
    high = value.astype(jnp.bfloat16)
    return high, (value - high.astype(jnp.float32)).astype(jnp.bfloat16)


def small_fft(values):
    count = len(values)
    if count == 1:
        return values
    even, odd = small_fft(values[0::2]), small_fft(values[1::2])
    first, second = [], []
    root_half = math.sqrt(0.5)
    for place in range(count // 2):
        (er, ei), (re, im) = even[place], odd[place]
        turn = place * 8 // count
        if turn == 1:
            re, im = (re + im) * root_half, (im - re) * root_half
        elif turn == 2:
            re, im = im, -re
        elif turn == 3:
            re, im = (im - re) * root_half, (re + im) * -root_half
        first.append((er + re, ei + im))
        second.append((er - re, ei - im))
    return first + second


def dot(left, right):
    return jnp.dot(left, right, preferred_element_type=jnp.float32)


def y_kernel(count, pick, coef_ref, *refs):
    inputs, (table_ref, twist_ref, *out_refs, mix_ref, split_ref, step_ref) = refs[:count], refs[count:]
    length = mix_ref.shape[1]
    inner = length // RADIX
    rows_each = 128
    for start in range(0, length, rows_each):
        rows = pl.ds(start, rows_each)
        for which in range(2):
            tiles = []
            for lane in (0, LANES):
                mixed = inputs[0][rows, pl.ds(lane, LANES)] * coef_ref[which, 0]
                for place in range(1, count):
                    mixed = mixed + inputs[place][rows, pl.ds(lane, LANES)] * coef_ref[which, place]
                tiles.append(mixed)
            for tile in range(2):
                mix_ref[2 * tile + which, rows, :] = pick_columns(*tiles, tile) if pick else tiles[tile]
    for tile, out_ref in enumerate(out_refs):
        for which in range(2):
            for s in range(RADIX):
                parts = split_value(mix_ref[2 * tile + which, pl.ds(s, inner, stride=RADIX), :])
                for place, value in enumerate(parts):
                    split_ref[tile, place, pl.ds(which * inner, inner), pl.ds(s * LANES, LANES)] = value
        half = inner // 2
        for part in range(2):
            table = [table_ref[place, pl.ds(part * inner, inner), :] for place in (0, 1, 0)]
            values = [split_ref[tile, place] for place in (0, 0, 1)]
            step_ref[part] = dot(jnp.concatenate(table, axis=1), jnp.concatenate(values, axis=0))
            for start in range(0, half, 16):
                values = []
                for s in range(RADIX):
                    cols = pl.ds(s * LANES, LANES)
                    re = step_ref[part, pl.ds(start, 16), cols]
                    im = step_ref[part, pl.ds(half + start, 16), cols]
                    if s:
                        cos, sin = [twist_ref[k, s, pl.ds(part * half + start, 16), :] for k in range(2)]
                        re, im = re * cos - im * sin, re * sin + im * cos
                    values.append((re, im))
                for kb, pair in enumerate(small_fft(values)):
                    rows = pl.ds(kb * inner + part * half + start, 16)
                    for which in range(2):
                        high, low = split_value(pair[which])
                        out_ref[2 * which, rows, :] = high
                        out_ref[2 * which + 1, rows, :] = low


def y_dft(inputs, pick, coefs, table, twist):
    length = inputs[0].shape[0]
    inner = length // RADIX
    whole = pl.BlockSpec(memory_space=pltpu.VMEM)
    return pl.pallas_call(
        functools.partial(y_kernel, len(inputs), pick),
        out_shape=[jax.ShapeDtypeStruct((4, length, LANES), jnp.bfloat16)] * 2,
        in_specs=[pl.BlockSpec(memory_space=pltpu.SMEM)] + [whole] * (len(inputs) + 2),
        out_specs=[whole] * 2,
        scratch_shapes=[
            pltpu.VMEM((4, length, LANES), jnp.float32),
            pltpu.VMEM((2, 2, 2 * inner, RADIX * LANES), jnp.bfloat16),
            pltpu.VMEM((2, inner, RADIX * LANES), jnp.float32),
        ],
        compiler_params=pltpu.CompilerParams(vmem_limit_bytes=Y_BYTES),
        cost_estimate=pl.CostEstimate(
            flops=160 * inner * length * LANES, bytes_accessed=8 * length * LANES * (len(inputs) + 3), transcendentals=0
        ),
        name="y_dft",
    )(coefs, *inputs, table, twist)


def x_kernel(count, *refs):
    parts, (even_ref, odd_ref, row_ref, col_ref, out_ref, total_ref) = refs[: 2 * count], refs[2 * count :]
    columns = out_ref.shape[3]
    lanes, rows_each, tiles = LANES, 2 * LANES, columns // (2 * LANES)
    totals = []

    def left(refs, rows):
        first = pl.multiple_of(pl.program_id(0) * out_ref.shape[2], out_ref.shape[2])
        rows = pl.ds(first + rows, rows_each)
        high, low = [[ref[k + which, rows, :] for ref in refs for k in (0, 2)] for which in range(2)]
        return jnp.concatenate(high + low + high, axis=1)

    def multiply(sides, tile):
        cols = pl.ds(tile * 2 * lanes, 2 * lanes)
        return [
            dot(side, jnp.concatenate([table_ref[place, :, cols] for place in (0, 0, 1)], axis=0))
            for side, table_ref in zip(sides, (even_ref, odd_ref))
        ]

    def finish(start, tile, even, odd):
        rows = pl.ds(start, rows_each)
        row_scale, row_rate = [
            jnp.concatenate(
                [
                    jnp.broadcast_to(row_ref[which, 0, c : c + 1, :], (lanes, lanes)).T
                    for c in range(start // lanes, (start + rows_each) // lanes)
                ],
                0,
            )
            for which in range(2)
        ]
        for upper in range(2):
            cols = pl.ds(upper * columns // 2 + tile * lanes, lanes)
            spec = even - odd if upper else even + odd
            col_scale, col_shift, col_mix = col_ref[0:1, cols], col_ref[1:2, cols], col_ref[2:3, cols]
            scale = row_scale * col_scale
            latent_u = spec[:, :lanes] * scale
            latent_v = spec[:, lanes:] * scale
            log_scale = row_rate * jnp.tanh(latent_u + col_shift)
            latent_w = latent_v * jnp.exp(log_scale) + col_mix * latent_u
            out_ref[0, 0, rows, cols] = latent_u
            out_ref[1, 0, rows, cols] = latent_w
            terms = log_scale - 0.5 * (latent_u * latent_u + latent_w * latent_w)
            totals.append(jnp.sum(terms.reshape(-1, 8, lanes), axis=0))

    before = None
    for start in range(0, out_ref.shape[2], rows_each):
        sides = [left(group, start) for group in (parts[:count], parts[count:])]
        for tile in range(tiles):
            products = multiply(sides, tile)
            if before is not None:
                finish(*before)
            before = (start, tile, *products)
    finish(*before)

    @pl.when(pl.program_id(0) == 0)
    def _():
        total_ref[...] = jnp.zeros_like(total_ref)

    total_ref[...] += sum(totals)


def x_dft(even_parts, odd_parts, even_table, odd_table, row_pair, col_trio):
    parts, count, length = even_parts + odd_parts, len(even_parts), even_parts[0].shape[1]
    columns = even_table.shape[2]
    rows = length // row_pair.shape[1]
    whole = [pl.BlockSpec(memory_space=pltpu.VMEM)] * (len(parts) + 2)
    return pl.pallas_call(
        functools.partial(x_kernel, count),
        out_shape=(
            jax.ShapeDtypeStruct((2, 1, length, columns), jnp.float32),
            jax.ShapeDtypeStruct((8, LANES), jnp.float32),
        ),
        grid=(length // rows,),
        in_specs=whole
        + [
            pl.BlockSpec((2, 1, rows // LANES, LANES), lambda i: (0, i, 0, 0)),
            pl.BlockSpec(col_trio.shape, lambda i: (0, 0)),
        ],
        out_specs=(
            pl.BlockSpec((2, 1, rows, columns), lambda i: (0, 0, i, 0)),
            pl.BlockSpec((8, LANES), lambda i: (0, 0)),
        ),
        compiler_params=pltpu.CompilerParams(vmem_limit_bytes=X_BYTES),
        cost_estimate=pl.CostEstimate(
            flops=6 * length * even_table.size,
            bytes_accessed=16 * length * columns,
            transcendentals=2 * length * columns,
        ),
        name="x_dft",
    )(*parts, even_table, odd_table, row_pair, col_trio)


def sum_everywhere(tile):
    axes = ("gx", "gy")
    devices = lax.axis_size("gx") * lax.axis_size("gy")
    copies = jnp.broadcast_to(tile[None], (devices,) + tile.shape)
    return jnp.sum(lax.all_to_all(copies, axes, split_axis=0, concat_axis=0, tiled=True))


def four_way(field, row_scale, col_scale, row_rate, col_shift, col_mix):
    position = lax.axis_index("gx")
    planes, rows, columns = field.shape
    length, width = planes * rows, columns // 4
    groups = [slice(0, planes // 2), slice(planes // 2, None)]
    field_b, field_rest = lax.optimization_barrier((field[:, :, 2 * width :], field))
    field_a = [field_rest[group, :, : 2 * width] for group in groups]
    sign = jnp.where(position < 2, 1.0, -1.0)

    own_real = jnp.where(position == 1, -1.0, jnp.where(position == 3, 0.0, 1.0))
    other_real = jnp.where(position == 2, 0.0, 1.0)
    own_imag = jnp.where(position == 3, 1.0, 0.0)
    other_imag = jnp.where(position == 2, -1.0, 0.0)
    coefs_a = jnp.stack([own_real, other_real, own_imag, other_imag]).reshape(2, 2)
    coefs_b = jnp.concatenate([coefs_a, coefs_a * sign], axis=1)

    inner = length // RADIX
    index = jnp.arange(inner, dtype=jnp.int32)
    cos, sin = root_table(index, index, inner)
    y_table = [jnp.concatenate(pair, 1).reshape(2, 1, inner // 2, 2 * inner) for pair in ((cos, -sin), (sin, cos))]
    y_table = jnp.concatenate(y_table, 1).reshape(2 * inner, 2 * inner)
    y_table = split_table(y_table)
    grid = [lax.broadcasted_iota(jnp.int32, (RADIX, inner, LANES), axis) for axis in range(2)]
    angle = (grid[0] * grid[1]).astype(jnp.float32) * (-2.0 * math.pi / length)
    twist = jnp.stack([jnp.cos(angle), jnp.sin(angle)])
    order = jnp.arange(width, dtype=jnp.int32) * 2

    def x_table(odd):
        rows = jnp.concatenate([order + (2 * width + odd), order + odd])
        cos, sin = [part[:, : 2 * width] for part in x_tables(rows, columns, 4, position)]

        def lay(left, right):
            spans = [slice(tile * width, (tile + 1) * width) for tile in range(2)]
            return jnp.concatenate([side[:, span] for span in spans for side in (left, right)], 1)

        real, imag = lay(cos, sin), lay(-sin, cos)
        table = jnp.concatenate([real[:width], imag[:width], real[width:], imag[width:]], 0)
        return split_table(table)

    norm = 1.0 / math.sqrt(length * columns * 4)
    row_pair = jnp.stack([row_scale * norm, row_rate]).reshape(2, 4, length // 4 // LANES, LANES)
    col_trio = jnp.stack([col_scale, col_shift, col_mix])
    fixed = 2.0 * (columns * jnp.sum(jnp.log(row_scale)) + length * jnp.sum(jnp.log(col_scale)))
    fixed = fixed - length * columns * math.log(2.0 * math.pi)

    first_a = combine(sign.reshape(1), [(from_partner(part, "gx", 1), part) for part in field_a])
    tables = (y_table, twist, x_table(0), x_table(1), row_pair, col_trio, coefs_a, coefs_b, fixed)
    first_a, first_b, tables = lax.optimization_barrier((first_a, to_planes(field_b)[0], tables))
    y_table, twist, even_table, odd_table, row_pair, col_trio, coefs_a, coefs_b, fixed = tables
    second_a = to_planes(first_a)[0]
    second_b = from_partner(first_b, "gx", 1)
    group = [second_b, from_partner(second_b, "gx", 0), first_b, from_partner(first_b, "gx", 0)]
    even_b, odd_b = y_dft(group, True, coefs_b, y_table, twist)
    even_a, odd_a = y_dft([second_a, from_partner(second_a, "gx", 0)], False, coefs_a, y_table, twist)
    latent, tile = x_dft([even_b, even_a], [odd_b, odd_a], even_table, odd_table, row_pair, col_trio)
    tile = tile + fixed / tile.size
    modes = length * columns * lax.axis_size("gx") * lax.axis_size("gy")
    return (latent, sum_everywhere(tile) / modes)


def complex_einsum(form, real_part, imag_part, cos_part, sin_part):
    first = jnp.einsum(form, real_part, cos_part, precision=precision_top)
    second = jnp.einsum(form, real_part, sin_part, precision=precision_top)
    first = first - jnp.einsum(form, imag_part, sin_part, precision=precision_top)
    second = second + jnp.einsum(form, imag_part, cos_part, precision=precision_top)
    return (first, second)


def x_butterfly(field):
    devices = lax.axis_size("gx")
    levels = devices.bit_length() - 1
    position = lax.axis_index("gx")
    real_part, imag_part = field, jnp.zeros_like(field)
    for level in range(levels - 1, -1, -1):
        half = 1 << level
        lower = position // half % 2 == 0
        offset = position % half
        angle = offset.astype(jnp.float32) * (-math.pi / half)
        cos_twist = jnp.where(lower, 1.0, jnp.cos(angle))
        sin_twist = jnp.where(lower, 0.0, jnp.sin(angle))
        other = from_partner(jnp.stack([real_part, imag_part]), "gx", level)
        diff_real = jnp.where(lower, real_part + other[0], other[0] - real_part)
        diff_imag = jnp.where(lower, imag_part + other[1], other[1] - imag_part)
        real_part = diff_real * cos_twist - diff_imag * sin_twist
        imag_part = diff_real * sin_twist + diff_imag * cos_twist
    width = field.shape[2]
    cos_part, sin_part = x_tables(jnp.arange(width, dtype=jnp.int32), width, devices, position)
    real_part, imag_part = complex_einsum("zyn,nk->zyk", real_part, imag_part, cos_part, sin_part)
    return (to_planes(real_part), to_planes(imag_part))


def y_transform(real_part, imag_part):
    planes, length, width = real_part.shape
    outer = 1 << (length.bit_length() - 1) // 2
    inner = length // outer
    outer_index = jnp.arange(outer, dtype=jnp.int32)
    inner_index = jnp.arange(inner, dtype=jnp.int32)
    cos_one, sin_one = root_table(outer_index, outer_index, outer)
    cos_two, sin_two = root_table(inner_index, inner_index, inner)
    cos_mid, sin_mid = root_table(outer_index, inner_index, length)
    shaped_real = real_part.reshape(planes, outer, inner, width)
    shaped_imag = imag_part.reshape(planes, outer, inner, width)
    step_real, step_imag = complex_einsum("zabc,ak->zkbc", shaped_real, shaped_imag, cos_one, sin_one)
    twist_cos = cos_mid[None, :, :, None]
    twist_sin = sin_mid[None, :, :, None]
    turned_real = step_real * twist_cos - step_imag * twist_sin
    turned_imag = step_real * twist_sin + step_imag * twist_cos
    final_real, final_imag = complex_einsum("zkbc,bj->zjkc", turned_real, turned_imag, cos_two, sin_two)
    return (final_real.reshape(planes, length, width), final_imag.reshape(planes, length, width))


def any_way(field, row_scale, col_scale, row_rate, col_shift, col_mix):
    spec_real, spec_imag = y_transform(*x_butterfly(field))
    length = spec_real.shape[1]
    total_cols = spec_real.shape[2] * lax.axis_size("gx")
    norm_factor = 1.0 / math.sqrt(length * total_cols)
    scale = row_scale[None, :, None] * col_scale[None, None, :]
    latent_u = spec_real * norm_factor * scale
    latent_v = spec_imag * norm_factor * scale
    log_scale = row_rate[None, :, None] * jnp.tanh(latent_u + col_shift[None, None, :])
    latent_w = latent_v * jnp.exp(log_scale) + col_mix[None, None, :] * latent_u
    terms = (
        -0.5 * (latent_u * latent_u + latent_w * latent_w)
        - math.log(2.0 * math.pi)
        + log_scale
        + 2.0 * jnp.log(scale)
    )
    mode_count = spec_real.size * lax.axis_size("gx") * lax.axis_size("gy")
    loglik = lax.psum(jnp.sum(terms), ("gx", "gy")) / mode_count
    return (jnp.stack([latent_u, latent_w]), loglik)


def per_device(field, *scales):
    return (four_way if lax.axis_size("gx") == 4 else any_way)(field, *scales)


def solution(mesh):
    return jax.shard_map(
        per_device,
        mesh=mesh,
        in_specs=(P(None, "gy", "gx"), P(), P("gx"), P(), P("gx"), P("gx")),
        out_specs=(P(None, "gy", None, "gx"), P()),
        check_vma=False,
    )
```

```python
import functools
import math

import jax
import jax.numpy as jnp
from jax import lax
from jax.experimental import pallas as pl
from jax.experimental.pallas import tpu as pltpu
from jax.sharding import PartitionSpec as P

precision_top = lax.Precision.HIGHEST
RADIX = 8
LANES = 128
SMALL_BYTES, Y_BYTES, X_BYTES = [size * 1024 * 1024 for size in (8, 27, 26)]


def from_partner(value, axis, stride):
    mask = 2**stride
    pairs = [(source, source ^ mask) for source in range(lax.axis_size(axis))]
    return lax.ppermute(value, axis, pairs)


def to_planes(values):
    return lax.all_to_all(values, "gy", split_axis=0, concat_axis=1, tiled=True)


def pick_columns(left, right, odd):
    lane = lax.broadcasted_iota(jnp.int32, left.shape, 1)
    index = (2 * lane + odd) & (LANES - 1)
    chosen = [jnp.take_along_axis(tile, index, axis=1, mode="promise_in_bounds") for tile in (left, right)]
    return jnp.where(lane < LANES // 2, *chosen)


def combine_kernel(sign_ref, late_ref, early_ref, *refs):
    out_ref = refs[-1]
    sign = sign_ref[0]
    for plane in range(late_ref.shape[0]):
        left, right = [
            late_ref[plane, :, pl.ds(lane, LANES)] + sign * early_ref[plane, :, pl.ds(lane, LANES)] for lane in (0, LANES)
        ]
        for odd in range(2):
            out_ref[plane, :, pl.ds(odd * LANES, LANES)] = pick_columns(left, right, odd)


def combine(sign, parts):
    planes, rows, columns = parts[0][0].shape
    result = ()
    for place, pair in enumerate(parts):
        block = pl.BlockSpec((planes // 2, rows, columns), lambda i: (i, 0, 0))
        result = pl.pallas_call(
            combine_kernel,
            out_shape=[jax.ShapeDtypeStruct((planes * len(parts), rows, columns), jnp.float32)],
            grid=(2,),
            in_specs=[pl.BlockSpec(memory_space=pltpu.SMEM), block, block]
            + [pl.BlockSpec(memory_space=pl.ANY)] * len(result),
            out_specs=[pl.BlockSpec((planes // 2, rows, columns), lambda i, place=place: (2 * place + i, 0, 0))],
            input_output_aliases={3: 0} if result else {},
            cost_estimate=pl.CostEstimate(
                flops=2 * pair[0].size, bytes_accessed=12 * pair[0].size, transcendentals=0
            ),
            compiler_params=pltpu.CompilerParams(vmem_limit_bytes=SMALL_BYTES),
            name="combine",
        )(sign, *pair, *result)
    return result[0]


def reverse_bits(value, count):
    result = value * 0
    for place in range(count):
        result = result + (value >> place & 1) * (1 << count - 1 - place)
    return result


def root_table(row_index, freqs, length):
    phase = row_index[:, None] * freqs[None, :] % length
    angle = phase.astype(jnp.float32) * (-2.0 * math.pi / length)
    return (jnp.cos(angle), jnp.sin(angle))


def x_tables(rows, width, devices, position):
    levels = devices.bit_length() - 1
    local_index = jnp.arange(width, dtype=jnp.int32)
    freqs = reverse_bits(position, levels) + devices * local_index
    return root_table(rows, freqs, devices * width)


def split_table(table):
    high = lax.reduce_precision(table, 8, 7)
    return jnp.stack([high.astype(jnp.bfloat16), (table - high).astype(jnp.bfloat16)])


def split_value(value):
    high = value.astype(jnp.bfloat16)
    return high, (value - high.astype(jnp.float32)).astype(jnp.bfloat16)


def small_fft(values):
    count = len(values)
    if count == 1:
        return values
    even, odd = small_fft(values[0::2]), small_fft(values[1::2])
    first, second = [], []
    root_half = math.sqrt(0.5)
    for place in range(count // 2):
        (er, ei), (re, im) = even[place], odd[place]
        turn = place * 8 // count
        if turn == 1:
            re, im = (re + im) * root_half, (im - re) * root_half
        elif turn == 2:
            re, im = im, -re
        elif turn == 3:
            re, im = (im - re) * root_half, (re + im) * -root_half
        first.append((er + re, ei + im))
        second.append((er - re, ei - im))
    return first + second


def dot(left, right):
    return jnp.dot(left, right, preferred_element_type=jnp.float32)


def y_kernel(count, pick, coef_ref, *refs):
    inputs, (table_ref, twist_ref, *out_refs, mix_ref, split_ref, step_ref) = refs[:count], refs[count:]
    length = mix_ref.shape[1]
    inner = length // RADIX
    rows_each = 128
    for start in range(0, length, rows_each):
        rows = pl.ds(start, rows_each)
        for which in range(2):
            tiles = []
            for lane in (0, LANES):
                mixed = inputs[0][rows, pl.ds(lane, LANES)] * coef_ref[which, 0]
                for place in range(1, count):
                    mixed = mixed + inputs[place][rows, pl.ds(lane, LANES)] * coef_ref[which, place]
                tiles.append(mixed)
            for tile in range(2):
                mix_ref[2 * tile + which, rows, :] = pick_columns(*tiles, tile) if pick else tiles[tile]
    half = inner // 2

    def split(tile):
        for which in range(2):
            for s in range(RADIX):
                parts = split_value(mix_ref[2 * tile + which, pl.ds(s, inner, stride=RADIX), :])
                for place, value in enumerate(parts):
                    split_ref[tile, place, pl.ds(which * inner, inner), pl.ds(s * LANES, LANES)] = value

    def multiply(tile, part):
        table = [table_ref[place, pl.ds(part * inner, inner), :] for place in (0, 1, 0)]
        values = [split_ref[tile, place] for place in (0, 0, 1)]
        step_ref[part] = dot(jnp.concatenate(table, axis=1), jnp.concatenate(values, axis=0))

    def finish(tile, part):
        for start in range(0, half, 16):
            values = []
            for s in range(RADIX):
                cols = pl.ds(s * LANES, LANES)
                re = step_ref[part, pl.ds(start, 16), cols]
                im = step_ref[part, pl.ds(half + start, 16), cols]
                if s:
                    cos, sin = [twist_ref[k, s, pl.ds(part * half + start, 16), :] for k in range(2)]
                    re, im = re * cos - im * sin, re * sin + im * cos
                values.append((re, im))
            for kb, pair in enumerate(small_fft(values)):
                rows = pl.ds(kb * inner + part * half + start, 16)
                for which in range(2):
                    high, low = split_value(pair[which])
                    out_refs[tile][2 * which, rows, :] = high
                    out_refs[tile][2 * which + 1, rows, :] = low

    jobs = [(tile, part) for tile in range(len(out_refs)) for part in range(2)]
    split(0)
    multiply(*jobs[0])
    for before, job in zip(jobs, jobs[1:]):
        if job[1]:
            if job[0] + 1 < len(out_refs):
                split(job[0] + 1)
        multiply(*job)
        finish(*before)
    finish(*jobs[-1])


def y_dft(inputs, pick, coefs, table, twist):
    length = inputs[0].shape[0]
    inner = length // RADIX
    whole = pl.BlockSpec(memory_space=pltpu.VMEM)
    return pl.pallas_call(
        functools.partial(y_kernel, len(inputs), pick),
        out_shape=[jax.ShapeDtypeStruct((4, length, LANES), jnp.bfloat16)] * 2,
        in_specs=[pl.BlockSpec(memory_space=pltpu.SMEM)] + [whole] * (len(inputs) + 2),
        out_specs=[whole] * 2,
        scratch_shapes=[
            pltpu.VMEM((4, length, LANES), jnp.float32),
            pltpu.VMEM((2, 2, 2 * inner, RADIX * LANES), jnp.bfloat16),
            pltpu.VMEM((2, inner, RADIX * LANES), jnp.float32),
        ],
        compiler_params=pltpu.CompilerParams(vmem_limit_bytes=Y_BYTES),
        cost_estimate=pl.CostEstimate(
            flops=160 * inner * length * LANES, bytes_accessed=8 * length * LANES * (len(inputs) + 3), transcendentals=0
        ),
        name="y_dft",
    )(coefs, *inputs, table, twist)


def x_kernel(count, *refs):
    parts, (even_ref, odd_ref, row_ref, col_ref, out_ref, total_ref) = refs[: 2 * count], refs[2 * count :]
    columns = out_ref.shape[3]
    lanes, rows_each, tiles = LANES, 2 * LANES, columns // (2 * LANES)
    totals = []

    def left(refs, rows):
        first = pl.multiple_of(pl.program_id(0) * out_ref.shape[2], out_ref.shape[2])
        rows = pl.ds(first + rows, rows_each)
        high, low = [[ref[k + which, rows, :] for ref in refs for k in (0, 2)] for which in range(2)]
        return jnp.concatenate(high + low + high, axis=1)

    def multiply(sides, tile):
        cols = pl.ds(tile * 2 * lanes, 2 * lanes)
        return [
            dot(side, jnp.concatenate([table_ref[place, :, cols] for place in (0, 0, 1)], axis=0))
            for side, table_ref in zip(sides, (even_ref, odd_ref))
        ]

    def finish(start, tile, even, odd):
        rows = pl.ds(start, rows_each)
        row_scale, row_rate = [
            jnp.concatenate(
                [
                    jnp.broadcast_to(row_ref[which, 0, c : c + 1, :], (lanes, lanes)).T
                    for c in range(start // lanes, (start + rows_each) // lanes)
                ],
                0,
            )
            for which in range(2)
        ]
        for upper in range(2):
            cols = pl.ds(upper * columns // 2 + tile * lanes, lanes)
            spec = even - odd if upper else even + odd
            col_scale, col_shift, col_mix = col_ref[0:1, cols], col_ref[1:2, cols], col_ref[2:3, cols]
            scale = row_scale * col_scale
            latent_u = spec[:, :lanes] * scale
            latent_v = spec[:, lanes:] * scale
            log_scale = row_rate * jnp.tanh(latent_u + col_shift)
            latent_w = latent_v * jnp.exp(log_scale) + col_mix * latent_u
            out_ref[0, 0, rows, cols] = latent_u
            out_ref[1, 0, rows, cols] = latent_w
            terms = log_scale - 0.5 * (latent_u * latent_u + latent_w * latent_w)
            totals.append(jnp.sum(terms.reshape(-1, 8, lanes), axis=0))

    before = None
    for start in range(0, out_ref.shape[2], rows_each):
        sides = [left(group, start) for group in (parts[:count], parts[count:])]
        for tile in range(tiles):
            products = multiply(sides, tile)
            if before is not None:
                finish(*before)
            before = (start, tile, *products)
    finish(*before)

    @pl.when(pl.program_id(0) == 0)
    def _():
        total_ref[...] = jnp.zeros_like(total_ref)

    total_ref[...] += sum(totals)


def x_dft(even_parts, odd_parts, even_table, odd_table, row_pair, col_trio):
    parts, count, length = even_parts + odd_parts, len(even_parts), even_parts[0].shape[1]
    columns = even_table.shape[2]
    rows = length // row_pair.shape[1]
    whole = [pl.BlockSpec(memory_space=pltpu.VMEM)] * (len(parts) + 2)
    return pl.pallas_call(
        functools.partial(x_kernel, count),
        out_shape=(
            jax.ShapeDtypeStruct((2, 1, length, columns), jnp.float32),
            jax.ShapeDtypeStruct((8, LANES), jnp.float32),
        ),
        grid=(length // rows,),
        in_specs=whole
        + [
            pl.BlockSpec((2, 1, rows // LANES, LANES), lambda i: (0, i, 0, 0)),
            pl.BlockSpec(col_trio.shape, lambda i: (0, 0)),
        ],
        out_specs=(
            pl.BlockSpec((2, 1, rows, columns), lambda i: (0, 0, i, 0)),
            pl.BlockSpec((8, LANES), lambda i: (0, 0)),
        ),
        compiler_params=pltpu.CompilerParams(vmem_limit_bytes=X_BYTES),
        cost_estimate=pl.CostEstimate(
            flops=6 * length * even_table.size,
            bytes_accessed=16 * length * columns,
            transcendentals=2 * length * columns,
        ),
        name="x_dft",
    )(*parts, even_table, odd_table, row_pair, col_trio)


def sum_everywhere(tile):
    axes = ("gx", "gy")
    devices = lax.axis_size("gx") * lax.axis_size("gy")
    copies = jnp.broadcast_to(tile[None], (devices,) + tile.shape)
    return jnp.sum(lax.all_to_all(copies, axes, split_axis=0, concat_axis=0, tiled=True))


def four_way(field, row_scale, col_scale, row_rate, col_shift, col_mix):
    position = lax.axis_index("gx")
    planes, rows, columns = field.shape
    length, width = planes * rows, columns // 4
    groups = [slice(0, planes // 2), slice(planes // 2, None)]
    field_b, field_rest = lax.optimization_barrier((field[:, :, 2 * width :], field))
    field_a = [field_rest[group, :, : 2 * width] for group in groups]
    sign = jnp.where(position < 2, 1.0, -1.0)

    own_real = jnp.where(position == 1, -1.0, jnp.where(position == 3, 0.0, 1.0))
    other_real = jnp.where(position == 2, 0.0, 1.0)
    own_imag = jnp.where(position == 3, 1.0, 0.0)
    other_imag = jnp.where(position == 2, -1.0, 0.0)
    coefs_a = jnp.stack([own_real, other_real, own_imag, other_imag]).reshape(2, 2)
    coefs_b = jnp.concatenate([coefs_a, coefs_a * sign], axis=1)

    inner = length // RADIX
    index = jnp.arange(inner, dtype=jnp.int32)
    cos, sin = root_table(index, index, inner)
    y_table = [jnp.concatenate(pair, 1).reshape(2, 1, inner // 2, 2 * inner) for pair in ((cos, -sin), (sin, cos))]
    y_table = jnp.concatenate(y_table, 1).reshape(2 * inner, 2 * inner)
    y_table = split_table(y_table)
    grid = [lax.broadcasted_iota(jnp.int32, (RADIX, inner, LANES), axis) for axis in range(2)]
    angle = (grid[0] * grid[1]).astype(jnp.float32) * (-2.0 * math.pi / length)
    twist = jnp.stack([jnp.cos(angle), jnp.sin(angle)])
    order = jnp.arange(width, dtype=jnp.int32) * 2

    def x_table(odd):
        rows = jnp.concatenate([order + (2 * width + odd), order + odd])
        cos, sin = [part[:, : 2 * width] for part in x_tables(rows, columns, 4, position)]

        def lay(left, right):
            spans = [slice(tile * width, (tile + 1) * width) for tile in range(2)]
            return jnp.concatenate([side[:, span] for span in spans for side in (left, right)], 1)

        real, imag = lay(cos, sin), lay(-sin, cos)
        table = jnp.concatenate([real[:width], imag[:width], real[width:], imag[width:]], 0)
        return split_table(table)

    norm = 1.0 / math.sqrt(length * columns * 4)
    row_pair = jnp.stack([row_scale * norm, row_rate]).reshape(2, 4, length // 4 // LANES, LANES)
    col_trio = jnp.stack([col_scale, col_shift, col_mix])
    fixed = 2.0 * (columns * jnp.sum(jnp.log(row_scale)) + length * jnp.sum(jnp.log(col_scale)))
    fixed = fixed - length * columns * math.log(2.0 * math.pi)

    first_a = combine(sign.reshape(1), [(from_partner(part, "gx", 1), part) for part in field_a])
    tables = (y_table, twist, x_table(0), x_table(1), row_pair, col_trio, coefs_a, coefs_b, fixed)
    first_a, first_b, tables = lax.optimization_barrier((first_a, to_planes(field_b)[0], tables))
    y_table, twist, even_table, odd_table, row_pair, col_trio, coefs_a, coefs_b, fixed = tables
    second_a = to_planes(first_a)[0]
    second_b = from_partner(first_b, "gx", 1)
    group = [second_b, from_partner(second_b, "gx", 0), first_b, from_partner(first_b, "gx", 0)]
    even_b, odd_b = y_dft(group, True, coefs_b, y_table, twist)
    even_a, odd_a = y_dft([second_a, from_partner(second_a, "gx", 0)], False, coefs_a, y_table, twist)
    latent, tile = x_dft([even_b, even_a], [odd_b, odd_a], even_table, odd_table, row_pair, col_trio)
    tile = tile + fixed / tile.size
    modes = length * columns * lax.axis_size("gx") * lax.axis_size("gy")
    return (latent, sum_everywhere(tile) / modes)


def complex_einsum(form, real_part, imag_part, cos_part, sin_part):
    first = jnp.einsum(form, real_part, cos_part, precision=precision_top)
    second = jnp.einsum(form, real_part, sin_part, precision=precision_top)
    first = first - jnp.einsum(form, imag_part, sin_part, precision=precision_top)
    second = second + jnp.einsum(form, imag_part, cos_part, precision=precision_top)
    return (first, second)


def x_butterfly(field):
    devices = lax.axis_size("gx")
    levels = devices.bit_length() - 1
    position = lax.axis_index("gx")
    real_part, imag_part = field, jnp.zeros_like(field)
    for level in range(levels - 1, -1, -1):
        half = 1 << level
        lower = position // half % 2 == 0
        offset = position % half
        angle = offset.astype(jnp.float32) * (-math.pi / half)
        cos_twist = jnp.where(lower, 1.0, jnp.cos(angle))
        sin_twist = jnp.where(lower, 0.0, jnp.sin(angle))
        other = from_partner(jnp.stack([real_part, imag_part]), "gx", level)
        diff_real = jnp.where(lower, real_part + other[0], other[0] - real_part)
        diff_imag = jnp.where(lower, imag_part + other[1], other[1] - imag_part)
        real_part = diff_real * cos_twist - diff_imag * sin_twist
        imag_part = diff_real * sin_twist + diff_imag * cos_twist
    width = field.shape[2]
    cos_part, sin_part = x_tables(jnp.arange(width, dtype=jnp.int32), width, devices, position)
    real_part, imag_part = complex_einsum("zyn,nk->zyk", real_part, imag_part, cos_part, sin_part)
    return (to_planes(real_part), to_planes(imag_part))


def y_transform(real_part, imag_part):
    planes, length, width = real_part.shape
    outer = 1 << (length.bit_length() - 1) // 2
    inner = length // outer
    outer_index = jnp.arange(outer, dtype=jnp.int32)
    inner_index = jnp.arange(inner, dtype=jnp.int32)
    cos_one, sin_one = root_table(outer_index, outer_index, outer)
    cos_two, sin_two = root_table(inner_index, inner_index, inner)
    cos_mid, sin_mid = root_table(outer_index, inner_index, length)
    shaped_real = real_part.reshape(planes, outer, inner, width)
    shaped_imag = imag_part.reshape(planes, outer, inner, width)
    step_real, step_imag = complex_einsum("zabc,ak->zkbc", shaped_real, shaped_imag, cos_one, sin_one)
    twist_cos = cos_mid[None, :, :, None]
    twist_sin = sin_mid[None, :, :, None]
    turned_real = step_real * twist_cos - step_imag * twist_sin
    turned_imag = step_real * twist_sin + step_imag * twist_cos
    final_real, final_imag = complex_einsum("zkbc,bj->zjkc", turned_real, turned_imag, cos_two, sin_two)
    return (final_real.reshape(planes, length, width), final_imag.reshape(planes, length, width))


def any_way(field, row_scale, col_scale, row_rate, col_shift, col_mix):
    spec_real, spec_imag = y_transform(*x_butterfly(field))
    length = spec_real.shape[1]
    total_cols = spec_real.shape[2] * lax.axis_size("gx")
    norm_factor = 1.0 / math.sqrt(length * total_cols)
    scale = row_scale[None, :, None] * col_scale[None, None, :]
    latent_u = spec_real * norm_factor * scale
    latent_v = spec_imag * norm_factor * scale
    log_scale = row_rate[None, :, None] * jnp.tanh(latent_u + col_shift[None, None, :])
    latent_w = latent_v * jnp.exp(log_scale) + col_mix[None, None, :] * latent_u
    terms = (
        -0.5 * (latent_u * latent_u + latent_w * latent_w)
        - math.log(2.0 * math.pi)
        + log_scale
        + 2.0 * jnp.log(scale)
    )
    mode_count = spec_real.size * lax.axis_size("gx") * lax.axis_size("gy")
    loglik = lax.psum(jnp.sum(terms), ("gx", "gy")) / mode_count
    return (jnp.stack([latent_u, latent_w]), loglik)


def per_device(field, *scales):
    return (four_way if lax.axis_size("gx") == 4 else any_way)(field, *scales)


def solution(mesh):
    return jax.shard_map(
        per_device,
        mesh=mesh,
        in_specs=(P(None, "gy", "gx"), P(), P("gx"), P(), P("gx"), P("gx")),
        out_specs=(P(None, "gy", None, "gx"), P()),
        check_vma=False,
    )
```

```python
import functools
import math

import jax
import jax.numpy as jnp
from jax import lax
from jax.experimental import pallas as pl
from jax.experimental.pallas import tpu as pltpu
from jax.sharding import PartitionSpec as P

precision_top = lax.Precision.HIGHEST
RADIX = 8
LANES = 128
SMALL_BYTES, Y_BYTES, X_BYTES = [size * 1024 * 1024 for size in (8, 27, 26)]


def from_partner(value, axis, stride):
    mask = 2**stride
    pairs = [(source, source ^ mask) for source in range(lax.axis_size(axis))]
    return lax.ppermute(value, axis, pairs)


def to_planes(values):
    return lax.all_to_all(values, "gy", split_axis=0, concat_axis=1, tiled=True)


def pick_columns(left, right, odd):
    lane = lax.broadcasted_iota(jnp.int32, left.shape, 1)
    index = (2 * lane + odd) & (LANES - 1)
    chosen = [jnp.take_along_axis(tile, index, axis=1, mode="promise_in_bounds") for tile in (left, right)]
    return jnp.where(lane < LANES // 2, *chosen)


def combine_kernel(sign_ref, late_ref, early_ref, *refs):
    out_ref = refs[-1]
    sign = sign_ref[0]
    for plane in range(late_ref.shape[0]):
        left, right = [
            late_ref[plane, :, pl.ds(lane, LANES)] + sign * early_ref[plane, :, pl.ds(lane, LANES)] for lane in (0, LANES)
        ]
        for odd in range(2):
            out_ref[plane, :, pl.ds(odd * LANES, LANES)] = pick_columns(left, right, odd)


def combine(sign, parts):
    planes, rows, columns = parts[0][0].shape
    result = ()
    for place, pair in enumerate(parts):
        block = pl.BlockSpec((planes // 2, rows, columns), lambda i: (i, 0, 0))
        result = pl.pallas_call(
            combine_kernel,
            out_shape=[jax.ShapeDtypeStruct((planes * len(parts), rows, columns), jnp.float32)],
            grid=(2,),
            in_specs=[pl.BlockSpec(memory_space=pltpu.SMEM), block, block]
            + [pl.BlockSpec(memory_space=pl.ANY)] * len(result),
            out_specs=[pl.BlockSpec((planes // 2, rows, columns), lambda i, place=place: (2 * place + i, 0, 0))],
            input_output_aliases={3: 0} if result else {},
            cost_estimate=pl.CostEstimate(
                flops=2 * pair[0].size, bytes_accessed=12 * pair[0].size, transcendentals=0
            ),
            compiler_params=pltpu.CompilerParams(vmem_limit_bytes=SMALL_BYTES),
            name="combine",
        )(sign, *pair, *result)
    return result[0]


def reverse_bits(value, count):
    result = value * 0
    for place in range(count):
        result = result + (value >> place & 1) * (1 << count - 1 - place)
    return result


def root_table(row_index, freqs, length):
    phase = row_index[:, None] * freqs[None, :] % length
    angle = phase.astype(jnp.float32) * (-2.0 * math.pi / length)
    return (jnp.cos(angle), jnp.sin(angle))


def x_tables(rows, width, devices, position):
    levels = devices.bit_length() - 1
    local_index = jnp.arange(width, dtype=jnp.int32)
    freqs = reverse_bits(position, levels) + devices * local_index
    return root_table(rows, freqs, devices * width)


def split_table(table):
    high = lax.reduce_precision(table, 8, 7)
    return jnp.stack([high.astype(jnp.bfloat16), (table - high).astype(jnp.bfloat16)])


def split_value(value):
    high = value.astype(jnp.bfloat16)
    return high, (value - high.astype(jnp.float32)).astype(jnp.bfloat16)


def small_fft(values):
    count = len(values)
    if count == 1:
        return values
    even, odd = small_fft(values[0::2]), small_fft(values[1::2])
    first, second = [], []
    root_half = math.sqrt(0.5)
    for place in range(count // 2):
        (er, ei), (re, im) = even[place], odd[place]
        turn = place * 8 // count
        if turn == 1:
            re, im = (re + im) * root_half, (im - re) * root_half
        elif turn == 2:
            re, im = im, -re
        elif turn == 3:
            re, im = (im - re) * root_half, (re + im) * -root_half
        first.append((er + re, ei + im))
        second.append((er - re, ei - im))
    return first + second


def dot(left, right):
    return jnp.dot(left, right, preferred_element_type=jnp.float32)


def y_kernel(count, pick, coef_ref, *refs):
    inputs, (table_ref, twist_ref, *out_refs, mix_ref, split_ref, step_ref) = refs[:count], refs[count:]
    length = mix_ref.shape[1]
    inner = length // RADIX
    rows_each = 128
    for start in range(0, length, rows_each):
        rows = pl.ds(start, rows_each)
        for which in range(2):
            tiles = []
            for lane in (0, LANES):
                mixed = inputs[0][rows, pl.ds(lane, LANES)] * coef_ref[which, 0]
                for place in range(1, count):
                    mixed = mixed + inputs[place][rows, pl.ds(lane, LANES)] * coef_ref[which, place]
                tiles.append(mixed)
            for tile in range(2):
                mix_ref[2 * tile + which, rows, :] = pick_columns(*tiles, tile) if pick else tiles[tile]
    half = inner // 2

    def split(tile):
        for which in range(2):
            for s in range(RADIX):
                parts = split_value(mix_ref[2 * tile + which, pl.ds(s, inner, stride=RADIX), :])
                for place, value in enumerate(parts):
                    split_ref[tile, place, pl.ds(which * inner, inner), pl.ds(s * LANES, LANES)] = value

    def multiply(tile, part):
        table = [table_ref[place, pl.ds(part * inner, inner), :] for place in (0, 1, 0)]
        values = [split_ref[tile, place] for place in (0, 0, 1)]
        step_ref[part] = dot(jnp.concatenate(table, axis=1), jnp.concatenate(values, axis=0))

    def finish(tile, part):
        for start in range(0, half, 16):
            values = []
            for s in range(RADIX):
                cols = pl.ds(s * LANES, LANES)
                re = step_ref[part, pl.ds(start, 16), cols]
                im = step_ref[part, pl.ds(half + start, 16), cols]
                if s:
                    cos, sin = [twist_ref[k, s, pl.ds(part * half + start, 16), :] for k in range(2)]
                    re, im = re * cos - im * sin, re * sin + im * cos
                values.append((re, im))
            for kb, pair in enumerate(small_fft(values)):
                rows = pl.ds(kb * inner + part * half + start, 16)
                for which in range(2):
                    high, low = split_value(pair[which])
                    out_refs[tile][2 * which, rows, :] = high
                    out_refs[tile][2 * which + 1, rows, :] = low

    jobs = [(tile, part) for tile in range(len(out_refs)) for part in range(2)]
    split(0)
    multiply(*jobs[0])
    for before, job in zip(jobs, jobs[1:]):
        if job[1]:
            if job[0] + 1 < len(out_refs):
                split(job[0] + 1)
        multiply(*job)
        finish(*before)
    finish(*jobs[-1])


def y_dft(inputs, pick, coefs, table, twist):
    length = inputs[0].shape[0]
    inner = length // RADIX
    whole = pl.BlockSpec(memory_space=pltpu.VMEM)
    return pl.pallas_call(
        functools.partial(y_kernel, len(inputs), pick),
        out_shape=[jax.ShapeDtypeStruct((4, length, LANES), jnp.bfloat16)] * 2,
        in_specs=[pl.BlockSpec(memory_space=pltpu.SMEM)] + [whole] * (len(inputs) + 2),
        out_specs=[whole] * 2,
        scratch_shapes=[
            pltpu.VMEM((4, length, LANES), jnp.float32),
            pltpu.VMEM((2, 2, 2 * inner, RADIX * LANES), jnp.bfloat16),
            pltpu.VMEM((2, inner, RADIX * LANES), jnp.float32),
        ],
        compiler_params=pltpu.CompilerParams(vmem_limit_bytes=Y_BYTES),
        cost_estimate=pl.CostEstimate(
            flops=160 * inner * length * LANES, bytes_accessed=8 * length * LANES * (len(inputs) + 3), transcendentals=0
        ),
        name="y_dft",
    )(coefs, *inputs, table, twist)


def x_kernel(count, *refs):
    parts, (even_ref, odd_ref, row_ref, col_ref, out_ref, total_ref) = refs[: 2 * count], refs[2 * count :]
    columns = out_ref.shape[3]
    lanes, rows_each, tiles = LANES, 2 * LANES, columns // (2 * LANES)
    totals = []

    def left(refs, rows):
        first = pl.multiple_of(pl.program_id(0) * out_ref.shape[2], out_ref.shape[2])
        rows = pl.ds(first + rows, rows_each)
        high, low = [[ref[k + which, rows, :] for ref in refs for k in (0, 2)] for which in range(2)]
        return jnp.concatenate(high + low + high, axis=1)

    def multiply(sides, tile):
        cols = pl.ds(tile * 2 * lanes, 2 * lanes)
        return [
            dot(side, jnp.concatenate([table_ref[place, :, cols] for place in (0, 0, 1)], axis=0))
            for side, table_ref in zip(sides, (even_ref, odd_ref))
        ]

    def finish(start, tile, even, odd):
        rows = pl.ds(start, rows_each)
        row_scale, row_rate = [
            jnp.concatenate(
                [
                    jnp.broadcast_to(row_ref[which, 0, c : c + 1, :], (lanes, lanes)).T
                    for c in range(start // lanes, (start + rows_each) // lanes)
                ],
                0,
            )
            for which in range(2)
        ]
        for upper in range(2):
            cols = pl.ds(upper * columns // 2 + tile * lanes, lanes)
            spec = even - odd if upper else even + odd
            col_scale, col_shift, col_mix = col_ref[0:1, cols], col_ref[1:2, cols], col_ref[2:3, cols]
            scale = row_scale * col_scale
            latent_u = spec[:, :lanes] * scale
            latent_v = spec[:, lanes:] * scale
            log_scale = row_rate * jnp.tanh(latent_u + col_shift)
            latent_w = latent_v * jnp.exp(log_scale) + col_mix * latent_u
            out_ref[0, 0, rows, cols] = latent_u
            out_ref[1, 0, rows, cols] = latent_w
            terms = log_scale - 0.5 * (latent_u * latent_u + latent_w * latent_w)
            totals.append(jnp.sum(terms.reshape(-1, 8, lanes), axis=0))

    before = None
    for start in range(0, out_ref.shape[2], rows_each):
        sides = [left(group, start) for group in (parts[:count], parts[count:])]
        for tile in range(tiles):
            products = multiply(sides, tile)
            if before is not None:
                finish(*before)
            before = (start, tile, *products)
    finish(*before)

    @pl.when(pl.program_id(0) == 0)
    def _():
        total_ref[...] = jnp.zeros_like(total_ref)

    total_ref[...] += sum(totals)


def x_dft(even_parts, odd_parts, even_table, odd_table, row_pair, col_trio):
    parts, count, length = even_parts + odd_parts, len(even_parts), even_parts[0].shape[1]
    columns = even_table.shape[2]
    rows = length // row_pair.shape[1]
    whole = [pl.BlockSpec(memory_space=pltpu.VMEM)] * (len(parts) + 2)
    return pl.pallas_call(
        functools.partial(x_kernel, count),
        out_shape=(
            jax.ShapeDtypeStruct((2, 1, length, columns), jnp.float32),
            jax.ShapeDtypeStruct((8, LANES), jnp.float32),
        ),
        grid=(length // rows,),
        in_specs=whole
        + [
            pl.BlockSpec((2, 1, rows // LANES, LANES), lambda i: (0, i, 0, 0)),
            pl.BlockSpec(col_trio.shape, lambda i: (0, 0)),
        ],
        out_specs=(
            pl.BlockSpec((2, 1, rows, columns), lambda i: (0, 0, i, 0)),
            pl.BlockSpec((8, LANES), lambda i: (0, 0)),
        ),
        compiler_params=pltpu.CompilerParams(vmem_limit_bytes=X_BYTES),
        cost_estimate=pl.CostEstimate(
            flops=6 * length * even_table.size,
            bytes_accessed=16 * length * columns,
            transcendentals=2 * length * columns,
        ),
        name="x_dft",
    )(*parts, even_table, odd_table, row_pair, col_trio)


def sum_everywhere(tile):
    axes = ("gx", "gy")
    devices = lax.axis_size("gx") * lax.axis_size("gy")
    copies = jnp.broadcast_to(tile[None], (devices,) + tile.shape)
    return jnp.sum(lax.all_to_all(copies, axes, split_axis=0, concat_axis=0, tiled=True))


def four_way(field, row_scale, col_scale, row_rate, col_shift, col_mix):
    position = lax.axis_index("gx")
    planes, rows, columns = field.shape
    length, width = planes * rows, columns // 4
    groups = [slice(0, planes // 2), slice(planes // 2, None)]
    field_b, field_rest = lax.optimization_barrier((field[:, :, 2 * width :], field))
    field_a = [field_rest[group, :, : 2 * width] for group in groups]
    sign = jnp.where(position < 2, 1.0, -1.0)

    own_real = jnp.where(position == 1, -1.0, jnp.where(position == 3, 0.0, 1.0))
    other_real = jnp.where(position == 2, 0.0, 1.0)
    own_imag = jnp.where(position == 3, 1.0, 0.0)
    other_imag = jnp.where(position == 2, -1.0, 0.0)
    coefs_a = jnp.stack([own_real, other_real, own_imag, other_imag]).reshape(2, 2)
    coefs_b = jnp.concatenate([coefs_a, coefs_a * sign], axis=1)

    inner = length // RADIX
    index = jnp.arange(inner, dtype=jnp.int32)
    cos, sin = root_table(index, index, inner)
    y_table = [jnp.concatenate(pair, 1).reshape(2, 1, inner // 2, 2 * inner) for pair in ((cos, -sin), (sin, cos))]
    y_table = jnp.concatenate(y_table, 1).reshape(2 * inner, 2 * inner)
    y_table = split_table(y_table)
    grid = [lax.broadcasted_iota(jnp.int32, (RADIX, inner, LANES), axis) for axis in range(2)]
    angle = (grid[0] * grid[1]).astype(jnp.float32) * (-2.0 * math.pi / length)
    twist = jnp.stack([jnp.cos(angle), jnp.sin(angle)])
    order = jnp.arange(width, dtype=jnp.int32) * 2

    def x_table(odd):
        rows = jnp.concatenate([order + (2 * width + odd), order + odd])
        cos, sin = [part[:, : 2 * width] for part in x_tables(rows, columns, 4, position)]

        def lay(left, right):
            spans = [slice(tile * width, (tile + 1) * width) for tile in range(2)]
            return jnp.concatenate([side[:, span] for span in spans for side in (left, right)], 1)

        real, imag = lay(cos, sin), lay(-sin, cos)
        table = jnp.concatenate([real[:width], imag[:width], real[width:], imag[width:]], 0)
        return split_table(table)

    norm = 1.0 / math.sqrt(length * columns * 4)
    row_pair = jnp.stack([row_scale * norm, row_rate]).reshape(2, 4, length // 4 // LANES, LANES)
    col_trio = jnp.stack([col_scale, col_shift, col_mix])
    fixed = 2.0 * (columns * jnp.sum(jnp.log(row_scale)) + length * jnp.sum(jnp.log(col_scale)))
    fixed = fixed - length * columns * math.log(2.0 * math.pi)

    first_a = combine(sign.reshape(1), [(from_partner(part, "gx", 1), part) for part in field_a])
    tables = (y_table, twist, x_table(0), x_table(1), row_pair, col_trio, coefs_a, coefs_b, fixed)
    first_b, tables = lax.optimization_barrier((to_planes(field_b)[0], tables))
    y_table, twist, even_table, odd_table, row_pair, col_trio, coefs_a, coefs_b, fixed = tables
    second_a = to_planes(first_a)[0]
    second_b = from_partner(first_b, "gx", 1)
    group = [second_b, from_partner(second_b, "gx", 0), first_b, from_partner(first_b, "gx", 0)]
    even_b, odd_b = y_dft(group, True, coefs_b, y_table, twist)
    even_a, odd_a = y_dft([second_a, from_partner(second_a, "gx", 0)], False, coefs_a, y_table, twist)
    latent, tile = x_dft([even_b, even_a], [odd_b, odd_a], even_table, odd_table, row_pair, col_trio)
    tile = tile + fixed / tile.size
    modes = length * columns * lax.axis_size("gx") * lax.axis_size("gy")
    return (latent, sum_everywhere(tile) / modes)


def complex_einsum(form, real_part, imag_part, cos_part, sin_part):
    first = jnp.einsum(form, real_part, cos_part, precision=precision_top)
    second = jnp.einsum(form, real_part, sin_part, precision=precision_top)
    first = first - jnp.einsum(form, imag_part, sin_part, precision=precision_top)
    second = second + jnp.einsum(form, imag_part, cos_part, precision=precision_top)
    return (first, second)


def x_butterfly(field):
    devices = lax.axis_size("gx")
    levels = devices.bit_length() - 1
    position = lax.axis_index("gx")
    real_part, imag_part = field, jnp.zeros_like(field)
    for level in range(levels - 1, -1, -1):
        half = 1 << level
        lower = position // half % 2 == 0
        offset = position % half
        angle = offset.astype(jnp.float32) * (-math.pi / half)
        cos_twist = jnp.where(lower, 1.0, jnp.cos(angle))
        sin_twist = jnp.where(lower, 0.0, jnp.sin(angle))
        other = from_partner(jnp.stack([real_part, imag_part]), "gx", level)
        diff_real = jnp.where(lower, real_part + other[0], other[0] - real_part)
        diff_imag = jnp.where(lower, imag_part + other[1], other[1] - imag_part)
        real_part = diff_real * cos_twist - diff_imag * sin_twist
        imag_part = diff_real * sin_twist + diff_imag * cos_twist
    width = field.shape[2]
    cos_part, sin_part = x_tables(jnp.arange(width, dtype=jnp.int32), width, devices, position)
    real_part, imag_part = complex_einsum("zyn,nk->zyk", real_part, imag_part, cos_part, sin_part)
    return (to_planes(real_part), to_planes(imag_part))


def y_transform(real_part, imag_part):
    planes, length, width = real_part.shape
    outer = 1 << (length.bit_length() - 1) // 2
    inner = length // outer
    outer_index = jnp.arange(outer, dtype=jnp.int32)
    inner_index = jnp.arange(inner, dtype=jnp.int32)
    cos_one, sin_one = root_table(outer_index, outer_index, outer)
    cos_two, sin_two = root_table(inner_index, inner_index, inner)
    cos_mid, sin_mid = root_table(outer_index, inner_index, length)
    shaped_real = real_part.reshape(planes, outer, inner, width)
    shaped_imag = imag_part.reshape(planes, outer, inner, width)
    step_real, step_imag = complex_einsum("zabc,ak->zkbc", shaped_real, shaped_imag, cos_one, sin_one)
    twist_cos = cos_mid[None, :, :, None]
    twist_sin = sin_mid[None, :, :, None]
    turned_real = step_real * twist_cos - step_imag * twist_sin
    turned_imag = step_real * twist_sin + step_imag * twist_cos
    final_real, final_imag = complex_einsum("zkbc,bj->zjkc", turned_real, turned_imag, cos_two, sin_two)
    return (final_real.reshape(planes, length, width), final_imag.reshape(planes, length, width))


def any_way(field, row_scale, col_scale, row_rate, col_shift, col_mix):
    spec_real, spec_imag = y_transform(*x_butterfly(field))
    length = spec_real.shape[1]
    total_cols = spec_real.shape[2] * lax.axis_size("gx")
    norm_factor = 1.0 / math.sqrt(length * total_cols)
    scale = row_scale[None, :, None] * col_scale[None, None, :]
    latent_u = spec_real * norm_factor * scale
    latent_v = spec_imag * norm_factor * scale
    log_scale = row_rate[None, :, None] * jnp.tanh(latent_u + col_shift[None, None, :])
    latent_w = latent_v * jnp.exp(log_scale) + col_mix[None, None, :] * latent_u
    terms = (
        -0.5 * (latent_u * latent_u + latent_w * latent_w)
        - math.log(2.0 * math.pi)
        + log_scale
        + 2.0 * jnp.log(scale)
    )
    mode_count = spec_real.size * lax.axis_size("gx") * lax.axis_size("gy")
    loglik = lax.psum(jnp.sum(terms), ("gx", "gy")) / mode_count
    return (jnp.stack([latent_u, latent_w]), loglik)


def per_device(field, *scales):
    return (four_way if lax.axis_size("gx") == 4 else any_way)(field, *scales)


def solution(mesh):
    return jax.shard_map(
        per_device,
        mesh=mesh,
        in_specs=(P(None, "gy", "gx"), P(), P("gx"), P(), P("gx"), P("gx")),
        out_specs=(P(None, "gy", None, "gx"), P()),
        check_vma=False,
    )
```

```python
import functools
import math

import jax
import jax.numpy as jnp
from jax import lax
from jax.experimental import pallas as pl
from jax.experimental.pallas import tpu as pltpu
from jax.sharding import PartitionSpec as P

precision_top = lax.Precision.HIGHEST
RADIX = 8
LANES = 128
SMALL_BYTES, Y_BYTES, X_BYTES = [size * 1024 * 1024 for size in (8, 27, 26)]


def from_partner(value, axis, stride):
    mask = 2**stride
    pairs = [(source, source ^ mask) for source in range(lax.axis_size(axis))]
    return lax.ppermute(value, axis, pairs)


def to_planes(values):
    return lax.all_to_all(values, "gy", split_axis=0, concat_axis=1, tiled=True)


def pick_columns(left, right, odd):
    lane = lax.broadcasted_iota(jnp.int32, left.shape, 1)
    index = (2 * lane + odd) & (LANES - 1)
    chosen = [jnp.take_along_axis(tile, index, axis=1, mode="promise_in_bounds") for tile in (left, right)]
    return jnp.where(lane < LANES // 2, *chosen)


def combine_kernel(sign_ref, late_ref, early_ref, *refs):
    out_ref = refs[-1]
    sign = sign_ref[0]
    for plane in range(late_ref.shape[0]):
        left, right = [
            late_ref[plane, :, pl.ds(lane, LANES)] + sign * early_ref[plane, :, pl.ds(lane, LANES)] for lane in (0, LANES)
        ]
        for odd in range(2):
            out_ref[plane, :, pl.ds(odd * LANES, LANES)] = pick_columns(left, right, odd)


def combine(sign, parts):
    planes, rows, columns = parts[0][0].shape
    result = ()
    for place, pair in enumerate(parts):
        block = pl.BlockSpec((planes // 2, rows, columns), lambda i: (i, 0, 0))
        result = pl.pallas_call(
            combine_kernel,
            out_shape=[jax.ShapeDtypeStruct((planes * len(parts), rows, columns), jnp.float32)],
            grid=(2,),
            in_specs=[pl.BlockSpec(memory_space=pltpu.SMEM), block, block]
            + [pl.BlockSpec(memory_space=pl.ANY)] * len(result),
            out_specs=[pl.BlockSpec((planes // 2, rows, columns), lambda i, place=place: (2 * place + i, 0, 0))],
            input_output_aliases={3: 0} if result else {},
            cost_estimate=pl.CostEstimate(
                flops=2 * pair[0].size, bytes_accessed=12 * pair[0].size, transcendentals=0
            ),
            compiler_params=pltpu.CompilerParams(vmem_limit_bytes=SMALL_BYTES),
            name="combine",
        )(sign, *pair, *result)
    return result[0]


def reverse_bits(value, count):
    result = value * 0
    for place in range(count):
        result = result + (value >> place & 1) * (1 << count - 1 - place)
    return result


def root_table(row_index, freqs, length):
    phase = row_index[:, None] * freqs[None, :] % length
    angle = phase.astype(jnp.float32) * (-2.0 * math.pi / length)
    return (jnp.cos(angle), jnp.sin(angle))


def x_tables(rows, width, devices, position):
    levels = devices.bit_length() - 1
    local_index = jnp.arange(width, dtype=jnp.int32)
    freqs = reverse_bits(position, levels) + devices * local_index
    return root_table(rows, freqs, devices * width)


def split_table(table):
    high = lax.reduce_precision(table, 8, 7)
    return jnp.stack([high.astype(jnp.bfloat16), (table - high).astype(jnp.bfloat16)])


def split_value(value):
    high = value.astype(jnp.bfloat16)
    return high, (value - high.astype(jnp.float32)).astype(jnp.bfloat16)


def small_fft(values):
    count = len(values)
    if count == 1:
        return values
    even, odd = small_fft(values[0::2]), small_fft(values[1::2])
    first, second = [], []
    root_half = math.sqrt(0.5)
    for place in range(count // 2):
        (er, ei), (re, im) = even[place], odd[place]
        turn = place * 8 // count
        if turn == 1:
            re, im = (re + im) * root_half, (im - re) * root_half
        elif turn == 2:
            re, im = im, -re
        elif turn == 3:
            re, im = (im - re) * root_half, (re + im) * -root_half
        first.append((er + re, ei + im))
        second.append((er - re, ei - im))
    return first + second


def dot(left, right):
    return jnp.dot(left, right, preferred_element_type=jnp.float32)


def y_kernel(count, pick, coef_ref, *refs):
    inputs, (table_ref, twist_ref, *out_refs, mix_ref, split_ref, step_ref) = refs[:count], refs[count:]
    length = mix_ref.shape[1]
    inner = length // RADIX
    rows_each = 32
    for start in range(0, length, rows_each):
        rows = pl.ds(start, rows_each)
        for which in range(2):
            tiles = []
            for lane in (0, LANES):
                mixed = inputs[0][rows, pl.ds(lane, LANES)] * coef_ref[which, 0]
                for place in range(1, count):
                    mixed = mixed + inputs[place][rows, pl.ds(lane, LANES)] * coef_ref[which, place]
                tiles.append(mixed)
            for tile in range(2):
                mix_ref[2 * tile + which, rows, :] = pick_columns(*tiles, tile) if pick else tiles[tile]
    half = inner // 2

    def split(tile):
        for which in range(2):
            for s in range(RADIX):
                for start in range(0, inner, 64):
                    parts = split_value(mix_ref[2 * tile + which, pl.ds(s + start * RADIX, 64, stride=RADIX), :])
                    for place, value in enumerate(parts):
                        split_ref[tile, place, pl.ds(which * inner + start, 64), pl.ds(s * LANES, LANES)] = value

    def multiply(tile, part):
        table = [table_ref[place, pl.ds(part * inner, inner), :] for place in (0, 1, 0)]
        values = [split_ref[tile, place] for place in (0, 0, 1)]
        step_ref[part] = dot(jnp.concatenate(table, axis=1), jnp.concatenate(values, axis=0))

    def finish(tile, part):
        for start in range(0, half, 16):
            values = []
            for s in range(RADIX):
                cols = pl.ds(s * LANES, LANES)
                re = step_ref[part, pl.ds(start, 16), cols]
                im = step_ref[part, pl.ds(half + start, 16), cols]
                if s:
                    cos, sin = [twist_ref[k, s, pl.ds(part * half + start, 16), :] for k in range(2)]
                    re, im = re * cos - im * sin, re * sin + im * cos
                values.append((re, im))
            for kb, pair in enumerate(small_fft(values)):
                rows = pl.ds(kb * inner + part * half + start, 16)
                for which in range(2):
                    high, low = split_value(pair[which])
                    out_refs[tile][2 * which, rows, :] = high
                    out_refs[tile][2 * which + 1, rows, :] = low

    jobs = [(tile, part) for tile in range(len(out_refs)) for part in range(2)]
    split(0)
    multiply(*jobs[0])
    for before, job in zip(jobs, jobs[1:]):
        if job[1]:
            if job[0] + 1 < len(out_refs):
                split(job[0] + 1)
        multiply(*job)
        finish(*before)
    finish(*jobs[-1])


def y_dft(inputs, pick, coefs, table, twist):
    length = inputs[0].shape[0]
    inner = length // RADIX
    whole = pl.BlockSpec(memory_space=pltpu.VMEM)
    return pl.pallas_call(
        functools.partial(y_kernel, len(inputs), pick),
        out_shape=[jax.ShapeDtypeStruct((4, length, LANES), jnp.bfloat16)] * 2,
        in_specs=[pl.BlockSpec(memory_space=pltpu.SMEM)] + [whole] * (len(inputs) + 2),
        out_specs=[whole] * 2,
        scratch_shapes=[
            pltpu.VMEM((4, length, LANES), jnp.float32),
            pltpu.VMEM((2, 2, 2 * inner, RADIX * LANES), jnp.bfloat16),
            pltpu.VMEM((2, inner, RADIX * LANES), jnp.float32),
        ],
        compiler_params=pltpu.CompilerParams(vmem_limit_bytes=Y_BYTES),
        cost_estimate=pl.CostEstimate(
            flops=160 * inner * length * LANES, bytes_accessed=8 * length * LANES * (len(inputs) + 3), transcendentals=0
        ),
        name="y_dft",
    )(coefs, *inputs, table, twist)


def x_kernel(count, *refs):
    parts, (even_ref, odd_ref, row_ref, col_ref, out_ref, total_ref) = refs[: 2 * count], refs[2 * count :]
    columns = out_ref.shape[3]
    lanes, rows_each, tiles = LANES, 2 * LANES, columns // (2 * LANES)
    totals = []

    def left(refs, rows):
        first = pl.multiple_of(pl.program_id(0) * out_ref.shape[2], out_ref.shape[2])
        rows = pl.ds(first + rows, rows_each)
        high, low = [[ref[k + which, rows, :] for ref in refs for k in (0, 2)] for which in range(2)]
        return jnp.concatenate(high + low + high, axis=1)

    def multiply(sides, tile):
        cols = pl.ds(tile * 2 * lanes, 2 * lanes)
        return [
            dot(side, jnp.concatenate([table_ref[place, :, cols] for place in (0, 0, 1)], axis=0))
            for side, table_ref in zip(sides, (even_ref, odd_ref))
        ]

    def row_factors(start):
        return [
            jnp.concatenate(
                [
                    jnp.broadcast_to(row_ref[which, 0, c : c + 1, :], (lanes, lanes)).T
                    for c in range(start // lanes, (start + rows_each) // lanes)
                ],
                0,
            )
            for which in range(2)
        ]

    def finish(start, tile, factors, even, odd):
        for upper in range(2):
            cols = pl.ds(upper * columns // 2 + tile * lanes, lanes)
            col_scale, col_shift, col_mix = col_ref[0:1, cols], col_ref[1:2, cols], col_ref[2:3, cols]
            total = None
            for first in range(0, rows_each, 32):
                rows, span = pl.ds(start + first, 32), slice(first, first + 32)
                spec = even[span] - odd[span] if upper else even[span] + odd[span]
                scale = factors[0][span] * col_scale
                latent_u = spec[:, :lanes] * scale
                latent_v = spec[:, lanes:] * scale
                log_scale = factors[1][span] * jnp.tanh(latent_u + col_shift)
                latent_w = latent_v * jnp.exp(log_scale) + col_mix * latent_u
                out_ref[0, 0, rows, cols] = latent_u
                out_ref[1, 0, rows, cols] = latent_w
                terms = log_scale - 0.5 * (latent_u * latent_u + latent_w * latent_w)
                terms = jnp.sum(terms.reshape(-1, 8, lanes), axis=0)
                total = terms if total is None else total + terms
            totals.append(total)

    before = None
    for start in range(0, out_ref.shape[2], rows_each):
        sides = [left(group, start) for group in (parts[:count], parts[count:])]
        factors = row_factors(start)
        for tile in range(tiles):
            products = multiply(sides, tile)
            if before is not None:
                finish(*before)
            before = (start, tile, factors, *products)
    finish(*before)

    @pl.when(pl.program_id(0) == 0)
    def _():
        total_ref[...] = jnp.zeros_like(total_ref)

    total_ref[...] += sum(totals)


def x_dft(even_parts, odd_parts, even_table, odd_table, row_pair, col_trio):
    parts, count, length = even_parts + odd_parts, len(even_parts), even_parts[0].shape[1]
    columns = even_table.shape[2]
    rows = length // row_pair.shape[1]
    whole = [pl.BlockSpec(memory_space=pltpu.VMEM)] * (len(parts) + 2)
    return pl.pallas_call(
        functools.partial(x_kernel, count),
        out_shape=(
            jax.ShapeDtypeStruct((2, 1, length, columns), jnp.float32),
            jax.ShapeDtypeStruct((8, LANES), jnp.float32),
        ),
        grid=(length // rows,),
        in_specs=whole
        + [
            pl.BlockSpec((2, 1, rows // LANES, LANES), lambda i: (0, i, 0, 0)),
            pl.BlockSpec(col_trio.shape, lambda i: (0, 0)),
        ],
        out_specs=(
            pl.BlockSpec((2, 1, rows, columns), lambda i: (0, 0, i, 0)),
            pl.BlockSpec((8, LANES), lambda i: (0, 0)),
        ),
        compiler_params=pltpu.CompilerParams(vmem_limit_bytes=X_BYTES),
        cost_estimate=pl.CostEstimate(
            flops=6 * length * even_table.size,
            bytes_accessed=16 * length * columns,
            transcendentals=2 * length * columns,
        ),
        name="x_dft",
    )(*parts, even_table, odd_table, row_pair, col_trio)


def sum_everywhere(tile):
    axes = ("gx", "gy")
    devices = lax.axis_size("gx") * lax.axis_size("gy")
    copies = jnp.broadcast_to(tile[None], (devices,) + tile.shape)
    return jnp.sum(lax.all_to_all(copies, axes, split_axis=0, concat_axis=0, tiled=True))


def four_way(field, row_scale, col_scale, row_rate, col_shift, col_mix):
    position = lax.axis_index("gx")
    planes, rows, columns = field.shape
    length, width = planes * rows, columns // 4
    groups = [slice(0, planes // 2), slice(planes // 2, None)]
    field_b, field_rest = lax.optimization_barrier((field[:, :, 2 * width :], field))
    field_a = [field_rest[group, :, : 2 * width] for group in groups]
    sign = jnp.where(position < 2, 1.0, -1.0)

    own_real = jnp.where(position == 1, -1.0, jnp.where(position == 3, 0.0, 1.0))
    other_real = jnp.where(position == 2, 0.0, 1.0)
    own_imag = jnp.where(position == 3, 1.0, 0.0)
    other_imag = jnp.where(position == 2, -1.0, 0.0)
    coefs_a = jnp.stack([own_real, other_real, own_imag, other_imag]).reshape(2, 2)
    coefs_b = jnp.concatenate([coefs_a, coefs_a * sign], axis=1)

    inner = length // RADIX
    index = jnp.arange(inner, dtype=jnp.int32)
    cos, sin = root_table(index, index, inner)
    y_table = [jnp.concatenate(pair, 1).reshape(2, 1, inner // 2, 2 * inner) for pair in ((cos, -sin), (sin, cos))]
    y_table = jnp.concatenate(y_table, 1).reshape(2 * inner, 2 * inner)
    y_table = split_table(y_table)
    grid = [lax.broadcasted_iota(jnp.int32, (RADIX, inner, LANES), axis) for axis in range(2)]
    angle = (grid[0] * grid[1]).astype(jnp.float32) * (-2.0 * math.pi / length)
    twist = jnp.stack([jnp.cos(angle), jnp.sin(angle)])
    order = jnp.arange(width, dtype=jnp.int32) * 2

    def x_table(odd):
        rows = jnp.concatenate([order + (2 * width + odd), order + odd])
        cos, sin = [part[:, : 2 * width] for part in x_tables(rows, columns, 4, position)]

        def lay(left, right):
            spans = [slice(tile * width, (tile + 1) * width) for tile in range(2)]
            return jnp.concatenate([side[:, span] for span in spans for side in (left, right)], 1)

        real, imag = lay(cos, sin), lay(-sin, cos)
        table = jnp.concatenate([real[:width], imag[:width], real[width:], imag[width:]], 0)
        return split_table(table)

    norm = 1.0 / math.sqrt(length * columns * 4)
    row_pair = jnp.stack([row_scale * norm, row_rate]).reshape(2, 4, length // 4 // LANES, LANES)
    col_trio = jnp.stack([col_scale, col_shift, col_mix])
    fixed = 2.0 * (columns * jnp.sum(jnp.log(row_scale)) + length * jnp.sum(jnp.log(col_scale)))
    fixed = fixed - length * columns * math.log(2.0 * math.pi)

    first_a = combine(sign.reshape(1), [(from_partner(part, "gx", 1), part) for part in field_a])
    tables = (y_table, twist, x_table(0), x_table(1), row_pair, col_trio, coefs_a, coefs_b, fixed)
    first_a, first_b, tables = lax.optimization_barrier((first_a, to_planes(field_b)[0], tables))
    y_table, twist, even_table, odd_table, row_pair, col_trio, coefs_a, coefs_b, fixed = tables
    second_a = to_planes(first_a)[0]
    second_b = from_partner(first_b, "gx", 1)
    group = [second_b, from_partner(second_b, "gx", 0), first_b, from_partner(first_b, "gx", 0)]
    even_b, odd_b = y_dft(group, True, coefs_b, y_table, twist)
    even_a, odd_a = y_dft([second_a, from_partner(second_a, "gx", 0)], False, coefs_a, y_table, twist)
    latent, tile = x_dft([even_b, even_a], [odd_b, odd_a], even_table, odd_table, row_pair, col_trio)
    tile = tile + fixed / tile.size
    modes = length * columns * lax.axis_size("gx") * lax.axis_size("gy")
    return (latent, sum_everywhere(tile) / modes)


def complex_einsum(form, real_part, imag_part, cos_part, sin_part):
    first = jnp.einsum(form, real_part, cos_part, precision=precision_top)
    second = jnp.einsum(form, real_part, sin_part, precision=precision_top)
    first = first - jnp.einsum(form, imag_part, sin_part, precision=precision_top)
    second = second + jnp.einsum(form, imag_part, cos_part, precision=precision_top)
    return (first, second)


def x_butterfly(field):
    devices = lax.axis_size("gx")
    levels = devices.bit_length() - 1
    position = lax.axis_index("gx")
    real_part, imag_part = field, jnp.zeros_like(field)
    for level in range(levels - 1, -1, -1):
        half = 1 << level
        lower = position // half % 2 == 0
        offset = position % half
        angle = offset.astype(jnp.float32) * (-math.pi / half)
        cos_twist = jnp.where(lower, 1.0, jnp.cos(angle))
        sin_twist = jnp.where(lower, 0.0, jnp.sin(angle))
        other = from_partner(jnp.stack([real_part, imag_part]), "gx", level)
        diff_real = jnp.where(lower, real_part + other[0], other[0] - real_part)
        diff_imag = jnp.where(lower, imag_part + other[1], other[1] - imag_part)
        real_part = diff_real * cos_twist - diff_imag * sin_twist
        imag_part = diff_real * sin_twist + diff_imag * cos_twist
    width = field.shape[2]
    cos_part, sin_part = x_tables(jnp.arange(width, dtype=jnp.int32), width, devices, position)
    real_part, imag_part = complex_einsum("zyn,nk->zyk", real_part, imag_part, cos_part, sin_part)
    return (to_planes(real_part), to_planes(imag_part))


def y_transform(real_part, imag_part):
    planes, length, width = real_part.shape
    outer = 1 << (length.bit_length() - 1) // 2
    inner = length // outer
    outer_index = jnp.arange(outer, dtype=jnp.int32)
    inner_index = jnp.arange(inner, dtype=jnp.int32)
    cos_one, sin_one = root_table(outer_index, outer_index, outer)
    cos_two, sin_two = root_table(inner_index, inner_index, inner)
    cos_mid, sin_mid = root_table(outer_index, inner_index, length)
    shaped_real = real_part.reshape(planes, outer, inner, width)
    shaped_imag = imag_part.reshape(planes, outer, inner, width)
    step_real, step_imag = complex_einsum("zabc,ak->zkbc", shaped_real, shaped_imag, cos_one, sin_one)
    twist_cos = cos_mid[None, :, :, None]
    twist_sin = sin_mid[None, :, :, None]
    turned_real = step_real * twist_cos - step_imag * twist_sin
    turned_imag = step_real * twist_sin + step_imag * twist_cos
    final_real, final_imag = complex_einsum("zkbc,bj->zjkc", turned_real, turned_imag, cos_two, sin_two)
    return (final_real.reshape(planes, length, width), final_imag.reshape(planes, length, width))


def any_way(field, row_scale, col_scale, row_rate, col_shift, col_mix):
    spec_real, spec_imag = y_transform(*x_butterfly(field))
    length = spec_real.shape[1]
    total_cols = spec_real.shape[2] * lax.axis_size("gx")
    norm_factor = 1.0 / math.sqrt(length * total_cols)
    scale = row_scale[None, :, None] * col_scale[None, None, :]
    latent_u = spec_real * norm_factor * scale
    latent_v = spec_imag * norm_factor * scale
    log_scale = row_rate[None, :, None] * jnp.tanh(latent_u + col_shift[None, None, :])
    latent_w = latent_v * jnp.exp(log_scale) + col_mix[None, None, :] * latent_u
    terms = (
        -0.5 * (latent_u * latent_u + latent_w * latent_w)
        - math.log(2.0 * math.pi)
        + log_scale
        + 2.0 * jnp.log(scale)
    )
    mode_count = spec_real.size * lax.axis_size("gx") * lax.axis_size("gy")
    loglik = lax.psum(jnp.sum(terms), ("gx", "gy")) / mode_count
    return (jnp.stack([latent_u, latent_w]), loglik)


def per_device(field, *scales):
    return (four_way if lax.axis_size("gx") == 4 else any_way)(field, *scales)


def solution(mesh):
    return jax.shard_map(
        per_device,
        mesh=mesh,
        in_specs=(P(None, "gy", "gx"), P(), P("gx"), P(), P("gx"), P("gx")),
        out_specs=(P(None, "gy", None, "gx"), P()),
        check_vma=False,
    )
```

```python
import functools
import math

import jax
import jax.numpy as jnp
from jax import lax
from jax.experimental import pallas as pl
from jax.experimental.pallas import tpu as pltpu
from jax.sharding import PartitionSpec as P

precision_top = lax.Precision.HIGHEST
RADIX = 8
LANES = 128
SMALL_BYTES, Y_BYTES, X_BYTES = [size * 1024 * 1024 for size in (8, 27, 26)]


def from_partner(value, axis, stride):
    mask = 2**stride
    pairs = [(source, source ^ mask) for source in range(lax.axis_size(axis))]
    return lax.ppermute(value, axis, pairs)


def to_planes(values):
    return lax.all_to_all(values, "gy", split_axis=0, concat_axis=1, tiled=True)


def pick_columns(left, right, odd):
    lane = lax.broadcasted_iota(jnp.int32, left.shape, 1)
    index = (2 * lane + odd) & (LANES - 1)
    chosen = [jnp.take_along_axis(tile, index, axis=1, mode="promise_in_bounds") for tile in (left, right)]
    return jnp.where(lane < LANES // 2, *chosen)


def combine_kernel(sign_ref, late_ref, early_ref, *refs):
    out_ref = refs[-1]
    sign = sign_ref[0]
    for plane in range(late_ref.shape[0]):
        left, right = [
            late_ref[plane, :, pl.ds(lane, LANES)] + sign * early_ref[plane, :, pl.ds(lane, LANES)] for lane in (0, LANES)
        ]
        for odd in range(2):
            out_ref[plane, :, pl.ds(odd * LANES, LANES)] = pick_columns(left, right, odd)


def combine(sign, parts):
    planes, rows, columns = parts[0][0].shape
    result = ()
    for place, pair in enumerate(parts):
        block = pl.BlockSpec((planes // 2, rows, columns), lambda i: (i, 0, 0))
        result = pl.pallas_call(
            combine_kernel,
            out_shape=[jax.ShapeDtypeStruct((planes * len(parts), rows, columns), jnp.float32)],
            grid=(2,),
            in_specs=[pl.BlockSpec(memory_space=pltpu.SMEM), block, block]
            + [pl.BlockSpec(memory_space=pl.ANY)] * len(result),
            out_specs=[pl.BlockSpec((planes // 2, rows, columns), lambda i, place=place: (2 * place + i, 0, 0))],
            input_output_aliases={3: 0} if result else {},
            cost_estimate=pl.CostEstimate(
                flops=2 * pair[0].size, bytes_accessed=12 * pair[0].size, transcendentals=0
            ),
            compiler_params=pltpu.CompilerParams(vmem_limit_bytes=SMALL_BYTES),
            name="combine",
        )(sign, *pair, *result)
    return result[0]


def reverse_bits(value, count):
    result = value * 0
    for place in range(count):
        result = result + (value >> place & 1) * (1 << count - 1 - place)
    return result


def root_table(row_index, freqs, length):
    phase = row_index[:, None] * freqs[None, :] % length
    angle = phase.astype(jnp.float32) * (-2.0 * math.pi / length)
    return (jnp.cos(angle), jnp.sin(angle))


def x_tables(rows, width, devices, position):
    levels = devices.bit_length() - 1
    local_index = jnp.arange(width, dtype=jnp.int32)
    freqs = reverse_bits(position, levels) + devices * local_index
    return root_table(rows, freqs, devices * width)


def split_table(table):
    high = lax.reduce_precision(table, 8, 7)
    return jnp.stack([high.astype(jnp.bfloat16), (table - high).astype(jnp.bfloat16)])


def split_value(value):
    high = value.astype(jnp.bfloat16)
    return high, (value - high.astype(jnp.float32)).astype(jnp.bfloat16)


def small_fft(values):
    count = len(values)
    if count == 1:
        return values
    even, odd = small_fft(values[0::2]), small_fft(values[1::2])
    first, second = [], []
    root_half = math.sqrt(0.5)
    for place in range(count // 2):
        (er, ei), (re, im) = even[place], odd[place]
        turn = place * 8 // count
        if turn == 1:
            re, im = (re + im) * root_half, (im - re) * root_half
        elif turn == 2:
            re, im = im, -re
        elif turn == 3:
            re, im = (im - re) * root_half, (re + im) * -root_half
        first.append((er + re, ei + im))
        second.append((er - re, ei - im))
    return first + second


def dot(left, right):
    return jnp.dot(left, right, preferred_element_type=jnp.float32)


def y_kernel(count, pick, coef_ref, *refs):
    sources, (table_ref, twist_ref, *out_refs, in_ref, mix_ref, split_ref, step_ref, sems) = refs[:count], refs[count:]
    length = mix_ref.shape[1]
    inner = length // RADIX
    chunks, rows_each = sems.shape[0], 32
    copies = []
    for chunk in range(chunks):
        rows = pl.ds(chunk * length // chunks, length // chunks)
        copies.append([
            pltpu.make_async_copy(source.at[rows, :], in_ref.at[place, rows, :], sems.at[chunk, place])
            for place, source in enumerate(sources)
        ])
    for group in copies:
        for copy in group:
            copy.start()
    for start in range(0, length, rows_each):
        if start % (length // chunks) == 0:
            for copy in copies[start * chunks // length]:
                copy.wait()
        rows = pl.ds(start, rows_each)
        for which in range(2):
            tiles = []
            for lane in (0, LANES):
                mixed = in_ref[0, rows, pl.ds(lane, LANES)] * coef_ref[which, 0]
                for place in range(1, count):
                    mixed = mixed + in_ref[place, rows, pl.ds(lane, LANES)] * coef_ref[which, place]
                tiles.append(mixed)
            for tile in range(2):
                mix_ref[2 * tile + which, rows, :] = pick_columns(*tiles, tile) if pick else tiles[tile]
    half = inner // 2

    def split(tile):
        for which in range(2):
            for s in range(RADIX):
                for start in range(0, inner, 64):
                    parts = split_value(mix_ref[2 * tile + which, pl.ds(s + start * RADIX, 64, stride=RADIX), :])
                    for place, value in enumerate(parts):
                        split_ref[tile, place, pl.ds(which * inner + start, 64), pl.ds(s * LANES, LANES)] = value

    def multiply(tile, part):
        table = [table_ref[place, pl.ds(part * inner, inner), :] for place in (0, 1, 0)]
        values = [split_ref[tile, place] for place in (0, 0, 1)]
        step_ref[part] = dot(jnp.concatenate(table, axis=1), jnp.concatenate(values, axis=0))

    def finish(tile, part):
        for start in range(0, half, 16):
            values = []
            for s in range(RADIX):
                cols = pl.ds(s * LANES, LANES)
                re = step_ref[part, pl.ds(start, 16), cols]
                im = step_ref[part, pl.ds(half + start, 16), cols]
                if s:
                    cos, sin = [twist_ref[k, s, pl.ds(part * half + start, 16), :] for k in range(2)]
                    re, im = re * cos - im * sin, re * sin + im * cos
                values.append((re, im))
            for kb, pair in enumerate(small_fft(values)):
                rows = pl.ds(kb * inner + part * half + start, 16)
                for which in range(2):
                    high, low = split_value(pair[which])
                    out_refs[tile][2 * which, rows, :] = high
                    out_refs[tile][2 * which + 1, rows, :] = low

    jobs = [(tile, part) for tile in range(len(out_refs)) for part in range(2)]
    split(0)
    multiply(*jobs[0])
    for before, job in zip(jobs, jobs[1:]):
        if job[1]:
            if job[0] + 1 < len(out_refs):
                split(job[0] + 1)
        multiply(*job)
        finish(*before)
    finish(*jobs[-1])


def y_dft(inputs, pick, coefs, table, twist):
    length = inputs[0].shape[0]
    inner = length // RADIX
    whole, anywhere = pl.BlockSpec(memory_space=pltpu.VMEM), pl.BlockSpec(memory_space=pl.ANY)
    return pl.pallas_call(
        functools.partial(y_kernel, len(inputs), pick),
        out_shape=[jax.ShapeDtypeStruct((4, length, LANES), jnp.bfloat16)] * 2,
        in_specs=[pl.BlockSpec(memory_space=pltpu.SMEM)] + [anywhere] * len(inputs) + [whole] * 2,
        out_specs=[whole] * 2,
        scratch_shapes=[
            pltpu.VMEM((len(inputs), length, 2 * LANES), jnp.float32),
            pltpu.VMEM((4, length, LANES), jnp.float32),
            pltpu.VMEM((2, 2, 2 * inner, RADIX * LANES), jnp.bfloat16),
            pltpu.VMEM((2, inner, RADIX * LANES), jnp.float32),
            pltpu.SemaphoreType.DMA((4, len(inputs))),
        ],
        compiler_params=pltpu.CompilerParams(vmem_limit_bytes=Y_BYTES),
        cost_estimate=pl.CostEstimate(
            flops=160 * inner * length * LANES, bytes_accessed=8 * length * LANES * (len(inputs) + 3), transcendentals=0
        ),
        name="y_dft",
    )(coefs, *inputs, table, twist)


def x_kernel(count, *refs):
    parts, (even_ref, odd_ref, row_ref, col_ref, out_ref, total_ref) = refs[: 2 * count], refs[2 * count :]
    columns = out_ref.shape[3]
    lanes, rows_each, tiles = LANES, 2 * LANES, columns // (2 * LANES)
    totals = []

    def left(refs, rows):
        first = pl.multiple_of(pl.program_id(0) * out_ref.shape[2], out_ref.shape[2])
        rows = pl.ds(first + rows, rows_each)
        high, low = [[ref[k + which, rows, :] for ref in refs for k in (0, 2)] for which in range(2)]
        return jnp.concatenate(high + low + high, axis=1)

    def multiply(sides, tile):
        cols = pl.ds(tile * 2 * lanes, 2 * lanes)
        return [
            dot(side, jnp.concatenate([table_ref[place, :, cols] for place in (0, 0, 1)], axis=0))
            for side, table_ref in zip(sides, (even_ref, odd_ref))
        ]

    def row_factors(start):
        return [
            jnp.concatenate(
                [
                    jnp.broadcast_to(row_ref[which, 0, c : c + 1, :], (lanes, lanes)).T
                    for c in range(start // lanes, (start + rows_each) // lanes)
                ],
                0,
            )
            for which in range(2)
        ]

    def finish(start, tile, factors, even, odd):
        for upper in range(2):
            cols = pl.ds(upper * columns // 2 + tile * lanes, lanes)
            col_scale, col_shift, col_mix = col_ref[0:1, cols], col_ref[1:2, cols], col_ref[2:3, cols]
            total = None
            for first in range(0, rows_each, 32):
                rows, span = pl.ds(start + first, 32), slice(first, first + 32)
                spec = even[span] - odd[span] if upper else even[span] + odd[span]
                scale = factors[0][span] * col_scale
                latent_u = spec[:, :lanes] * scale
                latent_v = spec[:, lanes:] * scale
                log_scale = factors[1][span] * jnp.tanh(latent_u + col_shift)
                latent_w = latent_v * jnp.exp(log_scale) + col_mix * latent_u
                out_ref[0, 0, rows, cols] = latent_u
                out_ref[1, 0, rows, cols] = latent_w
                terms = log_scale - 0.5 * (latent_u * latent_u + latent_w * latent_w)
                terms = jnp.sum(terms.reshape(-1, 8, lanes), axis=0)
                total = terms if total is None else total + terms
            totals.append(total)

    before = None
    for start in range(0, out_ref.shape[2], rows_each):
        sides = [left(group, start) for group in (parts[:count], parts[count:])]
        factors = row_factors(start)
        for tile in range(tiles):
            products = multiply(sides, tile)
            if before is not None:
                finish(*before)
            before = (start, tile, factors, *products)
    finish(*before)

    @pl.when(pl.program_id(0) == 0)
    def _():
        total_ref[...] = jnp.zeros_like(total_ref)

    total_ref[...] += sum(totals)


def x_dft(even_parts, odd_parts, even_table, odd_table, row_pair, col_trio):
    parts, count, length = even_parts + odd_parts, len(even_parts), even_parts[0].shape[1]
    columns = even_table.shape[2]
    rows = length // row_pair.shape[1]
    whole = [pl.BlockSpec(memory_space=pltpu.VMEM)] * (len(parts) + 2)
    return pl.pallas_call(
        functools.partial(x_kernel, count),
        out_shape=(
            jax.ShapeDtypeStruct((2, 1, length, columns), jnp.float32),
            jax.ShapeDtypeStruct((8, LANES), jnp.float32),
        ),
        grid=(length // rows,),
        in_specs=whole
        + [
            pl.BlockSpec((2, 1, rows // LANES, LANES), lambda i: (0, i, 0, 0)),
            pl.BlockSpec(col_trio.shape, lambda i: (0, 0)),
        ],
        out_specs=(
            pl.BlockSpec((2, 1, rows, columns), lambda i: (0, 0, i, 0)),
            pl.BlockSpec((8, LANES), lambda i: (0, 0)),
        ),
        compiler_params=pltpu.CompilerParams(vmem_limit_bytes=X_BYTES),
        cost_estimate=pl.CostEstimate(
            flops=6 * length * even_table.size,
            bytes_accessed=16 * length * columns,
            transcendentals=2 * length * columns,
        ),
        name="x_dft",
    )(*parts, even_table, odd_table, row_pair, col_trio)


def sum_everywhere(tile):
    axes = ("gx", "gy")
    devices = lax.axis_size("gx") * lax.axis_size("gy")
    copies = jnp.broadcast_to(tile[None], (devices,) + tile.shape)
    return jnp.sum(lax.all_to_all(copies, axes, split_axis=0, concat_axis=0, tiled=True))


def four_way(field, row_scale, col_scale, row_rate, col_shift, col_mix):
    position = lax.axis_index("gx")
    planes, rows, columns = field.shape
    length, width = planes * rows, columns // 4
    groups = [slice(0, planes // 2), slice(planes // 2, None)]
    field_b, field_rest = lax.optimization_barrier((field[:, :, 2 * width :], field))
    field_a = [field_rest[group, :, : 2 * width] for group in groups]
    sign = jnp.where(position < 2, 1.0, -1.0)

    own_real = jnp.where(position == 1, -1.0, jnp.where(position == 3, 0.0, 1.0))
    other_real = jnp.where(position == 2, 0.0, 1.0)
    own_imag = jnp.where(position == 3, 1.0, 0.0)
    other_imag = jnp.where(position == 2, -1.0, 0.0)
    coefs_a = jnp.stack([own_real, other_real, own_imag, other_imag]).reshape(2, 2)
    coefs_b = jnp.concatenate([coefs_a, coefs_a * sign], axis=1)

    inner = length // RADIX
    index = jnp.arange(inner, dtype=jnp.int32)
    cos, sin = root_table(index, index, inner)
    y_table = [jnp.concatenate(pair, 1).reshape(2, 1, inner // 2, 2 * inner) for pair in ((cos, -sin), (sin, cos))]
    y_table = jnp.concatenate(y_table, 1).reshape(2 * inner, 2 * inner)
    y_table = split_table(y_table)
    grid = [lax.broadcasted_iota(jnp.int32, (RADIX, inner, LANES), axis) for axis in range(2)]
    angle = (grid[0] * grid[1]).astype(jnp.float32) * (-2.0 * math.pi / length)
    twist = jnp.stack([jnp.cos(angle), jnp.sin(angle)])
    order = jnp.arange(width, dtype=jnp.int32) * 2

    def x_table(odd):
        rows = jnp.concatenate([order + (2 * width + odd), order + odd])
        cos, sin = [part[:, : 2 * width] for part in x_tables(rows, columns, 4, position)]

        def lay(left, right):
            spans = [slice(tile * width, (tile + 1) * width) for tile in range(2)]
            return jnp.concatenate([side[:, span] for span in spans for side in (left, right)], 1)

        real, imag = lay(cos, sin), lay(-sin, cos)
        table = jnp.concatenate([real[:width], imag[:width], real[width:], imag[width:]], 0)
        return split_table(table)

    norm = 1.0 / math.sqrt(length * columns * 4)
    row_pair = jnp.stack([row_scale * norm, row_rate]).reshape(2, 4, length // 4 // LANES, LANES)
    col_trio = jnp.stack([col_scale, col_shift, col_mix])
    fixed = 2.0 * (columns * jnp.sum(jnp.log(row_scale)) + length * jnp.sum(jnp.log(col_scale)))
    fixed = fixed - length * columns * math.log(2.0 * math.pi)

    first_a = combine(sign.reshape(1), [(from_partner(part, "gx", 1), part) for part in field_a])
    tables = (y_table, twist, x_table(0), x_table(1), row_pair, col_trio, coefs_a, coefs_b, fixed)
    first_a, first_b, tables = lax.optimization_barrier((first_a, to_planes(field_b)[0], tables))
    y_table, twist, even_table, odd_table, row_pair, col_trio, coefs_a, coefs_b, fixed = tables
    second_a = to_planes(first_a)[0]
    second_b = from_partner(first_b, "gx", 1)
    group = [second_b, from_partner(second_b, "gx", 0), first_b, from_partner(first_b, "gx", 0)]
    even_b, odd_b = y_dft(group, True, coefs_b, y_table, twist)
    even_a, odd_a = y_dft([second_a, from_partner(second_a, "gx", 0)], False, coefs_a, y_table, twist)
    latent, tile = x_dft([even_b, even_a], [odd_b, odd_a], even_table, odd_table, row_pair, col_trio)
    tile = tile + fixed / tile.size
    modes = length * columns * lax.axis_size("gx") * lax.axis_size("gy")
    return (latent, sum_everywhere(tile) / modes)


def complex_einsum(form, real_part, imag_part, cos_part, sin_part):
    first = jnp.einsum(form, real_part, cos_part, precision=precision_top)
    second = jnp.einsum(form, real_part, sin_part, precision=precision_top)
    first = first - jnp.einsum(form, imag_part, sin_part, precision=precision_top)
    second = second + jnp.einsum(form, imag_part, cos_part, precision=precision_top)
    return (first, second)


def x_butterfly(field):
    devices = lax.axis_size("gx")
    levels = devices.bit_length() - 1
    position = lax.axis_index("gx")
    real_part, imag_part = field, jnp.zeros_like(field)
    for level in range(levels - 1, -1, -1):
        half = 1 << level
        lower = position // half % 2 == 0
        offset = position % half
        angle = offset.astype(jnp.float32) * (-math.pi / half)
        cos_twist = jnp.where(lower, 1.0, jnp.cos(angle))
        sin_twist = jnp.where(lower, 0.0, jnp.sin(angle))
        other = from_partner(jnp.stack([real_part, imag_part]), "gx", level)
        diff_real = jnp.where(lower, real_part + other[0], other[0] - real_part)
        diff_imag = jnp.where(lower, imag_part + other[1], other[1] - imag_part)
        real_part = diff_real * cos_twist - diff_imag * sin_twist
        imag_part = diff_real * sin_twist + diff_imag * cos_twist
    width = field.shape[2]
    cos_part, sin_part = x_tables(jnp.arange(width, dtype=jnp.int32), width, devices, position)
    real_part, imag_part = complex_einsum("zyn,nk->zyk", real_part, imag_part, cos_part, sin_part)
    return (to_planes(real_part), to_planes(imag_part))


def y_transform(real_part, imag_part):
    planes, length, width = real_part.shape
    outer = 1 << (length.bit_length() - 1) // 2
    inner = length // outer
    outer_index = jnp.arange(outer, dtype=jnp.int32)
    inner_index = jnp.arange(inner, dtype=jnp.int32)
    cos_one, sin_one = root_table(outer_index, outer_index, outer)
    cos_two, sin_two = root_table(inner_index, inner_index, inner)
    cos_mid, sin_mid = root_table(outer_index, inner_index, length)
    shaped_real = real_part.reshape(planes, outer, inner, width)
    shaped_imag = imag_part.reshape(planes, outer, inner, width)
    step_real, step_imag = complex_einsum("zabc,ak->zkbc", shaped_real, shaped_imag, cos_one, sin_one)
    twist_cos = cos_mid[None, :, :, None]
    twist_sin = sin_mid[None, :, :, None]
    turned_real = step_real * twist_cos - step_imag * twist_sin
    turned_imag = step_real * twist_sin + step_imag * twist_cos
    final_real, final_imag = complex_einsum("zkbc,bj->zjkc", turned_real, turned_imag, cos_two, sin_two)
    return (final_real.reshape(planes, length, width), final_imag.reshape(planes, length, width))


def any_way(field, row_scale, col_scale, row_rate, col_shift, col_mix):
    spec_real, spec_imag = y_transform(*x_butterfly(field))
    length = spec_real.shape[1]
    total_cols = spec_real.shape[2] * lax.axis_size("gx")
    norm_factor = 1.0 / math.sqrt(length * total_cols)
    scale = row_scale[None, :, None] * col_scale[None, None, :]
    latent_u = spec_real * norm_factor * scale
    latent_v = spec_imag * norm_factor * scale
    log_scale = row_rate[None, :, None] * jnp.tanh(latent_u + col_shift[None, None, :])
    latent_w = latent_v * jnp.exp(log_scale) + col_mix[None, None, :] * latent_u
    terms = (
        -0.5 * (latent_u * latent_u + latent_w * latent_w)
        - math.log(2.0 * math.pi)
        + log_scale
        + 2.0 * jnp.log(scale)
    )
    mode_count = spec_real.size * lax.axis_size("gx") * lax.axis_size("gy")
    loglik = lax.psum(jnp.sum(terms), ("gx", "gy")) / mode_count
    return (jnp.stack([latent_u, latent_w]), loglik)


def per_device(field, *scales):
    return (four_way if lax.axis_size("gx") == 4 else any_way)(field, *scales)


def solution(mesh):
    return jax.shard_map(
        per_device,
        mesh=mesh,
        in_specs=(P(None, "gy", "gx"), P(), P("gx"), P(), P("gx"), P("gx")),
        out_specs=(P(None, "gy", None, "gx"), P()),
        check_vma=False,
    )
```

```python
import functools
import math

import jax
import jax.numpy as jnp
from jax import lax
from jax.experimental import pallas as pl
from jax.experimental.pallas import tpu as pltpu
from jax.sharding import PartitionSpec as P

precision_top = lax.Precision.HIGHEST
RADIX = 8
LANES = 128
SMALL_BYTES, Y_BYTES, X_BYTES = [size * 1024 * 1024 for size in (8, 27, 26)]


def from_partner(value, axis, stride):
    mask = 2**stride
    pairs = [(source, source ^ mask) for source in range(lax.axis_size(axis))]
    return lax.ppermute(value, axis, pairs)


def to_planes(values):
    return lax.all_to_all(values, "gy", split_axis=0, concat_axis=1, tiled=True)


def pick_columns(left, right, odd):
    lane = lax.broadcasted_iota(jnp.int32, left.shape, 1)
    index = (2 * lane + odd) & (LANES - 1)
    chosen = [jnp.take_along_axis(tile, index, axis=1, mode="promise_in_bounds") for tile in (left, right)]
    return jnp.where(lane < LANES // 2, *chosen)


def combine_kernel(sign_ref, late_ref, early_ref, *refs):
    out_ref = refs[-1]
    sign = sign_ref[0]
    for plane in range(late_ref.shape[0]):
        left, right = [
            late_ref[plane, :, pl.ds(lane, LANES)] + sign * early_ref[plane, :, pl.ds(lane, LANES)] for lane in (0, LANES)
        ]
        for odd in range(2):
            out_ref[plane, :, pl.ds(odd * LANES, LANES)] = pick_columns(left, right, odd)


def combine(sign, parts):
    planes, rows, columns = parts[0][0].shape
    result = ()
    for place, pair in enumerate(parts):
        block = pl.BlockSpec((planes // 2, rows, columns), lambda i: (i, 0, 0))
        result = pl.pallas_call(
            combine_kernel,
            out_shape=[jax.ShapeDtypeStruct((planes * len(parts), rows, columns), jnp.float32)],
            grid=(2,),
            in_specs=[pl.BlockSpec(memory_space=pltpu.SMEM), block, block]
            + [pl.BlockSpec(memory_space=pl.ANY)] * len(result),
            out_specs=[pl.BlockSpec((planes // 2, rows, columns), lambda i, place=place: (2 * place + i, 0, 0))],
            input_output_aliases={3: 0} if result else {},
            cost_estimate=pl.CostEstimate(
                flops=2 * pair[0].size, bytes_accessed=12 * pair[0].size, transcendentals=0
            ),
            compiler_params=pltpu.CompilerParams(vmem_limit_bytes=SMALL_BYTES),
            name="combine",
        )(sign, *pair, *result)
    return result[0]


def reverse_bits(value, count):
    result = value * 0
    for place in range(count):
        result = result + (value >> place & 1) * (1 << count - 1 - place)
    return result


def root_table(row_index, freqs, length):
    phase = row_index[:, None] * freqs[None, :] % length
    angle = phase.astype(jnp.float32) * (-2.0 * math.pi / length)
    return (jnp.cos(angle), jnp.sin(angle))


def x_tables(rows, width, devices, position):
    levels = devices.bit_length() - 1
    local_index = jnp.arange(width, dtype=jnp.int32)
    freqs = reverse_bits(position, levels) + devices * local_index
    return root_table(rows, freqs, devices * width)


def split_table(table):
    high = lax.reduce_precision(table, 8, 7)
    return jnp.stack([high.astype(jnp.bfloat16), (table - high).astype(jnp.bfloat16)])


def split_value(value):
    high = value.astype(jnp.bfloat16)
    return high, (value - high.astype(jnp.float32)).astype(jnp.bfloat16)


def small_fft(values):
    count = len(values)
    if count == 1:
        return values
    even, odd = small_fft(values[0::2]), small_fft(values[1::2])
    first, second = [], []
    root_half = math.sqrt(0.5)
    for place in range(count // 2):
        (er, ei), (re, im) = even[place], odd[place]
        turn = place * 8 // count
        if turn == 1:
            re, im = (re + im) * root_half, (im - re) * root_half
        elif turn == 2:
            re, im = im, -re
        elif turn == 3:
            re, im = (im - re) * root_half, (re + im) * -root_half
        first.append((er + re, ei + im))
        second.append((er - re, ei - im))
    return first + second


def dot(left, right):
    return jnp.dot(left, right, preferred_element_type=jnp.float32)


def y_kernel(count, pick, coef_ref, *refs):
    inputs, (table_ref, twist_ref, *out_refs, mix_ref, split_ref, step_ref) = refs[:count], refs[count:]
    length = mix_ref.shape[1]
    inner = length // RADIX
    rows_each = 32
    for start in range(0, length, rows_each):
        rows = pl.ds(start, rows_each)
        for which in range(2):
            tiles = []
            for lane in (0, LANES):
                mixed = inputs[0][rows, pl.ds(lane, LANES)] * coef_ref[which, 0]
                for place in range(1, count):
                    mixed = mixed + inputs[place][rows, pl.ds(lane, LANES)] * coef_ref[which, place]
                tiles.append(mixed)
            for tile in range(2):
                mix_ref[2 * tile + which, rows, :] = pick_columns(*tiles, tile) if pick else tiles[tile]
    half = inner // 2

    def split(tile):
        for which in range(2):
            for s in range(RADIX):
                for start in range(0, inner, 64):
                    parts = split_value(mix_ref[2 * tile + which, pl.ds(s + start * RADIX, 64, stride=RADIX), :])
                    for place, value in enumerate(parts):
                        split_ref[tile, place, pl.ds(which * inner + start, 64), pl.ds(s * LANES, LANES)] = value

    def multiply(tile, part):
        table = [table_ref[place, pl.ds(part * inner, inner), :] for place in (0, 1, 0)]
        values = [split_ref[tile, place] for place in (0, 0, 1)]
        step_ref[part] = dot(jnp.concatenate(table, axis=1), jnp.concatenate(values, axis=0))

    def finish(tile, part):
        for start in range(0, half, 16):
            values = []
            for s in range(RADIX):
                cols = pl.ds(s * LANES, LANES)
                re = step_ref[part, pl.ds(start, 16), cols]
                im = step_ref[part, pl.ds(half + start, 16), cols]
                if s:
                    cos, sin = [twist_ref[k, s, pl.ds(part * half + start, 16), :] for k in range(2)]
                    re, im = re * cos - im * sin, re * sin + im * cos
                values.append((re, im))
            for kb, pair in enumerate(small_fft(values)):
                rows = pl.ds(kb * inner + part * half + start, 16)
                for which in range(2):
                    high, low = split_value(pair[which])
                    out_refs[tile][2 * which, rows, :] = high
                    out_refs[tile][2 * which + 1, rows, :] = low

    jobs = [(tile, part) for tile in range(len(out_refs)) for part in range(2)]
    split(0)
    multiply(*jobs[0])
    for before, job in zip(jobs, jobs[1:]):
        if job[1]:
            if job[0] + 1 < len(out_refs):
                split(job[0] + 1)
        multiply(*job)
        finish(*before)
    finish(*jobs[-1])


def y_dft(inputs, pick, coefs, table, twist):
    length = inputs[0].shape[0]
    inner = length // RADIX
    whole = pl.BlockSpec(memory_space=pltpu.VMEM)
    return pl.pallas_call(
        functools.partial(y_kernel, len(inputs), pick),
        out_shape=[jax.ShapeDtypeStruct((4, length, LANES), jnp.bfloat16)] * 2,
        in_specs=[pl.BlockSpec(memory_space=pltpu.SMEM)] + [whole] * (len(inputs) + 2),
        out_specs=[whole] * 2,
        scratch_shapes=[
            pltpu.VMEM((4, length, LANES), jnp.float32),
            pltpu.VMEM((2, 2, 2 * inner, RADIX * LANES), jnp.bfloat16),
            pltpu.VMEM((2, inner, RADIX * LANES), jnp.float32),
        ],
        compiler_params=pltpu.CompilerParams(vmem_limit_bytes=Y_BYTES),
        cost_estimate=pl.CostEstimate(
            flops=160 * inner * length * LANES, bytes_accessed=8 * length * LANES * (len(inputs) + 3), transcendentals=0
        ),
        name="y_dft",
    )(coefs, *inputs, table, twist)


def x_kernel(count, *refs):
    parts, (even_ref, odd_ref, row_ref, col_ref, out_ref, total_ref) = refs[: 2 * count], refs[2 * count :]
    columns = out_ref.shape[3]
    lanes, rows_each, tiles = LANES, 2 * LANES, columns // (2 * LANES)
    totals = []

    def left(refs, rows):
        first = pl.multiple_of(pl.program_id(0) * out_ref.shape[2], out_ref.shape[2])
        rows = pl.ds(first + rows, rows_each)
        high, low = [[ref[k + which, rows, :] for ref in refs for k in (0, 2)] for which in range(2)]
        return jnp.concatenate(high + low + high, axis=1)

    def multiply(sides, tile):
        cols = pl.ds(tile * 2 * lanes, 2 * lanes)
        return [
            dot(side, jnp.concatenate([table_ref[place, :, cols] for place in (0, 0, 1)], axis=0))
            for side, table_ref in zip(sides, (even_ref, odd_ref))
        ]

    def row_factors(start):
        return [
            jnp.concatenate(
                [
                    jnp.broadcast_to(row_ref[which, 0, c : c + 1, :], (lanes, lanes)).T
                    for c in range(start // lanes, (start + rows_each) // lanes)
                ],
                0,
            )
            for which in range(2)
        ]

    def finish(start, tile, factors, even, odd):
        for upper in range(2):
            cols = pl.ds(upper * columns // 2 + tile * lanes, lanes)
            col_scale, col_shift, col_mix = col_ref[0:1, cols], col_ref[1:2, cols], col_ref[2:3, cols]
            total = None
            for first in range(0, rows_each, 32):
                rows, span = pl.ds(start + first, 32), slice(first, first + 32)
                spec = even[span] - odd[span] if upper else even[span] + odd[span]
                scale = factors[0][span] * col_scale
                latent_u = spec[:, :lanes] * scale
                latent_v = spec[:, lanes:] * scale
                log_scale = factors[1][span] * jnp.tanh(latent_u + col_shift)
                latent_w = latent_v * jnp.exp(log_scale) + col_mix * latent_u
                out_ref[0, 0, rows, cols] = latent_u
                out_ref[1, 0, rows, cols] = latent_w
                terms = log_scale - 0.5 * (latent_u * latent_u + latent_w * latent_w)
                terms = jnp.sum(terms.reshape(-1, 8, lanes), axis=0)
                total = terms if total is None else total + terms
            totals.append(total)

    before = None
    for start in range(0, out_ref.shape[2], rows_each):
        sides = [left(group, start) for group in (parts[:count], parts[count:])]
        factors = row_factors(start)
        for tile in range(tiles):
            products = multiply(sides, tile)
            if before is not None:
                finish(*before)
            before = (start, tile, factors, *products)
    finish(*before)

    @pl.when(pl.program_id(0) == 0)
    def _():
        total_ref[...] = jnp.zeros_like(total_ref)

    total_ref[...] += sum(totals)


def x_dft(even_parts, odd_parts, even_table, odd_table, row_pair, col_trio):
    parts, count, length = even_parts + odd_parts, len(even_parts), even_parts[0].shape[1]
    columns = even_table.shape[2]
    rows = length // row_pair.shape[1]
    whole = [pl.BlockSpec(memory_space=pltpu.VMEM)] * (len(parts) + 2)
    return pl.pallas_call(
        functools.partial(x_kernel, count),
        out_shape=(
            jax.ShapeDtypeStruct((2, 1, length, columns), jnp.float32),
            jax.ShapeDtypeStruct((8, LANES), jnp.float32),
        ),
        grid=(length // rows,),
        in_specs=whole
        + [
            pl.BlockSpec((2, 1, rows // LANES, LANES), lambda i: (0, i, 0, 0)),
            pl.BlockSpec(col_trio.shape, lambda i: (0, 0)),
        ],
        out_specs=(
            pl.BlockSpec((2, 1, rows, columns), lambda i: (0, 0, i, 0)),
            pl.BlockSpec((8, LANES), lambda i: (0, 0)),
        ),
        compiler_params=pltpu.CompilerParams(vmem_limit_bytes=X_BYTES),
        cost_estimate=pl.CostEstimate(
            flops=6 * length * even_table.size,
            bytes_accessed=16 * length * columns,
            transcendentals=2 * length * columns,
        ),
        name="x_dft",
    )(*parts, even_table, odd_table, row_pair, col_trio)


def sum_everywhere(tile):
    axes = ("gx", "gy")
    devices = lax.axis_size("gx") * lax.axis_size("gy")
    copies = jnp.broadcast_to(tile[None], (devices,) + tile.shape)
    return jnp.sum(lax.all_to_all(copies, axes, split_axis=0, concat_axis=0, tiled=True))


def four_way(field, row_scale, col_scale, row_rate, col_shift, col_mix):
    position = lax.axis_index("gx")
    planes, rows, columns = field.shape
    length, width = planes * rows, columns // 4
    groups = [slice(0, planes // 2), slice(planes // 2, None)]
    field_b, field_rest = lax.optimization_barrier((field[:, :, 2 * width :], field))
    field_a = [field_rest[group, :, : 2 * width] for group in groups]
    sign = jnp.where(position < 2, 1.0, -1.0)

    own_real = jnp.where(position == 1, -1.0, jnp.where(position == 3, 0.0, 1.0))
    other_real = jnp.where(position == 2, 0.0, 1.0)
    own_imag = jnp.where(position == 3, 1.0, 0.0)
    other_imag = jnp.where(position == 2, -1.0, 0.0)
    coefs_a = jnp.stack([own_real, other_real, own_imag, other_imag]).reshape(2, 2)
    coefs_b = jnp.concatenate([coefs_a, coefs_a * sign], axis=1)

    inner = length // RADIX
    index = jnp.arange(inner, dtype=jnp.int32)
    cos, sin = root_table(index, index, inner)
    y_table = [jnp.concatenate(pair, 1).reshape(2, 1, inner // 2, 2 * inner) for pair in ((cos, -sin), (sin, cos))]
    y_table = jnp.concatenate(y_table, 1).reshape(2 * inner, 2 * inner)
    y_table = split_table(y_table)
    grid = [lax.broadcasted_iota(jnp.int32, (RADIX, inner, LANES), axis) for axis in range(2)]
    angle = (grid[0] * grid[1]).astype(jnp.float32) * (-2.0 * math.pi / length)
    twist = jnp.stack([jnp.cos(angle), jnp.sin(angle)])
    order = jnp.arange(width, dtype=jnp.int32) * 2

    def x_table(odd):
        rows = jnp.concatenate([order + (2 * width + odd), order + odd])
        cos, sin = [part[:, : 2 * width] for part in x_tables(rows, columns, 4, position)]

        def lay(left, right):
            spans = [slice(tile * width, (tile + 1) * width) for tile in range(2)]
            return jnp.concatenate([side[:, span] for span in spans for side in (left, right)], 1)

        real, imag = lay(cos, sin), lay(-sin, cos)
        table = jnp.concatenate([real[:width], imag[:width], real[width:], imag[width:]], 0)
        return split_table(table)

    norm = 1.0 / math.sqrt(length * columns * 4)
    row_pair = jnp.stack([row_scale * norm, row_rate]).reshape(2, 4, length // 4 // LANES, LANES)
    col_trio = jnp.stack([col_scale, col_shift, col_mix])
    fixed = 2.0 * (columns * jnp.sum(jnp.log(row_scale)) + length * jnp.sum(jnp.log(col_scale)))
    fixed = fixed - length * columns * math.log(2.0 * math.pi)

    first_a = combine(sign.reshape(1), [(from_partner(part, "gx", 1), part) for part in field_a])
    tables = (y_table, twist, x_table(0), x_table(1), row_pair, col_trio, coefs_a, coefs_b, fixed)
    first_a, first_b, tables = lax.optimization_barrier((first_a, to_planes(field_b)[0], tables))
    y_table, twist, even_table, odd_table, row_pair, col_trio, coefs_a, coefs_b, fixed = tables
    second_a = to_planes(first_a)[0]
    late = (even_table, odd_table, row_pair, col_trio, fixed)
    second_b, late = lax.optimization_barrier((from_partner(first_b, "gx", 1), late))
    even_table, odd_table, row_pair, col_trio, fixed = late
    group = [second_b, from_partner(second_b, "gx", 0), first_b, from_partner(first_b, "gx", 0)]
    even_b, odd_b = y_dft(group, True, coefs_b, y_table, twist)
    even_a, odd_a = y_dft([second_a, from_partner(second_a, "gx", 0)], False, coefs_a, y_table, twist)
    latent, tile = x_dft([even_b, even_a], [odd_b, odd_a], even_table, odd_table, row_pair, col_trio)
    tile = tile + fixed / tile.size
    modes = length * columns * lax.axis_size("gx") * lax.axis_size("gy")
    return (latent, sum_everywhere(tile) / modes)


def complex_einsum(form, real_part, imag_part, cos_part, sin_part):
    first = jnp.einsum(form, real_part, cos_part, precision=precision_top)
    second = jnp.einsum(form, real_part, sin_part, precision=precision_top)
    first = first - jnp.einsum(form, imag_part, sin_part, precision=precision_top)
    second = second + jnp.einsum(form, imag_part, cos_part, precision=precision_top)
    return (first, second)


def x_butterfly(field):
    devices = lax.axis_size("gx")
    levels = devices.bit_length() - 1
    position = lax.axis_index("gx")
    real_part, imag_part = field, jnp.zeros_like(field)
    for level in range(levels - 1, -1, -1):
        half = 1 << level
        lower = position // half % 2 == 0
        offset = position % half
        angle = offset.astype(jnp.float32) * (-math.pi / half)
        cos_twist = jnp.where(lower, 1.0, jnp.cos(angle))
        sin_twist = jnp.where(lower, 0.0, jnp.sin(angle))
        other = from_partner(jnp.stack([real_part, imag_part]), "gx", level)
        diff_real = jnp.where(lower, real_part + other[0], other[0] - real_part)
        diff_imag = jnp.where(lower, imag_part + other[1], other[1] - imag_part)
        real_part = diff_real * cos_twist - diff_imag * sin_twist
        imag_part = diff_real * sin_twist + diff_imag * cos_twist
    width = field.shape[2]
    cos_part, sin_part = x_tables(jnp.arange(width, dtype=jnp.int32), width, devices, position)
    real_part, imag_part = complex_einsum("zyn,nk->zyk", real_part, imag_part, cos_part, sin_part)
    return (to_planes(real_part), to_planes(imag_part))


def y_transform(real_part, imag_part):
    planes, length, width = real_part.shape
    outer = 1 << (length.bit_length() - 1) // 2
    inner = length // outer
    outer_index = jnp.arange(outer, dtype=jnp.int32)
    inner_index = jnp.arange(inner, dtype=jnp.int32)
    cos_one, sin_one = root_table(outer_index, outer_index, outer)
    cos_two, sin_two = root_table(inner_index, inner_index, inner)
    cos_mid, sin_mid = root_table(outer_index, inner_index, length)
    shaped_real = real_part.reshape(planes, outer, inner, width)
    shaped_imag = imag_part.reshape(planes, outer, inner, width)
    step_real, step_imag = complex_einsum("zabc,ak->zkbc", shaped_real, shaped_imag, cos_one, sin_one)
    twist_cos = cos_mid[None, :, :, None]
    twist_sin = sin_mid[None, :, :, None]
    turned_real = step_real * twist_cos - step_imag * twist_sin
    turned_imag = step_real * twist_sin + step_imag * twist_cos
    final_real, final_imag = complex_einsum("zkbc,bj->zjkc", turned_real, turned_imag, cos_two, sin_two)
    return (final_real.reshape(planes, length, width), final_imag.reshape(planes, length, width))


def any_way(field, row_scale, col_scale, row_rate, col_shift, col_mix):
    spec_real, spec_imag = y_transform(*x_butterfly(field))
    length = spec_real.shape[1]
    total_cols = spec_real.shape[2] * lax.axis_size("gx")
    norm_factor = 1.0 / math.sqrt(length * total_cols)
    scale = row_scale[None, :, None] * col_scale[None, None, :]
    latent_u = spec_real * norm_factor * scale
    latent_v = spec_imag * norm_factor * scale
    log_scale = row_rate[None, :, None] * jnp.tanh(latent_u + col_shift[None, None, :])
    latent_w = latent_v * jnp.exp(log_scale) + col_mix[None, None, :] * latent_u
    terms = (
        -0.5 * (latent_u * latent_u + latent_w * latent_w)
        - math.log(2.0 * math.pi)
        + log_scale
        + 2.0 * jnp.log(scale)
    )
    mode_count = spec_real.size * lax.axis_size("gx") * lax.axis_size("gy")
    loglik = lax.psum(jnp.sum(terms), ("gx", "gy")) / mode_count
    return (jnp.stack([latent_u, latent_w]), loglik)


def per_device(field, *scales):
    return (four_way if lax.axis_size("gx") == 4 else any_way)(field, *scales)


def solution(mesh):
    return jax.shard_map(
        per_device,
        mesh=mesh,
        in_specs=(P(None, "gy", "gx"), P(), P("gx"), P(), P("gx"), P("gx")),
        out_specs=(P(None, "gy", None, "gx"), P()),
        check_vma=False,
    )
```

```python
import functools
import math

import jax
import jax.numpy as jnp
from jax import lax
from jax.experimental import pallas as pl
from jax.experimental.pallas import tpu as pltpu
from jax.sharding import PartitionSpec as P

precision_top = lax.Precision.HIGHEST
RADIX = 8
LANES = 128
SMALL_BYTES, Y_BYTES, X_BYTES = [size * 1024 * 1024 for size in (8, 27, 26)]


def from_partner(value, axis, stride):
    mask = 2**stride
    pairs = [(source, source ^ mask) for source in range(lax.axis_size(axis))]
    return lax.ppermute(value, axis, pairs)


def to_planes(values):
    return lax.all_to_all(values, "gy", split_axis=0, concat_axis=1, tiled=True)


def pick_columns(left, right, odd):
    lane = lax.broadcasted_iota(jnp.int32, left.shape, 1)
    index = (2 * lane + odd) & (LANES - 1)
    chosen = [jnp.take_along_axis(tile, index, axis=1, mode="promise_in_bounds") for tile in (left, right)]
    return jnp.where(lane < LANES // 2, *chosen)


def combine_kernel(sign_ref, late_ref, early_ref, *refs):
    out_ref = refs[-1]
    sign = sign_ref[0]
    for plane in range(late_ref.shape[0]):
        left, right = [
            late_ref[plane, :, pl.ds(lane, LANES)] + sign * early_ref[plane, :, pl.ds(lane, LANES)] for lane in (0, LANES)
        ]
        for odd in range(2):
            out_ref[plane, :, pl.ds(odd * LANES, LANES)] = pick_columns(left, right, odd)


def combine(sign, parts):
    planes, rows, columns = parts[0][0].shape
    result = ()
    for place, pair in enumerate(parts):
        block = pl.BlockSpec((planes // 2, rows, columns), lambda i: (i, 0, 0))
        result = pl.pallas_call(
            combine_kernel,
            out_shape=[jax.ShapeDtypeStruct((planes * len(parts), rows, columns), jnp.float32)],
            grid=(2,),
            in_specs=[pl.BlockSpec(memory_space=pltpu.SMEM), block, block]
            + [pl.BlockSpec(memory_space=pl.ANY)] * len(result),
            out_specs=[pl.BlockSpec((planes // 2, rows, columns), lambda i, place=place: (2 * place + i, 0, 0))],
            input_output_aliases={3: 0} if result else {},
            cost_estimate=pl.CostEstimate(
                flops=2 * pair[0].size, bytes_accessed=12 * pair[0].size, transcendentals=0
            ),
            compiler_params=pltpu.CompilerParams(vmem_limit_bytes=SMALL_BYTES),
            name="combine",
        )(sign, *pair, *result)
    return result[0]


def reverse_bits(value, count):
    result = value * 0
    for place in range(count):
        result = result + (value >> place & 1) * (1 << count - 1 - place)
    return result


def root_table(row_index, freqs, length):
    phase = row_index[:, None] * freqs[None, :] % length
    angle = phase.astype(jnp.float32) * (-2.0 * math.pi / length)
    return (jnp.cos(angle), jnp.sin(angle))


def x_tables(rows, width, devices, position):
    levels = devices.bit_length() - 1
    local_index = jnp.arange(width, dtype=jnp.int32)
    freqs = reverse_bits(position, levels) + devices * local_index
    return root_table(rows, freqs, devices * width)


def split_table(table):
    high = lax.reduce_precision(table, 8, 7)
    return jnp.stack([high.astype(jnp.bfloat16), (table - high).astype(jnp.bfloat16)])


def split_value(value):
    high = value.astype(jnp.bfloat16)
    return high, (value - high.astype(jnp.float32)).astype(jnp.bfloat16)


def small_fft(values):
    count = len(values)
    if count == 1:
        return values
    even, odd = small_fft(values[0::2]), small_fft(values[1::2])
    first, second = [], []
    root_half = math.sqrt(0.5)
    for place in range(count // 2):
        (er, ei), (re, im) = even[place], odd[place]
        turn = place * 8 // count
        if turn == 1:
            re, im = (re + im) * root_half, (im - re) * root_half
        elif turn == 2:
            re, im = im, -re
        elif turn == 3:
            re, im = (im - re) * root_half, (re + im) * -root_half
        first.append((er + re, ei + im))
        second.append((er - re, ei - im))
    return first + second


def dot(left, right):
    return jnp.dot(left, right, preferred_element_type=jnp.float32)


def y_kernel(count, pick, coef_ref, *refs):
    inputs, (table_ref, twist_ref, *out_refs, mix_ref, split_ref, step_ref) = refs[:count], refs[count:]
    length = mix_ref.shape[1]
    inner = length // RADIX
    rows_each = 32
    for start in range(0, length, rows_each):
        rows = pl.ds(start, rows_each)
        for which in range(2):
            tiles = []
            for lane in (0, LANES):
                mixed = inputs[0][rows, pl.ds(lane, LANES)] * coef_ref[which, 0]
                for place in range(1, count):
                    mixed = mixed + inputs[place][rows, pl.ds(lane, LANES)] * coef_ref[which, place]
                tiles.append(mixed)
            for tile in range(2):
                mix_ref[2 * tile + which, rows, :] = pick_columns(*tiles, tile) if pick else tiles[tile]
    half = inner // 2

    def split(tile):
        for which in range(2):
            for s in range(RADIX):
                for start in range(0, inner, 64):
                    parts = split_value(mix_ref[2 * tile + which, pl.ds(s + start * RADIX, 64, stride=RADIX), :])
                    for place, value in enumerate(parts):
                        split_ref[tile, place, pl.ds(which * inner + start, 64), pl.ds(s * LANES, LANES)] = value

    def multiply(tile, part):
        table = [table_ref[place, pl.ds(part * inner, inner), :] for place in (0, 1, 0)]
        values = [split_ref[tile, place] for place in (0, 0, 1)]
        step_ref[part] = dot(jnp.concatenate(table, axis=1), jnp.concatenate(values, axis=0))

    def finish(tile, part):
        for start in range(0, half, 16):
            values = []
            for s in range(RADIX):
                cols = pl.ds(s * LANES, LANES)
                re = step_ref[part, pl.ds(start, 16), cols]
                im = step_ref[part, pl.ds(half + start, 16), cols]
                if s:
                    cos, sin = [twist_ref[k, s, pl.ds(part * half + start, 16), :] for k in range(2)]
                    re, im = re * cos - im * sin, re * sin + im * cos
                values.append((re, im))
            for kb, pair in enumerate(small_fft(values)):
                rows = pl.ds(kb * inner + part * half + start, 16)
                for which in range(2):
                    high, low = split_value(pair[which])
                    out_refs[tile][2 * which, rows, :] = high
                    out_refs[tile][2 * which + 1, rows, :] = low

    jobs = [(tile, part) for tile in range(len(out_refs)) for part in range(2)]
    split(0)
    multiply(*jobs[0])
    for before, job in zip(jobs, jobs[1:]):
        if job[1]:
            if job[0] + 1 < len(out_refs):
                split(job[0] + 1)
        multiply(*job)
        finish(*before)
    finish(*jobs[-1])


def y_dft(inputs, pick, coefs, table, twist):
    length = inputs[0].shape[0]
    inner = length // RADIX
    whole = pl.BlockSpec(memory_space=pltpu.VMEM)
    return pl.pallas_call(
        functools.partial(y_kernel, len(inputs), pick),
        out_shape=[jax.ShapeDtypeStruct((4, length, LANES), jnp.bfloat16)] * 2,
        in_specs=[pl.BlockSpec(memory_space=pltpu.SMEM)] + [whole] * (len(inputs) + 2),
        out_specs=[whole] * 2,
        scratch_shapes=[
            pltpu.VMEM((4, length, LANES), jnp.float32),
            pltpu.VMEM((2, 2, 2 * inner, RADIX * LANES), jnp.bfloat16),
            pltpu.VMEM((2, inner, RADIX * LANES), jnp.float32),
        ],
        compiler_params=pltpu.CompilerParams(vmem_limit_bytes=Y_BYTES),
        cost_estimate=pl.CostEstimate(
            flops=160 * inner * length * LANES, bytes_accessed=8 * length * LANES * (len(inputs) + 3), transcendentals=0
        ),
        name="y_dft",
    )(coefs, *inputs, table, twist)


def x_kernel(count, *refs):
    parts, (even_ref, odd_ref, row_ref, col_ref, out_ref, total_ref) = refs[: 2 * count], refs[2 * count :]
    columns = out_ref.shape[3]
    lanes, rows_each, tiles = LANES, 2 * LANES, columns // (2 * LANES)
    totals = []

    def left(refs, rows):
        first = pl.multiple_of(pl.program_id(0) * out_ref.shape[2], out_ref.shape[2])
        rows = pl.ds(first + rows, rows_each)
        high, low = [[ref[k + which, rows, :] for ref in refs for k in (0, 2)] for which in range(2)]
        return jnp.concatenate(high + low + high, axis=1)

    def multiply(sides, tile):
        cols = pl.ds(tile * 2 * lanes, 2 * lanes)
        return [
            dot(side, jnp.concatenate([table_ref[place, :, cols] for place in (0, 0, 1)], axis=0))
            for side, table_ref in zip(sides, (even_ref, odd_ref))
        ]

    def row_factors(start):
        return [
            jnp.concatenate(
                [
                    jnp.broadcast_to(row_ref[which, 0, c : c + 1, :], (lanes, lanes)).T
                    for c in range(start // lanes, (start + rows_each) // lanes)
                ],
                0,
            )
            for which in range(2)
        ]

    def finish(start, tile, factors, even, odd):
        for upper in range(2):
            cols = pl.ds(upper * columns // 2 + tile * lanes, lanes)
            col_scale, col_shift, col_mix = col_ref[0:1, cols], col_ref[1:2, cols], col_ref[2:3, cols]
            total = None
            for first in range(0, rows_each, 32):
                rows, span = pl.ds(start + first, 32), slice(first, first + 32)
                spec = even[span] - odd[span] if upper else even[span] + odd[span]
                scale = factors[0][span] * col_scale
                latent_u = spec[:, :lanes] * scale
                latent_v = spec[:, lanes:] * scale
                log_scale = factors[1][span] * jnp.tanh(latent_u + col_shift)
                latent_w = latent_v * jnp.exp(log_scale) + col_mix * latent_u
                out_ref[0, 0, rows, cols] = latent_u
                out_ref[1, 0, rows, cols] = latent_w
                terms = log_scale - 0.5 * (latent_u * latent_u + latent_w * latent_w)
                terms = jnp.sum(terms.reshape(-1, 8, lanes), axis=0)
                total = terms if total is None else total + terms
            totals.append(total)

    before = None
    for start in range(0, out_ref.shape[2], rows_each):
        sides = [left(group, start) for group in (parts[:count], parts[count:])]
        factors = row_factors(start)
        for tile in range(tiles):
            products = multiply(sides, tile)
            if before is not None:
                finish(*before)
            before = (start, tile, factors, *products)
    finish(*before)

    @pl.when(pl.program_id(0) == 0)
    def _():
        total_ref[...] = jnp.zeros_like(total_ref)

    total_ref[...] += sum(totals)


def x_dft(even_parts, odd_parts, even_table, odd_table, row_pair, col_trio):
    parts, count, length = even_parts + odd_parts, len(even_parts), even_parts[0].shape[1]
    columns = even_table.shape[2]
    rows = length // row_pair.shape[1]
    whole = [pl.BlockSpec(memory_space=pltpu.VMEM)] * (len(parts) + 2)
    return pl.pallas_call(
        functools.partial(x_kernel, count),
        out_shape=(
            jax.ShapeDtypeStruct((2, 1, length, columns), jnp.float32),
            jax.ShapeDtypeStruct((8, LANES), jnp.float32),
        ),
        grid=(length // rows,),
        in_specs=whole
        + [
            pl.BlockSpec((2, 1, rows // LANES, LANES), lambda i: (0, i, 0, 0)),
            pl.BlockSpec(col_trio.shape, lambda i: (0, 0)),
        ],
        out_specs=(
            pl.BlockSpec((2, 1, rows, columns), lambda i: (0, 0, i, 0)),
            pl.BlockSpec((8, LANES), lambda i: (0, 0)),
        ),
        compiler_params=pltpu.CompilerParams(vmem_limit_bytes=X_BYTES),
        cost_estimate=pl.CostEstimate(
            flops=6 * length * even_table.size,
            bytes_accessed=16 * length * columns,
            transcendentals=2 * length * columns,
        ),
        name="x_dft",
    )(*parts, even_table, odd_table, row_pair, col_trio)


def sum_everywhere(tile):
    for axis in ("gx", "gy"):
        devices = lax.axis_size(axis)
        place = devices
        while place > 1:
            low = max(place // 4, 1)
            masks = range(low, place, low)
            others = [lax.ppermute(tile, axis, [(s, s ^ mask) for s in range(devices)]) for mask in masks]
            tile = functools.reduce(jnp.add, others, tile)
            place = low
    return jnp.sum(tile)


def four_way(field, row_scale, col_scale, row_rate, col_shift, col_mix):
    position = lax.axis_index("gx")
    planes, rows, columns = field.shape
    length, width = planes * rows, columns // 4
    groups = [slice(0, planes // 2), slice(planes // 2, None)]
    field_b, field_rest = lax.optimization_barrier((field[:, :, 2 * width :], field))
    field_a = [field_rest[group, :, : 2 * width] for group in groups]
    sign = jnp.where(position < 2, 1.0, -1.0)

    own_real = jnp.where(position == 1, -1.0, jnp.where(position == 3, 0.0, 1.0))
    other_real = jnp.where(position == 2, 0.0, 1.0)
    own_imag = jnp.where(position == 3, 1.0, 0.0)
    other_imag = jnp.where(position == 2, -1.0, 0.0)
    coefs_a = jnp.stack([own_real, other_real, own_imag, other_imag]).reshape(2, 2)
    coefs_b = jnp.concatenate([coefs_a, coefs_a * sign], axis=1)

    inner = length // RADIX
    index = jnp.arange(inner, dtype=jnp.int32)
    cos, sin = root_table(index, index, inner)
    y_table = [jnp.concatenate(pair, 1).reshape(2, 1, inner // 2, 2 * inner) for pair in ((cos, -sin), (sin, cos))]
    y_table = jnp.concatenate(y_table, 1).reshape(2 * inner, 2 * inner)
    y_table = split_table(y_table)
    grid = [lax.broadcasted_iota(jnp.int32, (RADIX, inner, LANES), axis) for axis in range(2)]
    angle = (grid[0] * grid[1]).astype(jnp.float32) * (-2.0 * math.pi / length)
    twist = jnp.stack([jnp.cos(angle), jnp.sin(angle)])
    order = jnp.arange(width, dtype=jnp.int32) * 2

    def x_table(odd):
        rows = jnp.concatenate([order + (2 * width + odd), order + odd])
        cos, sin = [part[:, : 2 * width] for part in x_tables(rows, columns, 4, position)]

        def lay(left, right):
            spans = [slice(tile * width, (tile + 1) * width) for tile in range(2)]
            return jnp.concatenate([side[:, span] for span in spans for side in (left, right)], 1)

        real, imag = lay(cos, sin), lay(-sin, cos)
        table = jnp.concatenate([real[:width], imag[:width], real[width:], imag[width:]], 0)
        return split_table(table)

    norm = 1.0 / math.sqrt(length * columns * 4)
    row_pair = jnp.stack([row_scale * norm, row_rate]).reshape(2, 4, length // 4 // LANES, LANES)
    col_trio = jnp.stack([col_scale, col_shift, col_mix])
    fixed = 2.0 * (columns * jnp.sum(jnp.log(row_scale)) + length * jnp.sum(jnp.log(col_scale)))
    fixed = fixed - length * columns * math.log(2.0 * math.pi)

    first_a = combine(sign.reshape(1), [(from_partner(part, "gx", 1), part) for part in field_a])
    tables = (y_table, twist, x_table(0), x_table(1), row_pair, col_trio, coefs_a, coefs_b, fixed)
    first_a, first_b, tables = lax.optimization_barrier((first_a, to_planes(field_b)[0], tables))
    y_table, twist, even_table, odd_table, row_pair, col_trio, coefs_a, coefs_b, fixed = tables
    second_a = to_planes(first_a)[0]
    second_b = from_partner(first_b, "gx", 1)
    group = [second_b, from_partner(second_b, "gx", 0), first_b, from_partner(first_b, "gx", 0)]
    even_b, odd_b = y_dft(group, True, coefs_b, y_table, twist)
    even_a, odd_a = y_dft([second_a, from_partner(second_a, "gx", 0)], False, coefs_a, y_table, twist)
    latent, tile = x_dft([even_b, even_a], [odd_b, odd_a], even_table, odd_table, row_pair, col_trio)
    tile = tile + fixed / tile.size
    modes = length * columns * lax.axis_size("gx") * lax.axis_size("gy")
    return (latent, sum_everywhere(tile) / modes)


def complex_einsum(form, real_part, imag_part, cos_part, sin_part):
    first = jnp.einsum(form, real_part, cos_part, precision=precision_top)
    second = jnp.einsum(form, real_part, sin_part, precision=precision_top)
    first = first - jnp.einsum(form, imag_part, sin_part, precision=precision_top)
    second = second + jnp.einsum(form, imag_part, cos_part, precision=precision_top)
    return (first, second)


def x_butterfly(field):
    devices = lax.axis_size("gx")
    levels = devices.bit_length() - 1
    position = lax.axis_index("gx")
    real_part, imag_part = field, jnp.zeros_like(field)
    for level in range(levels - 1, -1, -1):
        half = 1 << level
        lower = position // half % 2 == 0
        offset = position % half
        angle = offset.astype(jnp.float32) * (-math.pi / half)
        cos_twist = jnp.where(lower, 1.0, jnp.cos(angle))
        sin_twist = jnp.where(lower, 0.0, jnp.sin(angle))
        other = from_partner(jnp.stack([real_part, imag_part]), "gx", level)
        diff_real = jnp.where(lower, real_part + other[0], other[0] - real_part)
        diff_imag = jnp.where(lower, imag_part + other[1], other[1] - imag_part)
        real_part = diff_real * cos_twist - diff_imag * sin_twist
        imag_part = diff_real * sin_twist + diff_imag * cos_twist
    width = field.shape[2]
    cos_part, sin_part = x_tables(jnp.arange(width, dtype=jnp.int32), width, devices, position)
    real_part, imag_part = complex_einsum("zyn,nk->zyk", real_part, imag_part, cos_part, sin_part)
    return (to_planes(real_part), to_planes(imag_part))


def y_transform(real_part, imag_part):
    planes, length, width = real_part.shape
    outer = 1 << (length.bit_length() - 1) // 2
    inner = length // outer
    outer_index = jnp.arange(outer, dtype=jnp.int32)
    inner_index = jnp.arange(inner, dtype=jnp.int32)
    cos_one, sin_one = root_table(outer_index, outer_index, outer)
    cos_two, sin_two = root_table(inner_index, inner_index, inner)
    cos_mid, sin_mid = root_table(outer_index, inner_index, length)
    shaped_real = real_part.reshape(planes, outer, inner, width)
    shaped_imag = imag_part.reshape(planes, outer, inner, width)
    step_real, step_imag = complex_einsum("zabc,ak->zkbc", shaped_real, shaped_imag, cos_one, sin_one)
    twist_cos = cos_mid[None, :, :, None]
    twist_sin = sin_mid[None, :, :, None]
    turned_real = step_real * twist_cos - step_imag * twist_sin
    turned_imag = step_real * twist_sin + step_imag * twist_cos
    final_real, final_imag = complex_einsum("zkbc,bj->zjkc", turned_real, turned_imag, cos_two, sin_two)
    return (final_real.reshape(planes, length, width), final_imag.reshape(planes, length, width))


def any_way(field, row_scale, col_scale, row_rate, col_shift, col_mix):
    spec_real, spec_imag = y_transform(*x_butterfly(field))
    length = spec_real.shape[1]
    total_cols = spec_real.shape[2] * lax.axis_size("gx")
    norm_factor = 1.0 / math.sqrt(length * total_cols)
    scale = row_scale[None, :, None] * col_scale[None, None, :]
    latent_u = spec_real * norm_factor * scale
    latent_v = spec_imag * norm_factor * scale
    log_scale = row_rate[None, :, None] * jnp.tanh(latent_u + col_shift[None, None, :])
    latent_w = latent_v * jnp.exp(log_scale) + col_mix[None, None, :] * latent_u
    terms = (
        -0.5 * (latent_u * latent_u + latent_w * latent_w)
        - math.log(2.0 * math.pi)
        + log_scale
        + 2.0 * jnp.log(scale)
    )
    mode_count = spec_real.size * lax.axis_size("gx") * lax.axis_size("gy")
    loglik = lax.psum(jnp.sum(terms), ("gx", "gy")) / mode_count
    return (jnp.stack([latent_u, latent_w]), loglik)


def per_device(field, *scales):
    return (four_way if lax.axis_size("gx") == 4 else any_way)(field, *scales)


def solution(mesh):
    return jax.shard_map(
        per_device,
        mesh=mesh,
        in_specs=(P(None, "gy", "gx"), P(), P("gx"), P(), P("gx"), P("gx")),
        out_specs=(P(None, "gy", None, "gx"), P()),
        check_vma=False,
    )
```

```python
import functools
import math

import jax
import jax.numpy as jnp
from jax import lax
from jax.experimental import pallas as pl
from jax.experimental.pallas import tpu as pltpu
from jax.sharding import PartitionSpec as P

precision_top = lax.Precision.HIGHEST
RADIX = 8
LANES = 128
SMALL_BYTES, Y_BYTES, X_BYTES = [size * 1024 * 1024 for size in (8, 27, 26)]


def from_partner(value, axis, stride):
    mask = 2**stride
    pairs = [(source, source ^ mask) for source in range(lax.axis_size(axis))]
    return lax.ppermute(value, axis, pairs)


def to_planes(values):
    return lax.all_to_all(values, "gy", split_axis=0, concat_axis=1, tiled=True)


def pick_columns(left, right, odd):
    lane = lax.broadcasted_iota(jnp.int32, left.shape, 1)
    index = (2 * lane + odd) & (LANES - 1)
    chosen = [jnp.take_along_axis(tile, index, axis=1, mode="promise_in_bounds") for tile in (left, right)]
    return jnp.where(lane < LANES // 2, *chosen)


def combine_kernel(sign_ref, late_ref, early_ref, *refs):
    out_ref = refs[-1]
    sign = sign_ref[0]
    for plane in range(late_ref.shape[0]):
        left, right = [
            late_ref[plane, :, pl.ds(lane, LANES)] + sign * early_ref[plane, :, pl.ds(lane, LANES)] for lane in (0, LANES)
        ]
        for odd in range(2):
            out_ref[plane, :, pl.ds(odd * LANES, LANES)] = pick_columns(left, right, odd)


def combine(sign, parts):
    planes, rows, columns = parts[0][0].shape
    result = ()
    for place, pair in enumerate(parts):
        block = pl.BlockSpec((planes // 2, rows, columns), lambda i: (i, 0, 0))
        result = pl.pallas_call(
            combine_kernel,
            out_shape=[jax.ShapeDtypeStruct((planes * len(parts), rows, columns), jnp.float32)],
            grid=(2,),
            in_specs=[pl.BlockSpec(memory_space=pltpu.SMEM), block, block]
            + [pl.BlockSpec(memory_space=pl.ANY)] * len(result),
            out_specs=[pl.BlockSpec((planes // 2, rows, columns), lambda i, place=place: (2 * place + i, 0, 0))],
            input_output_aliases={3: 0} if result else {},
            cost_estimate=pl.CostEstimate(
                flops=2 * pair[0].size, bytes_accessed=12 * pair[0].size, transcendentals=0
            ),
            compiler_params=pltpu.CompilerParams(vmem_limit_bytes=SMALL_BYTES),
            name="combine",
        )(sign, *pair, *result)
    return result[0]


def reverse_bits(value, count):
    result = value * 0
    for place in range(count):
        result = result + (value >> place & 1) * (1 << count - 1 - place)
    return result


def root_table(row_index, freqs, length):
    phase = row_index[:, None] * freqs[None, :] % length
    angle = phase.astype(jnp.float32) * (-2.0 * math.pi / length)
    return (jnp.cos(angle), jnp.sin(angle))


def x_tables(rows, width, devices, position):
    levels = devices.bit_length() - 1
    local_index = jnp.arange(width, dtype=jnp.int32)
    freqs = reverse_bits(position, levels) + devices * local_index
    return root_table(rows, freqs, devices * width)


def split_table(table):
    high = lax.reduce_precision(table, 8, 7)
    return jnp.stack([high.astype(jnp.bfloat16), (table - high).astype(jnp.bfloat16)])


def split_value(value):
    high = value.astype(jnp.bfloat16)
    return high, (value - high.astype(jnp.float32)).astype(jnp.bfloat16)


def small_fft(values):
    count = len(values)
    if count == 1:
        return values
    even, odd = small_fft(values[0::2]), small_fft(values[1::2])
    first, second = [], []
    root_half = math.sqrt(0.5)
    for place in range(count // 2):
        (er, ei), (re, im) = even[place], odd[place]
        turn = place * 8 // count
        if turn == 1:
            re, im = (re + im) * root_half, (im - re) * root_half
        elif turn == 2:
            re, im = im, -re
        elif turn == 3:
            re, im = (im - re) * root_half, (re + im) * -root_half
        first.append((er + re, ei + im))
        second.append((er - re, ei - im))
    return first + second


def dot(left, right):
    return jnp.dot(left, right, preferred_element_type=jnp.float32)


def y_kernel(count, pick, coef_ref, *refs):
    inputs, (table_ref, twist_ref, *out_refs, mix_ref, split_ref, step_ref) = refs[:count], refs[count:]
    length = mix_ref.shape[1]
    inner = length // RADIX
    rows_each = 32
    for start in range(0, length, rows_each):
        rows = pl.ds(start, rows_each)
        for which in range(2):
            tiles = []
            for lane in (0, LANES):
                mixed = inputs[0][rows, pl.ds(lane, LANES)] * coef_ref[which, 0]
                for place in range(1, count):
                    mixed = mixed + inputs[place][rows, pl.ds(lane, LANES)] * coef_ref[which, place]
                tiles.append(mixed)
            for tile in range(2):
                mix_ref[2 * tile + which, rows, :] = pick_columns(*tiles, tile) if pick else tiles[tile]
    half = inner // 2

    def split(tile):
        for which in range(2):
            for s in range(RADIX):
                for start in range(0, inner, 64):
                    parts = split_value(mix_ref[2 * tile + which, pl.ds(s + start * RADIX, 64, stride=RADIX), :])
                    for place, value in enumerate(parts):
                        split_ref[tile, place, pl.ds(which * inner + start, 64), pl.ds(s * LANES, LANES)] = value

    def multiply(tile, part):
        table = [table_ref[place, pl.ds(part * inner, inner), :] for place in (0, 1, 0)]
        values = [split_ref[tile, place] for place in (0, 0, 1)]
        step_ref[part] = dot(jnp.concatenate(table, axis=1), jnp.concatenate(values, axis=0))

    def finish(tile, part):
        for start in range(0, half, 16):
            values = []
            for s in range(RADIX):
                cols = pl.ds(s * LANES, LANES)
                re = step_ref[part, pl.ds(start, 16), cols]
                im = step_ref[part, pl.ds(half + start, 16), cols]
                if s:
                    cos, sin = [twist_ref[k, s, pl.ds(part * half + start, 16), :] for k in range(2)]
                    re, im = re * cos - im * sin, re * sin + im * cos
                values.append((re, im))
            for kb, pair in enumerate(small_fft(values)):
                rows = pl.ds(kb * inner + part * half + start, 16)
                for which in range(2):
                    high, low = split_value(pair[which])
                    out_refs[tile][2 * which, rows, :] = high
                    out_refs[tile][2 * which + 1, rows, :] = low

    jobs = [(tile, part) for tile in range(len(out_refs)) for part in range(2)]
    split(0)
    multiply(*jobs[0])
    for before, job in zip(jobs, jobs[1:]):
        if job[1]:
            if job[0] + 1 < len(out_refs):
                split(job[0] + 1)
        multiply(*job)
        finish(*before)
    finish(*jobs[-1])


def y_dft(inputs, pick, coefs, table, twist):
    length = inputs[0].shape[0]
    inner = length // RADIX
    whole = pl.BlockSpec(memory_space=pltpu.VMEM)
    return pl.pallas_call(
        functools.partial(y_kernel, len(inputs), pick),
        out_shape=[jax.ShapeDtypeStruct((4, length, LANES), jnp.bfloat16)] * 2,
        in_specs=[pl.BlockSpec(memory_space=pltpu.SMEM)] + [whole] * (len(inputs) + 2),
        out_specs=[whole] * 2,
        scratch_shapes=[
            pltpu.VMEM((4, length, LANES), jnp.float32),
            pltpu.VMEM((2, 2, 2 * inner, RADIX * LANES), jnp.bfloat16),
            pltpu.VMEM((2, inner, RADIX * LANES), jnp.float32),
        ],
        compiler_params=pltpu.CompilerParams(vmem_limit_bytes=Y_BYTES),
        cost_estimate=pl.CostEstimate(
            flops=160 * inner * length * LANES, bytes_accessed=8 * length * LANES * (len(inputs) + 3), transcendentals=0
        ),
        name="y_dft",
    )(coefs, *inputs, table, twist)


def x_kernel(count, *refs):
    parts, (even_ref, odd_ref, row_ref, col_ref, out_ref, total_ref) = refs[: 2 * count], refs[2 * count :]
    columns = out_ref.shape[3]
    lanes, rows_each, tiles = LANES, 2 * LANES, columns // (2 * LANES)
    totals = []

    def left(refs, rows):
        first = pl.multiple_of(pl.program_id(0) * out_ref.shape[2], out_ref.shape[2])
        rows = pl.ds(first + rows, rows_each)
        high, low = [[ref[k + which, rows, :] for ref in refs for k in (0, 2)] for which in range(2)]
        return jnp.concatenate(high + low + high, axis=1)

    def multiply(sides, tile):
        cols = pl.ds(tile * 2 * lanes, 2 * lanes)
        return [
            dot(side, jnp.concatenate([table_ref[place, :, cols] for place in (0, 0, 1)], axis=0))
            for side, table_ref in zip(sides, (even_ref, odd_ref))
        ]

    def row_factors(start):
        return [
            jnp.concatenate(
                [
                    jnp.broadcast_to(row_ref[which, 0, c : c + 1, :], (lanes, lanes)).T
                    for c in range(start // lanes, (start + rows_each) // lanes)
                ],
                0,
            )
            for which in range(2)
        ]

    def finish(start, tile, factors, even, odd):
        for upper in range(2):
            cols = pl.ds(upper * columns // 2 + tile * lanes, lanes)
            col_scale, col_shift, col_mix = col_ref[0:1, cols], col_ref[1:2, cols], col_ref[2:3, cols]
            total = None
            for first in range(0, rows_each, 32):
                rows, span = pl.ds(start + first, 32), slice(first, first + 32)
                spec = even[span] - odd[span] if upper else even[span] + odd[span]
                scale = factors[0][span] * col_scale
                latent_u = spec[:, :lanes] * scale
                latent_v = spec[:, lanes:] * scale
                log_scale = factors[1][span] * jnp.tanh(latent_u + col_shift)
                latent_w = latent_v * jnp.exp(log_scale) + col_mix * latent_u
                out_ref[0, 0, rows, cols] = latent_u
                out_ref[1, 0, rows, cols] = latent_w
                terms = log_scale - 0.5 * (latent_u * latent_u + latent_w * latent_w)
                terms = jnp.sum(terms.reshape(-1, 8, lanes), axis=0)
                total = terms if total is None else total + terms
            totals.append(total)

    before = None
    for start in range(0, out_ref.shape[2], rows_each):
        sides = [left(group, start) for group in (parts[:count], parts[count:])]
        factors = row_factors(start)
        for tile in range(tiles):
            products = multiply(sides, tile)
            if before is not None:
                finish(*before)
            before = (start, tile, factors, *products)
    finish(*before)

    @pl.when(pl.program_id(0) == 0)
    def _():
        total_ref[...] = jnp.zeros_like(total_ref)

    total_ref[...] += sum(totals)


def x_dft(even_parts, odd_parts, even_table, odd_table, row_pair, col_trio):
    parts, count, length = even_parts + odd_parts, len(even_parts), even_parts[0].shape[1]
    columns = even_table.shape[2]
    rows = length // row_pair.shape[1]
    whole = [pl.BlockSpec(memory_space=pltpu.VMEM)] * (len(parts) + 2)
    return pl.pallas_call(
        functools.partial(x_kernel, count),
        out_shape=(
            jax.ShapeDtypeStruct((2, 1, length, columns), jnp.float32),
            jax.ShapeDtypeStruct((8, LANES), jnp.float32),
        ),
        grid=(length // rows,),
        in_specs=whole
        + [
            pl.BlockSpec((2, 1, rows // LANES, LANES), lambda i: (0, i, 0, 0)),
            pl.BlockSpec(col_trio.shape, lambda i: (0, 0)),
        ],
        out_specs=(
            pl.BlockSpec((2, 1, rows, columns), lambda i: (0, 0, i, 0)),
            pl.BlockSpec((8, LANES), lambda i: (0, 0)),
        ),
        compiler_params=pltpu.CompilerParams(vmem_limit_bytes=X_BYTES),
        cost_estimate=pl.CostEstimate(
            flops=6 * length * even_table.size,
            bytes_accessed=16 * length * columns,
            transcendentals=2 * length * columns,
        ),
        name="x_dft",
    )(*parts, even_table, odd_table, row_pair, col_trio)


def sum_everywhere(tile):
    axes = ("gx", "gy")
    devices = lax.axis_size("gx") * lax.axis_size("gy")
    row = jnp.sum(tile, axis=0, keepdims=True)
    copies = jnp.broadcast_to(row[None], (devices,) + row.shape)
    return jnp.sum(lax.all_to_all(copies, axes, split_axis=0, concat_axis=0, tiled=True))


def four_way(field, row_scale, col_scale, row_rate, col_shift, col_mix):
    position = lax.axis_index("gx")
    planes, rows, columns = field.shape
    length, width = planes * rows, columns // 4
    groups = [slice(0, planes // 2), slice(planes // 2, None)]
    field_b, field_rest = lax.optimization_barrier((field[:, :, 2 * width :], field))
    field_a = [field_rest[group, :, : 2 * width] for group in groups]
    sign = jnp.where(position < 2, 1.0, -1.0)

    own_real = jnp.where(position == 1, -1.0, jnp.where(position == 3, 0.0, 1.0))
    other_real = jnp.where(position == 2, 0.0, 1.0)
    own_imag = jnp.where(position == 3, 1.0, 0.0)
    other_imag = jnp.where(position == 2, -1.0, 0.0)
    coefs_a = jnp.stack([own_real, other_real, own_imag, other_imag]).reshape(2, 2)
    coefs_b = jnp.concatenate([coefs_a, coefs_a * sign], axis=1)

    inner = length // RADIX
    index = jnp.arange(inner, dtype=jnp.int32)
    cos, sin = root_table(index, index, inner)
    y_table = [jnp.concatenate(pair, 1).reshape(2, 1, inner // 2, 2 * inner) for pair in ((cos, -sin), (sin, cos))]
    y_table = jnp.concatenate(y_table, 1).reshape(2 * inner, 2 * inner)
    y_table = split_table(y_table)
    grid = [lax.broadcasted_iota(jnp.int32, (RADIX, inner, LANES), axis) for axis in range(2)]
    angle = (grid[0] * grid[1]).astype(jnp.float32) * (-2.0 * math.pi / length)
    twist = jnp.stack([jnp.cos(angle), jnp.sin(angle)])
    order = jnp.arange(width, dtype=jnp.int32) * 2

    def x_table(odd):
        rows = jnp.concatenate([order + (2 * width + odd), order + odd])
        cos, sin = [part[:, : 2 * width] for part in x_tables(rows, columns, 4, position)]

        def lay(left, right):
            spans = [slice(tile * width, (tile + 1) * width) for tile in range(2)]
            return jnp.concatenate([side[:, span] for span in spans for side in (left, right)], 1)

        real, imag = lay(cos, sin), lay(-sin, cos)
        table = jnp.concatenate([real[:width], imag[:width], real[width:], imag[width:]], 0)
        return split_table(table)

    norm = 1.0 / math.sqrt(length * columns * 4)
    row_pair = jnp.stack([row_scale * norm, row_rate]).reshape(2, 4, length // 4 // LANES, LANES)
    col_trio = jnp.stack([col_scale, col_shift, col_mix])
    fixed = 2.0 * (columns * jnp.sum(jnp.log(row_scale)) + length * jnp.sum(jnp.log(col_scale)))
    fixed = fixed - length * columns * math.log(2.0 * math.pi)

    first_a = combine(sign.reshape(1), [(from_partner(part, "gx", 1), part) for part in field_a])
    tables = (y_table, twist, x_table(0), x_table(1), row_pair, col_trio, coefs_a, coefs_b, fixed)
    first_a, first_b, tables = lax.optimization_barrier((first_a, to_planes(field_b)[0], tables))
    y_table, twist, even_table, odd_table, row_pair, col_trio, coefs_a, coefs_b, fixed = tables
    second_a = to_planes(first_a)[0]
    second_b = from_partner(first_b, "gx", 1)
    group = [second_b, from_partner(second_b, "gx", 0), first_b, from_partner(first_b, "gx", 0)]
    even_b, odd_b = y_dft(group, True, coefs_b, y_table, twist)
    even_a, odd_a = y_dft([second_a, from_partner(second_a, "gx", 0)], False, coefs_a, y_table, twist)
    latent, tile = x_dft([even_b, even_a], [odd_b, odd_a], even_table, odd_table, row_pair, col_trio)
    tile = tile + fixed / tile.size
    modes = length * columns * lax.axis_size("gx") * lax.axis_size("gy")
    return (latent, sum_everywhere(tile) / modes)


def complex_einsum(form, real_part, imag_part, cos_part, sin_part):
    first = jnp.einsum(form, real_part, cos_part, precision=precision_top)
    second = jnp.einsum(form, real_part, sin_part, precision=precision_top)
    first = first - jnp.einsum(form, imag_part, sin_part, precision=precision_top)
    second = second + jnp.einsum(form, imag_part, cos_part, precision=precision_top)
    return (first, second)


def x_butterfly(field):
    devices = lax.axis_size("gx")
    levels = devices.bit_length() - 1
    position = lax.axis_index("gx")
    real_part, imag_part = field, jnp.zeros_like(field)
    for level in range(levels - 1, -1, -1):
        half = 1 << level
        lower = position // half % 2 == 0
        offset = position % half
        angle = offset.astype(jnp.float32) * (-math.pi / half)
        cos_twist = jnp.where(lower, 1.0, jnp.cos(angle))
        sin_twist = jnp.where(lower, 0.0, jnp.sin(angle))
        other = from_partner(jnp.stack([real_part, imag_part]), "gx", level)
        diff_real = jnp.where(lower, real_part + other[0], other[0] - real_part)
        diff_imag = jnp.where(lower, imag_part + other[1], other[1] - imag_part)
        real_part = diff_real * cos_twist - diff_imag * sin_twist
        imag_part = diff_real * sin_twist + diff_imag * cos_twist
    width = field.shape[2]
    cos_part, sin_part = x_tables(jnp.arange(width, dtype=jnp.int32), width, devices, position)
    real_part, imag_part = complex_einsum("zyn,nk->zyk", real_part, imag_part, cos_part, sin_part)
    return (to_planes(real_part), to_planes(imag_part))


def y_transform(real_part, imag_part):
    planes, length, width = real_part.shape
    outer = 1 << (length.bit_length() - 1) // 2
    inner = length // outer
    outer_index = jnp.arange(outer, dtype=jnp.int32)
    inner_index = jnp.arange(inner, dtype=jnp.int32)
    cos_one, sin_one = root_table(outer_index, outer_index, outer)
    cos_two, sin_two = root_table(inner_index, inner_index, inner)
    cos_mid, sin_mid = root_table(outer_index, inner_index, length)
    shaped_real = real_part.reshape(planes, outer, inner, width)
    shaped_imag = imag_part.reshape(planes, outer, inner, width)
    step_real, step_imag = complex_einsum("zabc,ak->zkbc", shaped_real, shaped_imag, cos_one, sin_one)
    twist_cos = cos_mid[None, :, :, None]
    twist_sin = sin_mid[None, :, :, None]
    turned_real = step_real * twist_cos - step_imag * twist_sin
    turned_imag = step_real * twist_sin + step_imag * twist_cos
    final_real, final_imag = complex_einsum("zkbc,bj->zjkc", turned_real, turned_imag, cos_two, sin_two)
    return (final_real.reshape(planes, length, width), final_imag.reshape(planes, length, width))


def any_way(field, row_scale, col_scale, row_rate, col_shift, col_mix):
    spec_real, spec_imag = y_transform(*x_butterfly(field))
    length = spec_real.shape[1]
    total_cols = spec_real.shape[2] * lax.axis_size("gx")
    norm_factor = 1.0 / math.sqrt(length * total_cols)
    scale = row_scale[None, :, None] * col_scale[None, None, :]
    latent_u = spec_real * norm_factor * scale
    latent_v = spec_imag * norm_factor * scale
    log_scale = row_rate[None, :, None] * jnp.tanh(latent_u + col_shift[None, None, :])
    latent_w = latent_v * jnp.exp(log_scale) + col_mix[None, None, :] * latent_u
    terms = (
        -0.5 * (latent_u * latent_u + latent_w * latent_w)
        - math.log(2.0 * math.pi)
        + log_scale
        + 2.0 * jnp.log(scale)
    )
    mode_count = spec_real.size * lax.axis_size("gx") * lax.axis_size("gy")
    loglik = lax.psum(jnp.sum(terms), ("gx", "gy")) / mode_count
    return (jnp.stack([latent_u, latent_w]), loglik)


def per_device(field, *scales):
    return (four_way if lax.axis_size("gx") == 4 else any_way)(field, *scales)


def solution(mesh):
    return jax.shard_map(
        per_device,
        mesh=mesh,
        in_specs=(P(None, "gy", "gx"), P(), P("gx"), P(), P("gx"), P("gx")),
        out_specs=(P(None, "gy", None, "gx"), P()),
        check_vma=False,
    )
```
